32 devices in a mesh: cuts: 2 (over y), samp: 2 (over core), blk: 4 (over z), tile: 2 (over x).
Axes of the slice: x: 2, y: 2, z: 4, core: 2. Of those that a mesh axis runs over, the one named last changes fastest.
Arguments:
- residual: bfloat16 [2, 4096, 2, 512], P('samp', ('cuts', 'blk', 'tile')), parts along dimension 1, may hold values from -0.25 to 0.25
- uv_offsets: float32 [4096, 2, 512], P(('cuts', 'blk', 'tile')), parts along dimension 0, may hold values from -16 to 16
- counts: int32 [4096], P(('cuts', 'blk', 'tile')), parts along dimension 0, may hold values from 128 to 512
- tile_of_block: int32 [4096, 1], P(('cuts', 'blk', 'tile')), parts along dimension 0, may hold values from 0 to 7; in each aligned block of 256 rows (0 to 255, 256 to 511, ...) at most 64 rows name the same one
- slot_of_block: int32 [4096], P(('cuts', 'blk', 'tile')), parts along dimension 0, may hold values from 0 to 127
- owner_map: int32 [8], replicated, may hold values from 0 to 7, each once
Outputs:
- grid_tiles: float32 [512, 2, 4096], P(('cuts', 'blk', 'tile')), parts along dimension 0
The draws below stay inside these ranges and needn't reach their ends.
There are 2 independent parts, one for each index of `cuts`. The reference program is written for one: setup_inputs(seed, part) draws one part's arguments, and reference() takes and returns one part's arrays. A program takes and returns all parts, laid end to end along the dimension named above; an argument that names none is the same for every part. Nothing has to cross between parts.
Inputs may be any that keep to these rules, and one draw needn't show every extreme that they name: `tile_of_block`: in the rows of one device, no tile is named by more than 64 blocks; some tile is named by exactly 64. `owner_map`: each tile has one owner and each owner one tile.
All inputs are finite; a program needn't handle non-finite values.
Results may differ from the reference program's by a relative error of at most 0.0047.
Values may be sent and summed in bfloat16 or wider, within the bound.
No kernel may reach another device: no remote copies, remote signals or barrier semaphores. Data moves between devices by JAX's collectives and lax.ppermute only.
A program may use at most 64 MiB of HBM per device.

```python
import math
import jax
import jax.numpy as jnp
import numpy as np
from jax import lax

SUB = 32
SLOTS = 128
VB = 512
BLK_DEV = 256
SAMPLES = 2
TILES = 8
BLOCKS = 2048
CAP = 64


def touch_ends(array, stream_key, least, top_value):
    longest = array.shape.index(max(array.shape))
    spots = []
    for shift in (0, 1):
        where = [jax.random.randint(jax.random.fold_in(stream_key, axis), (), 0, length) for axis, length in enumerate(array.shape)]
        where[longest] = (where[longest] + shift) % array.shape[longest]
        spots.append(tuple(where))
    return array.at[spots[0]].set(least).at[spots[1]].set(top_value)


def block_levels(stream_key, dims, cuts, low, top_value):
    def one(axis_at, blocks):
        heights = jax.random.uniform(jax.random.fold_in(jax.random.fold_in(stream_key, 6), axis_at), (blocks,), jnp.float32, low / len(cuts), top_value / len(cuts))
        return jnp.repeat(jnp.exp(heights), dims[axis_at] // blocks).reshape((-1,) + (1,) * (len(dims) - axis_at - 1))

    factor_of = one(*cuts[0])
    for cut in cuts[1:]:
        factor_of = factor_of * one(*cut)
    return factor_of


def assign_block(rng, own, number, rows, count, top, reach, slope):
    ranking = jax.random.permutation(rng, count)
    crowded, ordinary = shares(count, rows * top, reach, slope, True), shares(count, rows * top, reach, slope, False)
    places = jnp.arange(count)

    def named(sizes, rotation):
        used = int((sizes > 0).sum())
        fixed = max(1, used // 4)
        shifted = fixed + (places - fixed + rotation * (used - fixed)) % max(1, count - fixed)
        return jnp.zeros((count,), jnp.int32).at[ranking[jnp.where(places < fixed, places, shifted)]].set(jnp.asarray(sizes, jnp.int32))

    sizes = jnp.where(number % 4 == 0, named(crowded, number // 4), named(ordinary, number - number // 4 - 1))
    mixed = jax.random.permutation(jax.random.fold_in(own, 3), count)
    donor, sink = mixed[0:count // 2 * 2:2], mixed[1:count // 2 * 2:2]
    margin = jnp.minimum(sizes[donor] - 1, reach - sizes[sink]) // 2
    margin = jnp.where((donor == ranking[0]) | (sink == ranking[0]) | (sizes[sink] == 0), 0, jnp.maximum(margin, 0))
    shifted = jax.random.randint(jax.random.fold_in(own, 4), (count // 2,), 0, 1 << 20) % (margin + 1)
    sizes = sizes.at[donor].add(-shifted).at[sink].add(shifted)
    members = jnp.searchsorted(jnp.cumsum(sizes), jnp.arange(rows * top), side="right").astype(jnp.int32)
    grid = members.reshape(top, rows).T
    grid = grid[jax.random.permutation(jax.random.fold_in(own, 1), rows)]
    rotation = jax.random.randint(jax.random.fold_in(own, 2), (rows, 1), 0, top)
    return jnp.take_along_axis(grid, (jnp.arange(top)[None, :] + rotation) % top, axis=1)


def shares(count, total, bound, slope, full):
    loads = [(1 << 20) // math.isqrt(standing ** slope) + 1 for standing in range(1, count + 1)]
    largest = bound if full else min(bound, max(-(-total // count), total * loads[0] // sum(loads)))
    least = 1 if total - largest >= count - 1 else 0
    given, rest = [largest] + [least] * (count - 1), total - largest - least * (count - 1)
    while rest > 0:
        candidates = [i for i in range(1, count) if given[i] < largest] or [i for i in range(1, count) if given[i] < bound]
        pool, remaining = sum([loads[i] for i in candidates]), rest
        for i in candidates:
            addition = min(bound - given[i], max(1, remaining * loads[i] // pool), rest)
            given[i] = given[i] + addition
            rest = rest - addition
    return np.array(given)


def scatter_about(stream_key, shape, deviation, bound, cuts=(), held_as=jnp.bfloat16):
    result = deviation * jax.random.normal(stream_key, shape, jnp.float32)
    if cuts:
        result = result * block_levels(stream_key, shape, cuts, -0.22, 0.18)
    return jnp.clip(result, -bound, bound).astype(held_as)


def setup_inputs(seed: int = 0, part: int = 0) -> dict:
    key_list = jax.random.split(jax.random.key(seed), 7)
    part_splits = jax.random.split(jax.random.fold_in(key_list[6], part), 7)
    residual = scatter_about(part_splits[0], (SAMPLES, BLOCKS, 2, VB), VB ** -0.5, 0.25, ((0, 2), (1, 8)))
    uv_offsets = jnp.clip(jax.random.uniform(part_splits[1], (BLOCKS, 2, VB), jnp.float32, -16.0, 16.0) * block_levels(part_splits[1], (BLOCKS, 2, VB), ((0, 8),), -0.4, 0.0), -16.0, 16.0)
    counts = touch_ends(jax.random.randint(part_splits[2], (BLOCKS,), VB // 4, VB + 1), jax.random.fold_in(part_splits[2], 1), VB // 4, VB).astype(jnp.int32)
    tile_of_block_keys = jax.random.split(jax.random.fold_in(part_splits[3], 1), BLOCKS // BLK_DEV)
    tile_of_block_turns = jax.random.permutation(jax.random.fold_in(part_splits[3], 3), BLOCKS // BLK_DEV)
    tile_of_block = jax.vmap(lambda own, number: assign_block(jax.random.fold_in(part_splits[3], 2), own, number, BLK_DEV, TILES, 1, CAP, 2))(tile_of_block_keys, tile_of_block_turns).reshape((BLOCKS, 1))
    slot_of_block = touch_ends(jax.random.randint(part_splits[4], (BLOCKS,), 0, SLOTS), jax.random.fold_in(part_splits[4], 1), 0, SLOTS - 1).astype(jnp.int32)
    owner_map = jax.random.permutation(key_list[5], TILES).astype(jnp.int32)
    return {"residual": residual, "uv_offsets": uv_offsets, "counts": counts, "tile_of_block": tile_of_block, "slot_of_block": slot_of_block, "owner_map": owner_map}


def kernels(resid_piece, uv_piece, count_piece):
    vis_count = resid_piece.shape[-1]
    centre = (jnp.arange(SUB, dtype=jnp.float32) - SUB / 2.0) / SUB
    live_mask = (jnp.arange(vis_count)[None, :] < count_piece[:, None]).astype(jnp.float32)
    phase_rows = 2.0 * jnp.pi * uv_piece[:, 0, :, None] * centre
    phase_cols = 2.0 * jnp.pi * uv_piece[:, 1, :, None] * centre
    real_part = resid_piece[:, 0, :, None].astype(jnp.float32) * live_mask[..., None]
    imag_part = resid_piece[:, 1, :, None].astype(jnp.float32) * live_mask[..., None]
    left_real = real_part * jnp.cos(phase_rows) - imag_part * jnp.sin(phase_rows)
    left_imag = real_part * jnp.sin(phase_rows) + imag_part * jnp.cos(phase_rows)
    left_kernel = jnp.concatenate([left_real, left_imag], -1).astype(jnp.bfloat16)
    right_kernel = jnp.concatenate([jnp.cos(phase_cols), jnp.sin(phase_cols)], -1).astype(jnp.bfloat16)
    return left_kernel, right_kernel


def combine(products):
    sum_real = products[:, :SUB, :SUB] - products[:, SUB:, SUB:]
    sum_imag = products[:, :SUB, SUB:] + products[:, SUB:, :SUB]
    stacked = jnp.stack([sum_real, sum_imag], 2).astype(jnp.bfloat16)
    return stacked.reshape(products.shape[0], 2 * SUB * SUB)


def reference(residual, uv_offsets, counts, tile_of_block, slot_of_block, owner_map):
    blocks = uv_offsets.shape[0]
    group_count = blocks // BLK_DEV
    flat_slot = (tile_of_block[:, 0] * SLOTS + slot_of_block).astype(jnp.int32)
    uv_groups = uv_offsets.reshape((group_count, BLK_DEV) + uv_offsets.shape[1:])
    count_groups = counts.reshape(group_count, BLK_DEV)
    slot_groups = flat_slot.reshape(group_count, BLK_DEV)
    running = jnp.zeros((TILES * SLOTS, 2 * SUB * SUB), jnp.float32)
    for sample in range(SAMPLES):
        resid_groups = residual[sample].reshape((group_count, BLK_DEV) + residual.shape[2:])

        def add_group(total, pieces):
            resid_piece, uv_piece, count_piece, indices = pieces
            left_kernel, right_kernel = kernels(resid_piece, uv_piece, count_piece)
            products = jnp.einsum("bkp,bkq->bpq", left_kernel.astype(jnp.float32), right_kernel.astype(jnp.float32), precision=lax.Precision.HIGHEST)
            subgrid = combine(products)
            return total.at[indices].add(subgrid.astype(jnp.float32)), None

        running, _ = lax.scan(add_group, running, (resid_groups, uv_groups, count_groups, slot_groups))
    tile_sum = running.reshape(TILES, SLOTS, SUB, 2, SUB)
    by_owner = jnp.zeros_like(tile_sum).at[owner_map].set(tile_sum)
    return by_owner.transpose(0, 2, 3, 1, 4).reshape(TILES * SUB, 2, SLOTS * SUB)
```

```python
import itertools

import jax
import jax.numpy as jnp
import numpy as np
from jax import lax
from jax.experimental import pallas as pl
from jax.experimental.pallas import tpu as pltpu
from jax.sharding import PartitionSpec as P

SUB = 32
HALF = SUB // 2
SLOTS = 128
FEATURE = 2 * HALF * SUB
CAP_MIN = 8
GROUP = 8
QUAD = 4
VMEM_LIMIT = 48 * 1024 * 1024


def turn_coefficients():
    knots = np.cos(np.pi * (np.arange(400) + 0.5) / 400)
    cheb = np.polynomial.chebyshev
    even = cheb.cheb2poly(cheb.chebfit(knots, np.cos(np.pi * knots), 12))[0::2]
    odd = cheb.cheb2poly(cheb.chebfit(knots, np.sin(np.pi * knots), 13))[1::2]
    return [float(x) for x in even], [float(x) for x in odd]


COS_COEF, SIN_COEF = turn_coefficients()


def horner(coef, x):
    total = coef[-1] * x + coef[-2]
    for value in coef[-3::-1]:
        total = total * x + value
    return total


def harmonics(offset):
    y = offset * (1.0 / HALF)
    x = y * y
    c1, s1 = horner(COS_COEF, x), horner(SIN_COEF, x) * y
    c2, s2 = 1.0 - 2.0 * s1 * s1, 2.0 * s1 * c1
    c3, s3 = c2 * c1 - s2 * s1, s2 * c1 + c2 * s1
    c4, s4 = 1.0 - 2.0 * s2 * s2, 2.0 * s2 * c2
    c8, s8 = 1.0 - 2.0 * s4 * s4, 2.0 * s4 * c4
    return (c1, c2, c3, c4, c8), (s1, s2, s3, s4, s8)


def fill_table(cos_ref, sin_ref, c, s):
    one = jnp.ones_like(c[0])
    cos_rows = (c[3], c[2], c[1], c[0], one, c[0], c[1], c[2])
    sin_rows = (-s[3], -s[2], -s[1], -s[0], jnp.zeros_like(one), s[0], s[1], s[2])
    for r in range(GROUP):
        for t in range(one.shape[1] // 128):
            at = pl.ds(t * GROUP * GROUP + r, GROUP, stride=GROUP)
            cos_ref[at, :] = cos_rows[r][:, t * 128 : (t + 1) * 128]
            sin_ref[at, :] = sin_rows[r][:, t * 128 : (t + 1) * 128]


def pair(halves):
    return jnp.concatenate(halves, 0).astype(jnp.bfloat16)


def subgrid_kernel(
    row_ref, side_ref, u_ref, v_ref, re_ref, im_ref, out_ref,
    cos_u, sin_u, cos_v, sin_v, dense, lefts, rights, stage,
):
    blocks = u_ref.shape[0]
    vis = u_ref.shape[1]
    rows = out_ref.shape[0]
    side = side_ref[0].astype(jnp.float32)
    lane = lax.broadcasted_iota(jnp.int32, (GROUP, 128), 1) // SUB

    @pl.loop(0, rows // 8)
    def _(i):
        stage[pl.ds(pl.multiple_of(i * 64, 64), 64), :] = jnp.zeros((64, 128), jnp.float32)

    @pl.loop(0, blocks // GROUP)
    def _(g):
        here = pl.ds(pl.multiple_of(g * GROUP, GROUP), GROUP)
        c, s = harmonics(u_ref[here, :])
        fill_table(cos_u, sin_u, c, s)
        s8 = s[4] * side
        re, im = re_ref[here, :], im_ref[here, :]
        vr, vi = re * c[4] - im * s8, re * s8 + im * c[4]
        a, b, e, f = vr * c[3], vi * s[3], vi * c[3], vr * s[3]
        dense[0] = a + b
        dense[1] = e - f
        dense[2] = a - b
        dense[3] = e + f
        c, s = harmonics(v_ref[here, :])
        fill_table(cos_v, sin_v, c, s)
        dense[4] = c[3]
        dense[5] = s[3]
        dense[6] = c[4] * c[3] - s[4] * s[3]
        dense[7] = s[4] * c[3] + c[4] * s[3]
        for quad in range(GROUP // QUAD):
            left, right = lefts.at[quad], rights.at[quad]
            for b, t in itertools.product(range(QUAD), range(vis // 128)):
                i = quad * QUAD + b
                mine = pl.ds((t * GROUP + i) * GROUP, GROUP)
                lanes = pl.ds(t * 128, 128)

                def spread(k):
                    return jnp.broadcast_to(dense[k, pl.ds(i, 1), lanes], (GROUP, 128))

                fc, fs = cos_u[mine, :], sin_u[mine, :]
                real, imag = [], []
                for h in range(2):
                    wr, wi = spread(2 * h), spread(2 * h + 1)
                    real.append(fc * wr - fs * wi)
                    imag.append(fs * wr + fc * wi)
                left[pl.ds(b * SUB, HALF), lanes] = pair(real)
                left[pl.ds(b * SUB + HALF, HALF), lanes] = pair(imag)
                gc, gs = cos_v[mine, :], sin_v[mine, :]
                cos_rows, sin_rows = [None] * 4, [None] * 4
                for h, (low, high) in enumerate(((1, 2), (0, 3))):
                    ch, sh = spread(4 + 2 * h), spread(5 + 2 * h)
                    p, q, r, x = gc * ch, gs * sh, gs * ch, gc * sh
                    cos_rows[low], cos_rows[high] = p + q, p - q
                    sin_rows[low], sin_rows[high] = r - x, r + x
                for h in range(2):
                    at = b * SUB + h * HALF
                    right[pl.ds(at, HALF), lanes] = pair(cos_rows[2 * h : 2 * h + 2])
                    right[pl.ds(QUAD * SUB + at, HALF), lanes] = pair(sin_rows[2 * h : 2 * h + 2])
            product = lax.dot_general(
                left[...], right[...], (((1,), (1,)), ((), ())), preferred_element_type=jnp.float32
            )
            for b in range(QUAD):
                mine = product[b * SUB : (b + 1) * SUB]
                with_cos, with_sin = mine[:, :128], mine[:, 128:]
                real = with_cos[:HALF] - with_sin[HALF:]
                imag = with_cos[HALF:] + with_sin[:HALF]
                parts = (real[:GROUP], real[GROUP:], imag[:GROUP], imag[GROUP:])
                total = None
                for k in range(4):
                    moved = parts[k]
                    if k != b:
                        moved = pltpu.roll(moved, ((k - b) % 4) * SUB, 1)
                    total = moved if total is None else jnp.where(lane == k, moved, total)
                row = row_ref[g * GROUP + quad * QUAD + b]
                stage[pl.ds(pl.multiple_of(row * 8, 8), 8), :] = total

    @pl.loop(0, rows // 16)
    def _(i):
        for k in range(8):
            piece = stage[pl.ds(i * 128 + k, 16, stride=8), :]
            out_ref[pl.ds(pl.multiple_of(i * 16, 16), 16), pl.ds(k * 128, 128)] = piece.astype(
                jnp.bfloat16
            )


def make_subgrids(rows, target, side, u, v, re, im):
    vis = u.shape[1]
    vmem = pl.BlockSpec(memory_space=pltpu.VMEM)
    smem = pl.BlockSpec(memory_space=pltpu.SMEM)
    table = pltpu.VMEM((GROUP * GROUP * (vis // 128), 128), jnp.float32)
    return pl.pallas_call(
        subgrid_kernel,
        out_shape=jax.ShapeDtypeStruct((rows, FEATURE), jnp.bfloat16),
        in_specs=[smem, smem, vmem, vmem, vmem, vmem],
        out_specs=vmem,
        scratch_shapes=[
            table, table, table, table,
            pltpu.VMEM((8, GROUP, vis), jnp.float32),
            pltpu.VMEM((GROUP // QUAD, QUAD * SUB, vis), jnp.bfloat16),
            pltpu.VMEM((GROUP // QUAD, 2 * QUAD * SUB, vis), jnp.bfloat16),
            pltpu.VMEM((rows * 8, 128), jnp.float32),
        ],
        compiler_params=pltpu.CompilerParams(vmem_limit_bytes=VMEM_LIMIT),
        name="subgrids",
    )(target, side, u, v, re, im)


def gather_kernel(slot_ref, x_ref, out_ref, hot, part):
    rows = x_ref.shape[0]
    lane = lax.broadcasted_iota(jnp.int32, (GROUP, 128), 1) // SUB
    wanted = lax.broadcasted_iota(jnp.int32, (SLOTS, rows), 0)
    wanted = (wanted % 32) * 4 + wanted // 32
    hot[...] = jnp.where(slot_ref[...] == wanted, 1.0, 0.0).astype(jnp.bfloat16)
    for k in range(8):
        part[...] = jnp.dot(
            hot[...], x_ref[:, pl.ds(k * 128, 128)], preferred_element_type=jnp.float32
        )
        for grp in range(4):
            given = [part[pl.ds(32 * jl + 8 * grp, 8), :] for jl in range(4)]
            for a in range(4):
                total = None
                for jl in range(4):
                    moved = given[jl]
                    if a != jl:
                        moved = pltpu.roll(moved, ((jl - a) % 4) * SUB, 1)
                    total = moved if total is None else jnp.where(lane == jl, moved, total)
                p = (a % 2) * 8 + k
                out_ref[pl.ds(p * 64 + grp * 16 + a // 2, 8, stride=2), :] = total


def sum_slots(slots, arrived):
    rows = arrived.shape[0]
    vmem = pl.BlockSpec(memory_space=pltpu.VMEM)
    return pl.pallas_call(
        gather_kernel,
        out_shape=jax.ShapeDtypeStruct((HALF * 64, 128), jnp.float32),
        in_specs=[vmem, vmem],
        out_specs=vmem,
        scratch_shapes=[
            pltpu.VMEM((SLOTS, rows), jnp.bfloat16),
            pltpu.VMEM((SLOTS, 128), jnp.float32),
        ],
        compiler_params=pltpu.CompilerParams(vmem_limit_bytes=VMEM_LIMIT),
        name="sum_slots",
    )(slots, arrived)


def local(residual, uv_offsets, counts, tile_of_block, slot_of_block, owner_map):
    blocks, _, vis = uv_offsets.shape
    owners = owner_map.shape[0]
    capacity = max(CAP_MIN, 2 * blocks // owners)
    rows = owners * capacity
    core = lax.axis_index("samp")
    me = lax.axis_index(("blk", "tile"))
    swap = [(0, 1), (1, 0)]
    own = residual[0]
    other = lax.ppermute(own, "samp", swap)

    tile_ids = tile_of_block[:, 0]
    owner_range = jnp.arange(owners, dtype=jnp.int32)
    owner_ids = jnp.sum(
        jnp.where(tile_ids[:, None] == owner_range[None, :], owner_map[None, :], 0), 1
    )
    code = owner_ids * SLOTS + slot_of_block
    codes = lax.all_gather(code, ("blk", "tile"), axis=0, tiled=False)
    same_owner = (owner_ids[:, None] == owner_range[None, :]).astype(jnp.int32)
    earlier = jnp.sum((jnp.cumsum(same_owner, 0) - same_owner) * same_owner, 1)
    target = owner_ids * capacity + earlier

    live = jnp.arange(vis, dtype=jnp.int32)[None, :] < counts[:, None]
    both = own.astype(jnp.float32) + other.astype(jnp.float32)
    both = jnp.where(live[:, None, :], both, 0.0)
    side = (2 * core - 1).astype(jnp.int32).reshape(1)
    outgoing = make_subgrids(
        rows, target, side, uv_offsets[:, 0], uv_offsets[:, 1], both[:, 0], both[:, 1]
    )
    arrived = lax.all_to_all(
        outgoing.reshape(owners, capacity, FEATURE), ("blk", "tile"),
        split_axis=0, concat_axis=0, tiled=True,
    ).reshape(rows, FEATURE)

    mine = (codes // SLOTS == me).astype(jnp.int32)
    order = jnp.cumsum(mine, 1) - mine
    place = jnp.where(mine > 0, order, capacity)
    rank = jnp.arange(capacity, dtype=jnp.int32)
    slots = jnp.sum(
        jnp.where(place[:, None, :] == rank[None, :, None], codes[:, None, :] % SLOTS + 1, 0), 2
    )
    slots = jnp.where(slots > 0, slots - 1, SLOTS).reshape(1, rows)
    half = sum_slots(slots, arrived)
    half = half.reshape(HALF, SLOTS // 4, 2, 128).transpose(0, 2, 1, 3).reshape(HALF, 2, SLOTS * SUB)
    theirs = lax.ppermute(half, "samp", swap)
    return jnp.where(
        core == 0,
        jnp.concatenate([half, theirs], 0),
        jnp.concatenate([theirs, half], 0),
    )


def solution(mesh):
    in_specs = (
        P("samp", ("cuts", "blk", "tile"), None, None),
        P(("cuts", "blk", "tile"), None, None),
        P(("cuts", "blk", "tile")),
        P(("cuts", "blk", "tile"), None),
        P(("cuts", "blk", "tile")),
        P(),
    )
    out_specs = P(("cuts", "blk", "tile"), None, None)
    return jax.shard_map(local, mesh=mesh, in_specs=in_specs, out_specs=out_specs, check_vma=False)
```

```python
import functools

import jax
import jax.numpy as jnp
import numpy as np
from jax import lax
from jax.experimental import pallas as pl
from jax.experimental.pallas import tpu as pltpu
from jax.sharding import PartitionSpec as P

SUB = 32
HALF = SUB // 2
SLOTS = 128
FEATURE = 2 * HALF * SUB
CAP_MIN = 8
GROUP = 8
QUAD = 4
PAIRED_MAX = 16
VMEM_LIMIT = 48 * 1024 * 1024


def turn_coefficients():
    knots = np.cos(np.pi * (np.arange(400) + 0.5) / 400)
    cheb = np.polynomial.chebyshev
    even = cheb.cheb2poly(cheb.chebfit(knots, np.cos(np.pi * knots), 12))[0::2]
    odd = cheb.cheb2poly(cheb.chebfit(knots, np.sin(np.pi * knots), 13))[1::2]
    return [float(x) for x in even], [float(x) for x in odd]


COS_COEF, SIN_COEF = turn_coefficients()


def horner(coef, x):
    total = coef[-1] * x + coef[-2]
    for value in coef[-3::-1]:
        total = total * x + value
    return total


def harmonics(offset):
    y = offset * (1.0 / HALF)
    x = y * y
    c1, s1 = horner(COS_COEF, x), horner(SIN_COEF, x) * y
    c2, s2 = 1.0 - 2.0 * s1 * s1, 2.0 * s1 * c1
    c3, s3 = c2 * c1 - s2 * s1, s2 * c1 + c2 * s1
    c4, s4 = 1.0 - 2.0 * s2 * s2, 2.0 * s2 * c2
    c8, s8 = 1.0 - 2.0 * s4 * s4, 2.0 * s4 * c4
    return (c1, c2, c3, c4, c8), (s1, s2, s3, s4, s8)


def fill_table(cos_ref, sin_ref, c, s):
    one = jnp.ones_like(c[0])
    cos_rows = (c[3], c[2], c[1], c[0], one, c[0], c[1], c[2])
    sin_rows = (-s[3], -s[2], -s[1], -s[0], jnp.zeros_like(one), s[0], s[1], s[2])
    for r in range(GROUP):
        for t in range(one.shape[1] // 128):
            at = pl.ds(t * GROUP * GROUP + r, GROUP, stride=GROUP)
            cos_ref[at, :] = cos_rows[r][:, t * 128 : (t + 1) * 128]
            sin_ref[at, :] = sin_rows[r][:, t * 128 : (t + 1) * 128]


def pair(halves):
    return jnp.concatenate(halves, 0).astype(jnp.bfloat16)


def subgrid_kernel(
    first, capacity, order_ref, start_ref, side_ref, uv_ref, res_ref, out_ref,
    gathered, cos_u, sin_u, cos_v, sin_v, dense, lefts, rights, stage,
):
    tiles = gathered.shape[0] // (4 * GROUP)
    vis = tiles * 128
    side = side_ref[0].astype(jnp.float32)
    lane = lax.broadcasted_iota(jnp.int32, (GROUP, 128), 1) // SUB

    def wide(ref, row, stride=1, step=GROUP):
        return jnp.concatenate(
            [ref[pl.ds(row + t * step, GROUP, stride=stride), :] for t in range(tiles)], 1
        )

    def serve(index):
        start = start_ref[first + index]
        count = start_ref[first + index + 1] - start
        turns = (count + GROUP - 1) // GROUP

        @pl.loop(turns, capacity // GROUP)
        def _(g):
            at = pl.ds(pl.multiple_of(g * GROUP * 8, GROUP * 8), GROUP * 8)
            stage[at, :] = jnp.zeros((GROUP * 8, 128), jnp.float32)

        @pl.loop(0, turns)
        def _(g):
            for i in range(GROUP):
                block = order_ref[start + g * GROUP + i]
                at = pl.ds(pl.multiple_of(block * 2 * tiles, 2 * tiles), 2 * tiles)
                gathered[pl.ds(i, 2 * tiles, stride=GROUP), :] = uv_ref[at, :]
                gathered[pl.ds(2 * tiles * GROUP + i, 2 * tiles, stride=GROUP), :] = res_ref[at, :]
            u, v, re, im = [
                wide(gathered, (k // 2) * 2 * tiles * GROUP + (k % 2) * GROUP, step=2 * GROUP)
                for k in range(4)
            ]

            def keep(k, value):
                for t in range(tiles):
                    dense[pl.ds((k * tiles + t) * GROUP, GROUP), :] = value[:, t * 128 : (t + 1) * 128]

            c, s = harmonics(u)
            fill_table(cos_u, sin_u, c, s)
            s8 = s[4] * side
            vr, vi = re * c[4] - im * s8, re * s8 + im * c[4]
            a, b, e, f = vr * c[3], vi * s[3], vi * c[3], vr * s[3]
            keep(0, a + b)
            keep(1, e - f)
            keep(2, a - b)
            keep(3, e + f)
            c, s = harmonics(v)
            fill_table(cos_v, sin_v, c, s)
            keep(4, c[3])
            keep(5, s[3])
            keep(6, c[4] * c[3] - s[4] * s[3])
            keep(7, s[4] * c[3] + c[4] * s[3])
            for quad in range(GROUP // QUAD):
                left, right = lefts.at[quad], rights.at[quad]
                for b in range(QUAD):
                    i = quad * QUAD + b

                    def spread(k):
                        return wide(dense, k * tiles * GROUP + i, stride=0)

                    def table(ref):
                        return wide(ref, i * GROUP, step=GROUP * GROUP)

                    fc, fs = table(cos_u), table(sin_u)
                    real, imag = [], []
                    for h in range(2):
                        wr, wi = spread(2 * h), spread(2 * h + 1)
                        real.append(fc * wr - fs * wi)
                        imag.append(fs * wr + fc * wi)
                    left[pl.ds(b * SUB, HALF), :] = pair(real)
                    left[pl.ds(b * SUB + HALF, HALF), :] = pair(imag)
                    gc, gs = table(cos_v), table(sin_v)
                    cos_rows, sin_rows = [None] * 4, [None] * 4
                    for h, (low, high) in enumerate(((1, 2), (0, 3))):
                        ch, sh = spread(4 + 2 * h), spread(5 + 2 * h)
                        p, q, r, x = gc * ch, gs * sh, gs * ch, gc * sh
                        cos_rows[low], cos_rows[high] = p + q, p - q
                        sin_rows[low], sin_rows[high] = r - x, r + x
                    for h in range(2):
                        at = b * SUB + h * HALF
                        right[pl.ds(at, HALF), :] = pair(cos_rows[2 * h : 2 * h + 2])
                        right[pl.ds(QUAD * SUB + at, HALF), :] = pair(sin_rows[2 * h : 2 * h + 2])
                product = lax.dot_general(
                    left[...], right[...], (((1,), (1,)), ((), ())), preferred_element_type=jnp.float32
                )
                for b in range(QUAD):
                    mine = product[b * SUB : (b + 1) * SUB]
                    with_cos, with_sin = mine[:, :128], mine[:, 128:]
                    real = with_cos[:HALF] - with_sin[HALF:]
                    imag = with_cos[HALF:] + with_sin[:HALF]
                    parts = (real[:GROUP], real[GROUP:], imag[:GROUP], imag[GROUP:])
                    total = None
                    for k in range(4):
                        moved = parts[k]
                        if k != b:
                            moved = pltpu.roll(moved, ((k - b) % 4) * SUB, 1)
                        total = moved if total is None else jnp.where(lane == k, moved, total)
                    row = g * GROUP + quad * QUAD + b
                    stage[pl.ds(pl.multiple_of(row * 8, 8), 8), :] = total

        for i in range(capacity // 16):
            for k in range(8):
                piece = stage[pl.ds(i * 128 + k, 16, stride=8), :]
                at = pl.ds(pl.multiple_of(index * capacity + i * 16, 16), 16)
                out_ref[at, pl.ds(k * 128, 128)] = piece.astype(jnp.bfloat16)

    destinations = out_ref.shape[0] // capacity
    if destinations == 1:
        serve(0)
    else:
        pl.loop(0, destinations)(serve)


def make_subgrids(first, destinations, capacity, order, start, side, uv, res, vis):
    rows = destinations * capacity
    tiles = vis // 128
    vmem = pl.BlockSpec(memory_space=pltpu.VMEM)
    smem = pl.BlockSpec(memory_space=pltpu.SMEM)
    table = pltpu.VMEM((GROUP * GROUP * tiles, 128), jnp.float32)
    return pl.pallas_call(
        functools.partial(subgrid_kernel, first, capacity),
        out_shape=jax.ShapeDtypeStruct((rows, FEATURE), jnp.bfloat16),
        in_specs=[smem, smem, smem, vmem, vmem],
        out_specs=vmem,
        scratch_shapes=[
            pltpu.VMEM((4 * tiles * GROUP, 128), jnp.float32),
            table, table, table, table,
            pltpu.VMEM((8 * tiles * GROUP, 128), jnp.float32),
            pltpu.VMEM((GROUP // QUAD, QUAD * SUB, vis), jnp.bfloat16),
            pltpu.VMEM((GROUP // QUAD, 2 * QUAD * SUB, vis), jnp.bfloat16),
            pltpu.VMEM((capacity * 8, 128), jnp.float32),
        ],
        compiler_params=pltpu.CompilerParams(vmem_limit_bytes=VMEM_LIMIT),
        cost_estimate=pl.CostEstimate(
            flops=rows * 4 * SUB * SUB * vis, bytes_accessed=8 * rows * FEATURE, transcendentals=0
        ),
        name="subgrids",
    )(order, start, side, uv, res)


def gather_kernel(slot_ref, *refs):
    x_refs, (out_ref, hot, part) = refs[:-3], refs[-3:]
    lane = lax.broadcasted_iota(jnp.int32, (GROUP, 128), 1) // SUB
    wanted = lax.broadcasted_iota(jnp.int32, hot.shape, 0)
    wanted = (wanted % 32) * 4 + wanted // 32
    hot[...] = jnp.where(slot_ref[...] == wanted, 1.0, 0.0).astype(jnp.bfloat16)
    for k in range(8):
        total, at = None, 0
        for x_ref in x_refs:
            term = jnp.dot(
                hot[:, pl.ds(at, x_ref.shape[0])], x_ref[:, pl.ds(k * 128, 128)],
                preferred_element_type=jnp.float32,
            )
            total = term if total is None else total + term
            at += x_ref.shape[0]
        part[...] = total
        for grp in range(4):
            given = [part[pl.ds(32 * jl + 8 * grp, 8), :] for jl in range(4)]
            for a in range(4):
                total = None
                for jl in range(4):
                    moved = given[jl]
                    if a != jl:
                        moved = pltpu.roll(moved, ((jl - a) % 4) * SUB, 1)
                    total = moved if total is None else jnp.where(lane == jl, moved, total)
                p = (a % 2) * 8 + k
                out_ref[pl.ds(p * 64 + grp * 16 + a // 2, 8, stride=2), :] = total


def sum_slots(slots, arrived):
    vmem = pl.BlockSpec(memory_space=pltpu.VMEM)
    return pl.pallas_call(
        gather_kernel,
        out_shape=jax.ShapeDtypeStruct((HALF * 64, 128), jnp.float32),
        in_specs=[vmem] * (1 + len(arrived)),
        out_specs=vmem,
        scratch_shapes=[
            pltpu.VMEM((SLOTS, slots.shape[1]), jnp.bfloat16),
            pltpu.VMEM((SLOTS, 128), jnp.float32),
        ],
        compiler_params=pltpu.CompilerParams(vmem_limit_bytes=VMEM_LIMIT),
        name="sum_slots",
    )(slots, *arrived)


def rows_of(array):
    blocks, parts, vis = array.shape
    tiles = vis // 128
    split = array.reshape(blocks, parts, tiles, 128)
    return split.transpose(0, 2, 1, 3).reshape(blocks * tiles * parts, 128)


def local(residual, uv_offsets, counts, tile_of_block, slot_of_block, owner_map):
    blocks, _, vis = uv_offsets.shape
    owners = owner_map.shape[0]
    capacity = -(-max(CAP_MIN, 2 * blocks // owners) // 16) * 16
    core = lax.axis_index("samp")
    me = lax.axis_index(("blk", "tile"))
    swap = [(0, 1), (1, 0)]
    own = residual[0]
    other = lax.ppermute(own, "samp", swap)

    tile_ids = tile_of_block[:, 0]
    owner_range = jnp.arange(owners, dtype=jnp.int32)
    owner_ids = jnp.sum(
        jnp.where(tile_ids[:, None] == owner_range[None, :], owner_map[None, :], 0), 1
    )
    paired = owners <= PAIRED_MAX and owners & (owners - 1) == 0
    offset = (owners - 1) - jnp.bitwise_xor(owner_ids, me) if paired else owner_ids
    index = jnp.arange(blocks, dtype=jnp.int32)
    same = offset[None, :] == offset[:, None]
    rank = jnp.sum((same & (index[None, :] < index[:, None])).astype(jnp.int32), 1)
    start = jnp.sum(
        (offset[None, :] < jnp.arange(owners + 1, dtype=jnp.int32)[:, None]).astype(jnp.int32), 1
    )
    before = jnp.sum((offset[None, :] < offset[:, None]).astype(jnp.int32), 1)
    place = before + rank
    wanted = jnp.arange(blocks + GROUP, dtype=jnp.int32)
    order = jnp.sum(jnp.where(place[None, :] == wanted[:, None], index[None, :], 0), 1)
    target = offset * capacity + rank
    wanted = jnp.arange(owners * capacity, dtype=jnp.int32)
    slots = jnp.sum(
        jnp.where(target[None, :] == wanted[:, None], slot_of_block[None, :] + 1, 0), 1
    )
    slots = jnp.where(slots > 0, slots - 1, SLOTS).reshape(owners, 1, capacity)

    live = jnp.arange(vis, dtype=jnp.int32)[None, None, :] < counts[:, None, None]
    both = own.astype(jnp.float32) + other.astype(jnp.float32)
    both = rows_of(jnp.where(live, both, 0.0))
    uv = rows_of(uv_offsets)
    side = (2 * core - 1).astype(jnp.int32).reshape(1)
    subgrids = functools.partial(
        make_subgrids, capacity=capacity, order=order, start=start, side=side, uv=uv, res=both, vis=vis
    )
    if paired:
        arrived, arrived_slots = [], []
        for turn in range(owners):
            distance = owners - 1 - turn
            rows = subgrids(turn, 1)
            row_slots = slots[turn]
            if distance:
                pairs = [(k, k ^ distance) for k in range(owners)]
                rows = lax.ppermute(rows, ("blk", "tile"), pairs)
                row_slots = lax.ppermute(row_slots, ("blk", "tile"), pairs)
            arrived.append(rows)
            arrived_slots.append(row_slots)
        arrived_slots = jnp.concatenate(arrived_slots, 1)
    else:
        move = functools.partial(
            lax.all_to_all, axis_name=("blk", "tile"), split_axis=0, concat_axis=0, tiled=True
        )
        rows = subgrids(0, owners).reshape(owners, capacity, FEATURE)
        arrived = [move(rows).reshape(owners * capacity, FEATURE)]
        arrived_slots = move(slots).reshape(1, owners * capacity)
    half = sum_slots(arrived_slots, arrived)
    half = half.reshape(HALF, SLOTS // 4, 2, 128).transpose(0, 2, 1, 3).reshape(HALF, 2, SLOTS * SUB)
    theirs = lax.ppermute(half, "samp", swap)
    return jnp.where(
        core == 0,
        jnp.concatenate([half, theirs], 0),
        jnp.concatenate([theirs, half], 0),
    )


def solution(mesh):
    in_specs = (
        P("samp", ("cuts", "blk", "tile"), None, None),
        P(("cuts", "blk", "tile"), None, None),
        P(("cuts", "blk", "tile")),
        P(("cuts", "blk", "tile"), None),
        P(("cuts", "blk", "tile")),
        P(),
    )
    out_specs = P(("cuts", "blk", "tile"), None, None)
    return jax.shard_map(local, mesh=mesh, in_specs=in_specs, out_specs=out_specs, check_vma=False)
```

```python
import functools

import jax
import jax.numpy as jnp
import numpy as np
from jax import lax
from jax.experimental import pallas as pl
from jax.experimental.pallas import tpu as pltpu
from jax.sharding import PartitionSpec as P

SUB = 32
HALF = SUB // 2
SLOTS = 128
LANES = 128
FEATURE = 2 * SUB * SUB
PIECES = FEATURE // LANES
WIDTH = FEATURE + LANES
CAP_MIN = 8
GROUP = 8
QUAD = 4
TABLES = 12
PAIRED_MAX = 16
VMEM_LIMIT = 48 * 1024 * 1024


def turn_coefficients():
    knots = np.cos(np.pi * (np.arange(400) + 0.5) / 400)
    cheb = np.polynomial.chebyshev
    even = cheb.cheb2poly(cheb.chebfit(knots, np.cos(np.pi * knots), 12))[0::2]
    odd = cheb.cheb2poly(cheb.chebfit(knots, np.sin(np.pi * knots), 13))[1::2]
    return [float(x) for x in even], [float(x) for x in odd]


COS_COEF, SIN_COEF = turn_coefficients()


def horner(coef, x):
    total = coef[-1] * x + coef[-2]
    for value in coef[-3::-1]:
        total = total * x + value
    return total


def harmonics(offset):
    y = offset * (1.0 / HALF)
    x = y * y
    c1, s1 = horner(COS_COEF, x), horner(SIN_COEF, x) * y
    c2, s2 = 1.0 - 2.0 * s1 * s1, 2.0 * s1 * c1
    c3, s3 = c2 * c1 - s2 * s1, s2 * c1 + c2 * s1
    c4, s4 = 1.0 - 2.0 * s2 * s2, 2.0 * s2 * c2
    c8, s8 = 1.0 - 2.0 * s4 * s4, 2.0 * s4 * c4
    c12, s12 = c8 * c4 - s8 * s4, s8 * c4 + c8 * s4
    return (c1, c2, c3, c4, c12), (s1, s2, s3, s4, s12)


def tile_of(value, t):
    return value[:, t * LANES : (t + 1) * LANES]


def fill_table(cos_ref, sin_ref, base, c, s):
    one = jnp.ones_like(c[0])
    cos_rows = (c[3], c[2], c[1], c[0], one, c[0], c[1], c[2])
    sin_rows = (-s[3], -s[2], -s[1], -s[0], jnp.zeros_like(one), s[0], s[1], s[2])
    for r in range(GROUP):
        for t in range(one.shape[1] // LANES):
            at = pl.ds(base + (t * GROUP * GROUP + r), GROUP, stride=GROUP)
            cos_ref[at, :] = tile_of(cos_rows[r], t)
            sin_ref[at, :] = tile_of(sin_rows[r], t)


def pair(halves):
    return jnp.concatenate(halves, 0).astype(jnp.bfloat16)


def subgrid_kernel(
    first, destinations, capacity, order_ref, row_ref, slot_ref, start_ref, uv_ref, res_ref, *refs
):
    out_refs, scratch = refs[:-12], refs[-12:]
    gathered, cos_u, sin_u, cos_v, sin_v, dense, left_a, right_a, left_b, right_b, stage, tags = scratch
    tiles = gathered.shape[0] // (4 * GROUP)
    rows = destinations * capacity
    lane = lax.broadcasted_iota(jnp.int32, (GROUP, LANES), 1) // SUB
    low, high = start_ref[first], start_ref[first + destinations]
    turns = (high - low + GROUP - 1) // GROUP
    last = order_ref.shape[0] - 1

    def wide(ref, row, stride=1, step=GROUP):
        return jnp.concatenate(
            [ref[pl.ds(row + t * step, GROUP, stride=stride), :] for t in range(tiles)], 1
        )

    def tabulate(g):
        for i in range(GROUP):
            block = order_ref[jnp.minimum(low + g * GROUP + i, last)]
            at = pl.ds(pl.multiple_of(block * 2 * tiles, 2 * tiles), 2 * tiles)
            gathered[pl.ds(i, 2 * tiles, stride=GROUP), :] = uv_ref[at, :]
            gathered[pl.ds(2 * tiles * GROUP + i, 2 * tiles, stride=GROUP), :] = res_ref[at, :]
        u, v, re, im = [
            wide(gathered, (k // 2) * 2 * tiles * GROUP + (k % 2) * GROUP, step=2 * GROUP)
            for k in range(4)
        ]
        table_at = pl.multiple_of(g * (tiles * GROUP * GROUP), tiles * GROUP * GROUP)

        def keep(k, value):
            base = pl.multiple_of(g * (TABLES * tiles * GROUP), TABLES * tiles * GROUP)
            for t in range(tiles):
                dense[pl.ds(base + (k * tiles + t) * GROUP, GROUP), :] = tile_of(value, t)

        c, s = harmonics(u)
        fill_table(cos_u, sin_u, table_at, c, s)
        for h in range(2):
            ch, sh = c[3 + h], s[3 + h]
            a, b, e, f = re * ch, im * sh, im * ch, re * sh
            keep(4 * h, a + b)
            keep(4 * h + 1, e - f)
            keep(4 * h + 2, a - b)
            keep(4 * h + 3, e + f)
        c, s = harmonics(v)
        fill_table(cos_v, sin_v, table_at, c, s)
        for h in range(2):
            keep(8 + 2 * h, c[3 + h])
            keep(9 + 2 * h, s[3 + h])

    def expand(g, quad, left, right):
        for b in range(QUAD):
            i = quad * QUAD + b

            def spread(k):
                base = pl.multiple_of(g * (TABLES * tiles * GROUP), TABLES * tiles * GROUP)
                return wide(dense, base + (k * tiles * GROUP + i), stride=0)

            def table(ref):
                base = pl.multiple_of(g * (tiles * GROUP * GROUP), tiles * GROUP * GROUP)
                return wide(ref, base + i * GROUP, step=GROUP * GROUP)

            fc, fs = table(cos_u), table(sin_u)
            real, imag = [None] * 4, [None] * 4
            for k, at in enumerate((1, 2, 0, 3)):
                wr, wi = spread(2 * k), spread(2 * k + 1)
                real[at] = fc * wr - fs * wi
                imag[at] = fs * wr + fc * wi
            gc, gs = table(cos_v), table(sin_v)
            cos_rows, sin_rows = [None] * 4, [None] * 4
            for h, (down, up) in enumerate(((1, 2), (0, 3))):
                ch, sh = spread(8 + 2 * h), spread(9 + 2 * h)
                p, q, r, x = gc * ch, gs * sh, gs * ch, gc * sh
                cos_rows[down], cos_rows[up] = p + q, p - q
                sin_rows[down], sin_rows[up] = r - x, r + x
            for h in range(2):
                two = slice(2 * h, 2 * h + 2)
                left[pl.ds(2 * b * SUB + h * HALF, HALF), :] = pair(real[two])
                left[pl.ds(2 * b * SUB + SUB + h * HALF, HALF), :] = pair(imag[two])
                right[pl.ds(b * SUB + h * HALF, HALF), :] = pair(cos_rows[two])
                right[pl.ds(QUAD * SUB + b * SUB + h * HALF, HALF), :] = pair(sin_rows[two])

    def multiply(left, right):
        return lax.dot_general(
            left[...], right[...], (((1,), (1,)), ((), ())), preferred_element_type=jnp.float32
        )

    def finish(product, turn):
        for b in range(QUAD):
            mine = product[2 * b * SUB : 2 * (b + 1) * SUB]
            with_cos, with_sin = mine[:, :LANES], mine[:, LANES:]
            index = low + turn * QUAD + b
            known = (index >= low) & (index < high)
            index = jnp.clip(index, 0, last)
            row = jnp.where(known, row_ref[index] - first * capacity, rows)
            for part in range(2):
                if part == 0:
                    whole = with_cos[:SUB] - with_sin[SUB:]
                else:
                    whole = with_cos[SUB:] + with_sin[:SUB]
                total = None
                for k in range(4):
                    moved = whole[k * GROUP : (k + 1) * GROUP]
                    if k != b:
                        moved = pltpu.roll(moved, ((k - b) % 4) * SUB, 1)
                    total = moved if total is None else jnp.where(lane == k, moved, total)
                stage[pl.ds(pl.multiple_of(row * PIECES, PIECES) + part * GROUP, GROUP), :] = total
            tag = (slot_ref[index] + 1).astype(jnp.float32)
            tags[pl.ds(row, 1), :] = jnp.full((1, LANES), tag, jnp.float32)

    @pl.loop(0, rows // GROUP)
    def _(i):
        at = pl.multiple_of(i * GROUP, GROUP)
        stage[pl.ds(at * PIECES, GROUP * PIECES), :] = jnp.zeros((GROUP * PIECES, LANES), jnp.float32)
        tags[pl.ds(at, GROUP), :] = jnp.zeros((GROUP, LANES), jnp.float32)

    pl.loop(0, turns)(tabulate)

    @pl.loop(0, turns)
    def _(g):
        product = multiply(left_b, right_b)
        expand(g, 0, left_a, right_a)
        finish(product, 2 * g - 1)
        product = multiply(left_a, right_a)
        expand(g, 1, left_b, right_b)
        finish(product, 2 * g)

    finish(multiply(left_b, right_b), 2 * turns - 1)

    at = 0
    for out_ref in out_refs:

        @pl.loop(0, out_ref.shape[0] // 16)
        def _(i):
            here = pl.multiple_of(i * 16, 16)
            for k in range(PIECES):
                piece = stage[pl.ds((at + here) * PIECES + k, 16, stride=PIECES), :]
                out_ref[pl.ds(here, 16), pl.ds(k * LANES, LANES)] = piece.astype(jnp.bfloat16)
            out_ref[pl.ds(here, 16), pl.ds(FEATURE, LANES)] = tags[pl.ds(at + here, 16), :].astype(
                jnp.bfloat16
            )

        at += out_ref.shape[0]


def make_subgrids(first, outs, capacity, order, row, slot, start, uv, res, vis):
    tiles = vis // LANES
    destinations = sum(outs)
    rows = destinations * capacity
    groups = min(rows, order.shape[0]) // GROUP + 1
    vmem = pl.BlockSpec(memory_space=pltpu.VMEM)
    smem = pl.BlockSpec(memory_space=pltpu.SMEM)
    table = pltpu.VMEM((groups * GROUP * GROUP * tiles, LANES), jnp.float32)
    quad = pltpu.VMEM((2 * QUAD * SUB, vis), jnp.bfloat16)
    return pl.pallas_call(
        functools.partial(subgrid_kernel, first, destinations, capacity),
        out_shape=[jax.ShapeDtypeStruct((n * capacity, WIDTH), jnp.bfloat16) for n in outs],
        in_specs=[smem, smem, smem, smem, vmem, vmem],
        out_specs=[vmem] * len(outs),
        scratch_shapes=[
            pltpu.VMEM((4 * tiles * GROUP, LANES), jnp.float32),
            table, table, table, table,
            pltpu.VMEM((groups * TABLES * tiles * GROUP, LANES), jnp.float32),
            quad, quad, quad, quad,
            pltpu.VMEM(((rows + 1) * PIECES, LANES), jnp.float32),
            pltpu.VMEM((rows + GROUP, LANES), jnp.float32),
        ],
        compiler_params=pltpu.CompilerParams(vmem_limit_bytes=VMEM_LIMIT),
        cost_estimate=pl.CostEstimate(
            flops=rows * 8 * SUB * SUB * vis, bytes_accessed=8 * rows * FEATURE, transcendentals=0
        ),
        name="subgrids",
    )(order, row, slot, start, uv, res)


def gather_kernel(*refs):
    x_refs, (out_ref, xs, hot, part) = refs[:-4], refs[-4:]
    lane = lax.broadcasted_iota(jnp.int32, (GROUP, LANES), 1) // SUB
    at = 0
    for x_ref in x_refs:
        xs[pl.ds(at, x_ref.shape[0]), :] = x_ref[...]
        at += x_ref.shape[0]
    tags = xs[:, pl.ds(FEATURE, LANES)].astype(jnp.float32)
    wanted = lax.broadcasted_iota(jnp.int32, tags.shape, 1)
    wanted = (wanted % 32) * 4 + wanted // 32 + 1
    hot[...] = jnp.where(tags == wanted.astype(jnp.float32), 1.0, 0.0).T.astype(jnp.bfloat16)
    for k in range(PIECES):
        part[...] = jnp.dot(
            hot[...], xs[:, pl.ds(k * LANES, LANES)], preferred_element_type=jnp.float32
        )
        for grp in range(4):
            given = [part[pl.ds(32 * jl + 8 * grp, 8), :] for jl in range(4)]
            for a in range(4):
                total = None
                for jl in range(4):
                    moved = given[jl]
                    if a != jl:
                        moved = pltpu.roll(moved, ((jl - a) % 4) * SUB, 1)
                    total = moved if total is None else jnp.where(lane == jl, moved, total)
                p = a * GROUP + k % GROUP
                out_ref[pl.ds(p * 64 + grp * 16 + k // GROUP, 8, stride=2), :] = total


def sum_slots(arrived):
    rows = sum(x.shape[0] for x in arrived)
    vmem = pl.BlockSpec(memory_space=pltpu.VMEM)
    return pl.pallas_call(
        gather_kernel,
        out_shape=jax.ShapeDtypeStruct((SUB * 64, LANES), jnp.float32),
        in_specs=[vmem] * len(arrived),
        out_specs=vmem,
        scratch_shapes=[
            pltpu.VMEM((rows, WIDTH), jnp.bfloat16),
            pltpu.VMEM((SLOTS, rows), jnp.bfloat16),
            pltpu.VMEM((SLOTS, LANES), jnp.float32),
        ],
        compiler_params=pltpu.CompilerParams(vmem_limit_bytes=VMEM_LIMIT),
        name="sum_slots",
    )(*arrived)


def rows_of(array):
    blocks, parts, vis = array.shape
    tiles = vis // LANES
    split = array.reshape(blocks, parts, tiles, LANES)
    return split.transpose(0, 2, 1, 3).reshape(blocks * tiles * parts, LANES)


def local(residual, uv_offsets, counts, tile_of_block, slot_of_block, owner_map):
    blocks, _, vis = uv_offsets.shape
    owners = owner_map.shape[0]
    capacity = -(-max(CAP_MIN, 2 * blocks // owners) // 32) * 16
    core = lax.axis_index("samp")
    me = lax.axis_index(("blk", "tile"))
    swap = [(0, 1), (1, 0)]
    own = residual[0]
    other = lax.ppermute(own, "samp", swap)

    tile_ids = tile_of_block[:, 0]
    owner_range = jnp.arange(owners, dtype=jnp.int32)
    owner_ids = jnp.sum(
        jnp.where(tile_ids[:, None] == owner_range[None, :], owner_map[None, :], 0), 1
    )
    paired = owners <= PAIRED_MAX and owners & (owners - 1) == 0
    offset = (owners - 1) - jnp.bitwise_xor(owner_ids, me) if paired else owner_ids
    index = jnp.arange(blocks, dtype=jnp.int32)
    same = (offset[None, :] == offset[:, None]) & (index[None, :] < index[:, None])
    rank = jnp.sum(same.astype(jnp.int32), 1)
    mine = (rank & 1) == core
    edges = jnp.arange(owners + 1, dtype=jnp.int32)
    start = jnp.sum((mine[None, :] & (offset[None, :] < edges[:, None])).astype(jnp.int32), 1)
    before = jnp.sum((mine[None, :] & (offset[None, :] < offset[:, None])).astype(jnp.int32), 1)
    place = jnp.where(mine, before + rank // 2, -1)
    wanted = jnp.arange((blocks + owners) // 2 + GROUP, dtype=jnp.int32)
    chosen = place[None, :] == wanted[:, None]
    order = jnp.sum(jnp.where(chosen, index[None, :], 0), 1)
    row = jnp.sum(jnp.where(chosen, (offset * capacity + rank // 2)[None, :], 0), 1)
    slot = jnp.sum(jnp.where(chosen, slot_of_block[None, :], 0), 1)

    live = jnp.arange(vis, dtype=jnp.int32)[None, None, :] < counts[:, None, None]
    both = own.astype(jnp.float32) + other.astype(jnp.float32)
    both = rows_of(jnp.where(live, both, 0.0))
    uv = rows_of(uv_offsets)
    subgrids = functools.partial(
        make_subgrids, capacity=capacity, order=order, row=row, slot=slot, start=start,
        uv=uv, res=both, vis=vis,
    )
    if paired:
        far = owners // 2
        rows = subgrids(0, (1,) * far) + subgrids(far, (1,) * (owners - far))
        arrived = []
        for turn in range(owners):
            distance = owners - 1 - turn
            piece = rows[turn]
            if distance:
                pairs = [(k, k ^ distance) for k in range(owners)]
                piece = lax.ppermute(piece, ("blk", "tile"), pairs)
            arrived.append(piece)
    else:
        each = max(d for d in range(1, 17) if owners % d == 0)
        rows = [subgrids(k, (each,))[0] for k in range(0, owners, each)]
        rows = jnp.concatenate(rows, 0).reshape(owners, capacity, WIDTH)
        rows = lax.all_to_all(rows, ("blk", "tile"), split_axis=0, concat_axis=0, tiled=True)
        arrived = [rows.reshape(owners * capacity, WIDTH)]
    part = sum_slots(arrived)
    part = part.reshape(SUB, SLOTS // 4, 2, LANES).transpose(0, 2, 1, 3).reshape(SUB, 2, SLOTS * SUB)
    return part + lax.ppermute(part, "samp", swap)


def solution(mesh):
    in_specs = (
        P("samp", ("cuts", "blk", "tile"), None, None),
        P(("cuts", "blk", "tile"), None, None),
        P(("cuts", "blk", "tile")),
        P(("cuts", "blk", "tile"), None),
        P(("cuts", "blk", "tile")),
        P(),
    )
    out_specs = P(("cuts", "blk", "tile"), None, None)
    return jax.shard_map(local, mesh=mesh, in_specs=in_specs, out_specs=out_specs, check_vma=False)
```

```python
import functools

import jax
import jax.numpy as jnp
import numpy as np
from jax import lax
from jax.experimental import pallas as pl
from jax.experimental.pallas import tpu as pltpu
from jax.sharding import PartitionSpec as P

SUB = 32
HALF = SUB // 2
SLOTS = 128
LANES = 128
FEATURE = 2 * SUB * SUB
PIECES = FEATURE // LANES
WIDTH = FEATURE + LANES
CAP_MIN = 8
GROUP = 8
QUAD = 4
TABLES = 12
PAIRED_MAX = 16
CALLS = (0, 2, 4, 8)
VMEM_LIMIT = 48 * 1024 * 1024


def turn_coefficients():
    knots = np.cos(np.pi * (np.arange(400) + 0.5) / 400)
    cheb = np.polynomial.chebyshev
    even = cheb.cheb2poly(cheb.chebfit(knots, np.cos(np.pi * knots), 12))[0::2]
    odd = cheb.cheb2poly(cheb.chebfit(knots, np.sin(np.pi * knots), 13))[1::2]
    return [float(x) for x in even], [float(x) for x in odd]


COS_COEF, SIN_COEF = turn_coefficients()


def horner(coef, x):
    total = coef[-1] * x + coef[-2]
    for value in coef[-3::-1]:
        total = total * x + value
    return total


def harmonics(offset):
    y = offset * (1.0 / HALF)
    x = y * y
    c1, s1 = horner(COS_COEF, x), horner(SIN_COEF, x) * y
    c2, s2 = 1.0 - 2.0 * s1 * s1, 2.0 * s1 * c1
    c3, s3 = c2 * c1 - s2 * s1, s2 * c1 + c2 * s1
    c4, s4 = 1.0 - 2.0 * s2 * s2, 2.0 * s2 * c2
    c8, s8 = 1.0 - 2.0 * s4 * s4, 2.0 * s4 * c4
    c12, s12 = c8 * c4 - s8 * s4, s8 * c4 + c8 * s4
    return (c1, c2, c3, c4, c12), (s1, s2, s3, s4, s12)


def tile_of(value, t):
    return value[:, t * LANES : (t + 1) * LANES]


def fill_table(cos_ref, sin_ref, base, c, s):
    one = jnp.ones_like(c[0])
    cos_rows = (c[3], c[2], c[1], c[0], one, c[0], c[1], c[2])
    sin_rows = (-s[3], -s[2], -s[1], -s[0], jnp.zeros_like(one), s[0], s[1], s[2])
    for r in range(GROUP):
        for t in range(one.shape[1] // LANES):
            at = pl.ds(base + (t * GROUP * GROUP + r), GROUP, stride=GROUP)
            cos_ref[at, :] = tile_of(cos_rows[r], t)
            sin_ref[at, :] = tile_of(sin_rows[r], t)


def pair(halves):
    return jnp.concatenate(halves, 0).astype(jnp.bfloat16)


def subgrid_kernel(
    first, destinations, capacity, order_ref, row_ref, slot_ref, start_ref, count_ref, token_ref,
    uv_ref, own_ref, other_ref, *refs
):
    out_refs, next_ref, scratch = refs[:-13], refs[-13], refs[-12:]
    next_ref[...] = jnp.zeros_like(next_ref)
    gathered, cos_u, sin_u, cos_v, sin_v, dense, left_a, right_a, left_b, right_b, stage, tags = scratch
    tiles = gathered.shape[0] // (4 * GROUP)
    rows = destinations * capacity
    lane = lax.broadcasted_iota(jnp.int32, (GROUP, LANES), 1) // SUB
    vis_at = lax.broadcasted_iota(jnp.int32, (2 * tiles, LANES), 1) + LANES * (
        lax.broadcasted_iota(jnp.int32, (2 * tiles, LANES), 0) // 2
    )
    low, high = start_ref[first], start_ref[first + destinations]
    turns = (high - low + GROUP - 1) // GROUP
    last = order_ref.shape[0] - 1

    def wide(ref, row, stride=1, step=GROUP):
        return jnp.concatenate(
            [ref[pl.ds(row + t * step, GROUP, stride=stride), :] for t in range(tiles)], 1
        )

    def tabulate(g):
        for i in range(GROUP):
            block = order_ref[jnp.minimum(low + g * GROUP + i, last)]
            at = pl.ds(pl.multiple_of(block * 2 * tiles, 2 * tiles), 2 * tiles)
            gathered[pl.ds(i, 2 * tiles, stride=GROUP), :] = uv_ref[at, :]
            two = pl.ds(pl.multiple_of((block // 2) * 4 * tiles, 4 * tiles), 4 * tiles)
            both = own_ref[two, :].astype(jnp.float32) + other_ref[two, :].astype(jnp.float32)
            both = jnp.where(block % 2 == 1, both[2 * tiles :], both[: 2 * tiles])
            both = jnp.where(vis_at < count_ref[block], both, 0.0)
            gathered[pl.ds(2 * tiles * GROUP + i, 2 * tiles, stride=GROUP), :] = both
        u, v, re, im = [
            wide(gathered, (k // 2) * 2 * tiles * GROUP + (k % 2) * GROUP, step=2 * GROUP)
            for k in range(4)
        ]
        table_at = pl.multiple_of(g * (tiles * GROUP * GROUP), tiles * GROUP * GROUP)

        def keep(k, value):
            base = pl.multiple_of(g * (TABLES * tiles * GROUP), TABLES * tiles * GROUP)
            for t in range(tiles):
                dense[pl.ds(base + (k * tiles + t) * GROUP, GROUP), :] = tile_of(value, t)

        c, s = harmonics(u)
        fill_table(cos_u, sin_u, table_at, c, s)
        for h in range(2):
            ch, sh = c[3 + h], s[3 + h]
            a, b, e, f = re * ch, im * sh, im * ch, re * sh
            keep(4 * h, a + b)
            keep(4 * h + 1, e - f)
            keep(4 * h + 2, a - b)
            keep(4 * h + 3, e + f)
        c, s = harmonics(v)
        fill_table(cos_v, sin_v, table_at, c, s)
        for h in range(2):
            keep(8 + 2 * h, c[3 + h])
            keep(9 + 2 * h, s[3 + h])

    def expand(g, quad, left, right):
        for b in range(QUAD):
            i = quad * QUAD + b

            def spread(k):
                base = pl.multiple_of(g * (TABLES * tiles * GROUP), TABLES * tiles * GROUP)
                return wide(dense, base + (k * tiles * GROUP + i), stride=0)

            def table(ref):
                base = pl.multiple_of(g * (tiles * GROUP * GROUP), tiles * GROUP * GROUP)
                return wide(ref, base + i * GROUP, step=GROUP * GROUP)

            fc, fs = table(cos_u), table(sin_u)
            real, imag = [None] * 4, [None] * 4
            for k, at in enumerate((1, 2, 0, 3)):
                wr, wi = spread(2 * k), spread(2 * k + 1)
                real[at] = fc * wr - fs * wi
                imag[at] = fs * wr + fc * wi
            gc, gs = table(cos_v), table(sin_v)
            cos_rows, sin_rows = [None] * 4, [None] * 4
            for h, (down, up) in enumerate(((1, 2), (0, 3))):
                ch, sh = spread(8 + 2 * h), spread(9 + 2 * h)
                p, q, r, x = gc * ch, gs * sh, gs * ch, gc * sh
                cos_rows[down], cos_rows[up] = p + q, p - q
                sin_rows[down], sin_rows[up] = r - x, r + x
            for h in range(2):
                two = slice(2 * h, 2 * h + 2)
                left[pl.ds(2 * b * SUB + h * HALF, HALF), :] = pair(real[two])
                left[pl.ds(2 * b * SUB + SUB + h * HALF, HALF), :] = pair(imag[two])
                right[pl.ds(b * SUB + h * HALF, HALF), :] = pair(cos_rows[two])
                right[pl.ds(QUAD * SUB + b * SUB + h * HALF, HALF), :] = pair(sin_rows[two])

    def multiply(left, right):
        return lax.dot_general(
            left[...], right[...], (((1,), (1,)), ((), ())), preferred_element_type=jnp.float32
        )

    def finish(product, turn):
        for b in range(QUAD):
            mine = product[2 * b * SUB : 2 * (b + 1) * SUB]
            with_cos, with_sin = mine[:, :LANES], mine[:, LANES:]
            index = low + turn * QUAD + b
            known = (index >= low) & (index < high)
            index = jnp.clip(index, 0, last)
            row = jnp.where(known, row_ref[index] - first * capacity, rows)
            for part in range(2):
                if part == 0:
                    whole = with_cos[:SUB] - with_sin[SUB:]
                else:
                    whole = with_cos[SUB:] + with_sin[:SUB]
                total = None
                for k in range(4):
                    moved = whole[k * GROUP : (k + 1) * GROUP]
                    if k != b:
                        moved = pltpu.roll(moved, ((k - b) % 4) * SUB, 1)
                    total = moved if total is None else jnp.where(lane == k, moved, total)
                stage[pl.ds(pl.multiple_of(row * PIECES, PIECES) + part * GROUP, GROUP), :] = total
            tag = (slot_ref[index] + 1).astype(jnp.float32)
            tags[pl.ds(row, 1), :] = jnp.full((1, LANES), tag, jnp.float32)

    @pl.loop(0, rows // GROUP)
    def _(i):
        at = pl.multiple_of(i * GROUP, GROUP)
        stage[pl.ds(at * PIECES, GROUP * PIECES), :] = jnp.zeros((GROUP * PIECES, LANES), jnp.float32)
        tags[pl.ds(at, GROUP), :] = jnp.zeros((GROUP, LANES), jnp.float32)

    pl.loop(0, turns)(tabulate)

    @pl.loop(0, turns)
    def _(g):
        product = multiply(left_b, right_b)
        expand(g, 0, left_a, right_a)
        finish(product, 2 * g - 1)
        product = multiply(left_a, right_a)
        expand(g, 1, left_b, right_b)
        finish(product, 2 * g)

    finish(multiply(left_b, right_b), 2 * turns - 1)

    at = 0
    for out_ref in out_refs:

        @pl.loop(0, out_ref.shape[0] // 16)
        def _(i):
            here = pl.multiple_of(i * 16, 16)
            for k in range(PIECES):
                piece = stage[pl.ds((at + here) * PIECES + k, 16, stride=PIECES), :]
                out_ref[pl.ds(here, 16), pl.ds(k * LANES, LANES)] = piece.astype(jnp.bfloat16)
            out_ref[pl.ds(here, 16), pl.ds(FEATURE, LANES)] = tags[pl.ds(at + here, 16), :].astype(
                jnp.bfloat16
            )

        at += out_ref.shape[0]


def make_subgrids(first, outs, token, capacity, order, row, slot, start, counts, uv, own, other, vis):
    tiles = vis // LANES
    destinations = sum(outs)
    rows = destinations * capacity
    groups = min(rows, order.shape[0]) // GROUP + 1
    vmem = pl.BlockSpec(memory_space=pltpu.VMEM)
    smem = pl.BlockSpec(memory_space=pltpu.SMEM)
    table = pltpu.VMEM((groups * GROUP * GROUP * tiles, LANES), jnp.float32)
    quad = pltpu.VMEM((2 * QUAD * SUB, vis), jnp.bfloat16)
    return pl.pallas_call(
        functools.partial(subgrid_kernel, first, destinations, capacity),
        out_shape=[jax.ShapeDtypeStruct((n * capacity, WIDTH), jnp.bfloat16) for n in outs]
        + [jax.ShapeDtypeStruct(token.shape, token.dtype)],
        in_specs=[smem] * 5 + [vmem] * 4,
        out_specs=[vmem] * (len(outs) + 1),
        scratch_shapes=[
            pltpu.VMEM((4 * tiles * GROUP, LANES), jnp.float32),
            table, table, table, table,
            pltpu.VMEM((groups * TABLES * tiles * GROUP, LANES), jnp.float32),
            quad, quad, quad, quad,
            pltpu.VMEM(((rows + 1) * PIECES, LANES), jnp.float32),
            pltpu.VMEM((rows + GROUP, LANES), jnp.float32),
        ],
        compiler_params=pltpu.CompilerParams(vmem_limit_bytes=VMEM_LIMIT),
        cost_estimate=pl.CostEstimate(
            flops=rows * 8 * SUB * SUB * vis, bytes_accessed=8 * rows * FEATURE, transcendentals=0
        ),
        name="subgrids",
    )(order, row, slot, start, counts, token, uv, own, other)


def gather_kernel(*refs):
    x_refs, (out_ref, xs, hot, part) = refs[:-4], refs[-4:]
    lane = lax.broadcasted_iota(jnp.int32, (GROUP, LANES), 1) // SUB
    at = 0
    for x_ref in x_refs:
        xs[pl.ds(at, x_ref.shape[0]), :] = x_ref[...]
        at += x_ref.shape[0]
    tags = xs[:, pl.ds(FEATURE, LANES)].astype(jnp.float32)
    wanted = lax.broadcasted_iota(jnp.int32, tags.shape, 1)
    wanted = (wanted % 32) * 4 + wanted // 32 + 1
    hot[...] = jnp.where(tags == wanted.astype(jnp.float32), 1.0, 0.0).T.astype(jnp.bfloat16)
    for k in range(PIECES):
        part[...] = jnp.dot(
            hot[...], xs[:, pl.ds(k * LANES, LANES)], preferred_element_type=jnp.float32
        )
        for grp in range(4):
            given = [part[pl.ds(32 * jl + 8 * grp, 8), :] for jl in range(4)]
            for a in range(4):
                total = None
                for jl in range(4):
                    moved = given[jl]
                    if a != jl:
                        moved = pltpu.roll(moved, ((jl - a) % 4) * SUB, 1)
                    total = moved if total is None else jnp.where(lane == jl, moved, total)
                p = a * GROUP + k % GROUP
                out_ref[pl.ds(p * 64 + grp * 16 + k // GROUP, 8, stride=2), :] = total


def sum_slots(arrived):
    rows = sum(x.shape[0] for x in arrived)
    vmem = pl.BlockSpec(memory_space=pltpu.VMEM)
    return pl.pallas_call(
        gather_kernel,
        out_shape=jax.ShapeDtypeStruct((SUB * 64, LANES), jnp.float32),
        in_specs=[vmem] * len(arrived),
        out_specs=vmem,
        scratch_shapes=[
            pltpu.VMEM((rows, WIDTH), jnp.bfloat16),
            pltpu.VMEM((SLOTS, rows), jnp.bfloat16),
            pltpu.VMEM((SLOTS, LANES), jnp.float32),
        ],
        compiler_params=pltpu.CompilerParams(vmem_limit_bytes=VMEM_LIMIT),
        name="sum_slots",
    )(*arrived)


def rows_of(array):
    blocks, parts, vis = array.shape
    tiles = vis // LANES
    split = array.reshape(blocks, parts, tiles, LANES)
    return split.transpose(0, 2, 1, 3).reshape(blocks * tiles * parts, LANES)


def local(residual, uv_offsets, counts, tile_of_block, slot_of_block, owner_map):
    blocks, _, vis = uv_offsets.shape
    owners = owner_map.shape[0]
    capacity = -(-max(CAP_MIN, 2 * blocks // owners) // 32) * 16
    core = lax.axis_index("samp")
    me = lax.axis_index(("blk", "tile"))
    swap = [(0, 1), (1, 0)]
    own = residual[0]
    other = lax.ppermute(own, "samp", swap)

    tile_ids = tile_of_block[:, 0]
    owner_range = jnp.arange(owners, dtype=jnp.int32)
    owner_ids = jnp.sum(
        jnp.where(tile_ids[:, None] == owner_range[None, :], owner_map[None, :], 0), 1
    )
    paired = owners <= PAIRED_MAX and owners & (owners - 1) == 0
    offset = (owners - 1) - jnp.bitwise_xor(owner_ids, me) if paired else owner_ids
    index = jnp.arange(blocks, dtype=jnp.int32)
    same = (offset[None, :] == offset[:, None]) & (index[None, :] < index[:, None])
    rank = jnp.sum(same.astype(jnp.int32), 1)
    mine = (rank & 1) == core
    edges = jnp.arange(owners + 1, dtype=jnp.int32)
    start = jnp.sum((mine[None, :] & (offset[None, :] < edges[:, None])).astype(jnp.int32), 1)
    before = jnp.sum((mine[None, :] & (offset[None, :] < offset[:, None])).astype(jnp.int32), 1)
    place = jnp.where(mine, before + rank // 2, -1)
    wanted = jnp.arange((blocks + owners) // 2 + GROUP, dtype=jnp.int32)
    chosen = place[None, :] == wanted[:, None]
    order = jnp.sum(jnp.where(chosen, index[None, :], 0), 1)
    row = jnp.sum(jnp.where(chosen, (offset * capacity + rank // 2)[None, :], 0), 1)
    slot = jnp.sum(jnp.where(chosen, slot_of_block[None, :], 0), 1)

    subgrids = functools.partial(
        make_subgrids, capacity=capacity, order=order, row=row, slot=slot, start=start,
        counts=counts, uv=rows_of(uv_offsets), own=rows_of(own), other=rows_of(other), vis=vis,
    )
    token = jnp.zeros((GROUP, LANES), jnp.int32)
    if paired:
        rows = []
        for first, last in zip(CALLS[:-1], CALLS[1:]):
            first, last = owners * first // CALLS[-1], owners * last // CALLS[-1]
            if first < last:
                *more, token = subgrids(first, (1,) * (last - first), token)
                rows += more
        arrived = []
        for turn in range(owners):
            distance = owners - 1 - turn
            piece = rows[turn]
            if distance:
                pairs = [(k, k ^ distance) for k in range(owners)]
                piece = lax.ppermute(piece, ("blk", "tile"), pairs)
            arrived.append(piece)
    else:
        each = max(d for d in range(1, 17) if owners % d == 0)
        rows = [subgrids(k, (each,), token)[0] for k in range(0, owners, each)]
        rows = jnp.concatenate(rows, 0).reshape(owners, capacity, WIDTH)
        rows = lax.all_to_all(rows, ("blk", "tile"), split_axis=0, concat_axis=0, tiled=True)
        arrived = [rows.reshape(owners * capacity, WIDTH)]
    part = sum_slots(arrived)
    whole = part + lax.ppermute(part, "samp", swap)
    whole = whole.reshape(SUB, SLOTS // 4, 2, LANES).transpose(0, 2, 1, 3)
    return whole.reshape(SUB, 2, SLOTS * SUB)


def solution(mesh):
    in_specs = (
        P("samp", ("cuts", "blk", "tile"), None, None),
        P(("cuts", "blk", "tile"), None, None),
        P(("cuts", "blk", "tile")),
        P(("cuts", "blk", "tile"), None),
        P(("cuts", "blk", "tile")),
        P(),
    )
    out_specs = P(("cuts", "blk", "tile"), None, None)
    return jax.shard_map(local, mesh=mesh, in_specs=in_specs, out_specs=out_specs, check_vma=False)
```

```python
import functools

import jax
import jax.numpy as jnp
import numpy as np
from jax import lax
from jax.experimental import pallas as pl
from jax.experimental.layout import Layout, with_layout_constraint
from jax.experimental.pallas import tpu as pltpu
from jax.sharding import PartitionSpec as P

SUB = 32
HALF = SUB // 2
SLOTS = 128
LANES = 128
FEATURE = 2 * SUB * SUB
PIECES = FEATURE // LANES
WIDTH = FEATURE + LANES
CAP_MIN = 8
GROUP = 8
QUAD = 4
TABLES = 12
COUNT_SPAN = 4096
PAIRED_MAX = 16
VMEM_LIMIT = 48 * 1024 * 1024


def turn_coefficients():
    knots = np.cos(np.pi * (np.arange(400) + 0.5) / 400)
    cheb = np.polynomial.chebyshev
    even = cheb.cheb2poly(cheb.chebfit(knots, np.cos(np.pi * knots), 12))[0::2]
    odd = cheb.cheb2poly(cheb.chebfit(knots, np.sin(np.pi * knots), 13))[1::2]
    return [float(x) for x in even], [float(x) for x in odd]


COS_COEF, SIN_COEF = turn_coefficients()


def horner(coef, x):
    total = coef[-1] * x + coef[-2]
    for value in coef[-3::-1]:
        total = total * x + value
    return total


def harmonics(offset):
    y = offset * (1.0 / HALF)
    x = y * y
    c1, s1 = horner(COS_COEF, x), horner(SIN_COEF, x) * y
    c2, s2 = 1.0 - 2.0 * s1 * s1, 2.0 * s1 * c1
    c3, s3 = c2 * c1 - s2 * s1, s2 * c1 + c2 * s1
    c4, s4 = 1.0 - 2.0 * s2 * s2, 2.0 * s2 * c2
    c8, s8 = 1.0 - 2.0 * s4 * s4, 2.0 * s4 * c4
    c12, s12 = c8 * c4 - s8 * s4, s8 * c4 + c8 * s4
    return (c1, c2, c3, c4, c12), (s1, s2, s3, s4, s12)


def tile_of(value, t):
    return value[:, t * LANES : (t + 1) * LANES]


def fill_table(cos_ref, sin_ref, base, c, s):
    one = jnp.ones_like(c[0])
    cos_rows = (c[3], c[2], c[1], c[0], one, c[0], c[1], c[2])
    sin_rows = (-s[3], -s[2], -s[1], -s[0], jnp.zeros_like(one), s[0], s[1], s[2])
    for r in range(GROUP):
        for t in range(one.shape[1] // LANES):
            at = pl.ds(base + (t * GROUP * GROUP + r), GROUP, stride=GROUP)
            cos_ref[at, :] = tile_of(cos_rows[r], t)
            sin_ref[at, :] = tile_of(sin_rows[r], t)


def pair(halves):
    return jnp.concatenate(halves, 0).astype(jnp.bfloat16)


def subgrid_kernel(
    first, destinations, capacity, block_ref, row_ref, start_ref, token_ref, uv_any, res_ref, *refs
):
    out_refs, next_ref, uv_ref, uv_sem, scratch = refs[:-15], refs[-15], refs[-14], refs[-13], refs[-12:]
    fetch = pltpu.make_async_copy(uv_any, uv_ref, uv_sem)
    fetch.start()
    next_ref[...] = jnp.zeros_like(next_ref)
    gathered, cos_u, sin_u, cos_v, sin_v, dense, left_a, right_a, left_b, right_b, stage, tags = scratch
    tiles = gathered.shape[0] // (4 * GROUP)
    rows = destinations * capacity
    lane = lax.broadcasted_iota(jnp.int32, (GROUP, LANES), 1) // SUB
    vis_at = lax.broadcasted_iota(jnp.int32, (2 * tiles, LANES), 1) + LANES * (
        lax.broadcasted_iota(jnp.int32, (2 * tiles, LANES), 0) // 2
    )
    low, high = start_ref[first], start_ref[first + destinations]
    turns = (high - low + GROUP - 1) // GROUP
    last = block_ref.shape[0] - 1

    def wide(ref, row, stride=1, step=GROUP):
        return jnp.concatenate(
            [ref[pl.ds(row + t * step, GROUP, stride=stride), :] for t in range(tiles)], 1
        )

    def tabulate(g):
        for i in range(GROUP):
            packed = block_ref[jnp.minimum(low + g * GROUP + i, last)]
            block, count = packed // COUNT_SPAN, packed % COUNT_SPAN
            at = pl.ds(pl.multiple_of(block * 2 * tiles, 2 * tiles), 2 * tiles)
            gathered[pl.ds(i, 2 * tiles, stride=GROUP), :] = uv_ref[at, :]
            both = jnp.where(vis_at < count, res_ref[at, :], 0.0)
            gathered[pl.ds(2 * tiles * GROUP + i, 2 * tiles, stride=GROUP), :] = both
        u, v, re, im = [
            wide(gathered, (k // 2) * 2 * tiles * GROUP + (k % 2) * GROUP, step=2 * GROUP)
            for k in range(4)
        ]
        table_at = pl.multiple_of(g * (tiles * GROUP * GROUP), tiles * GROUP * GROUP)

        def keep(k, value):
            base = pl.multiple_of(g * (TABLES * tiles * GROUP), TABLES * tiles * GROUP)
            for t in range(tiles):
                dense[pl.ds(base + (k * tiles + t) * GROUP, GROUP), :] = tile_of(value, t)

        c, s = harmonics(u)
        fill_table(cos_u, sin_u, table_at, c, s)
        for h in range(2):
            ch, sh = c[3 + h], s[3 + h]
            a, b, e, f = re * ch, im * sh, im * ch, re * sh
            keep(4 * h, a + b)
            keep(4 * h + 1, e - f)
            keep(4 * h + 2, a - b)
            keep(4 * h + 3, e + f)
        c, s = harmonics(v)
        fill_table(cos_v, sin_v, table_at, c, s)
        for h in range(2):
            keep(8 + 2 * h, c[3 + h])
            keep(9 + 2 * h, s[3 + h])

    def expand(g, quad, left, right):
        for b in range(QUAD):
            i = quad * QUAD + b

            def spread(k):
                base = pl.multiple_of(g * (TABLES * tiles * GROUP), TABLES * tiles * GROUP)
                return wide(dense, base + (k * tiles * GROUP + i), stride=0)

            def table(ref):
                base = pl.multiple_of(g * (tiles * GROUP * GROUP), tiles * GROUP * GROUP)
                return wide(ref, base + i * GROUP, step=GROUP * GROUP)

            fc, fs = table(cos_u), table(sin_u)
            real, imag = [None] * 4, [None] * 4
            for k, at in enumerate((1, 2, 0, 3)):
                wr, wi = spread(2 * k), spread(2 * k + 1)
                real[at] = fc * wr - fs * wi
                imag[at] = fs * wr + fc * wi
            gc, gs = table(cos_v), table(sin_v)
            cos_rows, sin_rows = [None] * 4, [None] * 4
            for h, (down, up) in enumerate(((1, 2), (0, 3))):
                ch, sh = spread(8 + 2 * h), spread(9 + 2 * h)
                p, q, r, x = gc * ch, gs * sh, gs * ch, gc * sh
                cos_rows[down], cos_rows[up] = p + q, p - q
                sin_rows[down], sin_rows[up] = r - x, r + x
            for h in range(2):
                two = slice(2 * h, 2 * h + 2)
                left[pl.ds(2 * b * SUB + h * HALF, HALF), :] = pair(real[two])
                left[pl.ds(2 * b * SUB + SUB + h * HALF, HALF), :] = pair(imag[two])
                right[pl.ds(b * SUB + h * HALF, HALF), :] = pair(cos_rows[two])
                right[pl.ds(QUAD * SUB + b * SUB + h * HALF, HALF), :] = pair(sin_rows[two])

    def multiply(left, right):
        return lax.dot_general(
            left[...], right[...], (((1,), (1,)), ((), ())), preferred_element_type=jnp.float32
        )

    def finish(product, turn):
        for b in range(QUAD):
            mine = product[2 * b * SUB : 2 * (b + 1) * SUB]
            with_cos, with_sin = mine[:, :LANES], mine[:, LANES:]
            index = low + turn * QUAD + b
            known = (index >= low) & (index < high)
            index = jnp.clip(index, 0, last)
            row = jnp.where(known, row_ref[index] // SLOTS - first * capacity, rows)
            for part in range(2):
                if part == 0:
                    whole = with_cos[:SUB] - with_sin[SUB:]
                else:
                    whole = with_cos[SUB:] + with_sin[:SUB]
                total = None
                for k in range(4):
                    moved = whole[k * GROUP : (k + 1) * GROUP]
                    if k != b:
                        moved = pltpu.roll(moved, ((k - b) % 4) * SUB, 1)
                    total = moved if total is None else jnp.where(lane == k, moved, total)
                stage[pl.ds(pl.multiple_of(row * PIECES, PIECES) + part * GROUP, GROUP), :] = total
            tag = (row_ref[index] % SLOTS + 1).astype(jnp.float32)
            tags[pl.ds(row, 1), :] = jnp.full((1, LANES), tag, jnp.float32)

    @pl.loop(0, rows // GROUP)
    def _(i):
        at = pl.multiple_of(i * GROUP, GROUP)
        stage[pl.ds(at * PIECES, GROUP * PIECES), :] = jnp.zeros((GROUP * PIECES, LANES), jnp.float32)
        tags[pl.ds(at, GROUP), :] = jnp.zeros((GROUP, LANES), jnp.float32)

    fetch.wait()
    pl.loop(0, turns)(tabulate)

    @pl.loop(0, turns)
    def _(g):
        product = multiply(left_b, right_b)
        expand(g, 0, left_a, right_a)
        finish(product, 2 * g - 1)
        product = multiply(left_a, right_a)
        expand(g, 1, left_b, right_b)
        finish(product, 2 * g)

    finish(multiply(left_b, right_b), 2 * turns - 1)

    at = 0
    for out_ref in out_refs:

        @pl.loop(0, out_ref.shape[0] // 16)
        def _(i):
            here = pl.multiple_of(i * 16, 16)
            for k in range(PIECES):
                piece = stage[pl.ds((at + here) * PIECES + k, 16, stride=PIECES), :]
                out_ref[pl.ds(here, 16), pl.ds(k * LANES, LANES)] = piece.astype(jnp.bfloat16)
            out_ref[pl.ds(here, 16), pl.ds(FEATURE, LANES)] = tags[pl.ds(at + here, 16), :].astype(
                jnp.bfloat16
            )

        at += out_ref.shape[0]


def make_subgrids(first, outs, token, capacity, block, row, start, uv, res, vis):
    tiles = vis // LANES
    destinations = sum(outs)
    rows = destinations * capacity
    groups = min(rows, block.shape[0]) // GROUP + 1
    vmem = pl.BlockSpec(memory_space=pltpu.VMEM)
    smem = pl.BlockSpec(memory_space=pltpu.SMEM)
    table = pltpu.VMEM((groups * GROUP * GROUP * tiles, LANES), jnp.float32)
    quad = pltpu.VMEM((2 * QUAD * SUB, vis), jnp.bfloat16)
    return pl.pallas_call(
        functools.partial(subgrid_kernel, first, destinations, capacity),
        out_shape=[jax.ShapeDtypeStruct((n * capacity, WIDTH), jnp.bfloat16) for n in outs]
        + [jax.ShapeDtypeStruct(token.shape, token.dtype)],
        in_specs=[smem] * 3 + [vmem, pl.BlockSpec(memory_space=pl.ANY), vmem],
        out_specs=[vmem] * (len(outs) + 1),
        scratch_shapes=[
            pltpu.VMEM(uv.shape, uv.dtype),
            pltpu.SemaphoreType.DMA,
            pltpu.VMEM((4 * tiles * GROUP, LANES), jnp.float32),
            table, table, table, table,
            pltpu.VMEM((groups * TABLES * tiles * GROUP, LANES), jnp.float32),
            quad, quad, quad, quad,
            pltpu.VMEM(((rows + 1) * PIECES, LANES), jnp.float32),
            pltpu.VMEM((rows + GROUP, LANES), jnp.float32),
        ],
        compiler_params=pltpu.CompilerParams(vmem_limit_bytes=VMEM_LIMIT),
        cost_estimate=pl.CostEstimate(
            flops=rows * 8 * SUB * SUB * vis, bytes_accessed=8 * rows * FEATURE, transcendentals=0
        ),
        name="subgrids",
    )(block, row, start, token, uv, res)


def gather_kernel(*refs):
    x_refs, (out_ref, xs, hot, part) = refs[:-4], refs[-4:]
    lane = lax.broadcasted_iota(jnp.int32, (GROUP, LANES), 1) // SUB
    at = 0
    for x_ref in x_refs:
        xs[pl.ds(at, x_ref.shape[0]), :] = x_ref[...]
        at += x_ref.shape[0]
    tags = xs[:, pl.ds(FEATURE, LANES)].astype(jnp.float32)
    wanted = lax.broadcasted_iota(jnp.int32, tags.shape, 1)
    wanted = (wanted % 32) * 4 + wanted // 32 + 1
    hot[...] = jnp.where(tags == wanted.astype(jnp.float32), 1.0, 0.0).T.astype(jnp.bfloat16)
    for k in range(PIECES):
        part[...] = jnp.dot(
            hot[...], xs[:, pl.ds(k * LANES, LANES)], preferred_element_type=jnp.float32
        )
        for grp in range(4):
            given = [part[pl.ds(32 * jl + 8 * grp, 8), :] for jl in range(4)]
            for a in range(4):
                total = None
                for jl in range(4):
                    moved = given[jl]
                    if a != jl:
                        moved = pltpu.roll(moved, ((jl - a) % 4) * SUB, 1)
                    total = moved if total is None else jnp.where(lane == jl, moved, total)
                p = a * GROUP + k % GROUP
                out_ref[pl.ds(p * 64 + grp * 16 + k // GROUP, 8, stride=2), :] = total


def sum_slots(arrived):
    rows = sum(x.shape[0] for x in arrived)
    vmem = pl.BlockSpec(memory_space=pltpu.VMEM)
    return pl.pallas_call(
        gather_kernel,
        out_shape=jax.ShapeDtypeStruct((SUB * 64, LANES), jnp.float32),
        in_specs=[vmem] * len(arrived),
        out_specs=vmem,
        scratch_shapes=[
            pltpu.VMEM((rows, WIDTH), jnp.bfloat16),
            pltpu.VMEM((SLOTS, rows), jnp.bfloat16),
            pltpu.VMEM((SLOTS, LANES), jnp.float32),
        ],
        compiler_params=pltpu.CompilerParams(vmem_limit_bytes=VMEM_LIMIT),
        name="sum_slots",
    )(*arrived)


def rows_of(array):
    blocks, parts, vis = array.shape
    tiles = vis // LANES
    split = array.reshape(blocks, parts, tiles, LANES)
    return split.transpose(0, 2, 1, 3).reshape(blocks * tiles * parts, LANES)


def in_rows(array):
    return with_layout_constraint(array, Layout(major_to_minor=(0, 1)))


def local(residual, uv_offsets, counts, tile_of_block, slot_of_block, owner_map):
    blocks, _, vis = uv_offsets.shape
    owners = owner_map.shape[0]
    capacity = -(-max(CAP_MIN, 2 * blocks // owners) // 32) * 16
    core = lax.axis_index("samp")
    me = lax.axis_index(("blk", "tile"))
    swap = [(0, 1), (1, 0)]
    own = in_rows(rows_of(residual[0]))
    other = in_rows(lax.ppermute(own, "samp", swap))

    tile_ids = tile_of_block[:, 0]
    owner_range = jnp.arange(owners, dtype=jnp.int32)
    owner_ids = jnp.sum(
        jnp.where(tile_ids[:, None] == owner_range[None, :], owner_map[None, :], 0), 1
    )
    paired = owners <= PAIRED_MAX and owners & (owners - 1) == 0
    offset = (owners - 1) - jnp.bitwise_xor(owner_ids, me) if paired else owner_ids
    index = jnp.arange(blocks, dtype=jnp.int32)
    same = (offset[None, :] == offset[:, None]) & (index[None, :] < index[:, None])
    rank = jnp.sum(same.astype(jnp.int32), 1)
    mine = (rank & 1) == core
    edges = jnp.arange(owners + 1, dtype=jnp.int32)
    start = jnp.sum((mine[None, :] & (offset[None, :] < edges[:, None])).astype(jnp.int32), 1)
    before = jnp.sum((mine[None, :] & (offset[None, :] < offset[:, None])).astype(jnp.int32), 1)
    place = jnp.where(mine, before + rank // 2, -1)
    wanted = jnp.arange((blocks + owners) // 2 + GROUP, dtype=jnp.int32)
    chosen = place[None, :] == wanted[:, None]
    block_and_count = index * COUNT_SPAN + counts
    row_and_slot = (offset * capacity + rank // 2) * SLOTS + slot_of_block
    block = jnp.sum(jnp.where(chosen, block_and_count[None, :], 0), 1)
    row = jnp.sum(jnp.where(chosen, row_and_slot[None, :], 0), 1)

    subgrids = functools.partial(
        make_subgrids, capacity=capacity, block=block, row=row, start=start, uv=rows_of(uv_offsets),
        res=own.astype(jnp.float32) + other.astype(jnp.float32), vis=vis,
    )
    token = jnp.zeros((GROUP, LANES), jnp.int32)
    if paired:
        far = owners * 3 // 8
        *rows, token = subgrids(0, (1,) * far, token)
        rows += subgrids(far, (1,) * (owners - far), token)[:-1]
        arrived = []
        for turn in range(owners):
            distance = owners - 1 - turn
            piece = rows[turn]
            if distance:
                pairs = [(k, k ^ distance) for k in range(owners)]
                piece = lax.ppermute(piece, ("blk", "tile"), pairs)
            arrived.append(piece)
    else:
        each = max(d for d in range(1, 17) if owners % d == 0)
        rows = [subgrids(k, (each,), token)[0] for k in range(0, owners, each)]
        rows = jnp.concatenate(rows, 0).reshape(owners, capacity, WIDTH)
        rows = lax.all_to_all(rows, ("blk", "tile"), split_axis=0, concat_axis=0, tiled=True)
        arrived = [rows.reshape(owners * capacity, WIDTH)]
    part = sum_slots(arrived)
    whole = part + lax.ppermute(part, "samp", swap)
    whole = whole.reshape(SUB, SLOTS // 4, 2, LANES).transpose(0, 2, 1, 3)
    return whole.reshape(SUB, 2, SLOTS * SUB)


def solution(mesh):
    in_specs = (
        P("samp", ("cuts", "blk", "tile"), None, None),
        P(("cuts", "blk", "tile"), None, None),
        P(("cuts", "blk", "tile")),
        P(("cuts", "blk", "tile"), None),
        P(("cuts", "blk", "tile")),
        P(),
    )
    out_specs = P(("cuts", "blk", "tile"), None, None)
    return jax.shard_map(local, mesh=mesh, in_specs=in_specs, out_specs=out_specs, check_vma=False)
```

```python
import functools

import jax
import jax.numpy as jnp
import numpy as np
from jax import lax
from jax.experimental import pallas as pl
from jax.experimental.layout import Layout, with_layout_constraint
from jax.experimental.pallas import tpu as pltpu
from jax.sharding import PartitionSpec as P

SUB = 32
STEPS = SUB // 2
SLOTS = 128
LANES = 128
FEATURE = 2 * SUB * SUB
PIECES = FEATURE // LANES
CAP_MIN = 8
GROUP = 8
QUAD = 4
TAG_ROWS = 16
COUNT_SPAN = 4096
PAIRED_MAX = 16
VMEM_LIMIT = 48 * 1024 * 1024


def turn_coefficients():
    knots = np.cos(np.pi * (np.arange(400) + 0.5) / 400)
    cheb = np.polynomial.chebyshev
    even = cheb.cheb2poly(cheb.chebfit(knots, np.cos(np.pi * knots), 12))[0::2]
    odd = cheb.cheb2poly(cheb.chebfit(knots, np.sin(np.pi * knots), 13))[1::2]
    return [float(x) for x in even], [float(x) for x in odd]


COS_COEF, SIN_COEF = turn_coefficients()


def horner(coef, x):
    total = coef[-1] * x + coef[-2]
    for value in coef[-3::-1]:
        total = total * x + value
    return total


def first_angle(offset):
    y = offset * (1.0 / STEPS)
    x = y * y
    return horner(COS_COEF, x), horner(SIN_COEF, x) * y


def tile_of(value, t):
    return value[:, t * LANES : (t + 1) * LANES]


def by_quad(even, odd):
    top = lax.broadcasted_iota(jnp.int32, even.shape, 0) < QUAD
    return (
        jnp.where(top, even, pltpu.roll(odd, QUAD, 0)),
        jnp.where(top, pltpu.roll(even, QUAD, 0), odd),
    )


def sequence(before, middle, factor):
    values = [None] * STEPS
    values[STEPS // 2 - 1], values[STEPS // 2] = before, middle
    for j in range(STEPS // 2 + 1, STEPS):
        values[j] = factor * values[j - 1] - values[j - 2]
    for j in range(STEPS // 2 - 2, -1, -1):
        values[j] = factor * values[j + 1] - values[j + 2]
    return values


def subgrid_kernel(
    first, destinations, capacity, block_ref, row_ref, start_ref, token_ref, uv_any, res_ref, *refs
):
    out_refs, (next_ref, uv_ref, uv_sem, gathered, found, tags, mover) = refs[:-7], refs[-7:]
    fetch = pltpu.make_async_copy(uv_any, uv_ref, uv_sem)
    fetch.start()
    next_ref[...] = jnp.zeros_like(next_ref)
    tiles = gathered.shape[0] // (4 * GROUP)
    spare = destinations * capacity // QUAD
    low, high = start_ref[first], start_ref[first + destinations]
    last = block_ref.shape[0] - 1
    vis_at = lax.broadcasted_iota(jnp.int32, (2 * tiles, LANES), 1) + LANES * (
        lax.broadcasted_iota(jnp.int32, (2 * tiles, LANES), 0) // 2
    )
    same_block = (
        lax.broadcasted_iota(jnp.int32, (2 * STEPS * QUAD, LANES), 0) % QUAD
        == lax.broadcasted_iota(jnp.int32, (2 * STEPS * QUAD, LANES), 1) % QUAD
    )
    quad_row = lax.broadcasted_iota(jnp.int32, (QUAD, LANES), 0)
    top = lax.broadcasted_iota(jnp.int32, (GROUP, LANES), 0) < QUAD

    source = lax.broadcasted_iota(jnp.int32, mover.shape, 0)
    lane = lax.broadcasted_iota(jnp.int32, mover.shape, 1)
    moves = (source // LANES == lane // SUB) & (source % LANES // QUAD == lane % SUB)
    mover[...] = jnp.where(moves, 1.0, 0.0).astype(jnp.bfloat16)
    tags[...] = jnp.zeros_like(tags)
    fetch.wait()

    @pl.loop(0, (high - low + 1) // 2)
    def _(g):
        quad_at = low + 2 * g
        for i in range(GROUP):
            packed = block_ref[jnp.minimum(quad_at * QUAD + i, last)]
            block, count = packed // COUNT_SPAN, packed % COUNT_SPAN
            at = pl.ds(pl.multiple_of(block * 2 * tiles, 2 * tiles), 2 * tiles)
            both = jnp.where(vis_at < count, res_ref[at, :], 0.0)
            gathered[pl.ds(i, 2 * tiles, stride=GROUP), :] = uv_ref[at, :]
            gathered[pl.ds(2 * tiles * GROUP + i, 2 * tiles, stride=GROUP), :] = both
        u, v, re, im = [
            jnp.concatenate(
                [
                    gathered[pl.ds(((k // 2) * 2 * tiles + 2 * t + k % 2) * GROUP, GROUP), :]
                    for t in range(tiles)
                ],
                1,
            )
            for k in range(4)
        ]
        c, s = first_angle(u)
        a, b, e, f = re * c, im * s, im * c, re * s
        after = (a - b, e + f)
        before = (a + b, e - f)
        second = [2.0 * c * near - far for near, far in zip(before, (re, im))]
        left_mid = [by_quad(x, y) for x, y in zip((re, im), after)]
        left_low = [by_quad(x, y) for x, y in zip(second, before)]
        factor = 2.0 - 4.0 * s * s
        left_factor = by_quad(factor, factor)
        c, s = first_angle(v)
        c2, s2 = 1.0 - 2.0 * s * s, 2.0 * s * c
        right_mid = [by_quad(jnp.ones_like(c), c), by_quad(jnp.zeros_like(s), s)]
        right_low = [by_quad(c2, c), by_quad(-s2, -s)]
        factor = 2.0 * c2
        right_factor = by_quad(factor, factor)
        for quad in range(2):
            left, right = [], []
            for part in range(2):
                left += sequence(left_low[part][quad], left_mid[part][quad], left_factor[quad])
                right += sequence(right_low[part][quad], right_mid[part][quad], right_factor[quad])
            product = lax.dot_general(
                jnp.concatenate(left, 0).astype(jnp.bfloat16),
                jnp.concatenate(right, 0).astype(jnp.bfloat16),
                (((1,), (1,)), ((), ())),
                preferred_element_type=jnp.float32,
            )
            half = product.shape[0] // 2
            wholes = (
                product[:half, :LANES] - product[half:, LANES:],
                product[half:, :LANES] + product[:half, LANES:],
            )
            rows = []
            for whole in wholes:
                whole = jnp.where(same_block, whole, 0.0)
                for j in range(0, STEPS, 4):
                    four = [whole[(j + k) * GROUP : (j + k + 1) * GROUP] for k in range(4)]
                    rows.append(jnp.concatenate(four, 1))
            index = (quad_at + quad) * QUAD
            known = quad_at + quad < high
            index = jnp.minimum(index, last + 1 - QUAD)
            place = row_ref[index] // (2 * SLOTS * QUAD) - first * (capacity // QUAD)
            place = jnp.where(known, place, spare)
            found[place] = jnp.concatenate(rows, 0).astype(jnp.bfloat16)
            tag = jnp.zeros((QUAD, LANES), jnp.int32)
            for b in range(QUAD):
                tag = jnp.where(quad_row == b, row_ref[index + b] % (2 * SLOTS), tag)
            tags[place] = tag.astype(jnp.float32)

    shares = capacity // TAG_ROWS
    share = lax.broadcasted_iota(jnp.int32, (TAG_ROWS, LANES), 1) // (LANES // shares)
    for d, out_ref in enumerate(out_refs):
        for m in range(out_ref.shape[0] // message_rows(capacity)):
            base = m * message_rows(capacity)
            sent = start_ref[first + d + m + 1] - start_ref[first + d + m]
            slot = (d + m) * (capacity // QUAD)
            tag = jnp.zeros((TAG_ROWS, LANES), jnp.float32)
            for n in range(shares):
                at = slot + n * 4
                four = jnp.concatenate([tags[at + k] for k in range(4)], 0)
                tag = jnp.where(share == n, four, tag)
                rows = jnp.concatenate([found[at + k] for k in range(4)], 0)
                moved = jnp.dot(rows, mover[...], preferred_element_type=jnp.float32)
                for piece in range(PIECES // 2):
                    part = []
                    for k in range(4):
                        value = moved[(k * 8 + piece) * GROUP : (k * 8 + piece + 1) * GROUP]
                        part.append(jnp.where(n * 4 + k < sent, value, 0.0))
                    for parity in range(2):
                        pair = []
                        for k in (0, 2):
                            if parity == 0:
                                pair.append(jnp.where(top, part[k], pltpu.roll(part[k + 1], QUAD, 0)))
                            else:
                                pair.append(jnp.where(top, pltpu.roll(part[k], QUAD, 0), part[k + 1]))
                        put = base + (piece * 2 + parity) * capacity + n * TAG_ROWS
                        out_ref[pl.ds(put, TAG_ROWS), :] = jnp.concatenate(pair, 0).astype(jnp.bfloat16)
            out_ref[pl.ds(base + PIECES * capacity, TAG_ROWS), :] = tag.astype(jnp.bfloat16)


def message_rows(capacity):
    return PIECES * capacity + TAG_ROWS


def make_subgrids(first, outs, token, capacity, block, row, start, uv, res, vis):
    tiles = vis // LANES
    destinations = sum(outs)
    quads = destinations * capacity // QUAD
    vmem = pl.BlockSpec(memory_space=pltpu.VMEM)
    smem = pl.BlockSpec(memory_space=pltpu.SMEM)
    return pl.pallas_call(
        functools.partial(subgrid_kernel, first, destinations, capacity),
        out_shape=[
            jax.ShapeDtypeStruct((n * message_rows(capacity), LANES), jnp.bfloat16) for n in outs
        ]
        + [jax.ShapeDtypeStruct(token.shape, token.dtype)],
        in_specs=[smem] * 3 + [vmem, pl.BlockSpec(memory_space=pl.ANY), vmem],
        out_specs=[vmem] * (len(outs) + 1),
        scratch_shapes=[
            pltpu.VMEM(uv.shape, uv.dtype),
            pltpu.SemaphoreType.DMA,
            pltpu.VMEM((4 * tiles * GROUP, LANES), jnp.float32),
            pltpu.VMEM((quads + 1, FEATURE // SUB, 4 * LANES), jnp.bfloat16),
            pltpu.VMEM((quads + 1, QUAD, LANES), jnp.float32),
            pltpu.VMEM((4 * LANES, LANES), jnp.bfloat16),
        ],
        compiler_params=pltpu.CompilerParams(vmem_limit_bytes=VMEM_LIMIT),
        cost_estimate=pl.CostEstimate(
            flops=quads * 32 * SUB * SUB * vis, bytes_accessed=16 * quads * FEATURE, transcendentals=0
        ),
        name="subgrids",
    )(block, row, start, token, uv, res)


def gather_kernel(capacity, *refs):
    x_refs, (out_ref, xs, tags, hot, part) = refs[:-5], refs[-5:]
    lane = lax.broadcasted_iota(jnp.int32, (GROUP, LANES), 1) // SUB
    shares = capacity // TAG_ROWS
    at = 0
    for x_ref in x_refs:
        for base in range(0, x_ref.shape[0], message_rows(capacity)):
            for piece in range(PIECES):
                xs[piece, pl.ds(at, capacity), :] = x_ref[pl.ds(base + piece * capacity, capacity), :]
            tag = x_ref[pl.ds(base + PIECES * capacity, TAG_ROWS), :].astype(jnp.float32)
            for n in range(shares):
                column = n * (LANES // shares)
                tags[pl.ds(at + n * TAG_ROWS, TAG_ROWS), :] = jnp.broadcast_to(
                    tag[:, column : column + 1], (TAG_ROWS, LANES)
                )
            at += capacity
    wanted = lax.broadcasted_iota(jnp.int32, tags.shape, 1)
    wanted = (wanted % 32) * 4 + wanted // 32 + 1
    hot[...] = jnp.where(tags[...] == wanted.astype(jnp.float32), 1.0, 0.0).T.astype(jnp.bfloat16)
    for piece in range(PIECES):
        c, rows, parity = piece // 8, piece // 2 % 4, piece % 2
        part[...] = jnp.dot(hot[...], xs[piece], preferred_element_type=jnp.float32)
        for grp in range(4):
            given = [part[pl.ds(32 * jl + 8 * grp, 8), :] for jl in range(4)]
            for a in range(4):
                total = None
                for jl in range(4):
                    moved = given[jl]
                    if a != jl:
                        moved = pltpu.roll(moved, ((jl - a) % 4) * SUB, 1)
                    total = moved if total is None else jnp.where(lane == jl, moved, total)
                p = rows * 8 + a * 2 + parity
                out_ref[pl.ds(p * 64 + grp * 16 + c, 8, stride=2), :] = total


def sum_slots(arrived, capacity):
    rows = sum(x.shape[0] for x in arrived) // message_rows(capacity) * capacity
    vmem = pl.BlockSpec(memory_space=pltpu.VMEM)
    return pl.pallas_call(
        functools.partial(gather_kernel, capacity),
        out_shape=jax.ShapeDtypeStruct((SUB * 64, LANES), jnp.float32),
        in_specs=[vmem] * len(arrived),
        out_specs=vmem,
        scratch_shapes=[
            pltpu.VMEM((PIECES, rows, LANES), jnp.bfloat16),
            pltpu.VMEM((rows, LANES), jnp.float32),
            pltpu.VMEM((SLOTS, rows), jnp.bfloat16),
            pltpu.VMEM((SLOTS, LANES), jnp.float32),
        ],
        compiler_params=pltpu.CompilerParams(vmem_limit_bytes=VMEM_LIMIT),
        name="sum_slots",
    )(*arrived)


def rows_of(array):
    blocks, parts, vis = array.shape
    tiles = vis // LANES
    split = array.reshape(blocks, parts, tiles, LANES)
    return split.transpose(0, 2, 1, 3).reshape(blocks * tiles * parts, LANES)


def in_rows(array):
    return with_layout_constraint(array, Layout(major_to_minor=(0, 1)))


def local(residual, uv_offsets, counts, tile_of_block, slot_of_block, owner_map):
    blocks, _, vis = uv_offsets.shape
    owners = owner_map.shape[0]
    capacity = -(-max(CAP_MIN, 2 * blocks // owners) // 32) * 16
    core = lax.axis_index("samp")
    me = lax.axis_index(("blk", "tile"))
    swap = [(0, 1), (1, 0)]
    own = in_rows(rows_of(residual[0]))
    other = in_rows(lax.ppermute(own, "samp", swap))

    tile_ids = tile_of_block[:, 0]
    owner_range = jnp.arange(owners, dtype=jnp.int32)
    owner_ids = jnp.sum(
        jnp.where(tile_ids[:, None] == owner_range[None, :], owner_map[None, :], 0), 1
    )
    paired = owners <= PAIRED_MAX and owners & (owners - 1) == 0
    offset = (owners - 1) - jnp.bitwise_xor(owner_ids, me) if paired else owner_ids
    index = jnp.arange(blocks, dtype=jnp.int32)
    same = (offset[None, :] == offset[:, None]) & (index[None, :] < index[:, None])
    rank = jnp.sum(same.astype(jnp.int32), 1)
    mine = (rank & 1) == core
    counted = jnp.sum((mine[None, :] & (offset[None, :] == owner_range[:, None])).astype(jnp.int32), 1)
    quads = (counted + QUAD - 1) // QUAD
    edges = jnp.arange(owners + 1, dtype=jnp.int32)
    start = jnp.sum(jnp.where(owner_range[None, :] < edges[:, None], quads[None, :], 0), 1)
    before = jnp.sum(jnp.where(owner_range[None, :] < offset[:, None], quads[None, :], 0), 1)
    place = jnp.where(mine, before * QUAD + rank // 2, -1)
    longest = ((blocks + owners) // 2 + owners * (QUAD - 1)) // GROUP * GROUP + GROUP
    wanted = jnp.arange(longest, dtype=jnp.int32)
    chosen = place[None, :] == wanted[:, None]
    block_and_count = index * COUNT_SPAN + counts
    row_and_tag = (offset * capacity + rank // 2) * (2 * SLOTS) + slot_of_block + 1
    block = jnp.sum(jnp.where(chosen, block_and_count[None, :], 0), 1)
    row = jnp.sum(jnp.where(chosen, row_and_tag[None, :], 0), 1)

    subgrids = functools.partial(
        make_subgrids, capacity=capacity, block=block, row=row, start=start, uv=rows_of(uv_offsets),
        res=own.astype(jnp.float32) + other.astype(jnp.float32), vis=vis,
    )
    token = jnp.zeros((GROUP, LANES), jnp.int32)
    if paired:
        far = owners * 3 // 8
        *rows, token = subgrids(0, (1,) * far, token)
        rows += subgrids(far, (1,) * (owners - far), token)[:-1]
        arrived = []
        for turn in range(owners):
            distance = owners - 1 - turn
            piece = rows[turn]
            if distance:
                pairs = [(k, k ^ distance) for k in range(owners)]
                piece = lax.ppermute(piece, ("blk", "tile"), pairs)
            arrived.append(piece)
    else:
        each = max(d for d in range(1, 17) if owners % d == 0)
        rows = [subgrids(k, (each,), token)[0] for k in range(0, owners, each)]
        rows = jnp.concatenate(rows, 0).reshape(owners, message_rows(capacity), LANES)
        rows = lax.all_to_all(rows, ("blk", "tile"), split_axis=0, concat_axis=0, tiled=True)
        arrived = [rows.reshape(owners * message_rows(capacity), LANES)]
    part = sum_slots(arrived, capacity)
    whole = part + lax.ppermute(part, "samp", swap)
    whole = whole.reshape(SUB, SLOTS // 4, 2, LANES).transpose(0, 2, 1, 3)
    return whole.reshape(SUB, 2, SLOTS * SUB)


def solution(mesh):
    in_specs = (
        P("samp", ("cuts", "blk", "tile"), None, None),
        P(("cuts", "blk", "tile"), None, None),
        P(("cuts", "blk", "tile")),
        P(("cuts", "blk", "tile"), None),
        P(("cuts", "blk", "tile")),
        P(),
    )
    out_specs = P(("cuts", "blk", "tile"), None, None)
    return jax.shard_map(local, mesh=mesh, in_specs=in_specs, out_specs=out_specs, check_vma=False)
```

```python
import functools

import jax
import jax.numpy as jnp
import numpy as np
from jax import lax
from jax.experimental import pallas as pl
from jax.experimental.layout import Layout, with_layout_constraint
from jax.experimental.pallas import tpu as pltpu
from jax.sharding import PartitionSpec as P

SUB = 32
STEPS = SUB // 2
SLOTS = 128
LANES = 128
FEATURE = 2 * SUB * SUB
PIECES = FEATURE // LANES
CAP_MIN = 8
GROUP = 8
QUAD = 4
TAG_ROWS = 16
COUNT_SPAN = 4096
PAIRED_MAX = 16
CALLS = (0, 1, 4, 8)
VMEM_LIMIT = 48 * 1024 * 1024


def turn_coefficients():
    knots = np.cos(np.pi * (np.arange(400) + 0.5) / 400)
    cheb = np.polynomial.chebyshev
    even = cheb.cheb2poly(cheb.chebfit(knots, np.cos(np.pi * knots), 12))[0::2]
    odd = cheb.cheb2poly(cheb.chebfit(knots, np.sin(np.pi * knots), 13))[1::2]
    return [float(x) for x in even], [float(x) for x in odd]


COS_COEF, SIN_COEF = turn_coefficients()


def horner(coef, x):
    total = coef[-1] * x + coef[-2]
    for value in coef[-3::-1]:
        total = total * x + value
    return total


def first_angle(offset):
    y = offset * (1.0 / STEPS)
    x = y * y
    return horner(COS_COEF, x), horner(SIN_COEF, x) * y


def tile_of(value, t):
    return value[:, t * LANES : (t + 1) * LANES]


def by_quad(even, odd):
    top = lax.broadcasted_iota(jnp.int32, even.shape, 0) < QUAD
    return (
        jnp.where(top, even, pltpu.roll(odd, QUAD, 0)),
        jnp.where(top, pltpu.roll(even, QUAD, 0), odd),
    )


def sequence(before, middle, factor):
    values = [None] * STEPS
    values[STEPS // 2 - 1], values[STEPS // 2] = before, middle
    for j in range(STEPS // 2 + 1, STEPS):
        values[j] = factor * values[j - 1] - values[j - 2]
    for j in range(STEPS // 2 - 2, -1, -1):
        values[j] = factor * values[j + 1] - values[j + 2]
    return values


def subgrid_kernel(
    first, destinations, capacity, block_ref, row_ref, start_ref, token_ref, uv_ref, res_ref, *refs
):
    out_refs, (next_ref, gathered, found, tags, mover) = refs[:-5], refs[-5:]
    next_ref[...] = jnp.zeros_like(next_ref)
    tiles = gathered.shape[0] // (4 * GROUP)
    spare = destinations * capacity // QUAD
    low, high = start_ref[first], start_ref[first + destinations]
    last = block_ref.shape[0] - 1
    vis_at = lax.broadcasted_iota(jnp.int32, (2 * tiles, LANES), 1) + LANES * (
        lax.broadcasted_iota(jnp.int32, (2 * tiles, LANES), 0) // 2
    )
    same_block = (
        lax.broadcasted_iota(jnp.int32, (2 * STEPS * QUAD, LANES), 0) % QUAD
        == lax.broadcasted_iota(jnp.int32, (2 * STEPS * QUAD, LANES), 1) % QUAD
    )
    quad_row = lax.broadcasted_iota(jnp.int32, (QUAD, LANES), 0)
    top = lax.broadcasted_iota(jnp.int32, (GROUP, LANES), 0) < QUAD

    source = lax.broadcasted_iota(jnp.int32, mover.shape, 0)
    lane = lax.broadcasted_iota(jnp.int32, mover.shape, 1)
    moves = (source // LANES == lane // SUB) & (source % LANES // QUAD == lane % SUB)
    mover[...] = jnp.where(moves, 1.0, 0.0).astype(jnp.bfloat16)
    tags[...] = jnp.zeros_like(tags)

    def finish(operands, quad_at):
        product = lax.dot_general(
            *operands, (((1,), (1,)), ((), ())), preferred_element_type=jnp.float32
        )
        half = product.shape[0] // 2
        wholes = (
            product[:half, :LANES] - product[half:, LANES:],
            product[half:, :LANES] + product[:half, LANES:],
        )
        rows = []
        for whole in wholes:
            whole = jnp.where(same_block, whole, 0.0)
            for j in range(0, STEPS, 4):
                four = [whole[(j + k) * GROUP : (j + k + 1) * GROUP] for k in range(4)]
                rows.append(jnp.concatenate(four, 1))
        index = jnp.clip(quad_at * QUAD, 0, last + 1 - QUAD)
        place = row_ref[index] // (2 * SLOTS * QUAD) - first * (capacity // QUAD)
        place = jnp.where((quad_at >= low) & (quad_at < high), place, spare)
        found[place] = jnp.concatenate(rows, 0).astype(jnp.bfloat16)
        tag = jnp.zeros((QUAD, LANES), jnp.int32)
        for b in range(QUAD):
            tag = jnp.where(quad_row == b, row_ref[index + b] % (2 * SLOTS), tag)
        tags[place] = tag.astype(jnp.float32)

    def turn(g, carried):
        quad_at = low + 2 * g
        finish(carried, quad_at - 1)
        for i in range(GROUP):
            packed = block_ref[jnp.minimum(quad_at * QUAD + i, last)]
            block, count = packed // COUNT_SPAN, packed % COUNT_SPAN
            at = pl.ds(pl.multiple_of(block * 2 * tiles, 2 * tiles), 2 * tiles)
            both = jnp.where(vis_at < count, res_ref[at, :], 0.0)
            gathered[pl.ds(i, 2 * tiles, stride=GROUP), :] = uv_ref[at, :]
            gathered[pl.ds(2 * tiles * GROUP + i, 2 * tiles, stride=GROUP), :] = both
        u, v, re, im = [
            jnp.concatenate(
                [
                    gathered[pl.ds(((k // 2) * 2 * tiles + 2 * t + k % 2) * GROUP, GROUP), :]
                    for t in range(tiles)
                ],
                1,
            )
            for k in range(4)
        ]
        c, s = first_angle(u)
        a, b, e, f = re * c, im * s, im * c, re * s
        after = (a - b, e + f)
        before = (a + b, e - f)
        second = [2.0 * c * near - far for near, far in zip(before, (re, im))]
        left_mid = [by_quad(x, y) for x, y in zip((re, im), after)]
        left_low = [by_quad(x, y) for x, y in zip(second, before)]
        factor = 2.0 - 4.0 * s * s
        left_factor = by_quad(factor, factor)
        c, s = first_angle(v)
        c2, s2 = 1.0 - 2.0 * s * s, 2.0 * s * c
        right_mid = [by_quad(jnp.ones_like(c), c), by_quad(jnp.zeros_like(s), s)]
        right_low = [by_quad(c2, c), by_quad(-s2, -s)]
        factor = 2.0 * c2
        right_factor = by_quad(factor, factor)
        rows = []
        for quad in range(2):
            left, right = [], []
            for part in range(2):
                left += sequence(left_low[part][quad], left_mid[part][quad], left_factor[quad])
                right += sequence(right_low[part][quad], right_mid[part][quad], right_factor[quad])
            rows.append([jnp.concatenate(x, 0).astype(jnp.bfloat16) for x in (left, right)])
        finish(rows[0], quad_at)
        return rows[1]

    turns = (high - low + 1) // 2
    nothing = jnp.zeros((4 * STEPS * QUAD, tiles * LANES), jnp.bfloat16)
    finish(lax.fori_loop(0, turns, turn, [nothing, nothing]), low + 2 * turns - 1)

    shares = capacity // TAG_ROWS
    share = lax.broadcasted_iota(jnp.int32, (TAG_ROWS, LANES), 1) // (LANES // shares)
    for d, out_ref in enumerate(out_refs):
        for m in range(out_ref.shape[0] // message_rows(capacity)):
            base = m * message_rows(capacity)
            sent = start_ref[first + d + m + 1] - start_ref[first + d + m]
            slot = (d + m) * (capacity // QUAD)
            tag = jnp.zeros((TAG_ROWS, LANES), jnp.float32)
            for n in range(shares):
                at = slot + n * 4
                four = jnp.concatenate([tags[at + k] for k in range(4)], 0)
                tag = jnp.where(share == n, four, tag)
                rows = jnp.concatenate([found[at + k] for k in range(4)], 0)
                moved = jnp.dot(rows, mover[...], preferred_element_type=jnp.float32)
                for piece in range(PIECES // 2):
                    part = []
                    for k in range(4):
                        value = moved[(k * 8 + piece) * GROUP : (k * 8 + piece + 1) * GROUP]
                        part.append(jnp.where(n * 4 + k < sent, value, 0.0))
                    for parity in range(2):
                        pair = []
                        for k in (0, 2):
                            if parity == 0:
                                pair.append(jnp.where(top, part[k], pltpu.roll(part[k + 1], QUAD, 0)))
                            else:
                                pair.append(jnp.where(top, pltpu.roll(part[k], QUAD, 0), part[k + 1]))
                        put = base + (piece * 2 + parity) * capacity + n * TAG_ROWS
                        out_ref[pl.ds(put, TAG_ROWS), :] = jnp.concatenate(pair, 0).astype(jnp.bfloat16)
            out_ref[pl.ds(base + PIECES * capacity, TAG_ROWS), :] = tag.astype(jnp.bfloat16)


def message_rows(capacity):
    return PIECES * capacity + TAG_ROWS


def make_subgrids(first, outs, token, capacity, block, row, start, uv, res, vis):
    tiles = vis // LANES
    destinations = sum(outs)
    quads = destinations * capacity // QUAD
    vmem = pl.BlockSpec(memory_space=pltpu.VMEM)
    smem = pl.BlockSpec(memory_space=pltpu.SMEM)
    return pl.pallas_call(
        functools.partial(subgrid_kernel, first, destinations, capacity),
        out_shape=[
            jax.ShapeDtypeStruct((n * message_rows(capacity), LANES), jnp.bfloat16) for n in outs
        ]
        + [jax.ShapeDtypeStruct(token.shape, token.dtype)],
        in_specs=[smem] * 3 + [vmem] * 3,
        out_specs=[vmem] * (len(outs) + 1),
        scratch_shapes=[
            pltpu.VMEM((4 * tiles * GROUP, LANES), jnp.float32),
            pltpu.VMEM((quads + 1, FEATURE // SUB, 4 * LANES), jnp.bfloat16),
            pltpu.VMEM((quads + 1, QUAD, LANES), jnp.float32),
            pltpu.VMEM((4 * LANES, LANES), jnp.bfloat16),
        ],
        compiler_params=pltpu.CompilerParams(vmem_limit_bytes=VMEM_LIMIT),
        cost_estimate=pl.CostEstimate(
            flops=quads * 32 * SUB * SUB * vis, bytes_accessed=16 * quads * FEATURE, transcendentals=0
        ),
        name="subgrids",
    )(block, row, start, token, uv, res)


def gather_kernel(capacity, *refs):
    x_refs, (out_ref, xs, tags, hot, part) = refs[:-5], refs[-5:]
    lane = lax.broadcasted_iota(jnp.int32, (GROUP, LANES), 1) // SUB
    shares = capacity // TAG_ROWS
    at = 0
    for x_ref in x_refs:
        for base in range(0, x_ref.shape[0], message_rows(capacity)):
            for piece in range(PIECES):
                xs[piece, pl.ds(at, capacity), :] = x_ref[pl.ds(base + piece * capacity, capacity), :]
            tag = x_ref[pl.ds(base + PIECES * capacity, TAG_ROWS), :].astype(jnp.float32)
            for n in range(shares):
                column = n * (LANES // shares)
                tags[pl.ds(at + n * TAG_ROWS, TAG_ROWS), :] = jnp.broadcast_to(
                    tag[:, column : column + 1], (TAG_ROWS, LANES)
                )
            at += capacity
    wanted = lax.broadcasted_iota(jnp.int32, tags.shape, 1)
    wanted = (wanted % 32) * 4 + wanted // 32 + 1
    hot[...] = jnp.where(tags[...] == wanted.astype(jnp.float32), 1.0, 0.0).T.astype(jnp.bfloat16)
    for piece in range(PIECES):
        c, rows, parity = piece // 8, piece // 2 % 4, piece % 2
        part[...] = jnp.dot(hot[...], xs[piece], preferred_element_type=jnp.float32)
        for grp in range(4):
            given = [part[pl.ds(32 * jl + 8 * grp, 8), :] for jl in range(4)]
            for a in range(4):
                total = None
                for jl in range(4):
                    moved = given[jl]
                    if a != jl:
                        moved = pltpu.roll(moved, ((jl - a) % 4) * SUB, 1)
                    total = moved if total is None else jnp.where(lane == jl, moved, total)
                p = rows * 8 + a * 2 + parity
                out_ref[pl.ds(p * 64 + grp * 16 + c, 8, stride=2), :] = total


def sum_slots(arrived, capacity):
    rows = sum(x.shape[0] for x in arrived) // message_rows(capacity) * capacity
    vmem = pl.BlockSpec(memory_space=pltpu.VMEM)
    return pl.pallas_call(
        functools.partial(gather_kernel, capacity),
        out_shape=jax.ShapeDtypeStruct((SUB * 64, LANES), jnp.float32),
        in_specs=[vmem] * len(arrived),
        out_specs=vmem,
        scratch_shapes=[
            pltpu.VMEM((PIECES, rows, LANES), jnp.bfloat16),
            pltpu.VMEM((rows, LANES), jnp.float32),
            pltpu.VMEM((SLOTS, rows), jnp.bfloat16),
            pltpu.VMEM((SLOTS, LANES), jnp.float32),
        ],
        compiler_params=pltpu.CompilerParams(vmem_limit_bytes=VMEM_LIMIT),
        name="sum_slots",
    )(*arrived)


def rows_of(array):
    blocks, parts, vis = array.shape
    tiles = vis // LANES
    split = array.reshape(blocks, parts, tiles, LANES)
    return split.transpose(0, 2, 1, 3).reshape(blocks * tiles * parts, LANES)


def in_rows(array):
    return with_layout_constraint(array, Layout(major_to_minor=(0, 1)))


def local(residual, uv_offsets, counts, tile_of_block, slot_of_block, owner_map):
    blocks, _, vis = uv_offsets.shape
    owners = owner_map.shape[0]
    capacity = -(-max(CAP_MIN, 2 * blocks // owners) // 32) * 16
    core = lax.axis_index("samp")
    me = lax.axis_index(("blk", "tile"))
    swap = [(0, 1), (1, 0)]
    own = in_rows(rows_of(residual[0]))
    other = in_rows(lax.ppermute(own, "samp", swap))

    tile_ids = tile_of_block[:, 0]
    owner_range = jnp.arange(owners, dtype=jnp.int32)
    owner_ids = jnp.sum(
        jnp.where(tile_ids[:, None] == owner_range[None, :], owner_map[None, :], 0), 1
    )
    paired = owners <= PAIRED_MAX and owners & (owners - 1) == 0
    offset = (owners - 1) - jnp.bitwise_xor(owner_ids, me) if paired else owner_ids
    index = jnp.arange(blocks, dtype=jnp.int32)
    same = (offset[None, :] == offset[:, None]) & (index[None, :] < index[:, None])
    rank = jnp.sum(same.astype(jnp.int32), 1)
    mine = (rank & 1) == core
    counted = jnp.sum((mine[None, :] & (offset[None, :] == owner_range[:, None])).astype(jnp.int32), 1)
    quads = (counted + QUAD - 1) // QUAD
    edges = jnp.arange(owners + 1, dtype=jnp.int32)
    start = jnp.sum(jnp.where(owner_range[None, :] < edges[:, None], quads[None, :], 0), 1)
    before = jnp.sum(jnp.where(owner_range[None, :] < offset[:, None], quads[None, :], 0), 1)
    place = jnp.where(mine, before * QUAD + rank // 2, -1)
    longest = ((blocks + owners) // 2 + owners * (QUAD - 1)) // GROUP * GROUP + GROUP
    wanted = jnp.arange(longest, dtype=jnp.int32)
    chosen = place[None, :] == wanted[:, None]
    block_and_count = index * COUNT_SPAN + counts
    row_and_tag = (offset * capacity + rank // 2) * (2 * SLOTS) + slot_of_block + 1
    block = jnp.sum(jnp.where(chosen, block_and_count[None, :], 0), 1)
    row = jnp.sum(jnp.where(chosen, row_and_tag[None, :], 0), 1)

    subgrids = functools.partial(
        make_subgrids, capacity=capacity, block=block, row=row, start=start, uv=rows_of(uv_offsets),
        res=own.astype(jnp.float32) + other.astype(jnp.float32), vis=vis,
    )
    token = jnp.zeros((GROUP, LANES), jnp.int32)
    if paired:
        rows = []
        for first, last in zip(CALLS[:-1], CALLS[1:]):
            first, last = owners * first // CALLS[-1], owners * last // CALLS[-1]
            if first < last:
                *more, token = subgrids(first, (1,) * (last - first), token)
                rows += more
        arrived = []
        for turn in range(owners):
            distance = owners - 1 - turn
            piece = rows[turn]
            if distance:
                pairs = [(k, k ^ distance) for k in range(owners)]
                piece = lax.ppermute(piece, ("blk", "tile"), pairs)
            arrived.append(piece)
    else:
        each = max(d for d in range(1, 17) if owners % d == 0)
        rows = [subgrids(k, (each,), token)[0] for k in range(0, owners, each)]
        rows = jnp.concatenate(rows, 0).reshape(owners, message_rows(capacity), LANES)
        rows = lax.all_to_all(rows, ("blk", "tile"), split_axis=0, concat_axis=0, tiled=True)
        arrived = [rows.reshape(owners * message_rows(capacity), LANES)]
    part = sum_slots(arrived, capacity)
    whole = part + lax.ppermute(part, "samp", swap)
    whole = whole.reshape(SUB, SLOTS // 4, 2, LANES).transpose(0, 2, 1, 3)
    return whole.reshape(SUB, 2, SLOTS * SUB)


def solution(mesh):
    in_specs = (
        P("samp", ("cuts", "blk", "tile"), None, None),
        P(("cuts", "blk", "tile"), None, None),
        P(("cuts", "blk", "tile")),
        P(("cuts", "blk", "tile"), None),
        P(("cuts", "blk", "tile")),
        P(),
    )
    out_specs = P(("cuts", "blk", "tile"), None, None)
    return jax.shard_map(local, mesh=mesh, in_specs=in_specs, out_specs=out_specs, check_vma=False)
```

```python
import functools

import jax
import jax.numpy as jnp
import numpy as np
from jax import lax
from jax.experimental import pallas as pl
from jax.experimental.layout import Layout, with_layout_constraint
from jax.experimental.pallas import tpu as pltpu
from jax.sharding import PartitionSpec as P

SUB = 32
STEPS = SUB // 2
SLOTS = 128
LANES = 128
FEATURE = 2 * SUB * SUB
PIECES = FEATURE // LANES
CAP_MIN = 8
GROUP = 8
QUAD = 4
TAG_ROWS = 16
COUNT_SPAN = 4096
PAIRED_MAX = 16
VMEM_LIMIT = 48 * 1024 * 1024


def turn_coefficients():
    knots = np.cos(np.pi * (np.arange(400) + 0.5) / 400)
    cheb = np.polynomial.chebyshev
    even = cheb.cheb2poly(cheb.chebfit(knots, np.cos(np.pi * knots), 12))[0::2]
    odd = cheb.cheb2poly(cheb.chebfit(knots, np.sin(np.pi * knots), 13))[1::2]
    return [float(x) for x in even], [float(x) for x in odd]


COS_COEF, SIN_COEF = turn_coefficients()


def horner(coef, x):
    total = coef[-1] * x + coef[-2]
    for value in coef[-3::-1]:
        total = total * x + value
    return total


def first_angle(offset):
    y = offset * (1.0 / STEPS)
    x = y * y
    return horner(COS_COEF, x), horner(SIN_COEF, x) * y


def tile_of(value, t):
    return value[:, t * LANES : (t + 1) * LANES]


def by_quad(even, odd):
    top = lax.broadcasted_iota(jnp.int32, even.shape, 0) < QUAD
    return (
        jnp.where(top, even, pltpu.roll(odd, QUAD, 0)),
        jnp.where(top, pltpu.roll(even, QUAD, 0), odd),
    )


def sequence(before, middle, factor):
    def pair(*two):
        return jnp.concatenate(two, 0).astype(jnp.bfloat16)

    up, down = [], []
    last, value = before, middle
    for _ in range(STEPS // 4):
        after = factor * value - last
        up.append(pair(value, after))
        last, value = after, factor * after - value
    last, value = middle, before
    for _ in range(STEPS // 4):
        after = factor * value - last
        down.append(pair(after, value))
        last, value = after, factor * after - value
    return down[::-1] + up


def subgrid_kernel(
    first, destinations, capacity, block_ref, row_ref, start_ref, token_ref, uv_ref, res_ref, *refs
):
    out_refs, (next_ref, gathered, found, tags, mover) = refs[:-5], refs[-5:]
    next_ref[...] = jnp.zeros_like(next_ref)
    tiles = gathered.shape[0] // (4 * GROUP)
    spare = destinations * capacity // QUAD
    low, high = start_ref[first], start_ref[first + destinations]
    last = block_ref.shape[0] - 1
    vis_at = lax.broadcasted_iota(jnp.int32, (2 * tiles, LANES), 1) + LANES * (
        lax.broadcasted_iota(jnp.int32, (2 * tiles, LANES), 0) // 2
    )
    same_block = (
        lax.broadcasted_iota(jnp.int32, (2 * STEPS * QUAD, LANES), 0) % QUAD
        == lax.broadcasted_iota(jnp.int32, (2 * STEPS * QUAD, LANES), 1) % QUAD
    )
    quad_row = lax.broadcasted_iota(jnp.int32, (QUAD, LANES), 0)
    top = lax.broadcasted_iota(jnp.int32, (GROUP, LANES), 0) < QUAD

    source = lax.broadcasted_iota(jnp.int32, mover.shape, 0)
    lane = lax.broadcasted_iota(jnp.int32, mover.shape, 1)
    moves = (source // LANES == lane // SUB) & (source % LANES // QUAD == lane % SUB)
    mover[...] = jnp.where(moves, 1.0, 0.0).astype(jnp.bfloat16)
    tags[...] = jnp.zeros_like(tags)

    def finish(operands, quad_at):
        product = lax.dot_general(
            *operands, (((1,), (1,)), ((), ())), preferred_element_type=jnp.float32
        )
        half = product.shape[0] // 2
        wholes = (
            product[:half, :LANES] - product[half:, LANES:],
            product[half:, :LANES] + product[:half, LANES:],
        )
        rows = []
        for whole in wholes:
            whole = jnp.where(same_block, whole, 0.0)
            for j in range(0, STEPS, 4):
                four = [whole[(j + k) * GROUP : (j + k + 1) * GROUP] for k in range(4)]
                rows.append(jnp.concatenate(four, 1))
        index = jnp.clip(quad_at * QUAD, 0, last + 1 - QUAD)
        place = row_ref[index] // (2 * SLOTS * QUAD) - first * (capacity // QUAD)
        place = jnp.where((quad_at >= low) & (quad_at < high), place, spare)
        found[place] = jnp.concatenate(rows, 0).astype(jnp.bfloat16)
        tag = jnp.zeros((QUAD, LANES), jnp.int32)
        for b in range(QUAD):
            tag = jnp.where(quad_row == b, row_ref[index + b] % (2 * SLOTS), tag)
        tags[place] = tag.astype(jnp.float32)

    def turn(g, carried):
        quad_at = low + 2 * g
        finish(carried, quad_at - 1)
        for i in range(GROUP):
            packed = block_ref[jnp.minimum(quad_at * QUAD + i, last)]
            block, count = packed // COUNT_SPAN, packed % COUNT_SPAN
            at = pl.ds(pl.multiple_of(block * 2 * tiles, 2 * tiles), 2 * tiles)
            both = jnp.where(vis_at < count, res_ref[at, :], 0.0)
            gathered[pl.ds(i, 2 * tiles, stride=GROUP), :] = uv_ref[at, :]
            gathered[pl.ds(2 * tiles * GROUP + i, 2 * tiles, stride=GROUP), :] = both
        u, v, re, im = [
            jnp.concatenate(
                [
                    gathered[pl.ds(((k // 2) * 2 * tiles + 2 * t + k % 2) * GROUP, GROUP), :]
                    for t in range(tiles)
                ],
                1,
            )
            for k in range(4)
        ]
        c, s = first_angle(u)
        a, b, e, f = re * c, im * s, im * c, re * s
        after = (a - b, e + f)
        before = (a + b, e - f)
        second = [2.0 * c * near - far for near, far in zip(before, (re, im))]
        left_mid = [by_quad(x, y) for x, y in zip((re, im), after)]
        left_low = [by_quad(x, y) for x, y in zip(second, before)]
        factor = 2.0 - 4.0 * s * s
        left_factor = by_quad(factor, factor)
        c, s = first_angle(v)
        c2, s2 = 1.0 - 2.0 * s * s, 2.0 * s * c
        right_mid = [by_quad(jnp.ones_like(c), c), by_quad(jnp.zeros_like(s), s)]
        right_low = [by_quad(c2, c), by_quad(-s2, -s)]
        factor = 2.0 * c2
        right_factor = by_quad(factor, factor)
        rows = []
        for quad in range(2):
            left, right = [], []
            for part in range(2):
                left += sequence(left_low[part][quad], left_mid[part][quad], left_factor[quad])
                right += sequence(right_low[part][quad], right_mid[part][quad], right_factor[quad])
            rows.append([jnp.concatenate(x, 0) for x in (left, right)])
        finish(rows[0], quad_at)
        return rows[1]

    turns = (high - low + 1) // 2
    nothing = jnp.zeros((4 * STEPS * QUAD, tiles * LANES), jnp.bfloat16)
    finish(lax.fori_loop(0, turns, turn, [nothing, nothing]), low + 2 * turns - 1)

    shares = capacity // TAG_ROWS
    share = lax.broadcasted_iota(jnp.int32, (TAG_ROWS, LANES), 1) // (LANES // shares)
    for d, out_ref in enumerate(out_refs):
        for m in range(out_ref.shape[0] // message_rows(capacity)):
            base = m * message_rows(capacity)
            sent = start_ref[first + d + m + 1] - start_ref[first + d + m]
            slot = (d + m) * (capacity // QUAD)
            tag = jnp.zeros((TAG_ROWS, LANES), jnp.float32)
            for n in range(shares):
                at = slot + n * 4
                four = jnp.concatenate([tags[at + k] for k in range(4)], 0)
                tag = jnp.where(share == n, four, tag)
                rows = jnp.concatenate([found[at + k] for k in range(4)], 0)
                moved = jnp.dot(rows, mover[...], preferred_element_type=jnp.float32)
                for piece in range(PIECES // 2):
                    part = []
                    for k in range(4):
                        value = moved[(k * 8 + piece) * GROUP : (k * 8 + piece + 1) * GROUP]
                        part.append(jnp.where(n * 4 + k < sent, value, 0.0))
                    for parity in range(2):
                        pair = []
                        for k in (0, 2):
                            if parity == 0:
                                pair.append(jnp.where(top, part[k], pltpu.roll(part[k + 1], QUAD, 0)))
                            else:
                                pair.append(jnp.where(top, pltpu.roll(part[k], QUAD, 0), part[k + 1]))
                        put = base + (piece * 2 + parity) * capacity + n * TAG_ROWS
                        out_ref[pl.ds(put, TAG_ROWS), :] = jnp.concatenate(pair, 0).astype(jnp.bfloat16)
            out_ref[pl.ds(base + PIECES * capacity, TAG_ROWS), :] = tag.astype(jnp.bfloat16)


def message_rows(capacity):
    return PIECES * capacity + TAG_ROWS


def make_subgrids(first, outs, token, capacity, block, row, start, uv, res, vis):
    tiles = vis // LANES
    destinations = sum(outs)
    quads = destinations * capacity // QUAD
    vmem = pl.BlockSpec(memory_space=pltpu.VMEM)
    smem = pl.BlockSpec(memory_space=pltpu.SMEM)
    return pl.pallas_call(
        functools.partial(subgrid_kernel, first, destinations, capacity),
        out_shape=[
            jax.ShapeDtypeStruct((n * message_rows(capacity), LANES), jnp.bfloat16) for n in outs
        ]
        + [jax.ShapeDtypeStruct(token.shape, token.dtype)],
        in_specs=[smem] * 3 + [vmem] * 3,
        out_specs=[vmem] * (len(outs) + 1),
        scratch_shapes=[
            pltpu.VMEM((4 * tiles * GROUP, LANES), jnp.float32),
            pltpu.VMEM((quads + 1, FEATURE // SUB, 4 * LANES), jnp.bfloat16),
            pltpu.VMEM((quads + 1, QUAD, LANES), jnp.float32),
            pltpu.VMEM((4 * LANES, LANES), jnp.bfloat16),
        ],
        compiler_params=pltpu.CompilerParams(vmem_limit_bytes=VMEM_LIMIT),
        cost_estimate=pl.CostEstimate(
            flops=quads * 32 * SUB * SUB * vis, bytes_accessed=16 * quads * FEATURE, transcendentals=0
        ),
        name="subgrids",
    )(block, row, start, token, uv, res)


def gather_kernel(capacity, *refs):
    x_refs, (out_ref, xs, tags, hot, part) = refs[:-5], refs[-5:]
    lane = lax.broadcasted_iota(jnp.int32, (GROUP, LANES), 1) // SUB
    shares = capacity // TAG_ROWS
    at = 0
    for x_ref in x_refs:
        for base in range(0, x_ref.shape[0], message_rows(capacity)):
            for piece in range(PIECES):
                xs[piece, pl.ds(at, capacity), :] = x_ref[pl.ds(base + piece * capacity, capacity), :]
            tag = x_ref[pl.ds(base + PIECES * capacity, TAG_ROWS), :].astype(jnp.float32)
            for n in range(shares):
                column = n * (LANES // shares)
                tags[pl.ds(at + n * TAG_ROWS, TAG_ROWS), :] = jnp.broadcast_to(
                    tag[:, column : column + 1], (TAG_ROWS, LANES)
                )
            at += capacity
    wanted = lax.broadcasted_iota(jnp.int32, tags.shape, 1)
    wanted = (wanted % 32) * 4 + wanted // 32 + 1
    hot[...] = jnp.where(tags[...] == wanted.astype(jnp.float32), 1.0, 0.0).T.astype(jnp.bfloat16)
    for piece in range(PIECES):
        c, rows, parity = piece // 8, piece // 2 % 4, piece % 2
        part[...] = jnp.dot(hot[...], xs[piece], preferred_element_type=jnp.float32)
        for grp in range(4):
            given = [part[pl.ds(32 * jl + 8 * grp, 8), :] for jl in range(4)]
            for a in range(4):
                total = None
                for jl in range(4):
                    moved = given[jl]
                    if a != jl:
                        moved = pltpu.roll(moved, ((jl - a) % 4) * SUB, 1)
                    total = moved if total is None else jnp.where(lane == jl, moved, total)
                p = rows * 8 + a * 2 + parity
                out_ref[pl.ds(p * 64 + grp * 16 + c, 8, stride=2), :] = total


def sum_slots(arrived, capacity):
    rows = sum(x.shape[0] for x in arrived) // message_rows(capacity) * capacity
    vmem = pl.BlockSpec(memory_space=pltpu.VMEM)
    return pl.pallas_call(
        functools.partial(gather_kernel, capacity),
        out_shape=jax.ShapeDtypeStruct((SUB * 64, LANES), jnp.float32),
        in_specs=[vmem] * len(arrived),
        out_specs=vmem,
        scratch_shapes=[
            pltpu.VMEM((PIECES, rows, LANES), jnp.bfloat16),
            pltpu.VMEM((rows, LANES), jnp.float32),
            pltpu.VMEM((SLOTS, rows), jnp.bfloat16),
            pltpu.VMEM((SLOTS, LANES), jnp.float32),
        ],
        compiler_params=pltpu.CompilerParams(vmem_limit_bytes=VMEM_LIMIT),
        name="sum_slots",
    )(*arrived)


def rows_of(array):
    blocks, parts, vis = array.shape
    tiles = vis // LANES
    split = array.reshape(blocks, parts, tiles, LANES)
    return split.transpose(0, 2, 1, 3).reshape(blocks * tiles * parts, LANES)


def sending_order(owners):
    near = [d for d in range(1, owners // 2) if d & 1] + [d for d in range(2, owners // 2, 2)]
    far = list(range(owners - 1, max(owners // 2, 1) - 1, -1))
    return near[:2] + far + near[2:] + [0]


def in_rows(array):
    return with_layout_constraint(array, Layout(major_to_minor=(0, 1)))


def local(residual, uv_offsets, counts, tile_of_block, slot_of_block, owner_map):
    blocks, _, vis = uv_offsets.shape
    owners = owner_map.shape[0]
    capacity = -(-max(CAP_MIN, 2 * blocks // owners) // 32) * 16
    core = lax.axis_index("samp")
    me = lax.axis_index(("blk", "tile"))
    swap = [(0, 1), (1, 0)]
    own = in_rows(rows_of(residual[0]))
    other = in_rows(lax.ppermute(own, "samp", swap))

    tile_ids = tile_of_block[:, 0]
    owner_range = jnp.arange(owners, dtype=jnp.int32)
    owner_ids = jnp.sum(
        jnp.where(tile_ids[:, None] == owner_range[None, :], owner_map[None, :], 0), 1
    )
    paired = owners <= PAIRED_MAX and owners & (owners - 1) == 0
    distances = sending_order(owners)
    offset = owner_ids
    if paired:
        offset = jnp.bitwise_xor(owner_ids, me)
        offset = jnp.sum(
            jnp.where(offset[:, None] == jnp.array(distances)[None, :], owner_range[None, :], 0), 1
        )
    index = jnp.arange(blocks, dtype=jnp.int32)
    same = (offset[None, :] == offset[:, None]) & (index[None, :] < index[:, None])
    rank = jnp.sum(same.astype(jnp.int32), 1)
    mine = (rank & 1) == core
    counted = jnp.sum((mine[None, :] & (offset[None, :] == owner_range[:, None])).astype(jnp.int32), 1)
    quads = (counted + QUAD - 1) // QUAD
    edges = jnp.arange(owners + 1, dtype=jnp.int32)
    start = jnp.sum(jnp.where(owner_range[None, :] < edges[:, None], quads[None, :], 0), 1)
    before = jnp.sum(jnp.where(owner_range[None, :] < offset[:, None], quads[None, :], 0), 1)
    place = jnp.where(mine, before * QUAD + rank // 2, -1)
    longest = ((blocks + owners) // 2 + owners * (QUAD - 1)) // GROUP * GROUP + GROUP
    wanted = jnp.arange(longest, dtype=jnp.int32)
    chosen = place[None, :] == wanted[:, None]
    block_and_count = index * COUNT_SPAN + counts
    row_and_tag = (offset * capacity + rank // 2) * (2 * SLOTS) + slot_of_block + 1
    block = jnp.sum(jnp.where(chosen, block_and_count[None, :], 0), 1)
    row = jnp.sum(jnp.where(chosen, row_and_tag[None, :], 0), 1)

    subgrids = functools.partial(
        make_subgrids, capacity=capacity, block=block, row=row, start=start, uv=rows_of(uv_offsets),
        res=own.astype(jnp.float32) + other.astype(jnp.float32), vis=vis,
    )
    token = jnp.zeros((GROUP, LANES), jnp.int32)
    if paired:
        rows = subgrids(0, (1,) * owners, token)[:-1]
        arrived = []
        for distance, piece in zip(distances, rows):
            if distance:
                pairs = [(k, k ^ distance) for k in range(owners)]
                piece = lax.ppermute(piece, ("blk", "tile"), pairs)
            arrived.append(piece)
    else:
        each = max(d for d in range(1, 17) if owners % d == 0)
        rows = [subgrids(k, (each,), token)[0] for k in range(0, owners, each)]
        rows = jnp.concatenate(rows, 0).reshape(owners, message_rows(capacity), LANES)
        rows = lax.all_to_all(rows, ("blk", "tile"), split_axis=0, concat_axis=0, tiled=True)
        arrived = [rows.reshape(owners * message_rows(capacity), LANES)]
    part = sum_slots(arrived, capacity)
    whole = part + lax.ppermute(part, "samp", swap)
    whole = whole.reshape(SUB, SLOTS // 4, 2, LANES).transpose(0, 2, 1, 3)
    return whole.reshape(SUB, 2, SLOTS * SUB)


def solution(mesh):
    in_specs = (
        P("samp", ("cuts", "blk", "tile"), None, None),
        P(("cuts", "blk", "tile"), None, None),
        P(("cuts", "blk", "tile")),
        P(("cuts", "blk", "tile"), None),
        P(("cuts", "blk", "tile")),
        P(),
    )
    out_specs = P(("cuts", "blk", "tile"), None, None)
    return jax.shard_map(local, mesh=mesh, in_specs=in_specs, out_specs=out_specs, check_vma=False)
```

```python
import functools

import jax
import jax.numpy as jnp
import numpy as np
from jax import lax
from jax.experimental import pallas as pl
from jax.experimental.layout import Layout, with_layout_constraint
from jax.experimental.pallas import tpu as pltpu
from jax.sharding import PartitionSpec as P

SUB = 32
STEPS = SUB // 2
SLOTS = 128
LANES = 128
FEATURE = 2 * SUB * SUB
PIECES = FEATURE // LANES
CAP_MIN = 8
GROUP = 8
QUAD = 4
TAG_ROWS = 16
COUNT_SPAN = 4096
CHUNK = 2 * LANES
PAIRED_MAX = 16
VMEM_LIMIT = 48 * 1024 * 1024


def turn_coefficients():
    knots = np.cos(np.pi * (np.arange(400) + 0.5) / 400)
    cheb = np.polynomial.chebyshev
    even = cheb.cheb2poly(cheb.chebfit(knots, np.cos(np.pi * knots), 12))[0::2]
    odd = cheb.cheb2poly(cheb.chebfit(knots, np.sin(np.pi * knots), 13))[1::2]
    return [float(x) for x in even], [float(x) for x in odd]


COS_COEF, SIN_COEF = turn_coefficients()


def horner(coef, x):
    total = coef[-1] * x + coef[-2]
    for value in coef[-3::-1]:
        total = total * x + value
    return total


def first_angle(offset):
    y = offset * (1.0 / STEPS)
    x = y * y
    return horner(COS_COEF, x), horner(SIN_COEF, x) * y


def tile_of(value, t):
    return value[:, t * LANES : (t + 1) * LANES]


def by_quad(even, odd):
    top = lax.broadcasted_iota(jnp.int32, even.shape, 0) < QUAD
    return (
        jnp.where(top, even, pltpu.roll(odd, QUAD, 0)),
        jnp.where(top, pltpu.roll(even, QUAD, 0), odd),
    )


def sequence(before, middle, factor):
    def pair(*two):
        return jnp.concatenate(two, 0).astype(jnp.bfloat16)

    up, down = [], []
    last, value = before, middle
    for _ in range(STEPS // 4):
        after = factor * value - last
        up.append(pair(value, after))
        last, value = after, factor * after - value
    last, value = middle, before
    for _ in range(STEPS // 4):
        after = factor * value - last
        down.append(pair(after, value))
        last, value = after, factor * after - value
    return down[::-1] + up


def subgrid_kernel(
    first, destinations, capacity, block_ref, row_ref, start_ref, token_ref, uv_ref, res_ref, *refs
):
    out_refs, (next_ref, gathered, found, tags, mover) = refs[:-5], refs[-5:]
    next_ref[...] = jnp.zeros_like(next_ref)
    tiles = gathered.shape[0] // (4 * GROUP)
    spare = destinations * capacity // QUAD
    low, high = start_ref[first], start_ref[first + destinations]
    last = block_ref.shape[0] - 1
    vis_at = lax.broadcasted_iota(jnp.int32, (2 * tiles, LANES), 1) + LANES * (
        lax.broadcasted_iota(jnp.int32, (2 * tiles, LANES), 0) // 2
    )
    same_block = (
        lax.broadcasted_iota(jnp.int32, (2 * STEPS * QUAD, LANES), 0) % QUAD
        == lax.broadcasted_iota(jnp.int32, (2 * STEPS * QUAD, LANES), 1) % QUAD
    )
    quad_row = lax.broadcasted_iota(jnp.int32, (QUAD, LANES), 0)
    top = lax.broadcasted_iota(jnp.int32, (GROUP, LANES), 0) < QUAD

    source = lax.broadcasted_iota(jnp.int32, mover.shape, 0)
    lane = lax.broadcasted_iota(jnp.int32, mover.shape, 1)
    moves = (source // LANES == lane // SUB) & (source % LANES // QUAD == lane % SUB)
    mover[...] = jnp.where(moves, 1.0, 0.0).astype(jnp.bfloat16)
    tags[...] = jnp.zeros_like(tags)

    def angles(quad_at):
        for i in range(GROUP):
            packed = block_ref[jnp.minimum(quad_at * QUAD + i, last)]
            block, count = packed // COUNT_SPAN, packed % COUNT_SPAN
            at = pl.ds(pl.multiple_of(block * 2 * tiles, 2 * tiles), 2 * tiles)
            both = jnp.where(vis_at < count, res_ref[at, :], 0.0)
            gathered[pl.ds(i, 2 * tiles, stride=GROUP), :] = uv_ref[at, :]
            gathered[pl.ds(2 * tiles * GROUP + i, 2 * tiles, stride=GROUP), :] = both
        u, v, re, im = [
            jnp.concatenate(
                [
                    gathered[pl.ds(((k // 2) * 2 * tiles + 2 * t + k % 2) * GROUP, GROUP), :]
                    for t in range(tiles)
                ],
                1,
            )
            for k in range(4)
        ]
        c, s = first_angle(u)
        a, b, e, f = re * c, im * s, im * c, re * s
        after = (a - b, e + f)
        before = (a + b, e - f)
        second = [2.0 * c * near - far for near, far in zip(before, (re, im))]
        factor = 2.0 - 4.0 * s * s
        left_factor = by_quad(factor, factor)
        left = [(by_quad(x, y), by_quad(z, w)) for x, y, z, w in zip(second, before, (re, im), after)]
        c, s = first_angle(v)
        c2, s2 = 1.0 - 2.0 * s * s, 2.0 * s * c
        factor = 2.0 * c2
        right_factor = by_quad(factor, factor)
        right = [
            (by_quad(c2, c), by_quad(jnp.ones_like(c), c)),
            (by_quad(-s2, -s), by_quad(jnp.zeros_like(s), s)),
        ]
        return [
            [
                (left[0][0][q], left[0][1][q], left[1][0][q], left[1][1][q], left_factor[q]),
                (right[0][0][q], right[0][1][q], right[1][0][q], right[1][1][q], right_factor[q]),
            ]
            for q in range(2)
        ]

    def finish(seeds, quad_at):
        product = None
        for lanes in range(0, tiles * LANES, CHUNK):
            operands = []
            for side in seeds[::-1]:
                before, middle, before_imag, middle_imag, factor = [
                    x[:, lanes : lanes + CHUNK] for x in side
                ]
                operands.append(
                    jnp.concatenate(
                        sequence(before, middle, factor)
                        + sequence(before_imag, middle_imag, factor),
                        0,
                    )
                )
            term = lax.dot_general(
                operands[1], operands[0], (((1,), (1,)), ((), ())),
                preferred_element_type=jnp.float32,
            )
            product = term if product is None else product + term
        half = product.shape[0] // 2
        wholes = (
            product[:half, :LANES] - product[half:, LANES:],
            product[half:, :LANES] + product[:half, LANES:],
        )
        rows = []
        for whole in wholes:
            whole = jnp.where(same_block, whole, 0.0)
            for j in range(0, STEPS, 4):
                four = [whole[(j + k) * GROUP : (j + k + 1) * GROUP] for k in range(4)]
                rows.append(jnp.concatenate(four, 1))
        index = jnp.clip(quad_at * QUAD, 0, last + 1 - QUAD)
        place = row_ref[index] // (2 * SLOTS * QUAD) - first * (capacity // QUAD)
        place = jnp.where((quad_at >= low) & (quad_at < high), place, spare)
        found[place] = jnp.concatenate(rows, 0).astype(jnp.bfloat16)
        tag = jnp.zeros((QUAD, LANES), jnp.int32)
        for b in range(QUAD):
            tag = jnp.where(quad_row == b, row_ref[index + b] % (2 * SLOTS), tag)
        tags[place] = tag.astype(jnp.float32)

    def turn(g, seeds):
        quad_at = low + 2 * g
        for q in range(2):
            finish(seeds[q], quad_at + q)
        return angles(quad_at + 2)

    lax.fori_loop(0, (high - low + 1) // 2, turn, angles(low))

    shares = capacity // TAG_ROWS
    share = lax.broadcasted_iota(jnp.int32, (TAG_ROWS, LANES), 1) // (LANES // shares)
    for d, out_ref in enumerate(out_refs):
        for m in range(out_ref.shape[0] // message_rows(capacity)):
            base = m * message_rows(capacity)
            sent = start_ref[first + d + m + 1] - start_ref[first + d + m]
            slot = (d + m) * (capacity // QUAD)
            tag = jnp.zeros((TAG_ROWS, LANES), jnp.float32)
            for n in range(shares):
                at = slot + n * 4
                four = jnp.concatenate([tags[at + k] for k in range(4)], 0)
                tag = jnp.where(share == n, four, tag)
                rows = jnp.concatenate([found[at + k] for k in range(4)], 0)
                moved = jnp.dot(rows, mover[...], preferred_element_type=jnp.float32)
                for piece in range(PIECES // 2):
                    part = []
                    for k in range(4):
                        value = moved[(k * 8 + piece) * GROUP : (k * 8 + piece + 1) * GROUP]
                        part.append(jnp.where(n * 4 + k < sent, value, 0.0))
                    for parity in range(2):
                        pair = []
                        for k in (0, 2):
                            if parity == 0:
                                pair.append(jnp.where(top, part[k], pltpu.roll(part[k + 1], QUAD, 0)))
                            else:
                                pair.append(jnp.where(top, pltpu.roll(part[k], QUAD, 0), part[k + 1]))
                        put = base + (piece * 2 + parity) * capacity + n * TAG_ROWS
                        out_ref[pl.ds(put, TAG_ROWS), :] = jnp.concatenate(pair, 0).astype(jnp.bfloat16)
            out_ref[pl.ds(base + PIECES * capacity, TAG_ROWS), :] = tag.astype(jnp.bfloat16)


def message_rows(capacity):
    return PIECES * capacity + TAG_ROWS


def make_subgrids(first, outs, token, capacity, block, row, start, uv, res, vis):
    tiles = vis // LANES
    destinations = sum(outs)
    quads = destinations * capacity // QUAD
    vmem = pl.BlockSpec(memory_space=pltpu.VMEM)
    smem = pl.BlockSpec(memory_space=pltpu.SMEM)
    return pl.pallas_call(
        functools.partial(subgrid_kernel, first, destinations, capacity),
        out_shape=[
            jax.ShapeDtypeStruct((n * message_rows(capacity), LANES), jnp.bfloat16) for n in outs
        ]
        + [jax.ShapeDtypeStruct(token.shape, token.dtype)],
        in_specs=[smem] * 3 + [vmem] * 3,
        out_specs=[vmem] * (len(outs) + 1),
        scratch_shapes=[
            pltpu.VMEM((4 * tiles * GROUP, LANES), jnp.float32),
            pltpu.VMEM((quads + 1, FEATURE // SUB, 4 * LANES), jnp.bfloat16),
            pltpu.VMEM((quads + 1, QUAD, LANES), jnp.float32),
            pltpu.VMEM((4 * LANES, LANES), jnp.bfloat16),
        ],
        compiler_params=pltpu.CompilerParams(vmem_limit_bytes=VMEM_LIMIT),
        cost_estimate=pl.CostEstimate(
            flops=quads * 32 * SUB * SUB * vis, bytes_accessed=16 * quads * FEATURE, transcendentals=0
        ),
        name="subgrids",
    )(block, row, start, token, uv, res)


def gather_kernel(capacity, *refs):
    x_refs, (out_ref, xs, tags, hot, part) = refs[:-5], refs[-5:]
    lane = lax.broadcasted_iota(jnp.int32, (GROUP, LANES), 1) // SUB
    shares = capacity // TAG_ROWS
    at = 0
    for x_ref in x_refs:
        for base in range(0, x_ref.shape[0], message_rows(capacity)):
            for piece in range(PIECES):
                xs[piece, pl.ds(at, capacity), :] = x_ref[pl.ds(base + piece * capacity, capacity), :]
            tag = x_ref[pl.ds(base + PIECES * capacity, TAG_ROWS), :].astype(jnp.float32)
            for n in range(shares):
                column = n * (LANES // shares)
                tags[pl.ds(at + n * TAG_ROWS, TAG_ROWS), :] = jnp.broadcast_to(
                    tag[:, column : column + 1], (TAG_ROWS, LANES)
                )
            at += capacity
    wanted = lax.broadcasted_iota(jnp.int32, tags.shape, 1)
    wanted = (wanted % 32) * 4 + wanted // 32 + 1
    hot[...] = jnp.where(tags[...] == wanted.astype(jnp.float32), 1.0, 0.0).T.astype(jnp.bfloat16)
    for piece in range(PIECES):
        c, rows, parity = piece // 8, piece // 2 % 4, piece % 2
        part[...] = jnp.dot(hot[...], xs[piece], preferred_element_type=jnp.float32)
        for grp in range(4):
            given = [part[pl.ds(32 * jl + 8 * grp, 8), :] for jl in range(4)]
            for a in range(4):
                total = None
                for jl in range(4):
                    moved = given[jl]
                    if a != jl:
                        moved = pltpu.roll(moved, ((jl - a) % 4) * SUB, 1)
                    total = moved if total is None else jnp.where(lane == jl, moved, total)
                p = rows * 8 + a * 2 + parity
                out_ref[pl.ds(p * 64 + grp * 16 + c, 8, stride=2), :] = total


def sum_slots(arrived, capacity):
    rows = sum(x.shape[0] for x in arrived) // message_rows(capacity) * capacity
    vmem = pl.BlockSpec(memory_space=pltpu.VMEM)
    return pl.pallas_call(
        functools.partial(gather_kernel, capacity),
        out_shape=jax.ShapeDtypeStruct((SUB * 64, LANES), jnp.float32),
        in_specs=[vmem] * len(arrived),
        out_specs=vmem,
        scratch_shapes=[
            pltpu.VMEM((PIECES, rows, LANES), jnp.bfloat16),
            pltpu.VMEM((rows, LANES), jnp.float32),
            pltpu.VMEM((SLOTS, rows), jnp.bfloat16),
            pltpu.VMEM((SLOTS, LANES), jnp.float32),
        ],
        compiler_params=pltpu.CompilerParams(vmem_limit_bytes=VMEM_LIMIT),
        name="sum_slots",
    )(*arrived)


def rows_of(array):
    blocks, parts, vis = array.shape
    tiles = vis // LANES
    split = array.reshape(blocks, parts, tiles, LANES)
    return split.transpose(0, 2, 1, 3).reshape(blocks * tiles * parts, LANES)


def sending_order(owners):
    return list(range(owners - 1, -1, -1))


def in_rows(array):
    return with_layout_constraint(array, Layout(major_to_minor=(0, 1)))


def local(residual, uv_offsets, counts, tile_of_block, slot_of_block, owner_map):
    blocks, _, vis = uv_offsets.shape
    owners = owner_map.shape[0]
    capacity = -(-max(CAP_MIN, 2 * blocks // owners) // 32) * 16
    core = lax.axis_index("samp")
    me = lax.axis_index(("blk", "tile"))
    swap = [(0, 1), (1, 0)]
    own = in_rows(rows_of(residual[0]))
    other = in_rows(lax.ppermute(own, "samp", swap))

    tile_ids = tile_of_block[:, 0]
    owner_range = jnp.arange(owners, dtype=jnp.int32)
    owner_ids = jnp.sum(
        jnp.where(tile_ids[:, None] == owner_range[None, :], owner_map[None, :], 0), 1
    )
    paired = owners <= PAIRED_MAX and owners & (owners - 1) == 0
    distances = sending_order(owners)
    offset = owner_ids
    if paired:
        offset = jnp.bitwise_xor(owner_ids, me)
        offset = jnp.sum(
            jnp.where(offset[:, None] == jnp.array(distances)[None, :], owner_range[None, :], 0), 1
        )
    index = jnp.arange(blocks, dtype=jnp.int32)
    same = (offset[None, :] == offset[:, None]) & (index[None, :] < index[:, None])
    rank = jnp.sum(same.astype(jnp.int32), 1)
    mine = (rank & 1) == core
    counted = jnp.sum((mine[None, :] & (offset[None, :] == owner_range[:, None])).astype(jnp.int32), 1)
    quads = (counted + QUAD - 1) // QUAD
    edges = jnp.arange(owners + 1, dtype=jnp.int32)
    start = jnp.sum(jnp.where(owner_range[None, :] < edges[:, None], quads[None, :], 0), 1)
    before = jnp.sum(jnp.where(owner_range[None, :] < offset[:, None], quads[None, :], 0), 1)
    place = jnp.where(mine, before * QUAD + rank // 2, -1)
    longest = ((blocks + owners) // 2 + owners * (QUAD - 1)) // GROUP * GROUP + GROUP
    wanted = jnp.arange(longest, dtype=jnp.int32)
    chosen = place[None, :] == wanted[:, None]
    block_and_count = index * COUNT_SPAN + counts
    row_and_tag = (offset * capacity + rank // 2) * (2 * SLOTS) + slot_of_block + 1
    block = jnp.sum(jnp.where(chosen, block_and_count[None, :], 0), 1)
    row = jnp.sum(jnp.where(chosen, row_and_tag[None, :], 0), 1)

    subgrids = functools.partial(
        make_subgrids, capacity=capacity, block=block, row=row, start=start, uv=rows_of(uv_offsets),
        res=own.astype(jnp.float32) + other.astype(jnp.float32), vis=vis,
    )
    token = jnp.zeros((GROUP, LANES), jnp.int32)
    if paired:
        far = owners * 3 // 8
        rows = []
        for first, last in ((0, far), (far, owners)):
            if first < last:
                *more, token = subgrids(first, (1,) * (last - first), token)
                rows += more
        arrived = []
        for distance, piece in zip(distances, rows):
            if distance:
                pairs = [(k, k ^ distance) for k in range(owners)]
                piece = lax.ppermute(piece, ("blk", "tile"), pairs)
            arrived.append(piece)
    else:
        each = max(d for d in range(1, 17) if owners % d == 0)
        rows = [subgrids(k, (each,), token)[0] for k in range(0, owners, each)]
        rows = jnp.concatenate(rows, 0).reshape(owners, message_rows(capacity), LANES)
        rows = lax.all_to_all(rows, ("blk", "tile"), split_axis=0, concat_axis=0, tiled=True)
        arrived = [rows.reshape(owners * message_rows(capacity), LANES)]
    part = sum_slots(arrived, capacity)
    whole = part + lax.ppermute(part, "samp", swap)
    whole = whole.reshape(SUB, SLOTS // 4, 2, LANES).transpose(0, 2, 1, 3)
    return whole.reshape(SUB, 2, SLOTS * SUB)


def solution(mesh):
    in_specs = (
        P("samp", ("cuts", "blk", "tile"), None, None),
        P(("cuts", "blk", "tile"), None, None),
        P(("cuts", "blk", "tile")),
        P(("cuts", "blk", "tile"), None),
        P(("cuts", "blk", "tile")),
        P(),
    )
    out_specs = P(("cuts", "blk", "tile"), None, None)
    return jax.shard_map(local, mesh=mesh, in_specs=in_specs, out_specs=out_specs, check_vma=False)
```

```python
import functools

import jax
import jax.numpy as jnp
import numpy as np
from jax import lax
from jax.experimental import pallas as pl
from jax.experimental.layout import Layout, with_layout_constraint
from jax.experimental.pallas import tpu as pltpu
from jax.sharding import PartitionSpec as P

SUB = 32
STEPS = SUB // 2
SLOTS = 128
LANES = 128
FEATURE = 2 * SUB * SUB
PIECES = FEATURE // LANES
CAP_MIN = 8
GROUP = 8
QUAD = 4
TAG_ROWS = 16
COUNT_SPAN = 4096
CHUNK = 2 * LANES
PAIRED_MAX = 16
CALLS = (0, 2, 4, 8)
VMEM_LIMIT = 48 * 1024 * 1024


def turn_coefficients():
    knots = np.cos(np.pi * (np.arange(400) + 0.5) / 400)
    cheb = np.polynomial.chebyshev
    even = cheb.cheb2poly(cheb.chebfit(knots, np.cos(np.pi * knots), 12))[0::2]
    odd = cheb.cheb2poly(cheb.chebfit(knots, np.sin(np.pi * knots), 13))[1::2]
    return [float(x) for x in even], [float(x) for x in odd]


COS_COEF, SIN_COEF = turn_coefficients()


def horner(coef, x):
    total = coef[-1] * x + coef[-2]
    for value in coef[-3::-1]:
        total = total * x + value
    return total


def first_angle(offset):
    y = offset * (1.0 / STEPS)
    x = y * y
    return horner(COS_COEF, x), horner(SIN_COEF, x) * y


def tile_of(value, t):
    return value[:, t * LANES : (t + 1) * LANES]


def by_quad(even, odd):
    top = lax.broadcasted_iota(jnp.int32, even.shape, 0) < QUAD
    return (
        jnp.where(top, even, pltpu.roll(odd, QUAD, 0)),
        jnp.where(top, pltpu.roll(even, QUAD, 0), odd),
    )


def sequence(before, middle, factor):
    def pair(*two):
        return jnp.concatenate(two, 0).astype(jnp.bfloat16)

    up, down = [], []
    last, value = before, middle
    for _ in range(STEPS // 4):
        after = factor * value - last
        up.append(pair(value, after))
        last, value = after, factor * after - value
    last, value = middle, before
    for _ in range(STEPS // 4):
        after = factor * value - last
        down.append(pair(after, value))
        last, value = after, factor * after - value
    return down[::-1] + up


def subgrid_kernel(
    first, destinations, capacity, block_ref, row_ref, start_ref, token_ref, uv_ref, res_ref, *refs
):
    out_refs, (next_ref, gathered, found, tags, mover) = refs[:-5], refs[-5:]
    next_ref[...] = jnp.zeros_like(next_ref)
    tiles = gathered.shape[0] // (4 * GROUP)
    spare = destinations * capacity // QUAD
    low, high = start_ref[first], start_ref[first + destinations]
    last = block_ref.shape[0] - 1
    vis_at = lax.broadcasted_iota(jnp.int32, (2 * tiles, LANES), 1) + LANES * (
        lax.broadcasted_iota(jnp.int32, (2 * tiles, LANES), 0) // 2
    )
    same_block = (
        lax.broadcasted_iota(jnp.int32, (2 * STEPS * QUAD, LANES), 0) % QUAD
        == lax.broadcasted_iota(jnp.int32, (2 * STEPS * QUAD, LANES), 1) % QUAD
    )
    quad_row = lax.broadcasted_iota(jnp.int32, (QUAD, LANES), 0)
    top = lax.broadcasted_iota(jnp.int32, (GROUP, LANES), 0) < QUAD

    source = lax.broadcasted_iota(jnp.int32, mover.shape, 0)
    lane = lax.broadcasted_iota(jnp.int32, mover.shape, 1)
    moves = (source // LANES == lane // SUB) & (source % LANES // QUAD == lane % SUB)
    mover[...] = jnp.where(moves, 1.0, 0.0).astype(jnp.bfloat16)
    tags[...] = jnp.zeros_like(tags)

    def angles(quad_at):
        for i in range(GROUP):
            packed = block_ref[jnp.minimum(quad_at * QUAD + i, last)]
            block, count = packed // COUNT_SPAN, packed % COUNT_SPAN
            at = pl.ds(pl.multiple_of(block * 2 * tiles, 2 * tiles), 2 * tiles)
            both = jnp.where(vis_at < count, res_ref[at, :], 0.0)
            gathered[pl.ds(i, 2 * tiles, stride=GROUP), :] = uv_ref[at, :]
            gathered[pl.ds(2 * tiles * GROUP + i, 2 * tiles, stride=GROUP), :] = both
        u, v, re, im = [
            jnp.concatenate(
                [
                    gathered[pl.ds(((k // 2) * 2 * tiles + 2 * t + k % 2) * GROUP, GROUP), :]
                    for t in range(tiles)
                ],
                1,
            )
            for k in range(4)
        ]
        c, s = first_angle(u)
        a, b, e, f = re * c, im * s, im * c, re * s
        after = (a - b, e + f)
        before = (a + b, e - f)
        second = [2.0 * c * near - far for near, far in zip(before, (re, im))]
        factor = 2.0 - 4.0 * s * s
        left_factor = by_quad(factor, factor)
        left = [(by_quad(x, y), by_quad(z, w)) for x, y, z, w in zip(second, before, (re, im), after)]
        c, s = first_angle(v)
        c2, s2 = 1.0 - 2.0 * s * s, 2.0 * s * c
        factor = 2.0 * c2
        right_factor = by_quad(factor, factor)
        right = [
            (by_quad(c2, c), by_quad(jnp.ones_like(c), c)),
            (by_quad(-s2, -s), by_quad(jnp.zeros_like(s), s)),
        ]
        return [
            [
                (left[0][0][q], left[0][1][q], left[1][0][q], left[1][1][q], left_factor[q]),
                (right[0][0][q], right[0][1][q], right[1][0][q], right[1][1][q], right_factor[q]),
            ]
            for q in range(2)
        ]

    def finish(seeds, quad_at):
        product = None
        for lanes in range(0, tiles * LANES, CHUNK):
            operands = []
            for side in seeds[::-1]:
                before, middle, before_imag, middle_imag, factor = [
                    x[:, lanes : lanes + CHUNK] for x in side
                ]
                operands.append(
                    jnp.concatenate(
                        sequence(before, middle, factor)
                        + sequence(before_imag, middle_imag, factor),
                        0,
                    )
                )
            term = lax.dot_general(
                operands[1], operands[0], (((1,), (1,)), ((), ())),
                preferred_element_type=jnp.float32,
            )
            product = term if product is None else product + term
        half = product.shape[0] // 2
        wholes = (
            product[:half, :LANES] - product[half:, LANES:],
            product[half:, :LANES] + product[:half, LANES:],
        )
        rows = []
        for whole in wholes:
            whole = jnp.where(same_block, whole, 0.0)
            for j in range(0, STEPS, 4):
                four = [whole[(j + k) * GROUP : (j + k + 1) * GROUP] for k in range(4)]
                rows.append(jnp.concatenate(four, 1))
        index = jnp.clip(quad_at * QUAD, 0, last + 1 - QUAD)
        place = row_ref[index] // (2 * SLOTS * QUAD) - first * (capacity // QUAD)
        place = jnp.where((quad_at >= low) & (quad_at < high), place, spare)
        found[place] = jnp.concatenate(rows, 0).astype(jnp.bfloat16)
        tag = jnp.zeros((QUAD, LANES), jnp.int32)
        for b in range(QUAD):
            tag = jnp.where(quad_row == b, row_ref[index + b] % (2 * SLOTS), tag)
        tags[place] = tag.astype(jnp.float32)

    def turn(g, seeds):
        quad_at = low + 2 * g
        for q in range(2):
            finish(seeds[q], quad_at + q)
        return angles(quad_at + 2)

    lax.fori_loop(0, (high - low + 1) // 2, turn, angles(low))

    shares = capacity // TAG_ROWS
    share = lax.broadcasted_iota(jnp.int32, (TAG_ROWS, LANES), 1) // (LANES // shares)
    for d, out_ref in enumerate(out_refs):
        for m in range(out_ref.shape[0] // message_rows(capacity)):
            base = m * message_rows(capacity)
            sent = start_ref[first + d + m + 1] - start_ref[first + d + m]
            slot = (d + m) * (capacity // QUAD)
            tag = jnp.zeros((TAG_ROWS, LANES), jnp.float32)
            for n in range(shares):
                at = slot + n * 4
                four = jnp.concatenate([tags[at + k] for k in range(4)], 0)
                tag = jnp.where(share == n, four, tag)
                rows = jnp.concatenate([found[at + k] for k in range(4)], 0)
                moved = jnp.dot(rows, mover[...], preferred_element_type=jnp.float32)
                for piece in range(PIECES // 2):
                    part = []
                    for k in range(4):
                        value = moved[(k * 8 + piece) * GROUP : (k * 8 + piece + 1) * GROUP]
                        part.append(jnp.where(n * 4 + k < sent, value, 0.0))
                    for parity in range(2):
                        pair = []
                        for k in (0, 2):
                            if parity == 0:
                                pair.append(jnp.where(top, part[k], pltpu.roll(part[k + 1], QUAD, 0)))
                            else:
                                pair.append(jnp.where(top, pltpu.roll(part[k], QUAD, 0), part[k + 1]))
                        put = base + (piece * 2 + parity) * capacity + n * TAG_ROWS
                        out_ref[pl.ds(put, TAG_ROWS), :] = jnp.concatenate(pair, 0).astype(jnp.bfloat16)
            out_ref[pl.ds(base + PIECES * capacity, TAG_ROWS), :] = tag.astype(jnp.bfloat16)


def message_rows(capacity):
    return PIECES * capacity + TAG_ROWS


def make_subgrids(first, outs, token, capacity, block, row, start, uv, res, vis):
    tiles = vis // LANES
    destinations = sum(outs)
    quads = destinations * capacity // QUAD
    vmem = pl.BlockSpec(memory_space=pltpu.VMEM)
    smem = pl.BlockSpec(memory_space=pltpu.SMEM)
    return pl.pallas_call(
        functools.partial(subgrid_kernel, first, destinations, capacity),
        out_shape=[
            jax.ShapeDtypeStruct((n * message_rows(capacity), LANES), jnp.bfloat16) for n in outs
        ]
        + [jax.ShapeDtypeStruct(token.shape, token.dtype)],
        in_specs=[smem] * 3 + [vmem] * 3,
        out_specs=[vmem] * (len(outs) + 1),
        scratch_shapes=[
            pltpu.VMEM((4 * tiles * GROUP, LANES), jnp.float32),
            pltpu.VMEM((quads + 1, FEATURE // SUB, 4 * LANES), jnp.bfloat16),
            pltpu.VMEM((quads + 1, QUAD, LANES), jnp.float32),
            pltpu.VMEM((4 * LANES, LANES), jnp.bfloat16),
        ],
        compiler_params=pltpu.CompilerParams(vmem_limit_bytes=VMEM_LIMIT),
        cost_estimate=pl.CostEstimate(
            flops=quads * 32 * SUB * SUB * vis, bytes_accessed=16 * quads * FEATURE, transcendentals=0
        ),
        name="subgrids",
    )(block, row, start, token, uv, res)


def gather_kernel(capacity, *refs):
    x_refs, (out_ref, xs, tags, hot, part) = refs[:-5], refs[-5:]
    lane = lax.broadcasted_iota(jnp.int32, (GROUP, LANES), 1) // SUB
    shares = capacity // TAG_ROWS
    at = 0
    for x_ref in x_refs:
        for base in range(0, x_ref.shape[0], message_rows(capacity)):
            for piece in range(PIECES):
                xs[piece, pl.ds(at, capacity), :] = x_ref[pl.ds(base + piece * capacity, capacity), :]
            tag = x_ref[pl.ds(base + PIECES * capacity, TAG_ROWS), :].astype(jnp.float32)
            for n in range(shares):
                column = n * (LANES // shares)
                tags[pl.ds(at + n * TAG_ROWS, TAG_ROWS), :] = jnp.broadcast_to(
                    tag[:, column : column + 1], (TAG_ROWS, LANES)
                )
            at += capacity
    wanted = lax.broadcasted_iota(jnp.int32, tags.shape, 1)
    wanted = (wanted % 32) * 4 + wanted // 32 + 1
    hot[...] = jnp.where(tags[...] == wanted.astype(jnp.float32), 1.0, 0.0).T.astype(jnp.bfloat16)
    for piece in range(PIECES):
        c, rows, parity = piece // 8, piece // 2 % 4, piece % 2
        part[...] = jnp.dot(hot[...], xs[piece], preferred_element_type=jnp.float32)
        for grp in range(4):
            given = [part[pl.ds(32 * jl + 8 * grp, 8), :] for jl in range(4)]
            for a in range(4):
                total = None
                for jl in range(4):
                    moved = given[jl]
                    if a != jl:
                        moved = pltpu.roll(moved, ((jl - a) % 4) * SUB, 1)
                    total = moved if total is None else jnp.where(lane == jl, moved, total)
                p = rows * 8 + a * 2 + parity
                out_ref[pl.ds(p * 64 + grp * 16 + c, 8, stride=2), :] = total


def sum_slots(arrived, capacity):
    rows = sum(x.shape[0] for x in arrived) // message_rows(capacity) * capacity
    vmem = pl.BlockSpec(memory_space=pltpu.VMEM)
    return pl.pallas_call(
        functools.partial(gather_kernel, capacity),
        out_shape=jax.ShapeDtypeStruct((SUB * 64, LANES), jnp.float32),
        in_specs=[vmem] * len(arrived),
        out_specs=vmem,
        scratch_shapes=[
            pltpu.VMEM((PIECES, rows, LANES), jnp.bfloat16),
            pltpu.VMEM((rows, LANES), jnp.float32),
            pltpu.VMEM((SLOTS, rows), jnp.bfloat16),
            pltpu.VMEM((SLOTS, LANES), jnp.float32),
        ],
        compiler_params=pltpu.CompilerParams(vmem_limit_bytes=VMEM_LIMIT),
        name="sum_slots",
    )(*arrived)


def rows_of(array):
    blocks, parts, vis = array.shape
    tiles = vis // LANES
    split = array.reshape(blocks, parts, tiles, LANES)
    return split.transpose(0, 2, 1, 3).reshape(blocks * tiles * parts, LANES)


def sending_order(owners):
    return list(range(owners - 1, -1, -1))


def in_rows(array):
    return with_layout_constraint(array, Layout(major_to_minor=(0, 1)))


def local(residual, uv_offsets, counts, tile_of_block, slot_of_block, owner_map):
    blocks, _, vis = uv_offsets.shape
    owners = owner_map.shape[0]
    capacity = -(-max(CAP_MIN, 2 * blocks // owners) // 32) * 16
    core = lax.axis_index("samp")
    me = lax.axis_index(("blk", "tile"))
    swap = [(0, 1), (1, 0)]
    own = in_rows(rows_of(residual[0]))
    other = in_rows(lax.ppermute(own, "samp", swap))

    tile_ids = tile_of_block[:, 0]
    owner_range = jnp.arange(owners, dtype=jnp.int32)
    packed = jnp.sum(
        jnp.where(tile_ids[:, None] == owner_range[None, :], owner_map[None, :] * (SLOTS * COUNT_SPAN), 0), 1
    ) + (slot_of_block * COUNT_SPAN + counts)
    owner_ids = packed // (SLOTS * COUNT_SPAN)
    paired = owners <= PAIRED_MAX and owners & (owners - 1) == 0
    distances = sending_order(owners)
    offset = owner_ids
    if paired:
        offset = jnp.bitwise_xor(owner_ids, me)
        offset = jnp.sum(
            jnp.where(offset[:, None] == jnp.array(distances)[None, :], owner_range[None, :], 0), 1
        )
    index = jnp.arange(blocks, dtype=jnp.int32)
    same = (offset[None, :] == offset[:, None]) & (index[None, :] < index[:, None])
    rank = jnp.sum(same.astype(jnp.int32), 1)
    mine = (rank & 1) == core
    counted = jnp.sum((mine[None, :] & (offset[None, :] == owner_range[:, None])).astype(jnp.int32), 1)
    quads = (counted + QUAD - 1) // QUAD
    edges = jnp.arange(owners + 1, dtype=jnp.int32)
    start = jnp.sum(jnp.where(owner_range[None, :] < edges[:, None], quads[None, :], 0), 1)
    before = jnp.sum(jnp.where(owner_range[None, :] < offset[:, None], quads[None, :], 0), 1)
    place = jnp.where(mine, before * QUAD + rank // 2, -1)
    longest = ((blocks + owners) // 2 + owners * (QUAD - 1)) // GROUP * GROUP + GROUP
    wanted = jnp.arange(longest, dtype=jnp.int32)
    chosen = place[None, :] == wanted[:, None]
    block_and_count = index * COUNT_SPAN + packed % COUNT_SPAN
    row_and_tag = (offset * capacity + rank // 2) * (2 * SLOTS) + packed // COUNT_SPAN % SLOTS + 1
    block = jnp.sum(jnp.where(chosen, block_and_count[None, :], 0), 1)
    row = jnp.sum(jnp.where(chosen, row_and_tag[None, :], 0), 1)

    subgrids = functools.partial(
        make_subgrids, capacity=capacity, block=block, row=row, start=start, uv=rows_of(uv_offsets),
        res=own.astype(jnp.float32) + other.astype(jnp.float32), vis=vis,
    )
    token = jnp.zeros((GROUP, LANES), jnp.int32)
    if paired:
        rows = []
        for first, last in zip(CALLS[:-1], CALLS[1:]):
            first, last = owners * first // CALLS[-1], owners * last // CALLS[-1]
            if first < last:
                *more, token = subgrids(first, (1,) * (last - first), token)
                rows += more
        arrived = []
        for distance, piece in zip(distances, rows):
            if distance:
                pairs = [(k, k ^ distance) for k in range(owners)]
                piece = lax.ppermute(piece, ("blk", "tile"), pairs)
            arrived.append(piece)
    else:
        each = max(d for d in range(1, 17) if owners % d == 0)
        rows = [subgrids(k, (each,), token)[0] for k in range(0, owners, each)]
        rows = jnp.concatenate(rows, 0).reshape(owners, message_rows(capacity), LANES)
        rows = lax.all_to_all(rows, ("blk", "tile"), split_axis=0, concat_axis=0, tiled=True)
        arrived = [rows.reshape(owners * message_rows(capacity), LANES)]
    part = sum_slots(arrived, capacity)
    whole = part + lax.ppermute(part, "samp", swap)
    whole = whole.reshape(SUB, SLOTS // 4, 2, LANES).transpose(0, 2, 1, 3)
    return whole.reshape(SUB, 2, SLOTS * SUB)


def solution(mesh):
    in_specs = (
        P("samp", ("cuts", "blk", "tile"), None, None),
        P(("cuts", "blk", "tile"), None, None),
        P(("cuts", "blk", "tile")),
        P(("cuts", "blk", "tile"), None),
        P(("cuts", "blk", "tile")),
        P(),
    )
    out_specs = P(("cuts", "blk", "tile"), None, None)
    return jax.shard_map(local, mesh=mesh, in_specs=in_specs, out_specs=out_specs, check_vma=False)
```

```python
import functools

import jax
import jax.numpy as jnp
import numpy as np
from jax import lax
from jax.experimental import pallas as pl
from jax.experimental.layout import Layout, with_layout_constraint
from jax.experimental.pallas import tpu as pltpu
from jax.sharding import PartitionSpec as P

SUB = 32
STEPS = SUB // 2
SLOTS = 128
LANES = 128
FEATURE = 2 * SUB * SUB
PIECES = FEATURE // LANES
CAP_MIN = 8
GROUP = 8
QUAD = 4
TAG_ROWS = 16
COUNT_SPAN = 4096
CHUNK = 2 * LANES
PAIRED_MAX = 16
CALLS = (0, 2, 4, 8)
VMEM_LIMIT = 48 * 1024 * 1024


def turn_coefficients():
    knots = np.cos(np.pi * (np.arange(400) + 0.5) / 400)
    cheb = np.polynomial.chebyshev
    even = cheb.cheb2poly(cheb.chebfit(knots, np.cos(np.pi * knots), 12))[0::2]
    odd = cheb.cheb2poly(cheb.chebfit(knots, np.sin(np.pi * knots), 13))[1::2]
    return [float(x) for x in even], [float(x) for x in odd]


COS_COEF, SIN_COEF = turn_coefficients()


def horner(coef, x):
    total = coef[-1] * x + coef[-2]
    for value in coef[-3::-1]:
        total = total * x + value
    return total


def first_angle(offset):
    y = offset * (1.0 / STEPS)
    x = y * y
    return horner(COS_COEF, x), horner(SIN_COEF, x) * y


def tile_of(value, t):
    return value[:, t * LANES : (t + 1) * LANES]


def by_quad(even, odd):
    top = lax.broadcasted_iota(jnp.int32, even.shape, 0) < QUAD
    return (
        jnp.where(top, even, pltpu.roll(odd, QUAD, 0)),
        jnp.where(top, pltpu.roll(even, QUAD, 0), odd),
    )


def sequence(before, middle, factor):
    def pair(*two):
        return jnp.concatenate(two, 0).astype(jnp.bfloat16)

    up, down = [], []
    last, value = before, middle
    for _ in range(STEPS // 4):
        after = factor * value - last
        up.append(pair(value, after))
        last, value = after, factor * after - value
    last, value = middle, before
    for _ in range(STEPS // 4):
        after = factor * value - last
        down.append(pair(after, value))
        last, value = after, factor * after - value
    return down[::-1] + up


def subgrid_kernel(
    first, destinations, capacity, block_ref, row_ref, start_ref, token_ref, uv_ref, res_ref, *refs
):
    out_refs, (next_ref, gathered, found, tags, mover) = refs[:-5], refs[-5:]
    next_ref[...] = jnp.zeros_like(next_ref)
    tiles = gathered.shape[0] // (4 * GROUP)
    spare = destinations * capacity // QUAD
    low, high = start_ref[first], start_ref[first + destinations]
    last = block_ref.shape[0] - 1
    vis_at = lax.broadcasted_iota(jnp.int32, (2 * tiles, LANES), 1) + LANES * (
        lax.broadcasted_iota(jnp.int32, (2 * tiles, LANES), 0) // 2
    )
    same_block = (
        lax.broadcasted_iota(jnp.int32, (2 * STEPS * QUAD, LANES), 0) % QUAD
        == lax.broadcasted_iota(jnp.int32, (2 * STEPS * QUAD, LANES), 1) % QUAD
    )
    quad_row = lax.broadcasted_iota(jnp.int32, (QUAD, LANES), 0)
    top = lax.broadcasted_iota(jnp.int32, (GROUP, LANES), 0) < QUAD

    source = lax.broadcasted_iota(jnp.int32, mover.shape, 0)
    lane = lax.broadcasted_iota(jnp.int32, mover.shape, 1)
    moves = (source // LANES == lane // SUB) & (source % LANES // QUAD == lane % SUB)
    mover[...] = jnp.where(moves, 1.0, 0.0).astype(jnp.bfloat16)
    tags[...] = jnp.zeros_like(tags)

    def angles(quad_at):
        for i in range(GROUP):
            packed = block_ref[jnp.minimum(quad_at * QUAD + i, last)]
            block, count = packed // COUNT_SPAN, packed % COUNT_SPAN
            at = pl.ds(pl.multiple_of(block * 2 * tiles, 2 * tiles), 2 * tiles)
            both = jnp.where(vis_at < count, res_ref[at, :], 0.0)
            gathered[pl.ds(i, 2 * tiles, stride=GROUP), :] = uv_ref[at, :]
            gathered[pl.ds(2 * tiles * GROUP + i, 2 * tiles, stride=GROUP), :] = both
        u, v, re, im = [
            jnp.concatenate(
                [
                    gathered[pl.ds(((k // 2) * 2 * tiles + 2 * t + k % 2) * GROUP, GROUP), :]
                    for t in range(tiles)
                ],
                1,
            )
            for k in range(4)
        ]
        c, s = first_angle(u)
        a, b, e, f = re * c, im * s, im * c, re * s
        after = (a - b, e + f)
        before = (a + b, e - f)
        second = [2.0 * c * near - far for near, far in zip(before, (re, im))]
        factor = 2.0 - 4.0 * s * s
        left_factor = by_quad(factor, factor)
        left = [(by_quad(x, y), by_quad(z, w)) for x, y, z, w in zip(second, before, (re, im), after)]
        c, s = first_angle(v)
        c2, s2 = 1.0 - 2.0 * s * s, 2.0 * s * c
        factor = 2.0 * c2
        right_factor = by_quad(factor, factor)
        right = [
            (by_quad(c2, c), by_quad(jnp.ones_like(c), c)),
            (by_quad(-s2, -s), by_quad(jnp.zeros_like(s), s)),
        ]
        return [
            [
                (left[0][0][q], left[0][1][q], left[1][0][q], left[1][1][q], left_factor[q]),
                (right[0][0][q], right[0][1][q], right[1][0][q], right[1][1][q], right_factor[q]),
            ]
            for q in range(2)
        ]

    def finish(seeds, quad_at):
        product = None
        for lanes in range(0, tiles * LANES, CHUNK):
            operands = []
            for side in seeds[::-1]:
                before, middle, before_imag, middle_imag, factor = [
                    x[:, lanes : lanes + CHUNK] for x in side
                ]
                operands.append(
                    jnp.concatenate(
                        sequence(before, middle, factor)
                        + sequence(before_imag, middle_imag, factor),
                        0,
                    )
                )
            term = lax.dot_general(
                operands[1], operands[0], (((1,), (1,)), ((), ())),
                preferred_element_type=jnp.float32,
            )
            product = term if product is None else product + term
        half = product.shape[0] // 2
        wholes = (
            product[:half, :LANES] - product[half:, LANES:],
            product[half:, :LANES] + product[:half, LANES:],
        )
        rows = []
        for whole in wholes:
            whole = jnp.where(same_block, whole, 0.0)
            for j in range(0, STEPS, 4):
                four = [whole[(j + k) * GROUP : (j + k + 1) * GROUP] for k in range(4)]
                rows.append(jnp.concatenate(four, 1))
        index = jnp.clip(quad_at * QUAD, 0, last + 1 - QUAD)
        place = row_ref[index] // (2 * SLOTS * QUAD) - first * (capacity // QUAD)
        place = jnp.where((quad_at >= low) & (quad_at < high), place, spare)
        found[place] = jnp.concatenate(rows, 0).astype(jnp.bfloat16)
        tag = jnp.zeros((QUAD, LANES), jnp.int32)
        for b in range(QUAD):
            tag = jnp.where(quad_row == b, row_ref[index + b] % (2 * SLOTS), tag)
        tags[place] = tag.astype(jnp.float32)

    def turn(g, seeds):
        quad_at = low + 2 * g
        for q in range(2):
            finish(seeds[q], quad_at + q)
        return angles(quad_at + 2)

    lax.fori_loop(0, (high - low + 1) // 2, turn, angles(low))

    shares = capacity // TAG_ROWS
    share = lax.broadcasted_iota(jnp.int32, (TAG_ROWS, LANES), 1) // (LANES // shares)
    for d, out_ref in enumerate(out_refs):
        for m in range(out_ref.shape[0] // message_rows(capacity)):
            base = m * message_rows(capacity)
            sent = start_ref[first + d + m + 1] - start_ref[first + d + m]
            slot = (d + m) * (capacity // QUAD)
            tag = jnp.zeros((TAG_ROWS, LANES), jnp.float32)
            for n in range(shares):
                at = slot + n * 4
                four = jnp.concatenate([tags[at + k] for k in range(4)], 0)
                tag = jnp.where(share == n, four, tag)
                rows = jnp.concatenate([found[at + k] for k in range(4)], 0)
                moved = jnp.dot(rows, mover[...], preferred_element_type=jnp.float32)
                for piece in range(PIECES // 2):
                    part = []
                    for k in range(4):
                        value = moved[(k * 8 + piece) * GROUP : (k * 8 + piece + 1) * GROUP]
                        part.append(jnp.where(n * 4 + k < sent, value, 0.0))
                    for parity in range(2):
                        pair = []
                        for k in (0, 2):
                            if parity == 0:
                                pair.append(jnp.where(top, part[k], pltpu.roll(part[k + 1], QUAD, 0)))
                            else:
                                pair.append(jnp.where(top, pltpu.roll(part[k], QUAD, 0), part[k + 1]))
                        put = base + (piece * 2 + parity) * capacity + n * TAG_ROWS
                        out_ref[pl.ds(put, TAG_ROWS), :] = jnp.concatenate(pair, 0).astype(jnp.bfloat16)
            out_ref[pl.ds(base + PIECES * capacity, TAG_ROWS), :] = tag.astype(jnp.bfloat16)


def message_rows(capacity):
    return PIECES * capacity + TAG_ROWS


def make_subgrids(first, outs, token, capacity, block, row, start, uv, res, vis):
    tiles = vis // LANES
    destinations = sum(outs)
    quads = destinations * capacity // QUAD
    vmem = pl.BlockSpec(memory_space=pltpu.VMEM)
    smem = pl.BlockSpec(memory_space=pltpu.SMEM)
    return pl.pallas_call(
        functools.partial(subgrid_kernel, first, destinations, capacity),
        out_shape=[
            jax.ShapeDtypeStruct((n * message_rows(capacity), LANES), jnp.bfloat16) for n in outs
        ]
        + [jax.ShapeDtypeStruct(token.shape, token.dtype)],
        in_specs=[smem] * 3 + [vmem] * 3,
        out_specs=[vmem] * (len(outs) + 1),
        scratch_shapes=[
            pltpu.VMEM((4 * tiles * GROUP, LANES), jnp.float32),
            pltpu.VMEM((quads + 1, FEATURE // SUB, 4 * LANES), jnp.bfloat16),
            pltpu.VMEM((quads + 1, QUAD, LANES), jnp.float32),
            pltpu.VMEM((4 * LANES, LANES), jnp.bfloat16),
        ],
        compiler_params=pltpu.CompilerParams(vmem_limit_bytes=VMEM_LIMIT),
        cost_estimate=pl.CostEstimate(
            flops=quads * 32 * SUB * SUB * vis, bytes_accessed=16 * quads * FEATURE, transcendentals=0
        ),
        name="subgrids",
    )(block, row, start, token, uv, res)


def gather_kernel(capacity, *refs):
    x_refs, (out_ref, xs, tags, hot, part) = refs[:-5], refs[-5:]
    lane = lax.broadcasted_iota(jnp.int32, (GROUP, LANES), 1) // SUB
    shares = capacity // TAG_ROWS
    at = 0
    for x_ref in x_refs:
        for base in range(0, x_ref.shape[0], message_rows(capacity)):
            for piece in range(PIECES):
                xs[piece, pl.ds(at, capacity), :] = x_ref[pl.ds(base + piece * capacity, capacity), :]
            tag = x_ref[pl.ds(base + PIECES * capacity, TAG_ROWS), :].astype(jnp.float32)
            for n in range(shares):
                column = n * (LANES // shares)
                tags[pl.ds(at + n * TAG_ROWS, TAG_ROWS), :] = jnp.broadcast_to(
                    tag[:, column : column + 1], (TAG_ROWS, LANES)
                )
            at += capacity
    wanted = lax.broadcasted_iota(jnp.int32, tags.shape, 1)
    wanted = (wanted % 32) * 4 + wanted // 32 + 1
    hot[...] = jnp.where(tags[...] == wanted.astype(jnp.float32), 1.0, 0.0).T.astype(jnp.bfloat16)
    for piece in range(PIECES):
        c, rows, parity = piece // 8, piece // 2 % 4, piece % 2
        part[...] = jnp.dot(hot[...], xs[piece], preferred_element_type=jnp.float32)
        for grp in range(4):
            given = [part[pl.ds(32 * jl + 8 * grp, 8), :] for jl in range(4)]
            for a in range(4):
                total = None
                for jl in range(4):
                    moved = given[jl]
                    if a != jl:
                        moved = pltpu.roll(moved, ((jl - a) % 4) * SUB, 1)
                    total = moved if total is None else jnp.where(lane == jl, moved, total)
                p = rows * 8 + a * 2 + parity
                out_ref[pl.ds(p * 64 + grp * 16 + c, 8, stride=2), :] = total


def sum_slots(arrived, capacity):
    rows = sum(x.shape[0] for x in arrived) // message_rows(capacity) * capacity
    vmem = pl.BlockSpec(memory_space=pltpu.VMEM)
    return pl.pallas_call(
        functools.partial(gather_kernel, capacity),
        out_shape=jax.ShapeDtypeStruct((SUB * 64, LANES), jnp.float32),
        in_specs=[vmem] * len(arrived),
        out_specs=vmem,
        scratch_shapes=[
            pltpu.VMEM((PIECES, rows, LANES), jnp.bfloat16),
            pltpu.VMEM((rows, LANES), jnp.float32),
            pltpu.VMEM((SLOTS, rows), jnp.bfloat16),
            pltpu.VMEM((SLOTS, LANES), jnp.float32),
        ],
        compiler_params=pltpu.CompilerParams(vmem_limit_bytes=VMEM_LIMIT),
        name="sum_slots",
    )(*arrived)


def rows_of(array):
    blocks, parts, vis = array.shape
    tiles = vis // LANES
    split = array.reshape(blocks, parts, tiles, LANES)
    return split.transpose(0, 2, 1, 3).reshape(blocks * tiles * parts, LANES)


def sending_order(owners):
    across, near = list(range(max(owners // 2, 1), owners)), list(range(1, owners // 2))
    order = [across.pop() for _ in range(owners // 4)]
    while across or near:
        order += [group.pop() for group in (across, near) if group]
    return order + [0]


def in_rows(array):
    return with_layout_constraint(array, Layout(major_to_minor=(0, 1)))


def local(residual, uv_offsets, counts, tile_of_block, slot_of_block, owner_map):
    blocks, _, vis = uv_offsets.shape
    owners = owner_map.shape[0]
    capacity = -(-max(CAP_MIN, 2 * blocks // owners) // 32) * 16
    core = lax.axis_index("samp")
    me = lax.axis_index(("blk", "tile"))
    swap = [(0, 1), (1, 0)]
    own = in_rows(rows_of(residual[0]))
    other = in_rows(lax.ppermute(own, "samp", swap))

    tile_ids = tile_of_block[:, 0]
    owner_range = jnp.arange(owners, dtype=jnp.int32)
    owner_ids = jnp.sum(
        jnp.where(tile_ids[:, None] == owner_range[None, :], owner_map[None, :], 0), 1
    )
    paired = owners <= PAIRED_MAX and owners & (owners - 1) == 0
    distances = sending_order(owners)
    offset = owner_ids
    if paired:
        offset = jnp.bitwise_xor(owner_ids, me)
        offset = jnp.sum(
            jnp.where(offset[:, None] == jnp.array(distances)[None, :], owner_range[None, :], 0), 1
        )
    index = jnp.arange(blocks, dtype=jnp.int32)
    same = (offset[None, :] == offset[:, None]) & (index[None, :] < index[:, None])
    rank = jnp.sum(same.astype(jnp.int32), 1)
    mine = (rank & 1) == core
    counted = jnp.sum((mine[None, :] & (offset[None, :] == owner_range[:, None])).astype(jnp.int32), 1)
    quads = (counted + QUAD - 1) // QUAD
    edges = jnp.arange(owners + 1, dtype=jnp.int32)
    start = jnp.sum(jnp.where(owner_range[None, :] < edges[:, None], quads[None, :], 0), 1)
    before = jnp.sum(jnp.where(owner_range[None, :] < offset[:, None], quads[None, :], 0), 1)
    place = jnp.where(mine, before * QUAD + rank // 2, -1)
    longest = ((blocks + owners) // 2 + owners * (QUAD - 1)) // GROUP * GROUP + GROUP
    wanted = jnp.arange(longest, dtype=jnp.int32)
    chosen = place[None, :] == wanted[:, None]
    block_and_count = index * COUNT_SPAN + counts
    row_and_tag = (offset * capacity + rank // 2) * (2 * SLOTS) + slot_of_block + 1
    block = jnp.sum(jnp.where(chosen, block_and_count[None, :], 0), 1)
    row = jnp.sum(jnp.where(chosen, row_and_tag[None, :], 0), 1)

    subgrids = functools.partial(
        make_subgrids, capacity=capacity, block=block, row=row, start=start, uv=rows_of(uv_offsets),
        res=own.astype(jnp.float32) + other.astype(jnp.float32), vis=vis,
    )
    token = jnp.zeros((GROUP, LANES), jnp.int32)
    if paired:
        rows = []
        for first, last in zip(CALLS[:-1], CALLS[1:]):
            first, last = owners * first // CALLS[-1], owners * last // CALLS[-1]
            if first < last:
                *more, token = subgrids(first, (1,) * (last - first), token)
                rows += more
        arrived = []
        for distance, piece in zip(distances, rows):
            if distance:
                pairs = [(k, k ^ distance) for k in range(owners)]
                piece = lax.ppermute(piece, ("blk", "tile"), pairs)
            arrived.append(piece)
    else:
        each = max(d for d in range(1, 17) if owners % d == 0)
        rows = [subgrids(k, (each,), token)[0] for k in range(0, owners, each)]
        rows = jnp.concatenate(rows, 0).reshape(owners, message_rows(capacity), LANES)
        rows = lax.all_to_all(rows, ("blk", "tile"), split_axis=0, concat_axis=0, tiled=True)
        arrived = [rows.reshape(owners * message_rows(capacity), LANES)]
    part = sum_slots(arrived, capacity)
    whole = part + lax.ppermute(part, "samp", swap)
    whole = whole.reshape(SUB, SLOTS // 4, 2, LANES).transpose(0, 2, 1, 3)
    return whole.reshape(SUB, 2, SLOTS * SUB)


def solution(mesh):
    in_specs = (
        P("samp", ("cuts", "blk", "tile"), None, None),
        P(("cuts", "blk", "tile"), None, None),
        P(("cuts", "blk", "tile")),
        P(("cuts", "blk", "tile"), None),
        P(("cuts", "blk", "tile")),
        P(),
    )
    out_specs = P(("cuts", "blk", "tile"), None, None)
    return jax.shard_map(local, mesh=mesh, in_specs=in_specs, out_specs=out_specs, check_vma=False)
```

```python
import functools

import jax
import jax.numpy as jnp
import numpy as np
from jax import lax
from jax.experimental import pallas as pl
from jax.experimental.layout import Layout, with_layout_constraint
from jax.experimental.pallas import tpu as pltpu
from jax.sharding import PartitionSpec as P

SUB = 32
STEPS = SUB // 2
SLOTS = 128
LANES = 128
FEATURE = 2 * SUB * SUB
PIECES = FEATURE // LANES
CAP_MIN = 8
GROUP = 8
QUAD = 4
TAG_ROWS = 16
COUNT_BITS = 12
TAG_BITS = 8
CHUNK = 2 * LANES
PAIRED_MAX = 16
CALLS = (0, 2, 4, 8)
VMEM_LIMIT = 48 * 1024 * 1024


def turn_coefficients():
    knots = np.cos(np.pi * (np.arange(400) + 0.5) / 400)
    cheb = np.polynomial.chebyshev
    even = cheb.cheb2poly(cheb.chebfit(knots, np.cos(np.pi * knots), 12))[0::2]
    odd = cheb.cheb2poly(cheb.chebfit(knots, np.sin(np.pi * knots), 13))[1::2]
    return [float(x) for x in even], [float(x) for x in odd]


COS_COEF, SIN_COEF = turn_coefficients()


def horner(coef, x):
    total = coef[-1] * x + coef[-2]
    for value in coef[-3::-1]:
        total = total * x + value
    return total


def first_angle(offset):
    y = offset * (1.0 / STEPS)
    x = y * y
    return horner(COS_COEF, x), horner(SIN_COEF, x) * y


def tile_of(value, t):
    return value[:, t * LANES : (t + 1) * LANES]


def by_quad(even, odd):
    top = lax.broadcasted_iota(jnp.int32, even.shape, 0) < QUAD
    return (
        jnp.where(top, even, pltpu.roll(odd, QUAD, 0)),
        jnp.where(top, pltpu.roll(even, QUAD, 0), odd),
    )


def sequence(before, middle, factor):
    def pair(*two):
        return jnp.concatenate(two, 0).astype(jnp.bfloat16)

    up, down = [], []
    last, value = before, middle
    for _ in range(STEPS // 4):
        after = factor * value - last
        up.append(pair(value, after))
        last, value = after, factor * after - value
    last, value = middle, before
    for _ in range(STEPS // 4):
        after = factor * value - last
        down.append(pair(after, value))
        last, value = after, factor * after - value
    return down[::-1] + up


def subgrid_kernel(
    first, destinations, capacity, block_ref, row_ref, start_ref, token_ref, uv_ref, res_ref, *refs
):
    out_refs, (next_ref, gathered, found, tags, mover) = refs[:-5], refs[-5:]
    next_ref[...] = jnp.zeros_like(next_ref)
    tiles = gathered.shape[0] // (4 * GROUP)
    spare = destinations * capacity // QUAD
    low, high = start_ref[first], start_ref[first + destinations]
    last = block_ref.shape[0] - 1
    vis_at = lax.broadcasted_iota(jnp.int32, (2 * tiles, LANES), 1) + LANES * (
        lax.broadcasted_iota(jnp.int32, (2 * tiles, LANES), 0) >> 1
    )
    same_block = (
        lax.broadcasted_iota(jnp.int32, (GROUP, LANES), 0) & (QUAD - 1)
        == lax.broadcasted_iota(jnp.int32, (GROUP, LANES), 1) & (QUAD - 1)
    )
    quad_row = lax.broadcasted_iota(jnp.int32, (QUAD, LANES), 0)
    top = lax.broadcasted_iota(jnp.int32, (GROUP, LANES), 0) < QUAD

    source = lax.broadcasted_iota(jnp.int32, mover.shape, 0)
    lane = lax.broadcasted_iota(jnp.int32, mover.shape, 1)
    moves = (source >> 7 == lane >> 5) & ((source & (LANES - 1)) >> 2 == lane & (SUB - 1))
    mover[...] = jnp.where(moves, 1.0, 0.0).astype(jnp.bfloat16)
    tags[...] = jnp.zeros_like(tags)

    def angles(quad_at):
        for i in range(GROUP):
            packed = block_ref[jnp.minimum(quad_at * QUAD + i, last)]
            block, count = packed >> COUNT_BITS, packed & ((1 << COUNT_BITS) - 1)
            at = pl.ds(pl.multiple_of(block * 2 * tiles, 2 * tiles), 2 * tiles)
            both = jnp.where(vis_at < count, res_ref[at, :], 0.0)
            gathered[pl.ds(i, 2 * tiles, stride=GROUP), :] = uv_ref[at, :]
            gathered[pl.ds(2 * tiles * GROUP + i, 2 * tiles, stride=GROUP), :] = both
        u, v, re, im = [
            jnp.concatenate(
                [
                    gathered[pl.ds(((k // 2) * 2 * tiles + 2 * t + k % 2) * GROUP, GROUP), :]
                    for t in range(tiles)
                ],
                1,
            )
            for k in range(4)
        ]
        c, s = first_angle(u)
        a, b, e, f = re * c, im * s, im * c, re * s
        after = (a - b, e + f)
        before = (a + b, e - f)
        second = [2.0 * c * near - far for near, far in zip(before, (re, im))]
        factor = 2.0 - 4.0 * s * s
        left_factor = by_quad(factor, factor)
        left = [(by_quad(x, y), by_quad(z, w)) for x, y, z, w in zip(second, before, (re, im), after)]
        c, s = first_angle(v)
        c2, s2 = 1.0 - 2.0 * s * s, 2.0 * s * c
        factor = 2.0 * c2
        right_factor = by_quad(factor, factor)
        right = [
            (by_quad(c2, c), by_quad(jnp.ones_like(c), c)),
            (by_quad(-s2, -s), by_quad(jnp.zeros_like(s), s)),
        ]
        return [
            [
                (left[0][0][q], left[0][1][q], left[1][0][q], left[1][1][q], left_factor[q]),
                (right[0][0][q], right[0][1][q], right[1][0][q], right[1][1][q], right_factor[q]),
            ]
            for q in range(2)
        ]

    def finish(seeds, quad_at):
        product = None
        for lanes in range(0, tiles * LANES, CHUNK):
            operands = []
            for side in seeds[::-1]:
                before, middle, before_imag, middle_imag, factor = [
                    x[:, lanes : lanes + CHUNK] for x in side
                ]
                operands.append(
                    jnp.concatenate(
                        sequence(before, middle, factor)
                        + sequence(before_imag, middle_imag, factor),
                        0,
                    )
                )
            term = lax.dot_general(
                operands[1], operands[0], (((1,), (1,)), ((), ())),
                preferred_element_type=jnp.float32,
            )
            product = term if product is None else product + term
        half = product.shape[0] // 2
        wholes = (
            product[:half, :LANES] - product[half:, LANES:],
            product[half:, :LANES] + product[:half, LANES:],
        )
        rows = []
        for whole in wholes:
            for j in range(0, STEPS, 4):
                four = [whole[(j + k) * GROUP : (j + k + 1) * GROUP] for k in range(4)]
                rows.append(jnp.concatenate([jnp.where(same_block, x, 0.0) for x in four], 1))
        index = jnp.clip(quad_at * QUAD, 0, last + 1 - QUAD)
        place = (row_ref[index] >> (TAG_BITS + 2)) - first * (capacity // QUAD)
        place = jnp.where((quad_at >= low) & (quad_at < high), place, spare)
        found[place] = jnp.concatenate(rows, 0).astype(jnp.bfloat16)
        tag = jnp.zeros((QUAD, LANES), jnp.int32)
        for b in range(QUAD):
            tag = jnp.where(quad_row == b, row_ref[index + b] & ((1 << TAG_BITS) - 1), tag)
        tags[place] = tag.astype(jnp.float32)

    def turn(g, seeds):
        quad_at = low + 2 * g
        for q in range(2):
            finish(seeds[q], quad_at + q)
        return angles(quad_at + 2)

    lax.fori_loop(0, (high - low + 1) // 2, turn, angles(low))

    shares = capacity // TAG_ROWS
    share = lax.broadcasted_iota(jnp.int32, (TAG_ROWS, LANES), 1) // (LANES // shares)

    def write_share(out_ref, base, slot, sent, n):
        rows = jnp.concatenate([found[slot + k] for k in range(4)], 0)
        moved = jnp.dot(rows, mover[...], preferred_element_type=jnp.float32)
        for piece in range(PIECES // 2):
            part = []
            for k in range(4):
                value = moved[(k * 8 + piece) * GROUP : (k * 8 + piece + 1) * GROUP]
                part.append(jnp.where(n * 4 + k < sent, value, 0.0))
            first_two, last_two = [], []
            for even, odd in (part[:2], part[2:]):
                first_two.append(jnp.where(top, even, pltpu.roll(odd, QUAD, 0)))
                last_two.append(jnp.where(top, pltpu.roll(even, QUAD, 0), odd))
            for parity, two in enumerate((first_two, last_two)):
                put = base + (piece * 2 + parity) * capacity + n * TAG_ROWS
                out_ref[pl.ds(put, TAG_ROWS), :] = jnp.concatenate(two, 0).astype(jnp.bfloat16)

    for d, out_ref in enumerate(out_refs):
        for m in range(out_ref.shape[0] // message_rows(capacity)):
            base = m * message_rows(capacity)
            sent = start_ref[first + d + m + 1] - start_ref[first + d + m]
            slot = (d + m) * (capacity // QUAD)
            tag = jnp.zeros((TAG_ROWS, LANES), jnp.float32)
            for n in range(shares):
                at = slot + n * 4
                four = jnp.concatenate([tags[at + k] for k in range(4)], 0)
                tag = jnp.where(share == n, four, tag)

                @pl.when(n * 4 < sent)
                def _():
                    write_share(out_ref, base, at, sent, n)

                @pl.when(n * 4 >= sent)
                def _():
                    for piece in range(PIECES):
                        put = base + piece * capacity + n * TAG_ROWS
                        out_ref[pl.ds(put, TAG_ROWS), :] = jnp.zeros((TAG_ROWS, LANES), jnp.bfloat16)

            out_ref[pl.ds(base + PIECES * capacity, TAG_ROWS), :] = tag.astype(jnp.bfloat16)


def message_rows(capacity):
    return PIECES * capacity + TAG_ROWS


def make_subgrids(first, outs, token, capacity, block, row, start, uv, res, vis):
    tiles = vis // LANES
    destinations = sum(outs)
    quads = destinations * capacity // QUAD
    vmem = pl.BlockSpec(memory_space=pltpu.VMEM)
    smem = pl.BlockSpec(memory_space=pltpu.SMEM)
    return pl.pallas_call(
        functools.partial(subgrid_kernel, first, destinations, capacity),
        out_shape=[
            jax.ShapeDtypeStruct((n * message_rows(capacity), LANES), jnp.bfloat16) for n in outs
        ]
        + [jax.ShapeDtypeStruct(token.shape, token.dtype)],
        in_specs=[smem] * 3 + [vmem] * 3,
        out_specs=[vmem] * (len(outs) + 1),
        scratch_shapes=[
            pltpu.VMEM((4 * tiles * GROUP, LANES), jnp.float32),
            pltpu.VMEM((quads + 1, FEATURE // SUB, 4 * LANES), jnp.bfloat16),
            pltpu.VMEM((quads + 1, QUAD, LANES), jnp.float32),
            pltpu.VMEM((4 * LANES, LANES), jnp.bfloat16),
        ],
        compiler_params=pltpu.CompilerParams(vmem_limit_bytes=VMEM_LIMIT),
        cost_estimate=pl.CostEstimate(
            flops=quads * 32 * SUB * SUB * vis, bytes_accessed=16 * quads * FEATURE, transcendentals=0
        ),
        name="subgrids",
    )(block, row, start, token, uv, res)


def gather_kernel(capacity, *refs):
    x_refs, (out_ref, xs, tags, hot, part) = refs[:-5], refs[-5:]
    lane = lax.broadcasted_iota(jnp.int32, (GROUP, LANES), 1) // SUB
    shares = capacity // TAG_ROWS
    at = 0
    for x_ref in x_refs:
        for base in range(0, x_ref.shape[0], message_rows(capacity)):
            for piece in range(PIECES):
                xs[piece, pl.ds(at, capacity), :] = x_ref[pl.ds(base + piece * capacity, capacity), :]
            tag = x_ref[pl.ds(base + PIECES * capacity, TAG_ROWS), :].astype(jnp.float32)
            for n in range(shares):
                column = n * (LANES // shares)
                tags[pl.ds(at + n * TAG_ROWS, TAG_ROWS), :] = jnp.broadcast_to(
                    tag[:, column : column + 1], (TAG_ROWS, LANES)
                )
            at += capacity
    wanted = lax.broadcasted_iota(jnp.int32, tags.shape, 1)
    wanted = (wanted % 32) * 4 + wanted // 32 + 1
    hot[...] = jnp.where(tags[...] == wanted.astype(jnp.float32), 1.0, 0.0).T.astype(jnp.bfloat16)
    for piece in range(PIECES):
        c, rows, parity = piece // 8, piece // 2 % 4, piece % 2
        part[...] = jnp.dot(hot[...], xs[piece], preferred_element_type=jnp.float32)
        for grp in range(4):
            given = [part[pl.ds(32 * jl + 8 * grp, 8), :] for jl in range(4)]
            for a in range(4):
                total = None
                for jl in range(4):
                    moved = given[jl]
                    if a != jl:
                        moved = pltpu.roll(moved, ((jl - a) % 4) * SUB, 1)
                    total = moved if total is None else jnp.where(lane == jl, moved, total)
                p = rows * 8 + a * 2 + parity
                out_ref[pl.ds(p * 64 + grp * 16 + c, 8, stride=2), :] = total


def sum_slots(arrived, capacity):
    rows = sum(x.shape[0] for x in arrived) // message_rows(capacity) * capacity
    vmem = pl.BlockSpec(memory_space=pltpu.VMEM)
    return pl.pallas_call(
        functools.partial(gather_kernel, capacity),
        out_shape=jax.ShapeDtypeStruct((SUB * 64, LANES), jnp.float32),
        in_specs=[vmem] * len(arrived),
        out_specs=vmem,
        scratch_shapes=[
            pltpu.VMEM((PIECES, rows, LANES), jnp.bfloat16),
            pltpu.VMEM((rows, LANES), jnp.float32),
            pltpu.VMEM((SLOTS, rows), jnp.bfloat16),
            pltpu.VMEM((SLOTS, LANES), jnp.float32),
        ],
        compiler_params=pltpu.CompilerParams(vmem_limit_bytes=VMEM_LIMIT),
        name="sum_slots",
    )(*arrived)


def rows_of(array):
    blocks, parts, vis = array.shape
    tiles = vis // LANES
    split = array.reshape(blocks, parts, tiles, LANES)
    return split.transpose(0, 2, 1, 3).reshape(blocks * tiles * parts, LANES)


def sending_order(owners):
    across, near = list(range(max(owners // 2, 1), owners)), list(range(1, owners // 2))
    order = [across.pop() for _ in range(owners // 4)]
    while across or near:
        order += [group.pop() for group in (across, near) if group]
    return order + [0]


def in_rows(array):
    return with_layout_constraint(array, Layout(major_to_minor=(0, 1)))


def local(residual, uv_offsets, counts, tile_of_block, slot_of_block, owner_map):
    blocks, _, vis = uv_offsets.shape
    owners = owner_map.shape[0]
    capacity = -(-max(CAP_MIN, 2 * blocks // owners) // 32) * 16
    core = lax.axis_index("samp")
    me = lax.axis_index(("blk", "tile"))
    swap = [(0, 1), (1, 0)]
    own = in_rows(rows_of(residual[0]))
    other = in_rows(lax.ppermute(own, "samp", swap))

    lists = jnp.concatenate([tile_of_block[:, 0], slot_of_block, counts])
    lists = lax.optimization_barrier(lists)
    tile_ids, slots, counts = lists[:blocks], lists[blocks : 2 * blocks], lists[2 * blocks :]
    owner_range = jnp.arange(owners, dtype=jnp.int32)
    owner_ids = jnp.sum(
        jnp.where(tile_ids[:, None] == owner_range[None, :], owner_map[None, :], 0), 1
    )
    paired = owners <= PAIRED_MAX and owners & (owners - 1) == 0
    distances = sending_order(owners)
    offset = owner_ids
    if paired:
        offset = jnp.bitwise_xor(owner_ids, me)
        offset = sum(jnp.where(offset == d, k, 0) for k, d in enumerate(distances) if k)
    index = jnp.arange(blocks, dtype=jnp.int32)
    same = (offset[None, :] == offset[:, None]) & (index[None, :] < index[:, None])
    rank = jnp.sum(same.astype(jnp.int32), 1)
    mine = (rank & 1) == core
    counted = jnp.sum((mine[None, :] & (offset[None, :] == owner_range[:, None])).astype(jnp.int32), 1)
    quads = (counted + QUAD - 1) >> 2
    edges = jnp.arange(owners + 1, dtype=jnp.int32)
    start = jnp.sum(jnp.where(owner_range[None, :] < edges[:, None], quads[None, :], 0), 1)
    before = jnp.sum(jnp.where(owner_range[None, :] < offset[:, None], quads[None, :], 0), 1)
    place = jnp.where(mine, before * QUAD + (rank >> 1), -1)
    longest = ((blocks + owners) // 2 + owners * (QUAD - 1)) // GROUP * GROUP + GROUP
    wanted = jnp.arange(longest, dtype=jnp.int32)
    chosen = place[None, :] == wanted[:, None]
    block_and_count = (index << COUNT_BITS) + counts
    row_and_tag = ((offset * capacity + (rank >> 1)) << TAG_BITS) + slots + 1
    block = jnp.sum(jnp.where(chosen, block_and_count[None, :], 0), 1)
    row = jnp.sum(jnp.where(chosen, row_and_tag[None, :], 0), 1)

    subgrids = functools.partial(
        make_subgrids, capacity=capacity, block=block, row=row, start=start, uv=rows_of(uv_offsets),
        res=own.astype(jnp.float32) + other.astype(jnp.float32), vis=vis,
    )
    token = jnp.zeros((GROUP, LANES), jnp.int32)
    if paired:
        rows = []
        for first, last in zip(CALLS[:-1], CALLS[1:]):
            first, last = owners * first // CALLS[-1], owners * last // CALLS[-1]
            if first < last:
                *more, token = subgrids(first, (1,) * (last - first), token)
                rows += more
        arrived = []
        for distance, piece in zip(distances, rows):
            if distance:
                pairs = [(k, k ^ distance) for k in range(owners)]
                piece = lax.ppermute(piece, ("blk", "tile"), pairs)
            arrived.append(piece)
    else:
        each = max(d for d in range(1, 17) if owners % d == 0)
        rows = [subgrids(k, (each,), token)[0] for k in range(0, owners, each)]
        rows = jnp.concatenate(rows, 0).reshape(owners, message_rows(capacity), LANES)
        rows = lax.all_to_all(rows, ("blk", "tile"), split_axis=0, concat_axis=0, tiled=True)
        arrived = [rows.reshape(owners * message_rows(capacity), LANES)]
    part = sum_slots(arrived, capacity)
    whole = part + lax.ppermute(part, "samp", swap)
    whole = whole.reshape(SUB, SLOTS // 4, 2, LANES).transpose(0, 2, 1, 3)
    return whole.reshape(SUB, 2, SLOTS * SUB)


def solution(mesh):
    in_specs = (
        P("samp", ("cuts", "blk", "tile"), None, None),
        P(("cuts", "blk", "tile"), None, None),
        P(("cuts", "blk", "tile")),
        P(("cuts", "blk", "tile"), None),
        P(("cuts", "blk", "tile")),
        P(),
    )
    out_specs = P(("cuts", "blk", "tile"), None, None)
    return jax.shard_map(local, mesh=mesh, in_specs=in_specs, out_specs=out_specs, check_vma=False)
```

```python
import functools

import jax
import jax.numpy as jnp
import numpy as np
from jax import lax
from jax.experimental import pallas as pl
from jax.experimental.layout import Layout, with_layout_constraint
from jax.experimental.pallas import tpu as pltpu
from jax.sharding import PartitionSpec as P

SUB = 32
STEPS = SUB // 2
SLOTS = 128
LANES = 128
FEATURE = 2 * SUB * SUB
PIECES = FEATURE // LANES
CAP_MIN = 8
GROUP = 8
QUAD = 4
TAG_ROWS = 16
COUNT_BITS = 12
TAG_BITS = 8
CHUNK = 2 * LANES
PAIRED_MAX = 16
CALLS = (0, 2, 4, 8)
VMEM_LIMIT = 48 * 1024 * 1024


def turn_coefficients():
    knots = np.cos(np.pi * (np.arange(400) + 0.5) / 400)
    cheb = np.polynomial.chebyshev
    even = cheb.cheb2poly(cheb.chebfit(knots, np.cos(np.pi * knots), 12))[0::2]
    odd = cheb.cheb2poly(cheb.chebfit(knots, np.sin(np.pi * knots), 13))[1::2]
    return [float(x) for x in even], [float(x) for x in odd]


COS_COEF, SIN_COEF = turn_coefficients()


def horner(coef, x):
    total = coef[-1] * x + coef[-2]
    for value in coef[-3::-1]:
        total = total * x + value
    return total


def first_angle(offset):
    y = offset * (1.0 / STEPS)
    x = y * y
    return horner(COS_COEF, x), horner(SIN_COEF, x) * y


def tile_of(value, t):
    return value[:, t * LANES : (t + 1) * LANES]


def by_quad(even, odd):
    top = lax.broadcasted_iota(jnp.int32, even.shape, 0) < QUAD
    return (
        jnp.where(top, even, pltpu.roll(odd, QUAD, 0)),
        jnp.where(top, pltpu.roll(even, QUAD, 0), odd),
    )


def sequence(before, middle, factor):
    def pair(*two):
        return jnp.concatenate(two, 0).astype(jnp.bfloat16)

    up, down = [], []
    last, value = before, middle
    for _ in range(STEPS // 4):
        after = factor * value - last
        up.append(pair(value, after))
        last, value = after, factor * after - value
    last, value = middle, before
    for _ in range(STEPS // 4):
        after = factor * value - last
        down.append(pair(after, value))
        last, value = after, factor * after - value
    return down[::-1] + up


def subgrid_kernel(
    first, destinations, capacity, block_ref, row_ref, start_ref, token_ref, uv_ref, res_ref, *refs
):
    out_refs, (next_ref, gathered, found, tags, mover) = refs[:-5], refs[-5:]
    next_ref[...] = jnp.zeros_like(next_ref)
    tiles = gathered.shape[0] // (4 * GROUP)
    spare = destinations * capacity // QUAD
    low, high = start_ref[first], start_ref[first + destinations]
    last = block_ref.shape[0] - 1
    vis_at = lax.broadcasted_iota(jnp.int32, (2 * tiles, LANES), 1) + LANES * (
        lax.broadcasted_iota(jnp.int32, (2 * tiles, LANES), 0) >> 1
    )
    same_block = (
        lax.broadcasted_iota(jnp.int32, (GROUP, LANES), 0) & (QUAD - 1)
        == lax.broadcasted_iota(jnp.int32, (GROUP, LANES), 1) & (QUAD - 1)
    )
    quad_row = lax.broadcasted_iota(jnp.int32, (QUAD, LANES), 0)
    top = lax.broadcasted_iota(jnp.int32, (GROUP, LANES), 0) < QUAD

    source = lax.broadcasted_iota(jnp.int32, mover.shape, 0)
    lane = lax.broadcasted_iota(jnp.int32, mover.shape, 1)
    moves = (source >> 7 == lane >> 5) & ((source & (LANES - 1)) >> 2 == lane & (SUB - 1))
    mover[...] = jnp.where(moves, 1.0, 0.0).astype(jnp.bfloat16)
    tags[...] = jnp.zeros_like(tags)

    def angles(quad_at):
        for i in range(GROUP):
            packed = block_ref[jnp.minimum(quad_at * QUAD + i, last)]
            block, count = packed >> COUNT_BITS, packed & ((1 << COUNT_BITS) - 1)
            at = pl.ds(pl.multiple_of(block * 2 * tiles, 2 * tiles), 2 * tiles)
            both = jnp.where(vis_at < count, res_ref[at, :], 0.0)
            gathered[pl.ds(i, 2 * tiles, stride=GROUP), :] = uv_ref[at, :]
            gathered[pl.ds(2 * tiles * GROUP + i, 2 * tiles, stride=GROUP), :] = both
        u, v, re, im = [
            jnp.concatenate(
                [
                    gathered[pl.ds(((k // 2) * 2 * tiles + 2 * t + k % 2) * GROUP, GROUP), :]
                    for t in range(tiles)
                ],
                1,
            )
            for k in range(4)
        ]
        c, s = first_angle(u)
        a, b, e, f = re * c, im * s, im * c, re * s
        after = (a - b, e + f)
        before = (a + b, e - f)
        second = [2.0 * c * near - far for near, far in zip(before, (re, im))]
        factor = 2.0 - 4.0 * s * s
        left_factor = by_quad(factor, factor)
        left = [(by_quad(x, y), by_quad(z, w)) for x, y, z, w in zip(second, before, (re, im), after)]
        c, s = first_angle(v)
        c2, s2 = 1.0 - 2.0 * s * s, 2.0 * s * c
        factor = 2.0 * c2
        right_factor = by_quad(factor, factor)
        right = [
            (by_quad(c2, c), by_quad(jnp.ones_like(c), c)),
            (by_quad(-s2, -s), by_quad(jnp.zeros_like(s), s)),
        ]
        return [
            [
                (left[0][0][q], left[0][1][q], left[1][0][q], left[1][1][q], left_factor[q]),
                (right[0][0][q], right[0][1][q], right[1][0][q], right[1][1][q], right_factor[q]),
            ]
            for q in range(2)
        ]

    def finish(seeds, quad_at):
        product = None
        for lanes in range(0, tiles * LANES, CHUNK):
            operands = []
            for side in seeds[::-1]:
                before, middle, before_imag, middle_imag, factor = [
                    x[:, lanes : lanes + CHUNK] for x in side
                ]
                operands.append(
                    jnp.concatenate(
                        sequence(before, middle, factor)
                        + sequence(before_imag, middle_imag, factor),
                        0,
                    )
                )
            term = lax.dot_general(
                operands[1], operands[0], (((1,), (1,)), ((), ())),
                preferred_element_type=jnp.float32,
            )
            product = term if product is None else product + term
        half = product.shape[0] // 2
        wholes = (
            product[:half, :LANES] - product[half:, LANES:],
            product[half:, :LANES] + product[:half, LANES:],
        )
        rows = []
        for whole in wholes:
            for j in range(0, STEPS, 4):
                four = [whole[(j + k) * GROUP : (j + k + 1) * GROUP] for k in range(4)]
                rows.append(jnp.concatenate([jnp.where(same_block, x, 0.0) for x in four], 1))
        index = jnp.clip(quad_at * QUAD, 0, last + 1 - QUAD)
        place = (row_ref[index] >> (TAG_BITS + 2)) - first * (capacity // QUAD)
        place = jnp.where((quad_at >= low) & (quad_at < high), place, spare)
        found[place] = jnp.concatenate(rows, 0).astype(jnp.bfloat16)
        tag = jnp.zeros((QUAD, LANES), jnp.int32)
        for b in range(QUAD):
            tag = jnp.where(quad_row == b, row_ref[index + b] & ((1 << TAG_BITS) - 1), tag)
        tags[place] = tag.astype(jnp.float32)

    def turn(g, seeds):
        quad_at = low + 2 * g
        for q in range(2):
            finish(seeds[q], quad_at + q)
        return angles(quad_at + 2)

    lax.fori_loop(0, (high - low + 1) // 2, turn, angles(low))

    shares = capacity // TAG_ROWS
    share = lax.broadcasted_iota(jnp.int32, (TAG_ROWS, LANES), 1) // (LANES // shares)

    def write_share(out_ref, base, slot, sent, n):
        rows = jnp.concatenate([found[slot + k] for k in range(4)], 0)
        moved = jnp.dot(rows, mover[...], preferred_element_type=jnp.float32)
        for piece in range(PIECES // 2):
            part = []
            for k in range(4):
                value = moved[(k * 8 + piece) * GROUP : (k * 8 + piece + 1) * GROUP]
                part.append(jnp.where(n * 4 + k < sent, value, 0.0))
            first_two, last_two = [], []
            for even, odd in (part[:2], part[2:]):
                first_two.append(jnp.where(top, even, pltpu.roll(odd, QUAD, 0)))
                last_two.append(jnp.where(top, pltpu.roll(even, QUAD, 0), odd))
            for parity, two in enumerate((first_two, last_two)):
                put = base + (piece * 2 + parity) * capacity + n * TAG_ROWS
                out_ref[pl.ds(put, TAG_ROWS), :] = jnp.concatenate(two, 0).astype(jnp.bfloat16)

    for d, out_ref in enumerate(out_refs):
        for m in range(out_ref.shape[0] // message_rows(capacity)):
            base = m * message_rows(capacity)
            sent = start_ref[first + d + m + 1] - start_ref[first + d + m]
            slot = (d + m) * (capacity // QUAD)
            tag = jnp.zeros((TAG_ROWS, LANES), jnp.float32)
            for n in range(shares):
                at = slot + n * 4
                four = jnp.concatenate([tags[at + k] for k in range(4)], 0)
                tag = jnp.where(share == n, four, tag)

                @pl.when(n * 4 < sent)
                def _():
                    write_share(out_ref, base, at, sent, n)

                @pl.when(n * 4 >= sent)
                def _():
                    for piece in range(PIECES):
                        put = base + piece * capacity + n * TAG_ROWS
                        out_ref[pl.ds(put, TAG_ROWS), :] = jnp.zeros((TAG_ROWS, LANES), jnp.bfloat16)

            out_ref[pl.ds(base + PIECES * capacity, TAG_ROWS), :] = tag.astype(jnp.bfloat16)


def message_rows(capacity):
    return PIECES * capacity + TAG_ROWS


def make_subgrids(first, outs, token, capacity, block, row, start, uv, res, vis):
    tiles = vis // LANES
    destinations = sum(outs)
    quads = destinations * capacity // QUAD
    vmem = pl.BlockSpec(memory_space=pltpu.VMEM)
    smem = pl.BlockSpec(memory_space=pltpu.SMEM)
    return pl.pallas_call(
        functools.partial(subgrid_kernel, first, destinations, capacity),
        out_shape=[
            jax.ShapeDtypeStruct((n * message_rows(capacity), LANES), jnp.bfloat16) for n in outs
        ]
        + [jax.ShapeDtypeStruct(token.shape, token.dtype)],
        in_specs=[smem] * 3 + [vmem] * 3,
        out_specs=[vmem] * (len(outs) + 1),
        scratch_shapes=[
            pltpu.VMEM((4 * tiles * GROUP, LANES), jnp.float32),
            pltpu.VMEM((quads + 1, FEATURE // SUB, 4 * LANES), jnp.bfloat16),
            pltpu.VMEM((quads + 1, QUAD, LANES), jnp.float32),
            pltpu.VMEM((4 * LANES, LANES), jnp.bfloat16),
        ],
        compiler_params=pltpu.CompilerParams(vmem_limit_bytes=VMEM_LIMIT),
        cost_estimate=pl.CostEstimate(
            flops=quads * 32 * SUB * SUB * vis, bytes_accessed=16 * quads * FEATURE, transcendentals=0
        ),
        name="subgrids",
    )(block, row, start, token, uv, res)


def pick_rows(hot, xs, part, out_ref, half):
    lane = lax.broadcasted_iota(jnp.int32, (GROUP, LANES), 1) >> 5
    for piece in range(PIECES):
        c, rows, parity = piece // 8, piece // 2 % 4 - 2 * half, piece % 2
        if not 0 <= rows < 2:
            continue
        part[...] = jnp.dot(hot[...], xs[piece], preferred_element_type=jnp.float32)
        for grp in range(4):
            given = [part[pl.ds(32 * jl + 8 * grp, 8), :] for jl in range(4)]
            for a in range(4):
                total = None
                for jl in range(4):
                    moved = given[jl]
                    if a != jl:
                        moved = pltpu.roll(moved, ((jl - a) % 4) * SUB, 1)
                    total = moved if total is None else jnp.where(lane == jl, moved, total)
                p = rows * 8 + a * 2 + parity
                out_ref[pl.ds(p * 64 + grp * 16 + c, 8, stride=2), :] = total


def first_half_kernel(capacity, *refs):
    x_refs, (out_ref, xs, hot, tags, part) = refs[:-5], refs[-5:]
    shares = capacity // TAG_ROWS
    at = 0
    for x_ref in x_refs:
        for base in range(0, x_ref.shape[0], message_rows(capacity)):
            for piece in range(PIECES):
                xs[piece, pl.ds(at, capacity), :] = x_ref[pl.ds(base + piece * capacity, capacity), :]
            tag = x_ref[pl.ds(base + PIECES * capacity, TAG_ROWS), :].astype(jnp.float32)
            for n in range(shares):
                column = n * (LANES // shares)
                tags[pl.ds(at + n * TAG_ROWS, TAG_ROWS), :] = jnp.broadcast_to(
                    tag[:, column : column + 1], (TAG_ROWS, LANES)
                )
            at += capacity
    wanted = lax.broadcasted_iota(jnp.int32, tags.shape, 1)
    wanted = ((wanted & 31) << 2) + (wanted >> 5) + 1
    hot[...] = jnp.where(tags[...] == wanted.astype(jnp.float32), 1.0, 0.0).T.astype(jnp.bfloat16)
    pick_rows(hot, xs, part, out_ref, 0)


def second_half_kernel(xs, hot, out_ref, part):
    pick_rows(hot, xs, part, out_ref, 1)


def sum_slots(arrived, capacity):
    rows = sum(x.shape[0] for x in arrived) // message_rows(capacity) * capacity
    vmem = pl.BlockSpec(memory_space=pltpu.VMEM)
    half = jax.ShapeDtypeStruct((SUB * 32, LANES), jnp.float32)
    params = pltpu.CompilerParams(vmem_limit_bytes=VMEM_LIMIT)
    part = pltpu.VMEM((SLOTS, LANES), jnp.float32)
    first, xs, hot = pl.pallas_call(
        functools.partial(first_half_kernel, capacity),
        out_shape=[
            half,
            jax.ShapeDtypeStruct((PIECES, rows, LANES), jnp.bfloat16),
            jax.ShapeDtypeStruct((SLOTS, rows), jnp.bfloat16),
        ],
        in_specs=[vmem] * len(arrived),
        out_specs=[vmem] * 3,
        scratch_shapes=[pltpu.VMEM((rows, LANES), jnp.float32), part],
        compiler_params=params,
        name="sum_first",
    )(*arrived)
    second = pl.pallas_call(
        second_half_kernel,
        out_shape=half,
        in_specs=[vmem] * 2,
        out_specs=vmem,
        scratch_shapes=[part],
        compiler_params=params,
        name="sum_second",
    )(xs, hot)
    return first, second


def add_kernel(at, mine_ref, theirs_ref, *refs):
    out_ref, total, sems = refs[-3:]
    step = total.shape[0] // sems.shape[0]
    copies = []
    for k in range(sems.shape[0]):
        here = pl.ds(k * step, step)
        total[here, :] = mine_ref[here, :] + theirs_ref[here, :]
        copy = pltpu.make_async_copy(
            total.at[here], out_ref.at[pl.ds(at + k * step, step)], sems.at[k]
        )
        copy.start()
        copies.append(copy)
    for copy in copies:
        copy.wait()


def add_half(at, mine, theirs, *whole):
    vmem, anywhere = pl.BlockSpec(memory_space=pltpu.VMEM), pl.BlockSpec(memory_space=pl.ANY)
    return pl.pallas_call(
        functools.partial(add_kernel, at),
        out_shape=jax.ShapeDtypeStruct((2 * mine.shape[0], LANES), jnp.float32),
        in_specs=[vmem, vmem] + [anywhere] * len(whole),
        out_specs=anywhere,
        scratch_shapes=[pltpu.VMEM(mine.shape, jnp.float32), pltpu.SemaphoreType.DMA((4,))],
        input_output_aliases={2: 0} if whole else {},
        compiler_params=pltpu.CompilerParams(vmem_limit_bytes=VMEM_LIMIT),
        name="add_half",
    )(mine, theirs, *whole)


def rows_of(array):
    blocks, parts, vis = array.shape
    tiles = vis // LANES
    split = array.reshape(blocks, parts, tiles, LANES)
    return split.transpose(0, 2, 1, 3).reshape(blocks * tiles * parts, LANES)


def sending_order(owners):
    across, near = list(range(max(owners // 2, 1), owners)), list(range(1, owners // 2))
    order = [across.pop() for _ in range(owners // 4)]
    while across or near:
        order += [group.pop() for group in (across, near) if group]
    return order + [0]


def in_rows(array):
    return with_layout_constraint(array, Layout(major_to_minor=(0, 1)))


def local(residual, uv_offsets, counts, tile_of_block, slot_of_block, owner_map):
    blocks, _, vis = uv_offsets.shape
    owners = owner_map.shape[0]
    capacity = -(-max(CAP_MIN, 2 * blocks // owners) // 32) * 16
    core = lax.axis_index("samp")
    me = lax.axis_index(("blk", "tile"))
    swap = [(0, 1), (1, 0)]
    own = in_rows(rows_of(residual[0]))
    other = in_rows(lax.ppermute(own, "samp", swap))

    lists = jnp.concatenate([tile_of_block[:, 0], slot_of_block, counts, owner_map])
    lists = lax.optimization_barrier(lists)
    tile_ids, slots, counts, owner_map = [
        lists[k * blocks : min((k + 1) * blocks, 3 * blocks + owners)] for k in range(4)
    ]
    owner_range = jnp.arange(owners, dtype=jnp.int32)
    owner_ids = jnp.sum(
        jnp.where(tile_ids[:, None] == owner_range[None, :], owner_map[None, :], 0), 1
    )
    paired = owners <= PAIRED_MAX and owners & (owners - 1) == 0
    distances = sending_order(owners)
    offset = owner_ids
    if paired:
        offset = jnp.bitwise_xor(owner_ids, me)
        offset = sum(jnp.where(offset == d, k, 0) for k, d in enumerate(distances) if k)
    index = jnp.arange(blocks, dtype=jnp.int32)
    same = (offset[None, :] == offset[:, None]) & (index[None, :] < index[:, None])
    rank = jnp.sum(same.astype(jnp.int32), 1)
    mine = (rank & 1) == core
    counted = jnp.sum((mine[None, :] & (offset[None, :] == owner_range[:, None])).astype(jnp.int32), 1)
    quads = (counted + QUAD - 1) >> 2
    edges = jnp.arange(owners + 1, dtype=jnp.int32)
    start = jnp.sum(jnp.where(owner_range[None, :] < edges[:, None], quads[None, :], 0), 1)
    before = jnp.sum(jnp.where(owner_range[None, :] < offset[:, None], quads[None, :], 0), 1)
    place = jnp.where(mine, before * QUAD + (rank >> 1), -1)
    longest = ((blocks + owners) // 2 + owners * (QUAD - 1)) // GROUP * GROUP + GROUP
    wanted = jnp.arange(longest, dtype=jnp.int32)
    chosen = place[None, :] == wanted[:, None]
    block_and_count = (index << COUNT_BITS) + counts
    row_and_tag = ((offset * capacity + (rank >> 1)) << TAG_BITS) + slots + 1
    block = jnp.sum(jnp.where(chosen, block_and_count[None, :], 0), 1)
    row = jnp.sum(jnp.where(chosen, row_and_tag[None, :], 0), 1)

    subgrids = functools.partial(
        make_subgrids, capacity=capacity, block=block, row=row, start=start, uv=rows_of(uv_offsets),
        res=own.astype(jnp.float32) + other.astype(jnp.float32), vis=vis,
    )
    token = jnp.zeros((GROUP, LANES), jnp.int32)
    if paired:
        rows = []
        for first, last in zip(CALLS[:-1], CALLS[1:]):
            first, last = owners * first // CALLS[-1], owners * last // CALLS[-1]
            if first < last:
                *more, token = subgrids(first, (1,) * (last - first), token)
                rows += more
        arrived = []
        for distance, piece in zip(distances, rows):
            if distance:
                pairs = [(k, k ^ distance) for k in range(owners)]
                piece = lax.ppermute(piece, ("blk", "tile"), pairs)
            arrived.append(piece)
    else:
        each = max(d for d in range(1, 17) if owners % d == 0)
        rows = [subgrids(k, (each,), token)[0] for k in range(0, owners, each)]
        rows = jnp.concatenate(rows, 0).reshape(owners, message_rows(capacity), LANES)
        rows = lax.all_to_all(rows, ("blk", "tile"), split_axis=0, concat_axis=0, tiled=True)
        arrived = [rows.reshape(owners * message_rows(capacity), LANES)]
    first, second = sum_slots(arrived, capacity)
    whole = add_half(0, first, lax.ppermute(first, "samp", swap))
    whole = add_half(first.shape[0], second, lax.ppermute(second, "samp", swap), whole)
    whole = whole.reshape(SUB, SLOTS // 4, 2, LANES).transpose(0, 2, 1, 3)
    return whole.reshape(SUB, 2, SLOTS * SUB)


def solution(mesh):
    in_specs = (
        P("samp", ("cuts", "blk", "tile"), None, None),
        P(("cuts", "blk", "tile"), None, None),
        P(("cuts", "blk", "tile")),
        P(("cuts", "blk", "tile"), None),
        P(("cuts", "blk", "tile")),
        P(),
    )
    out_specs = P(("cuts", "blk", "tile"), None, None)
    return jax.shard_map(local, mesh=mesh, in_specs=in_specs, out_specs=out_specs, check_vma=False)
```

```python
import functools

import jax
import jax.numpy as jnp
import numpy as np
from jax import lax
from jax.experimental import pallas as pl
from jax.experimental.layout import Layout, with_layout_constraint
from jax.experimental.pallas import tpu as pltpu
from jax.sharding import PartitionSpec as P

SUB = 32
STEPS = SUB // 2
SLOTS = 128
LANES = 128
FEATURE = 2 * SUB * SUB
PIECES = FEATURE // LANES
CAP_MIN = 8
GROUP = 8
QUAD = 4
TAG_ROWS = 16
COUNT_BITS = 12
TAG_BITS = 8
CHUNK = 2 * LANES
PAIRED_MAX = 16
CALLS = (0, 1, 3, 5, 8)
VMEM_LIMIT = 48 * 1024 * 1024


def turn_coefficients():
    knots = np.cos(np.pi * (np.arange(400) + 0.5) / 400)
    cheb = np.polynomial.chebyshev
    even = cheb.cheb2poly(cheb.chebfit(knots, np.cos(np.pi * knots), 12))[0::2]
    odd = cheb.cheb2poly(cheb.chebfit(knots, np.sin(np.pi * knots), 13))[1::2]
    return [float(x) for x in even], [float(x) for x in odd]


COS_COEF, SIN_COEF = turn_coefficients()


def horner(coef, x):
    total = coef[-1] * x + coef[-2]
    for value in coef[-3::-1]:
        total = total * x + value
    return total


def first_angle(offset):
    y = offset * (1.0 / STEPS)
    x = y * y
    return horner(COS_COEF, x), horner(SIN_COEF, x) * y


def tile_of(value, t):
    return value[:, t * LANES : (t + 1) * LANES]


def by_quad(even, odd):
    top = lax.broadcasted_iota(jnp.int32, even.shape, 0) < QUAD
    return (
        jnp.where(top, even, pltpu.roll(odd, QUAD, 0)),
        jnp.where(top, pltpu.roll(even, QUAD, 0), odd),
    )


def sequence(before, middle, factor):
    def pair(*two):
        return jnp.concatenate(two, 0).astype(jnp.bfloat16)

    up, down = [], []
    last, value = before, middle
    for _ in range(STEPS // 4):
        after = factor * value - last
        up.append(pair(value, after))
        last, value = after, factor * after - value
    last, value = middle, before
    for _ in range(STEPS // 4):
        after = factor * value - last
        down.append(pair(after, value))
        last, value = after, factor * after - value
    return down[::-1] + up


def subgrid_kernel(
    first, destinations, capacity, block_ref, row_ref, start_ref, token_ref, uv_ref, res_ref, *refs
):
    out_refs, (next_ref, gathered, found, tags, mover) = refs[:-5], refs[-5:]
    next_ref[...] = jnp.zeros_like(next_ref)
    tiles = gathered.shape[0] // (4 * GROUP)
    spare = destinations * capacity // QUAD
    low, high = start_ref[first], start_ref[first + destinations]
    last = block_ref.shape[0] - 1
    vis_at = lax.broadcasted_iota(jnp.int32, (2 * tiles, LANES), 1) + LANES * (
        lax.broadcasted_iota(jnp.int32, (2 * tiles, LANES), 0) >> 1
    )
    same_block = (
        lax.broadcasted_iota(jnp.int32, (GROUP, LANES), 0) & (QUAD - 1)
        == lax.broadcasted_iota(jnp.int32, (GROUP, LANES), 1) & (QUAD - 1)
    )
    quad_row = lax.broadcasted_iota(jnp.int32, (QUAD, LANES), 0)
    top = lax.broadcasted_iota(jnp.int32, (GROUP, LANES), 0) < QUAD

    source = lax.broadcasted_iota(jnp.int32, mover.shape, 0)
    lane = lax.broadcasted_iota(jnp.int32, mover.shape, 1)
    moves = (source >> 7 == lane >> 5) & ((source & (LANES - 1)) >> 2 == lane & (SUB - 1))
    mover[...] = jnp.where(moves, 1.0, 0.0).astype(jnp.bfloat16)
    tags[...] = jnp.zeros_like(tags)

    def angles(quad_at):
        for i in range(GROUP):
            packed = block_ref[jnp.minimum(quad_at * QUAD + i, last)]
            block, count = packed >> COUNT_BITS, packed & ((1 << COUNT_BITS) - 1)
            at = pl.ds(pl.multiple_of(block * 2 * tiles, 2 * tiles), 2 * tiles)
            both = jnp.where(vis_at < count, res_ref[at, :], 0.0)
            gathered[pl.ds(i, 2 * tiles, stride=GROUP), :] = uv_ref[at, :]
            gathered[pl.ds(2 * tiles * GROUP + i, 2 * tiles, stride=GROUP), :] = both
        u, v, re, im = [
            jnp.concatenate(
                [
                    gathered[pl.ds(((k // 2) * 2 * tiles + 2 * t + k % 2) * GROUP, GROUP), :]
                    for t in range(tiles)
                ],
                1,
            )
            for k in range(4)
        ]
        c, s = first_angle(u)
        a, b, e, f = re * c, im * s, im * c, re * s
        after = (a - b, e + f)
        before = (a + b, e - f)
        second = [2.0 * c * near - far for near, far in zip(before, (re, im))]
        factor = 2.0 - 4.0 * s * s
        left_factor = by_quad(factor, factor)
        left = [(by_quad(x, y), by_quad(z, w)) for x, y, z, w in zip(second, before, (re, im), after)]
        c, s = first_angle(v)
        c2, s2 = 1.0 - 2.0 * s * s, 2.0 * s * c
        factor = 2.0 * c2
        right_factor = by_quad(factor, factor)
        right = [
            (by_quad(c2, c), by_quad(jnp.ones_like(c), c)),
            (by_quad(-s2, -s), by_quad(jnp.zeros_like(s), s)),
        ]
        return [
            [
                (left[0][0][q], left[0][1][q], left[1][0][q], left[1][1][q], left_factor[q]),
                (right[0][0][q], right[0][1][q], right[1][0][q], right[1][1][q], right_factor[q]),
            ]
            for q in range(2)
        ]

    def finish(seeds, quad_at):
        product = None
        for lanes in range(0, tiles * LANES, CHUNK):
            operands = []
            for side in seeds[::-1]:
                before, middle, before_imag, middle_imag, factor = [
                    x[:, lanes : lanes + CHUNK] for x in side
                ]
                operands.append(
                    jnp.concatenate(
                        sequence(before, middle, factor)
                        + sequence(before_imag, middle_imag, factor),
                        0,
                    )
                )
            term = lax.dot_general(
                operands[1], operands[0], (((1,), (1,)), ((), ())),
                preferred_element_type=jnp.float32,
            )
            product = term if product is None else product + term
        half = product.shape[0] // 2
        wholes = (
            product[:half, :LANES] - product[half:, LANES:],
            product[half:, :LANES] + product[:half, LANES:],
        )
        rows = []
        for whole in wholes:
            for j in range(0, STEPS, 4):
                four = [whole[(j + k) * GROUP : (j + k + 1) * GROUP] for k in range(4)]
                rows.append(jnp.concatenate([jnp.where(same_block, x, 0.0) for x in four], 1))
        index = jnp.clip(quad_at * QUAD, 0, last + 1 - QUAD)
        place = (row_ref[index] >> (TAG_BITS + 2)) - first * (capacity // QUAD)
        place = jnp.where((quad_at >= low) & (quad_at < high), place, spare)
        found[place] = jnp.concatenate(rows, 0).astype(jnp.bfloat16)
        tag = jnp.zeros((QUAD, LANES), jnp.int32)
        for b in range(QUAD):
            tag = jnp.where(quad_row == b, row_ref[index + b] & ((1 << TAG_BITS) - 1), tag)
        tags[place] = tag.astype(jnp.float32)

    def turn(g, seeds):
        quad_at = low + 2 * g
        for q in range(2):
            finish(seeds[q], quad_at + q)
        return angles(quad_at + 2)

    lax.fori_loop(0, (high - low + 1) // 2, turn, angles(low))

    shares = capacity // TAG_ROWS
    share = lax.broadcasted_iota(jnp.int32, (TAG_ROWS, LANES), 1) // (LANES // shares)

    def write_share(out_ref, base, slot, sent, n):
        rows = jnp.concatenate([found[slot + k] for k in range(4)], 0)
        moved = jnp.dot(rows, mover[...], preferred_element_type=jnp.float32)
        for piece in range(PIECES // 2):
            part = []
            for k in range(4):
                value = moved[(k * 8 + piece) * GROUP : (k * 8 + piece + 1) * GROUP]
                part.append(jnp.where(n * 4 + k < sent, value, 0.0))
            first_two, last_two = [], []
            for even, odd in (part[:2], part[2:]):
                first_two.append(jnp.where(top, even, pltpu.roll(odd, QUAD, 0)))
                last_two.append(jnp.where(top, pltpu.roll(even, QUAD, 0), odd))
            for parity, two in enumerate((first_two, last_two)):
                put = base + (piece * 2 + parity) * capacity + n * TAG_ROWS
                out_ref[pl.ds(put, TAG_ROWS), :] = jnp.concatenate(two, 0).astype(jnp.bfloat16)

    for d, out_ref in enumerate(out_refs):
        for m in range(out_ref.shape[0] // message_rows(capacity)):
            base = m * message_rows(capacity)
            sent = start_ref[first + d + m + 1] - start_ref[first + d + m]
            slot = (d + m) * (capacity // QUAD)
            tag = jnp.zeros((TAG_ROWS, LANES), jnp.float32)
            for n in range(shares):
                at = slot + n * 4
                four = jnp.concatenate([tags[at + k] for k in range(4)], 0)
                tag = jnp.where(share == n, four, tag)

                @pl.when(n * 4 < sent)
                def _():
                    write_share(out_ref, base, at, sent, n)

                @pl.when(n * 4 >= sent)
                def _():
                    for piece in range(PIECES):
                        put = base + piece * capacity + n * TAG_ROWS
                        out_ref[pl.ds(put, TAG_ROWS), :] = jnp.zeros((TAG_ROWS, LANES), jnp.bfloat16)

            out_ref[pl.ds(base + PIECES * capacity, TAG_ROWS), :] = tag.astype(jnp.bfloat16)


def message_rows(capacity):
    return PIECES * capacity + TAG_ROWS


def make_subgrids(first, outs, token, capacity, block, row, start, uv, res, vis):
    tiles = vis // LANES
    destinations = sum(outs)
    quads = destinations * capacity // QUAD
    vmem = pl.BlockSpec(memory_space=pltpu.VMEM)
    smem = pl.BlockSpec(memory_space=pltpu.SMEM)
    return pl.pallas_call(
        functools.partial(subgrid_kernel, first, destinations, capacity),
        out_shape=[
            jax.ShapeDtypeStruct((n * message_rows(capacity), LANES), jnp.bfloat16) for n in outs
        ]
        + [jax.ShapeDtypeStruct(token.shape, token.dtype)],
        in_specs=[smem] * 3 + [vmem] * 3,
        out_specs=[vmem] * (len(outs) + 1),
        scratch_shapes=[
            pltpu.VMEM((4 * tiles * GROUP, LANES), jnp.float32),
            pltpu.VMEM((quads + 1, FEATURE // SUB, 4 * LANES), jnp.bfloat16),
            pltpu.VMEM((quads + 1, QUAD, LANES), jnp.float32),
            pltpu.VMEM((4 * LANES, LANES), jnp.bfloat16),
        ],
        compiler_params=pltpu.CompilerParams(vmem_limit_bytes=VMEM_LIMIT),
        cost_estimate=pl.CostEstimate(
            flops=quads * 32 * SUB * SUB * vis, bytes_accessed=16 * quads * FEATURE, transcendentals=0
        ),
        name="subgrids",
    )(block, row, start, token, uv, res)


def pick_rows(hot, xs, part, out_ref, half):
    lane = lax.broadcasted_iota(jnp.int32, (GROUP, LANES), 1) >> 5
    for piece in range(PIECES):
        c, rows, parity = piece // 8, piece // 2 % 4 - 2 * half, piece % 2
        if not 0 <= rows < 2:
            continue
        part[...] = jnp.dot(hot[...], xs[piece], preferred_element_type=jnp.float32)
        for grp in range(4):
            given = [part[pl.ds(32 * jl + 8 * grp, 8), :] for jl in range(4)]
            for a in range(4):
                total = None
                for jl in range(4):
                    moved = given[jl]
                    if a != jl:
                        moved = pltpu.roll(moved, ((jl - a) % 4) * SUB, 1)
                    total = moved if total is None else jnp.where(lane == jl, moved, total)
                p = rows * 8 + a * 2 + parity
                out_ref[pl.ds(p * 64 + grp * 16 + c, 8, stride=2), :] = total


def first_half_kernel(capacity, *refs):
    x_refs, (out_ref, xs, hot, tags, part) = refs[:-5], refs[-5:]
    shares = capacity // TAG_ROWS
    at = 0
    for x_ref in x_refs:
        for base in range(0, x_ref.shape[0], message_rows(capacity)):
            for piece in range(PIECES):
                xs[piece, pl.ds(at, capacity), :] = x_ref[pl.ds(base + piece * capacity, capacity), :]
            tag = x_ref[pl.ds(base + PIECES * capacity, TAG_ROWS), :].astype(jnp.float32)
            for n in range(shares):
                column = n * (LANES // shares)
                tags[pl.ds(at + n * TAG_ROWS, TAG_ROWS), :] = jnp.broadcast_to(
                    tag[:, column : column + 1], (TAG_ROWS, LANES)
                )
            at += capacity
    wanted = lax.broadcasted_iota(jnp.int32, tags.shape, 1)
    wanted = ((wanted & 31) << 2) + (wanted >> 5) + 1
    hot[...] = jnp.where(tags[...] == wanted.astype(jnp.float32), 1.0, 0.0).T.astype(jnp.bfloat16)
    pick_rows(hot, xs, part, out_ref, 0)


def second_half_kernel(xs, hot, out_ref, part):
    pick_rows(hot, xs, part, out_ref, 1)


def sum_slots(arrived, capacity):
    rows = sum(x.shape[0] for x in arrived) // message_rows(capacity) * capacity
    vmem = pl.BlockSpec(memory_space=pltpu.VMEM)
    half = jax.ShapeDtypeStruct((SUB * 32, LANES), jnp.float32)
    params = pltpu.CompilerParams(vmem_limit_bytes=VMEM_LIMIT)
    part = pltpu.VMEM((SLOTS, LANES), jnp.float32)
    first, xs, hot = pl.pallas_call(
        functools.partial(first_half_kernel, capacity),
        out_shape=[
            half,
            jax.ShapeDtypeStruct((PIECES, rows, LANES), jnp.bfloat16),
            jax.ShapeDtypeStruct((SLOTS, rows), jnp.bfloat16),
        ],
        in_specs=[vmem] * len(arrived),
        out_specs=[vmem] * 3,
        scratch_shapes=[pltpu.VMEM((rows, LANES), jnp.float32), part],
        compiler_params=params,
        name="sum_first",
    )(*arrived)
    second = pl.pallas_call(
        second_half_kernel,
        out_shape=half,
        in_specs=[vmem] * 2,
        out_specs=vmem,
        scratch_shapes=[part],
        compiler_params=params,
        name="sum_second",
    )(xs, hot)
    return first, second


def add_kernel(at, mine_ref, theirs_ref, *refs):
    out_ref, total, sems = refs[-3:]
    step = total.shape[0] // sems.shape[0]
    copies = []
    for k in range(sems.shape[0]):
        here = pl.ds(k * step, step)
        total[here, :] = mine_ref[here, :] + theirs_ref[here, :]
        copy = pltpu.make_async_copy(
            total.at[here], out_ref.at[pl.ds(at + k * step, step)], sems.at[k]
        )
        copy.start()
        copies.append(copy)
    for copy in copies:
        copy.wait()


def add_half(at, mine, theirs, *whole):
    vmem, anywhere = pl.BlockSpec(memory_space=pltpu.VMEM), pl.BlockSpec(memory_space=pl.ANY)
    return pl.pallas_call(
        functools.partial(add_kernel, at),
        out_shape=jax.ShapeDtypeStruct((2 * mine.shape[0], LANES), jnp.float32),
        in_specs=[vmem, vmem] + [anywhere] * len(whole),
        out_specs=anywhere,
        scratch_shapes=[pltpu.VMEM(mine.shape, jnp.float32), pltpu.SemaphoreType.DMA((4,))],
        input_output_aliases={2: 0} if whole else {},
        compiler_params=pltpu.CompilerParams(vmem_limit_bytes=VMEM_LIMIT),
        name="add_half",
    )(mine, theirs, *whole)


def rows_of(array):
    blocks, parts, vis = array.shape
    tiles = vis // LANES
    split = array.reshape(blocks, parts, tiles, LANES)
    return split.transpose(0, 2, 1, 3).reshape(blocks * tiles * parts, LANES)


def sending_order(owners):
    return list(range(owners - 1, -1, -1))


def in_rows(array):
    return with_layout_constraint(array, Layout(major_to_minor=(0, 1)))


def local(residual, uv_offsets, counts, tile_of_block, slot_of_block, owner_map):
    blocks, _, vis = uv_offsets.shape
    owners = owner_map.shape[0]
    capacity = -(-max(CAP_MIN, 2 * blocks // owners) // 32) * 16
    core = lax.axis_index("samp")
    me = lax.axis_index(("blk", "tile"))
    swap = [(0, 1), (1, 0)]
    own = in_rows(rows_of(residual[0]))
    other = in_rows(lax.ppermute(own, "samp", swap))

    lists = jnp.concatenate([tile_of_block[:, 0], slot_of_block, counts, owner_map])
    lists = lax.optimization_barrier(lists)
    tile_ids, slots, counts, owner_map = [
        lists[k * blocks : min((k + 1) * blocks, 3 * blocks + owners)] for k in range(4)
    ]
    owner_range = jnp.arange(owners, dtype=jnp.int32)
    owner_ids = jnp.sum(
        jnp.where(tile_ids[:, None] == owner_range[None, :], owner_map[None, :], 0), 1
    )
    paired = owners <= PAIRED_MAX and owners & (owners - 1) == 0
    distances = sending_order(owners)
    offset = owner_ids
    if paired:
        offset = jnp.bitwise_xor(owner_ids, me)
        offset = sum(jnp.where(offset == d, k, 0) for k, d in enumerate(distances) if k)
    index = jnp.arange(blocks, dtype=jnp.int32)
    same = (offset[None, :] == offset[:, None]) & (index[None, :] < index[:, None])
    rank = jnp.sum(same.astype(jnp.int32), 1)
    mine = (rank & 1) == core
    counted = jnp.sum((mine[None, :] & (offset[None, :] == owner_range[:, None])).astype(jnp.int32), 1)
    quads = (counted + QUAD - 1) >> 2
    edges = jnp.arange(owners + 1, dtype=jnp.int32)
    start = jnp.sum(jnp.where(owner_range[None, :] < edges[:, None], quads[None, :], 0), 1)
    before = jnp.sum(jnp.where(owner_range[None, :] < offset[:, None], quads[None, :], 0), 1)
    place = jnp.where(mine, before * QUAD + (rank >> 1), -1)
    longest = ((blocks + owners) // 2 + owners * (QUAD - 1)) // GROUP * GROUP + GROUP
    wanted = jnp.arange(longest, dtype=jnp.int32)
    chosen = place[None, :] == wanted[:, None]
    block_and_count = (index << COUNT_BITS) + counts
    row_and_tag = ((offset * capacity + (rank >> 1)) << TAG_BITS) + slots + 1
    block = jnp.sum(jnp.where(chosen, block_and_count[None, :], 0), 1)
    row = jnp.sum(jnp.where(chosen, row_and_tag[None, :], 0), 1)

    subgrids = functools.partial(
        make_subgrids, capacity=capacity, block=block, row=row, start=start, uv=rows_of(uv_offsets),
        res=own.astype(jnp.float32) + other.astype(jnp.float32), vis=vis,
    )
    token = jnp.zeros((GROUP, LANES), jnp.int32)
    if paired:
        rows = []
        for first, last in zip(CALLS[:-1], CALLS[1:]):
            first, last = owners * first // CALLS[-1], owners * last // CALLS[-1]
            if first < last:
                *more, token = subgrids(first, (1,) * (last - first), token)
                rows += more
        arrived = []
        for distance, piece in zip(distances, rows):
            if distance:
                pairs = [(k, k ^ distance) for k in range(owners)]
                piece = lax.ppermute(piece, ("blk", "tile"), pairs)
            arrived.append(piece)
    else:
        each = max(d for d in range(1, 17) if owners % d == 0)
        rows = [subgrids(k, (each,), token)[0] for k in range(0, owners, each)]
        rows = jnp.concatenate(rows, 0).reshape(owners, message_rows(capacity), LANES)
        rows = lax.all_to_all(rows, ("blk", "tile"), split_axis=0, concat_axis=0, tiled=True)
        arrived = [rows.reshape(owners * message_rows(capacity), LANES)]
    first, second = sum_slots(arrived, capacity)
    whole = add_half(0, first, lax.ppermute(first, "samp", swap))
    whole = add_half(first.shape[0], second, lax.ppermute(second, "samp", swap), whole)
    whole = whole.reshape(SUB, SLOTS // 4, 2, LANES).transpose(0, 2, 1, 3)
    return whole.reshape(SUB, 2, SLOTS * SUB)


def solution(mesh):
    in_specs = (
        P("samp", ("cuts", "blk", "tile"), None, None),
        P(("cuts", "blk", "tile"), None, None),
        P(("cuts", "blk", "tile")),
        P(("cuts", "blk", "tile"), None),
        P(("cuts", "blk", "tile")),
        P(),
    )
    out_specs = P(("cuts", "blk", "tile"), None, None)
    return jax.shard_map(local, mesh=mesh, in_specs=in_specs, out_specs=out_specs, check_vma=False)
```

```python
import functools

import jax
import jax.numpy as jnp
import numpy as np
from jax import lax
from jax.experimental import pallas as pl
from jax.experimental.layout import Layout, with_layout_constraint
from jax.experimental.pallas import tpu as pltpu
from jax.sharding import PartitionSpec as P

SUB = 32
STEPS = SUB // 2
SLOTS = 128
LANES = 128
FEATURE = 2 * SUB * SUB
PIECES = FEATURE // LANES
CAP_MIN = 8
GROUP = 8
QUAD = 4
TAG_ROWS = 16
COUNT_BITS = 12
TAG_BITS = 8
CHUNK = 2 * LANES
PAIRED_MAX = 16
CALLS = (0, 1, 3, 5, 7, 8)
VMEM_LIMIT = 48 * 1024 * 1024


def turn_coefficients():
    knots = np.cos(np.pi * (np.arange(400) + 0.5) / 400)
    cheb = np.polynomial.chebyshev
    even = cheb.cheb2poly(cheb.chebfit(knots, np.cos(np.pi * knots), 12))[0::2]
    odd = cheb.cheb2poly(cheb.chebfit(knots, np.sin(np.pi * knots), 13))[1::2]
    return [float(x) for x in even], [float(x) for x in odd]


COS_COEF, SIN_COEF = turn_coefficients()


def horner(coef, x):
    total = coef[-1] * x + coef[-2]
    for value in coef[-3::-1]:
        total = total * x + value
    return total


def first_angle(offset):
    y = offset * (1.0 / STEPS)
    x = y * y
    return horner(COS_COEF, x), horner(SIN_COEF, x) * y


def tile_of(value, t):
    return value[:, t * LANES : (t + 1) * LANES]


def by_quad(even, odd):
    top = lax.broadcasted_iota(jnp.int32, even.shape, 0) < QUAD
    return (
        jnp.where(top, even, pltpu.roll(odd, QUAD, 0)),
        jnp.where(top, pltpu.roll(even, QUAD, 0), odd),
    )


def sequence(before, middle, factor):
    def pair(*two):
        return jnp.concatenate(two, 0).astype(jnp.bfloat16)

    up, down = [], []
    last, value = before, middle
    for _ in range(STEPS // 4):
        after = factor * value - last
        up.append(pair(value, after))
        last, value = after, factor * after - value
    last, value = middle, before
    for _ in range(STEPS // 4):
        after = factor * value - last
        down.append(pair(after, value))
        last, value = after, factor * after - value
    return down[::-1] + up


def subgrid_kernel(
    first, destinations, capacity, block_ref, row_ref, start_ref, token_ref, uv_ref, res_ref, *refs
):
    out_refs, (next_ref, gathered, found, tags, mover) = refs[:-5], refs[-5:]
    next_ref[...] = jnp.zeros_like(next_ref)
    tiles = gathered.shape[0] // (4 * GROUP)
    spare = destinations * capacity // QUAD
    low, high = start_ref[first], start_ref[first + destinations]
    last = block_ref.shape[0] - 1
    vis_at = lax.broadcasted_iota(jnp.int32, (2 * tiles, LANES), 1) + LANES * (
        lax.broadcasted_iota(jnp.int32, (2 * tiles, LANES), 0) >> 1
    )
    same_block = (
        lax.broadcasted_iota(jnp.int32, (GROUP, LANES), 0) & (QUAD - 1)
        == lax.broadcasted_iota(jnp.int32, (GROUP, LANES), 1) & (QUAD - 1)
    )
    quad_row = lax.broadcasted_iota(jnp.int32, (QUAD, LANES), 0)
    top = lax.broadcasted_iota(jnp.int32, (GROUP, LANES), 0) < QUAD

    source = lax.broadcasted_iota(jnp.int32, mover.shape, 0)
    lane = lax.broadcasted_iota(jnp.int32, mover.shape, 1)
    moves = (source >> 7 == lane >> 5) & ((source & (LANES - 1)) >> 2 == lane & (SUB - 1))
    mover[...] = jnp.where(moves, 1.0, 0.0).astype(jnp.bfloat16)
    tags[...] = jnp.zeros_like(tags)

    def angles(quad_at):
        for i in range(GROUP):
            packed = block_ref[jnp.minimum(quad_at * QUAD + i, last)]
            block, count = packed >> COUNT_BITS, packed & ((1 << COUNT_BITS) - 1)
            at = pl.ds(pl.multiple_of(block * 2 * tiles, 2 * tiles), 2 * tiles)
            both = jnp.where(vis_at < count, res_ref[at, :], 0.0)
            gathered[pl.ds(i, 2 * tiles, stride=GROUP), :] = uv_ref[at, :]
            gathered[pl.ds(2 * tiles * GROUP + i, 2 * tiles, stride=GROUP), :] = both
        u, v, re, im = [
            jnp.concatenate(
                [
                    gathered[pl.ds(((k // 2) * 2 * tiles + 2 * t + k % 2) * GROUP, GROUP), :]
                    for t in range(tiles)
                ],
                1,
            )
            for k in range(4)
        ]
        c, s = first_angle(u)
        a, b, e, f = re * c, im * s, im * c, re * s
        after = (a - b, e + f)
        before = (a + b, e - f)
        second = [2.0 * c * near - far for near, far in zip(before, (re, im))]
        factor = 2.0 - 4.0 * s * s
        left_factor = by_quad(factor, factor)
        left = [(by_quad(x, y), by_quad(z, w)) for x, y, z, w in zip(second, before, (re, im), after)]
        c, s = first_angle(v)
        c2, s2 = 1.0 - 2.0 * s * s, 2.0 * s * c
        factor = 2.0 * c2
        right_factor = by_quad(factor, factor)
        right = [
            (by_quad(c2, c), by_quad(jnp.ones_like(c), c)),
            (by_quad(-s2, -s), by_quad(jnp.zeros_like(s), s)),
        ]
        return [
            [
                (left[0][0][q], left[0][1][q], left[1][0][q], left[1][1][q], left_factor[q]),
                (right[0][0][q], right[0][1][q], right[1][0][q], right[1][1][q], right_factor[q]),
            ]
            for q in range(2)
        ]

    def finish(seeds, quad_at):
        product = None
        for lanes in range(0, tiles * LANES, CHUNK):
            operands = []
            for side in seeds[::-1]:
                before, middle, before_imag, middle_imag, factor = [
                    x[:, lanes : lanes + CHUNK] for x in side
                ]
                operands.append(
                    jnp.concatenate(
                        sequence(before, middle, factor)
                        + sequence(before_imag, middle_imag, factor),
                        0,
                    )
                )
            term = lax.dot_general(
                operands[1], operands[0], (((1,), (1,)), ((), ())),
                preferred_element_type=jnp.float32,
            )
            product = term if product is None else product + term
        half = product.shape[0] // 2
        wholes = (
            product[:half, :LANES] - product[half:, LANES:],
            product[half:, :LANES] + product[:half, LANES:],
        )
        rows = []
        for whole in wholes:
            for j in range(0, STEPS, 4):
                four = [whole[(j + k) * GROUP : (j + k + 1) * GROUP] for k in range(4)]
                rows.append(jnp.concatenate([jnp.where(same_block, x, 0.0) for x in four], 1))
        index = jnp.clip(quad_at * QUAD, 0, last + 1 - QUAD)
        place = (row_ref[index] >> (TAG_BITS + 2)) - first * (capacity // QUAD)
        place = jnp.where((quad_at >= low) & (quad_at < high), place, spare)
        found[place] = jnp.concatenate(rows, 0).astype(jnp.bfloat16)
        tag = jnp.zeros((QUAD, LANES), jnp.int32)
        for b in range(QUAD):
            tag = jnp.where(quad_row == b, row_ref[index + b] & ((1 << TAG_BITS) - 1), tag)
        tags[place] = tag.astype(jnp.float32)

    def turn(g, seeds):
        quad_at = low + 2 * g
        for q in range(2):
            finish(seeds[q], quad_at + q)
        return angles(quad_at + 2)

    lax.fori_loop(0, (high - low + 1) // 2, turn, angles(low))

    shares = capacity // TAG_ROWS
    share = lax.broadcasted_iota(jnp.int32, (TAG_ROWS, LANES), 1) // (LANES // shares)

    def write_share(out_ref, base, slot, sent, n):
        rows = jnp.concatenate([found[slot + k] for k in range(4)], 0)
        moved = jnp.dot(rows, mover[...], preferred_element_type=jnp.float32)
        for piece in range(PIECES // 2):
            part = []
            for k in range(4):
                value = moved[(k * 8 + piece) * GROUP : (k * 8 + piece + 1) * GROUP]
                part.append(jnp.where(n * 4 + k < sent, value, 0.0))
            first_two, last_two = [], []
            for even, odd in (part[:2], part[2:]):
                first_two.append(jnp.where(top, even, pltpu.roll(odd, QUAD, 0)))
                last_two.append(jnp.where(top, pltpu.roll(even, QUAD, 0), odd))
            for parity, two in enumerate((first_two, last_two)):
                put = base + (piece * 2 + parity) * capacity + n * TAG_ROWS
                out_ref[pl.ds(put, TAG_ROWS), :] = jnp.concatenate(two, 0).astype(jnp.bfloat16)

    for d, out_ref in enumerate(out_refs):
        for m in range(out_ref.shape[0] // message_rows(capacity)):
            base = m * message_rows(capacity)
            sent = start_ref[first + d + m + 1] - start_ref[first + d + m]
            slot = (d + m) * (capacity // QUAD)
            tag = jnp.zeros((TAG_ROWS, LANES), jnp.float32)
            for n in range(shares):
                at = slot + n * 4
                four = jnp.concatenate([tags[at + k] for k in range(4)], 0)
                tag = jnp.where(share == n, four, tag)

                @pl.when(n * 4 < sent)
                def _():
                    write_share(out_ref, base, at, sent, n)

                @pl.when(n * 4 >= sent)
                def _():
                    for piece in range(PIECES):
                        put = base + piece * capacity + n * TAG_ROWS
                        out_ref[pl.ds(put, TAG_ROWS), :] = jnp.zeros((TAG_ROWS, LANES), jnp.bfloat16)

            out_ref[pl.ds(base + PIECES * capacity, TAG_ROWS), :] = tag.astype(jnp.bfloat16)


def message_rows(capacity):
    return PIECES * capacity + TAG_ROWS


def make_subgrids(first, outs, token, capacity, block, row, start, uv, res, vis):
    tiles = vis // LANES
    destinations = sum(outs)
    quads = destinations * capacity // QUAD
    vmem = pl.BlockSpec(memory_space=pltpu.VMEM)
    smem = pl.BlockSpec(memory_space=pltpu.SMEM)
    return pl.pallas_call(
        functools.partial(subgrid_kernel, first, destinations, capacity),
        out_shape=[
            jax.ShapeDtypeStruct((n * message_rows(capacity), LANES), jnp.bfloat16) for n in outs
        ]
        + [jax.ShapeDtypeStruct(token.shape, token.dtype)],
        in_specs=[smem] * 3 + [vmem] * 3,
        out_specs=[vmem] * (len(outs) + 1),
        scratch_shapes=[
            pltpu.VMEM((4 * tiles * GROUP, LANES), jnp.float32),
            pltpu.VMEM((quads + 1, FEATURE // SUB, 4 * LANES), jnp.bfloat16),
            pltpu.VMEM((quads + 1, QUAD, LANES), jnp.float32),
            pltpu.VMEM((4 * LANES, LANES), jnp.bfloat16),
        ],
        compiler_params=pltpu.CompilerParams(vmem_limit_bytes=VMEM_LIMIT),
        cost_estimate=pl.CostEstimate(
            flops=quads * 32 * SUB * SUB * vis, bytes_accessed=16 * quads * FEATURE, transcendentals=0
        ),
        name="subgrids",
    )(block, row, start, token, uv, res)


def pick_rows(hot, xs, part, out_ref, half):
    lane = lax.broadcasted_iota(jnp.int32, (GROUP, LANES), 1) >> 5
    for piece in range(PIECES):
        c, rows, parity = piece // 8, piece // 2 % 4 - 2 * half, piece % 2
        if not 0 <= rows < 2:
            continue
        part[...] = jnp.dot(hot[...], xs[piece], preferred_element_type=jnp.float32)
        for grp in range(4):
            given = [part[pl.ds(32 * jl + 8 * grp, 8), :] for jl in range(4)]
            for a in range(4):
                total = None
                for jl in range(4):
                    moved = given[jl]
                    if a != jl:
                        moved = pltpu.roll(moved, ((jl - a) % 4) * SUB, 1)
                    total = moved if total is None else jnp.where(lane == jl, moved, total)
                p = rows * 8 + a * 2 + parity
                out_ref[pl.ds(p * 64 + grp * 16 + c, 8, stride=2), :] = total


def first_half_kernel(capacity, *refs):
    x_refs, (out_ref, xs, hot, tags, part) = refs[:-5], refs[-5:]
    shares = capacity // TAG_ROWS
    at = 0
    for x_ref in x_refs:
        for base in range(0, x_ref.shape[0], message_rows(capacity)):
            for piece in range(PIECES):
                xs[piece, pl.ds(at, capacity), :] = x_ref[pl.ds(base + piece * capacity, capacity), :]
            tag = x_ref[pl.ds(base + PIECES * capacity, TAG_ROWS), :].astype(jnp.float32)
            for n in range(shares):
                column = n * (LANES // shares)
                tags[pl.ds(at + n * TAG_ROWS, TAG_ROWS), :] = jnp.broadcast_to(
                    tag[:, column : column + 1], (TAG_ROWS, LANES)
                )
            at += capacity
    wanted = lax.broadcasted_iota(jnp.int32, tags.shape, 1)
    wanted = ((wanted & 31) << 2) + (wanted >> 5) + 1
    hot[...] = jnp.where(tags[...] == wanted.astype(jnp.float32), 1.0, 0.0).T.astype(jnp.bfloat16)
    pick_rows(hot, xs, part, out_ref, 0)


def second_half_kernel(xs, hot, out_ref, part):
    pick_rows(hot, xs, part, out_ref, 1)


def sum_slots(arrived, capacity):
    rows = sum(x.shape[0] for x in arrived) // message_rows(capacity) * capacity
    vmem = pl.BlockSpec(memory_space=pltpu.VMEM)
    half = jax.ShapeDtypeStruct((SUB * 32, LANES), jnp.float32)
    params = pltpu.CompilerParams(vmem_limit_bytes=VMEM_LIMIT)
    part = pltpu.VMEM((SLOTS, LANES), jnp.float32)
    first, xs, hot = pl.pallas_call(
        functools.partial(first_half_kernel, capacity),
        out_shape=[
            half,
            jax.ShapeDtypeStruct((PIECES, rows, LANES), jnp.bfloat16),
            jax.ShapeDtypeStruct((SLOTS, rows), jnp.bfloat16),
        ],
        in_specs=[vmem] * len(arrived),
        out_specs=[vmem] * 3,
        scratch_shapes=[pltpu.VMEM((rows, LANES), jnp.float32), part],
        compiler_params=params,
        name="sum_first",
    )(*arrived)
    second = pl.pallas_call(
        second_half_kernel,
        out_shape=half,
        in_specs=[vmem] * 2,
        out_specs=vmem,
        scratch_shapes=[part],
        compiler_params=params,
        name="sum_second",
    )(xs, hot)
    return first, second


def add_kernel(at, mine_ref, theirs_ref, *refs):
    out_ref, total, sems = refs[-3:]
    step = total.shape[0] // sems.shape[0]
    copies = []
    for k in range(sems.shape[0]):
        here = pl.ds(k * step, step)
        total[here, :] = mine_ref[here, :] + theirs_ref[here, :]
        copy = pltpu.make_async_copy(
            total.at[here], out_ref.at[pl.ds(at + k * step, step)], sems.at[k]
        )
        copy.start()
        copies.append(copy)
    for copy in copies:
        copy.wait()


def add_half(at, mine, theirs, *whole):
    vmem, anywhere = pl.BlockSpec(memory_space=pltpu.VMEM), pl.BlockSpec(memory_space=pl.ANY)
    return pl.pallas_call(
        functools.partial(add_kernel, at),
        out_shape=jax.ShapeDtypeStruct((2 * mine.shape[0], LANES), jnp.float32),
        in_specs=[vmem, vmem] + [anywhere] * len(whole),
        out_specs=anywhere,
        scratch_shapes=[pltpu.VMEM(mine.shape, jnp.float32), pltpu.SemaphoreType.DMA((4,))],
        input_output_aliases={2: 0} if whole else {},
        compiler_params=pltpu.CompilerParams(vmem_limit_bytes=VMEM_LIMIT),
        name="add_half",
    )(mine, theirs, *whole)


def rows_of(array):
    blocks, parts, vis = array.shape
    tiles = vis // LANES
    split = array.reshape(blocks, parts, tiles, LANES)
    return split.transpose(0, 2, 1, 3).reshape(blocks * tiles * parts, LANES)


def sending_order(owners):
    return list(range(owners - 1, -1, -1))


def in_rows(array):
    return with_layout_constraint(array, Layout(major_to_minor=(0, 1)))


def local(residual, uv_offsets, counts, tile_of_block, slot_of_block, owner_map):
    blocks, _, vis = uv_offsets.shape
    owners = owner_map.shape[0]
    capacity = -(-max(CAP_MIN, 2 * blocks // owners) // 32) * 16
    core = lax.axis_index("samp")
    me = lax.axis_index(("blk", "tile"))
    swap = [(0, 1), (1, 0)]
    own = in_rows(rows_of(residual[0]))
    other = in_rows(lax.ppermute(own, "samp", swap))

    lists = jnp.concatenate([tile_of_block[:, 0], slot_of_block, counts, owner_map])
    lists = lax.optimization_barrier(lists)
    tile_ids, slots, counts, owner_map = [
        lists[k * blocks : min((k + 1) * blocks, 3 * blocks + owners)] for k in range(4)
    ]
    owner_range = jnp.arange(owners, dtype=jnp.int32)
    owner_ids = jnp.sum(
        jnp.where(tile_ids[:, None] == owner_range[None, :], owner_map[None, :], 0), 1
    )
    paired = owners <= PAIRED_MAX and owners & (owners - 1) == 0
    distances = sending_order(owners)
    offset = owner_ids
    if paired:
        offset = jnp.bitwise_xor(owner_ids, me)
        offset = sum(jnp.where(offset == d, k, 0) for k, d in enumerate(distances) if k)
    index = jnp.arange(blocks, dtype=jnp.int32)
    same = (offset[None, :] == offset[:, None]) & (index[None, :] < index[:, None])
    rank = jnp.sum(same.astype(jnp.int32), 1)
    mine = (rank & 1) == core
    counted = jnp.sum((mine[None, :] & (offset[None, :] == owner_range[:, None])).astype(jnp.int32), 1)
    quads = (counted + QUAD - 1) >> 2
    edges = jnp.arange(owners + 1, dtype=jnp.int32)
    start = jnp.sum(jnp.where(owner_range[None, :] < edges[:, None], quads[None, :], 0), 1)
    before = jnp.sum(jnp.where(owner_range[None, :] < offset[:, None], quads[None, :], 0), 1)
    place = jnp.where(mine, before * QUAD + (rank >> 1), -1)
    longest = ((blocks + owners) // 2 + owners * (QUAD - 1)) // GROUP * GROUP + GROUP
    wanted = jnp.arange(longest, dtype=jnp.int32)
    chosen = place[None, :] == wanted[:, None]
    block_and_count = (index << COUNT_BITS) + counts
    row_and_tag = ((offset * capacity + (rank >> 1)) << TAG_BITS) + slots + 1
    block = jnp.sum(jnp.where(chosen, block_and_count[None, :], 0), 1)
    row = jnp.sum(jnp.where(chosen, row_and_tag[None, :], 0), 1)

    subgrids = functools.partial(
        make_subgrids, capacity=capacity, block=block, row=row, start=start, uv=rows_of(uv_offsets),
        res=own.astype(jnp.float32) + other.astype(jnp.float32), vis=vis,
    )
    token = jnp.zeros((GROUP, LANES), jnp.int32)
    if paired:
        rows = []
        for first, last in zip(CALLS[:-1], CALLS[1:]):
            first, last = owners * first // CALLS[-1], owners * last // CALLS[-1]
            if first < last:
                *more, token = subgrids(first, (1,) * (last - first), token)
                rows += more
        arrived = []
        for distance, piece in zip(distances, rows):
            if distance:
                pairs = [(k, k ^ distance) for k in range(owners)]
                piece = lax.ppermute(piece, ("blk", "tile"), pairs)
            arrived.append(piece)
    else:
        each = max(d for d in range(1, 17) if owners % d == 0)
        rows = [subgrids(k, (each,), token)[0] for k in range(0, owners, each)]
        rows = jnp.concatenate(rows, 0).reshape(owners, message_rows(capacity), LANES)
        rows = lax.all_to_all(rows, ("blk", "tile"), split_axis=0, concat_axis=0, tiled=True)
        arrived = [rows.reshape(owners * message_rows(capacity), LANES)]
    first, second = sum_slots(arrived, capacity)
    whole = add_half(0, first, lax.ppermute(first, "samp", swap))
    whole = add_half(first.shape[0], second, lax.ppermute(second, "samp", swap), whole)
    whole = whole.reshape(SUB, SLOTS // 4, 2, LANES).transpose(0, 2, 1, 3)
    return whole.reshape(SUB, 2, SLOTS * SUB)


def solution(mesh):
    in_specs = (
        P("samp", ("cuts", "blk", "tile"), None, None),
        P(("cuts", "blk", "tile"), None, None),
        P(("cuts", "blk", "tile")),
        P(("cuts", "blk", "tile"), None),
        P(("cuts", "blk", "tile")),
        P(),
    )
    out_specs = P(("cuts", "blk", "tile"), None, None)
    return jax.shard_map(local, mesh=mesh, in_specs=in_specs, out_specs=out_specs, check_vma=False)
```

```python
import functools

import jax
import jax.numpy as jnp
import numpy as np
from jax import lax
from jax.experimental import pallas as pl
from jax.experimental.layout import Layout, with_layout_constraint
from jax.experimental.pallas import tpu as pltpu
from jax.sharding import PartitionSpec as P

SUB = 32
STEPS = SUB // 2
SLOTS = 128
LANES = 128
FEATURE = 2 * SUB * SUB
PIECES = FEATURE // LANES
CAP_MIN = 8
GROUP = 8
QUAD = 4
TAG_ROWS = 16
COUNT_BITS = 12
TAG_BITS = 8
CHUNK = 2 * LANES
PAIRED_MAX = 16
CALLS = (0, 2, 4, 7, 8)
VMEM_LIMIT = 48 * 1024 * 1024


def turn_coefficients():
    knots = np.cos(np.pi * (np.arange(400) + 0.5) / 400)
    cheb = np.polynomial.chebyshev
    even = cheb.cheb2poly(cheb.chebfit(knots, np.cos(np.pi * knots), 12))[0::2]
    odd = cheb.cheb2poly(cheb.chebfit(knots, np.sin(np.pi * knots), 13))[1::2]
    return [float(x) for x in even], [float(x) for x in odd]


COS_COEF, SIN_COEF = turn_coefficients()


def horner(coef, x):
    total = coef[-1] * x + coef[-2]
    for value in coef[-3::-1]:
        total = total * x + value
    return total


def first_angle(offset):
    y = offset * (1.0 / STEPS)
    x = y * y
    return horner(COS_COEF, x), horner(SIN_COEF, x) * y


def tile_of(value, t):
    return value[:, t * LANES : (t + 1) * LANES]


def by_quad(even, odd):
    top = lax.broadcasted_iota(jnp.int32, even.shape, 0) < QUAD
    return (
        jnp.where(top, even, pltpu.roll(odd, QUAD, 0)),
        jnp.where(top, pltpu.roll(even, QUAD, 0), odd),
    )


def sequence(before, middle, factor):
    def pair(*two):
        return jnp.concatenate(two, 0).astype(jnp.bfloat16)

    up, down = [], []
    last, value = before, middle
    for _ in range(STEPS // 4):
        after = factor * value - last
        up.append(pair(value, after))
        last, value = after, factor * after - value
    last, value = middle, before
    for _ in range(STEPS // 4):
        after = factor * value - last
        down.append(pair(after, value))
        last, value = after, factor * after - value
    return down[::-1] + up


def subgrid_kernel(
    first, destinations, capacity, block_ref, row_ref, start_ref, token_ref, uv_ref, res_low_ref,
    res_high_ref, *refs
):
    out_refs, (next_ref, gathered, found, tags, mover) = refs[:-5], refs[-5:]
    next_ref[...] = jnp.zeros_like(next_ref)
    tiles = gathered.shape[0] // (4 * GROUP)
    spare = destinations * capacity // QUAD
    low, high = start_ref[first], start_ref[first + destinations]
    last = block_ref.shape[0] - 1
    half_blocks = res_low_ref.shape[0] // (2 * tiles)
    vis_at = lax.broadcasted_iota(jnp.int32, (2 * tiles, LANES), 1) + LANES * (
        lax.broadcasted_iota(jnp.int32, (2 * tiles, LANES), 0) >> 1
    )
    same_block = (
        lax.broadcasted_iota(jnp.int32, (GROUP, LANES), 0) & (QUAD - 1)
        == lax.broadcasted_iota(jnp.int32, (GROUP, LANES), 1) & (QUAD - 1)
    )
    quad_row = lax.broadcasted_iota(jnp.int32, (QUAD, LANES), 0)
    top = lax.broadcasted_iota(jnp.int32, (GROUP, LANES), 0) < QUAD

    source = lax.broadcasted_iota(jnp.int32, mover.shape, 0)
    lane = lax.broadcasted_iota(jnp.int32, mover.shape, 1)
    moves = (source >> 7 == lane >> 5) & ((source & (LANES - 1)) >> 2 == lane & (SUB - 1))
    mover[...] = jnp.where(moves, 1.0, 0.0).astype(jnp.bfloat16)
    tags[...] = jnp.zeros_like(tags)

    def angles(quad_at):
        for i in range(GROUP):
            packed = block_ref[jnp.minimum(quad_at * QUAD + i, last)]
            block, count = packed >> COUNT_BITS, packed & ((1 << COUNT_BITS) - 1)
            at = pl.ds(pl.multiple_of(block * 2 * tiles, 2 * tiles), 2 * tiles)
            inner = jnp.where(block < half_blocks, block, block - half_blocks)
            inner = pl.ds(pl.multiple_of(inner * 2 * tiles, 2 * tiles), 2 * tiles)
            both = jnp.where(block < half_blocks, res_low_ref[inner, :], res_high_ref[inner, :])
            both = jnp.where(vis_at < count, both, 0.0)
            gathered[pl.ds(i, 2 * tiles, stride=GROUP), :] = uv_ref[at, :]
            gathered[pl.ds(2 * tiles * GROUP + i, 2 * tiles, stride=GROUP), :] = both
        u, v, re, im = [
            jnp.concatenate(
                [
                    gathered[pl.ds(((k // 2) * 2 * tiles + 2 * t + k % 2) * GROUP, GROUP), :]
                    for t in range(tiles)
                ],
                1,
            )
            for k in range(4)
        ]
        c, s = first_angle(u)
        a, b, e, f = re * c, im * s, im * c, re * s
        after = (a - b, e + f)
        before = (a + b, e - f)
        second = [2.0 * c * near - far for near, far in zip(before, (re, im))]
        factor = 2.0 - 4.0 * s * s
        left_factor = by_quad(factor, factor)
        left = [(by_quad(x, y), by_quad(z, w)) for x, y, z, w in zip(second, before, (re, im), after)]
        c, s = first_angle(v)
        c2, s2 = 1.0 - 2.0 * s * s, 2.0 * s * c
        factor = 2.0 * c2
        right_factor = by_quad(factor, factor)
        right = [
            (by_quad(c2, c), by_quad(jnp.ones_like(c), c)),
            (by_quad(-s2, -s), by_quad(jnp.zeros_like(s), s)),
        ]
        return [
            [
                (left[0][0][q], left[0][1][q], left[1][0][q], left[1][1][q], left_factor[q]),
                (right[0][0][q], right[0][1][q], right[1][0][q], right[1][1][q], right_factor[q]),
            ]
            for q in range(2)
        ]

    def finish(seeds, quad_at):
        product = None
        for lanes in range(0, tiles * LANES, CHUNK):
            operands = []
            for side in seeds[::-1]:
                before, middle, before_imag, middle_imag, factor = [
                    x[:, lanes : lanes + CHUNK] for x in side
                ]
                operands.append(
                    jnp.concatenate(
                        sequence(before, middle, factor)
                        + sequence(before_imag, middle_imag, factor),
                        0,
                    )
                )
            term = lax.dot_general(
                operands[1], operands[0], (((1,), (1,)), ((), ())),
                preferred_element_type=jnp.float32,
            )
            product = term if product is None else product + term
        half = product.shape[0] // 2
        wholes = (
            product[:half, :LANES] - product[half:, LANES:],
            product[half:, :LANES] + product[:half, LANES:],
        )
        rows = []
        for whole in wholes:
            for j in range(0, STEPS, 4):
                four = [whole[(j + k) * GROUP : (j + k + 1) * GROUP] for k in range(4)]
                rows.append(jnp.concatenate([jnp.where(same_block, x, 0.0) for x in four], 1))
        index = jnp.clip(quad_at * QUAD, 0, last + 1 - QUAD)
        place = (row_ref[index] >> (TAG_BITS + 2)) - first * (capacity // QUAD)
        place = jnp.where((quad_at >= low) & (quad_at < high), place, spare)
        found[place] = jnp.concatenate(rows, 0).astype(jnp.bfloat16)
        tag = jnp.zeros((QUAD, LANES), jnp.int32)
        for b in range(QUAD):
            tag = jnp.where(quad_row == b, row_ref[index + b] & ((1 << TAG_BITS) - 1), tag)
        tags[place] = tag.astype(jnp.float32)

    def turn(g, seeds):
        quad_at = low + 2 * g
        for q in range(2):
            finish(seeds[q], quad_at + q)
        return angles(quad_at + 2)

    lax.fori_loop(0, (high - low + 1) // 2, turn, angles(low))

    shares = capacity // TAG_ROWS
    share = lax.broadcasted_iota(jnp.int32, (TAG_ROWS, LANES), 1) // (LANES // shares)

    def write_share(out_ref, base, slot, sent, n):
        rows = jnp.concatenate([found[slot + k] for k in range(4)], 0)
        moved = jnp.dot(rows, mover[...], preferred_element_type=jnp.float32)
        for piece in range(PIECES // 2):
            part = []
            for k in range(4):
                value = moved[(k * 8 + piece) * GROUP : (k * 8 + piece + 1) * GROUP]
                part.append(jnp.where(n * 4 + k < sent, value, 0.0))
            first_two, last_two = [], []
            for even, odd in (part[:2], part[2:]):
                first_two.append(jnp.where(top, even, pltpu.roll(odd, QUAD, 0)))
                last_two.append(jnp.where(top, pltpu.roll(even, QUAD, 0), odd))
            for parity, two in enumerate((first_two, last_two)):
                put = base + (piece * 2 + parity) * capacity + n * TAG_ROWS
                out_ref[pl.ds(put, TAG_ROWS), :] = jnp.concatenate(two, 0).astype(jnp.bfloat16)

    for d, out_ref in enumerate(out_refs):
        for m in range(out_ref.shape[0] // message_rows(capacity)):
            base = m * message_rows(capacity)
            sent = start_ref[first + d + m + 1] - start_ref[first + d + m]
            slot = (d + m) * (capacity // QUAD)
            tag = jnp.zeros((TAG_ROWS, LANES), jnp.float32)
            for n in range(shares):
                at = slot + n * 4
                four = jnp.concatenate([tags[at + k] for k in range(4)], 0)
                tag = jnp.where(share == n, four, tag)

                @pl.when(n * 4 < sent)
                def _():
                    write_share(out_ref, base, at, sent, n)

                @pl.when(n * 4 >= sent)
                def _():
                    for piece in range(PIECES):
                        put = base + piece * capacity + n * TAG_ROWS
                        out_ref[pl.ds(put, TAG_ROWS), :] = jnp.zeros((TAG_ROWS, LANES), jnp.bfloat16)

            out_ref[pl.ds(base + PIECES * capacity, TAG_ROWS), :] = tag.astype(jnp.bfloat16)


def message_rows(capacity):
    return PIECES * capacity + TAG_ROWS


def make_subgrids(first, outs, token, capacity, block, row, start, uv, res, vis):
    tiles = vis // LANES
    destinations = sum(outs)
    quads = destinations * capacity // QUAD
    vmem = pl.BlockSpec(memory_space=pltpu.VMEM)
    smem = pl.BlockSpec(memory_space=pltpu.SMEM)
    return pl.pallas_call(
        functools.partial(subgrid_kernel, first, destinations, capacity),
        out_shape=[
            jax.ShapeDtypeStruct((n * message_rows(capacity), LANES), jnp.bfloat16) for n in outs
        ]
        + [jax.ShapeDtypeStruct(token.shape, token.dtype)],
        in_specs=[smem] * 3 + [vmem] * 4,
        out_specs=[vmem] * (len(outs) + 1),
        scratch_shapes=[
            pltpu.VMEM((4 * tiles * GROUP, LANES), jnp.float32),
            pltpu.VMEM((quads + 1, FEATURE // SUB, 4 * LANES), jnp.bfloat16),
            pltpu.VMEM((quads + 1, QUAD, LANES), jnp.float32),
            pltpu.VMEM((4 * LANES, LANES), jnp.bfloat16),
        ],
        compiler_params=pltpu.CompilerParams(vmem_limit_bytes=VMEM_LIMIT),
        cost_estimate=pl.CostEstimate(
            flops=quads * 32 * SUB * SUB * vis, bytes_accessed=16 * quads * FEATURE, transcendentals=0
        ),
        name="subgrids",
    )(block, row, start, token, uv, *res)


def pick_rows(hot, xs, part, out_ref, half):
    lane = lax.broadcasted_iota(jnp.int32, (GROUP, LANES), 1) >> 5
    for piece in range(PIECES):
        c, rows, parity = piece // 8, piece // 2 % 4 - 2 * half, piece % 2
        if not 0 <= rows < 2:
            continue
        part[...] = jnp.dot(hot[...], xs[piece], preferred_element_type=jnp.float32)
        for grp in range(4):
            given = [part[pl.ds(32 * jl + 8 * grp, 8), :] for jl in range(4)]
            for a in range(4):
                total = None
                for jl in range(4):
                    moved = given[jl]
                    if a != jl:
                        moved = pltpu.roll(moved, ((jl - a) % 4) * SUB, 1)
                    total = moved if total is None else jnp.where(lane == jl, moved, total)
                p = rows * 8 + a * 2 + parity
                out_ref[pl.ds(p * 64 + grp * 16 + c, 8, stride=2), :] = total


def first_half_kernel(capacity, *refs):
    x_refs, (out_ref, xs, hot, tags, part) = refs[:-5], refs[-5:]
    shares = capacity // TAG_ROWS
    at = 0
    for x_ref in x_refs:
        for base in range(0, x_ref.shape[0], message_rows(capacity)):
            for piece in range(PIECES):
                xs[piece, pl.ds(at, capacity), :] = x_ref[pl.ds(base + piece * capacity, capacity), :]
            tag = x_ref[pl.ds(base + PIECES * capacity, TAG_ROWS), :].astype(jnp.float32)
            for n in range(shares):
                column = n * (LANES // shares)
                tags[pl.ds(at + n * TAG_ROWS, TAG_ROWS), :] = jnp.broadcast_to(
                    tag[:, column : column + 1], (TAG_ROWS, LANES)
                )
            at += capacity
    wanted = lax.broadcasted_iota(jnp.int32, tags.shape, 1)
    wanted = ((wanted & 31) << 2) + (wanted >> 5) + 1
    hot[...] = jnp.where(tags[...] == wanted.astype(jnp.float32), 1.0, 0.0).T.astype(jnp.bfloat16)
    pick_rows(hot, xs, part, out_ref, 0)


def second_half_kernel(xs, hot, out_ref, part):
    pick_rows(hot, xs, part, out_ref, 1)


def sum_slots(arrived, capacity):
    rows = sum(x.shape[0] for x in arrived) // message_rows(capacity) * capacity
    vmem = pl.BlockSpec(memory_space=pltpu.VMEM)
    half = jax.ShapeDtypeStruct((SUB * 32, LANES), jnp.float32)
    params = pltpu.CompilerParams(vmem_limit_bytes=VMEM_LIMIT)
    part = pltpu.VMEM((SLOTS, LANES), jnp.float32)
    first, xs, hot = pl.pallas_call(
        functools.partial(first_half_kernel, capacity),
        out_shape=[
            half,
            jax.ShapeDtypeStruct((PIECES, rows, LANES), jnp.bfloat16),
            jax.ShapeDtypeStruct((SLOTS, rows), jnp.bfloat16),
        ],
        in_specs=[vmem] * len(arrived),
        out_specs=[vmem] * 3,
        scratch_shapes=[pltpu.VMEM((rows, LANES), jnp.float32), part],
        compiler_params=params,
        name="sum_first",
    )(*arrived)
    second = pl.pallas_call(
        second_half_kernel,
        out_shape=half,
        in_specs=[vmem] * 2,
        out_specs=vmem,
        scratch_shapes=[part],
        compiler_params=params,
        name="sum_second",
    )(xs, hot)
    return first, second


def add_kernel(*refs):
    pairs, (out_ref, total, sems) = refs[:-3], refs[-3:]
    step = total.shape[0] // sems.shape[0]
    copies = []
    for mine_ref, theirs_ref in zip(pairs[0::2], pairs[1::2]):
        for at in range(0, mine_ref.shape[0], step):
            here = pl.ds(len(copies) * step, step)
            total[here, :] = mine_ref[pl.ds(at, step), :] + theirs_ref[pl.ds(at, step), :]
            copies.append(
                pltpu.make_async_copy(total.at[here], out_ref.at[here], sems.at[len(copies)])
            )
            copies[-1].start()
    for copy in copies:
        copy.wait()


def add_halves(*pairs):
    rows = sum(mine.shape[0] for mine, _ in pairs)
    vmem = pl.BlockSpec(memory_space=pltpu.VMEM)
    return pl.pallas_call(
        add_kernel,
        out_shape=jax.ShapeDtypeStruct((rows, LANES), jnp.float32),
        in_specs=[vmem] * (2 * len(pairs)),
        out_specs=pl.BlockSpec(memory_space=pl.ANY),
        scratch_shapes=[pltpu.VMEM((rows, LANES), jnp.float32), pltpu.SemaphoreType.DMA((8,))],
        compiler_params=pltpu.CompilerParams(vmem_limit_bytes=VMEM_LIMIT),
        name="add_halves",
    )(*[x for pair in pairs for x in pair])


def rows_of(array):
    blocks, parts, vis = array.shape
    tiles = vis // LANES
    split = array.reshape(blocks, parts, tiles, LANES)
    return split.transpose(0, 2, 1, 3).reshape(blocks * tiles * parts, LANES)


def sending_order(owners):
    across, near = list(range(max(owners // 2, 1), owners)), list(range(1, owners // 2))
    order = [across.pop() for _ in range(owners // 4)]
    while across or near:
        order += [group.pop() for group in (across, near) if group]
    return order + [0]


def in_rows(array):
    return with_layout_constraint(array, Layout(major_to_minor=(0, 1)))


def local(residual, uv_offsets, counts, tile_of_block, slot_of_block, owner_map):
    blocks, _, vis = uv_offsets.shape
    owners = owner_map.shape[0]
    capacity = -(-max(CAP_MIN, 2 * blocks // owners) // 32) * 16
    core = lax.axis_index("samp")
    me = lax.axis_index(("blk", "tile"))
    swap = [(0, 1), (1, 0)]
    halves = [in_rows(x) for x in jnp.split(rows_of(residual[0]), 2)]
    others = [in_rows(lax.ppermute(x, "samp", swap)) for x in halves]
    both = [x.astype(jnp.float32) + y.astype(jnp.float32) for x, y in zip(halves, others)]

    lists = jnp.concatenate([tile_of_block[:, 0], slot_of_block, counts, owner_map])
    lists = lax.optimization_barrier(lists)
    tile_ids, slots, counts, owner_map = [
        lists[k * blocks : min((k + 1) * blocks, 3 * blocks + owners)] for k in range(4)
    ]
    owner_range = jnp.arange(owners, dtype=jnp.int32)
    owner_ids = jnp.sum(
        jnp.where(tile_ids[:, None] == owner_range[None, :], owner_map[None, :], 0), 1
    )
    paired = owners <= PAIRED_MAX and owners & (owners - 1) == 0
    distances = sending_order(owners)
    offset = owner_ids
    if paired:
        offset = jnp.bitwise_xor(owner_ids, me)
        offset = sum(jnp.where(offset == d, k, 0) for k, d in enumerate(distances) if k)
    index = jnp.arange(blocks, dtype=jnp.int32)
    same = (offset[None, :] == offset[:, None]) & (index[None, :] < index[:, None])
    rank = jnp.sum(same.astype(jnp.int32), 1)
    mine = (rank & 1) == core
    counted = jnp.sum((mine[None, :] & (offset[None, :] == owner_range[:, None])).astype(jnp.int32), 1)
    quads = (counted + QUAD - 1) >> 2
    edges = jnp.arange(owners + 1, dtype=jnp.int32)
    start = jnp.sum(jnp.where(owner_range[None, :] < edges[:, None], quads[None, :], 0), 1)
    before = jnp.sum(jnp.where(owner_range[None, :] < offset[:, None], quads[None, :], 0), 1)
    place = jnp.where(mine, before * QUAD + (rank >> 1), -1)
    longest = ((blocks + owners) // 2 + owners * (QUAD - 1)) // GROUP * GROUP + GROUP
    wanted = jnp.arange(longest, dtype=jnp.int32)
    chosen = place[None, :] == wanted[:, None]
    block_and_count = (index << COUNT_BITS) + counts
    row_and_tag = ((offset * capacity + (rank >> 1)) << TAG_BITS) + slots + 1
    block = jnp.sum(jnp.where(chosen, block_and_count[None, :], 0), 1)
    row = jnp.sum(jnp.where(chosen, row_and_tag[None, :], 0), 1)

    subgrids = functools.partial(
        make_subgrids, capacity=capacity, block=block, row=row, start=start, uv=rows_of(uv_offsets),
        res=both, vis=vis,
    )
    token = jnp.zeros((GROUP, LANES), jnp.int32)
    if paired:
        rows = []
        for first, last in zip(CALLS[:-1], CALLS[1:]):
            first, last = owners * first // CALLS[-1], owners * last // CALLS[-1]
            if first < last:
                *more, token = subgrids(first, (1,) * (last - first), token)
                rows += more
        arrived = []
        for distance, piece in zip(distances, rows):
            if distance:
                pairs = [(k, k ^ distance) for k in range(owners)]
                piece = lax.ppermute(piece, ("blk", "tile"), pairs)
            arrived.append(piece)
    else:
        each = max(d for d in range(1, 17) if owners % d == 0)
        rows = [subgrids(k, (each,), token)[0] for k in range(0, owners, each)]
        rows = jnp.concatenate(rows, 0).reshape(owners, message_rows(capacity), LANES)
        rows = lax.all_to_all(rows, ("blk", "tile"), split_axis=0, concat_axis=0, tiled=True)
        arrived = [rows.reshape(owners * message_rows(capacity), LANES)]
    first, second = sum_slots(arrived, capacity)
    whole = add_halves(*[(x, lax.ppermute(x, "samp", swap)) for x in (first, second)])
    whole = whole.reshape(SUB, SLOTS // 4, 2, LANES).transpose(0, 2, 1, 3)
    return whole.reshape(SUB, 2, SLOTS * SUB)


def solution(mesh):
    in_specs = (
        P("samp", ("cuts", "blk", "tile"), None, None),
        P(("cuts", "blk", "tile"), None, None),
        P(("cuts", "blk", "tile")),
        P(("cuts", "blk", "tile"), None),
        P(("cuts", "blk", "tile")),
        P(),
    )
    out_specs = P(("cuts", "blk", "tile"), None, None)
    return jax.shard_map(local, mesh=mesh, in_specs=in_specs, out_specs=out_specs, check_vma=False)
```

```python
import functools

import jax
import jax.numpy as jnp
import numpy as np
from jax import lax
from jax.experimental import pallas as pl
from jax.experimental.layout import Layout, with_layout_constraint
from jax.experimental.pallas import tpu as pltpu
from jax.sharding import PartitionSpec as P

SUB = 32
STEPS = SUB // 2
SLOTS = 128
LANES = 128
FEATURE = 2 * SUB * SUB
PIECES = FEATURE // LANES
CAP_MIN = 8
GROUP = 8
QUAD = 4
TAG_ROWS = 16
COUNT_BITS = 12
TAG_BITS = 8
CHUNK = 4 * LANES
PAIRED_MAX = 16
CALLS = (0, 2, 4, 8)
VMEM_LIMIT = 48 * 1024 * 1024


def turn_coefficients():
    knots = np.cos(np.pi * (np.arange(400) + 0.5) / 400)
    cheb = np.polynomial.chebyshev
    even = cheb.cheb2poly(cheb.chebfit(knots, np.cos(np.pi * knots), 12))[0::2]
    odd = cheb.cheb2poly(cheb.chebfit(knots, np.sin(np.pi * knots), 13))[1::2]
    return [float(x) for x in even], [float(x) for x in odd]


COS_COEF, SIN_COEF = turn_coefficients()


def horner(coef, x):
    total = coef[-1] * x + coef[-2]
    for value in coef[-3::-1]:
        total = total * x + value
    return total


def first_angle(offset):
    y = offset * (1.0 / STEPS)
    x = y * y
    return horner(COS_COEF, x), horner(SIN_COEF, x) * y


def tile_of(value, t):
    return value[:, t * LANES : (t + 1) * LANES]


def by_quad(even, odd):
    top = lax.broadcasted_iota(jnp.int32, even.shape, 0) < QUAD
    return (
        jnp.where(top, even, pltpu.roll(odd, QUAD, 0)),
        jnp.where(top, pltpu.roll(even, QUAD, 0), odd),
    )


def sequence(before, middle, factor):
    def pair(*two):
        return jnp.concatenate(two, 0).astype(jnp.bfloat16)

    up, down = [], []
    last, value = before, middle
    for _ in range(STEPS // 4):
        after = factor * value - last
        up.append(pair(value, after))
        last, value = after, factor * after - value
    last, value = middle, before
    for _ in range(STEPS // 4):
        after = factor * value - last
        down.append(pair(after, value))
        last, value = after, factor * after - value
    return down[::-1] + up


def subgrid_kernel(
    first, destinations, capacity, listed, plan_ref, token_ref, uv_ref, res_ref, *refs
):
    out_refs, (next_ref, gathered, found, tags, mover) = refs[:-5], refs[-5:]
    next_ref[...] = jnp.zeros_like(next_ref)
    tiles = gathered.shape[0] // (4 * GROUP)
    spare = destinations * capacity // QUAD

    def start_of(destination):
        return plan_ref[2 * listed + destination]

    low, high = start_of(first), start_of(first + destinations)
    last = listed - 1
    vis_at = lax.broadcasted_iota(jnp.int32, (2 * tiles, LANES), 1) + LANES * (
        lax.broadcasted_iota(jnp.int32, (2 * tiles, LANES), 0) >> 1
    )
    same_block = (
        lax.broadcasted_iota(jnp.int32, (GROUP, LANES), 0) & (QUAD - 1)
        == lax.broadcasted_iota(jnp.int32, (GROUP, LANES), 1) & (QUAD - 1)
    )
    quad_row = lax.broadcasted_iota(jnp.int32, (QUAD, LANES), 0)
    top = lax.broadcasted_iota(jnp.int32, (GROUP, LANES), 0) < QUAD

    source = lax.broadcasted_iota(jnp.int32, mover.shape, 0)
    lane = lax.broadcasted_iota(jnp.int32, mover.shape, 1)
    moves = (source >> 7 == lane >> 5) & ((source & (LANES - 1)) >> 2 == lane & (SUB - 1))
    mover[...] = jnp.where(moves, 1.0, 0.0).astype(jnp.bfloat16)
    tags[...] = jnp.zeros_like(tags)

    def angles(quad_at):
        for i in range(GROUP):
            packed = plan_ref[jnp.minimum(quad_at * QUAD + i, last)]
            block, count = packed >> COUNT_BITS, packed & ((1 << COUNT_BITS) - 1)
            at = pl.ds(pl.multiple_of(block * 2 * tiles, 2 * tiles), 2 * tiles)
            both = jnp.where(vis_at < count, res_ref[at, :], 0.0)
            gathered[pl.ds(i, 2 * tiles, stride=GROUP), :] = uv_ref[at, :]
            gathered[pl.ds(2 * tiles * GROUP + i, 2 * tiles, stride=GROUP), :] = both
        u, v, re, im = [
            jnp.concatenate(
                [
                    gathered[pl.ds(((k // 2) * 2 * tiles + 2 * t + k % 2) * GROUP, GROUP), :]
                    for t in range(tiles)
                ],
                1,
            )
            for k in range(4)
        ]
        c, s = first_angle(u)
        a, b, e, f = re * c, im * s, im * c, re * s
        after = (a - b, e + f)
        before = (a + b, e - f)
        second = [2.0 * c * near - far for near, far in zip(before, (re, im))]
        factor = 2.0 - 4.0 * s * s
        left_factor = by_quad(factor, factor)
        left = [(by_quad(x, y), by_quad(z, w)) for x, y, z, w in zip(second, before, (re, im), after)]
        c, s = first_angle(v)
        c2, s2 = 1.0 - 2.0 * s * s, 2.0 * s * c
        factor = 2.0 * c2
        right_factor = by_quad(factor, factor)
        right = [
            (by_quad(c2, c), by_quad(jnp.ones_like(c), c)),
            (by_quad(-s2, -s), by_quad(jnp.zeros_like(s), s)),
        ]
        return [
            [
                (left[0][0][q], left[0][1][q], left[1][0][q], left[1][1][q], left_factor[q]),
                (right[0][0][q], right[0][1][q], right[1][0][q], right[1][1][q], right_factor[q]),
            ]
            for q in range(2)
        ]

    def finish(seeds, quad_at):
        product = None
        for lanes in range(0, tiles * LANES, CHUNK):
            operands = []
            for side in seeds[::-1]:
                before, middle, before_imag, middle_imag, factor = [
                    x[:, lanes : lanes + CHUNK] for x in side
                ]
                operands.append(
                    jnp.concatenate(
                        sequence(before, middle, factor)
                        + sequence(before_imag, middle_imag, factor),
                        0,
                    )
                )
            term = lax.dot_general(
                operands[1], operands[0], (((1,), (1,)), ((), ())),
                preferred_element_type=jnp.float32,
            )
            product = term if product is None else product + term
        half = product.shape[0] // 2
        wholes = (
            product[:half, :LANES] - product[half:, LANES:],
            product[half:, :LANES] + product[:half, LANES:],
        )
        rows = []
        for whole in wholes:
            for j in range(0, STEPS, 4):
                four = [whole[(j + k) * GROUP : (j + k + 1) * GROUP] for k in range(4)]
                rows.append(jnp.concatenate([jnp.where(same_block, x, 0.0) for x in four], 1))
        index = jnp.clip(quad_at * QUAD, 0, last + 1 - QUAD)
        place = (plan_ref[listed + index] >> (TAG_BITS + 2)) - first * (capacity // QUAD)
        place = jnp.where((quad_at >= low) & (quad_at < high), place, spare)
        found[place] = jnp.concatenate(rows, 0).astype(jnp.bfloat16)
        tag = jnp.zeros((QUAD, LANES), jnp.int32)
        for b in range(QUAD):
            tag = jnp.where(quad_row == b, plan_ref[listed + index + b] & ((1 << TAG_BITS) - 1), tag)
        tags[place] = tag.astype(jnp.float32)

    def turn(g, seeds):
        quad_at = low + 2 * g
        for q in range(2):
            finish(seeds[q], quad_at + q)
        return angles(quad_at + 2)

    lax.fori_loop(0, (high - low + 1) // 2, turn, angles(low))

    shares = capacity // TAG_ROWS
    share = lax.broadcasted_iota(jnp.int32, (TAG_ROWS, LANES), 1) // (LANES // shares)

    def write_share(out_ref, base, slot, sent, n):
        rows = jnp.concatenate([found[slot + k] for k in range(4)], 0)
        moved = jnp.dot(rows, mover[...], preferred_element_type=jnp.float32)
        for piece in range(PIECES // 2):
            part = []
            for k in range(4):
                value = moved[(k * 8 + piece) * GROUP : (k * 8 + piece + 1) * GROUP]
                part.append(jnp.where(n * 4 + k < sent, value, 0.0))
            first_two, last_two = [], []
            for even, odd in (part[:2], part[2:]):
                first_two.append(jnp.where(top, even, pltpu.roll(odd, QUAD, 0)))
                last_two.append(jnp.where(top, pltpu.roll(even, QUAD, 0), odd))
            for parity, two in enumerate((first_two, last_two)):
                put = base + (piece * 2 + parity) * capacity + n * TAG_ROWS
                out_ref[pl.ds(put, TAG_ROWS), :] = jnp.concatenate(two, 0).astype(jnp.bfloat16)

    for d, out_ref in enumerate(out_refs):
        for m in range(out_ref.shape[0] // message_rows(capacity)):
            base = m * message_rows(capacity)
            sent = start_of(first + d + m + 1) - start_of(first + d + m)
            slot = (d + m) * (capacity // QUAD)
            tag = jnp.zeros((TAG_ROWS, LANES), jnp.float32)
            for n in range(shares):
                at = slot + n * 4
                four = jnp.concatenate([tags[at + k] for k in range(4)], 0)
                tag = jnp.where(share == n, four, tag)

                @pl.when(n * 4 < sent)
                def _():
                    write_share(out_ref, base, at, sent, n)

                @pl.when(n * 4 >= sent)
                def _():
                    for piece in range(PIECES):
                        put = base + piece * capacity + n * TAG_ROWS
                        out_ref[pl.ds(put, TAG_ROWS), :] = jnp.zeros((TAG_ROWS, LANES), jnp.bfloat16)

            out_ref[pl.ds(base + PIECES * capacity, TAG_ROWS), :] = tag.astype(jnp.bfloat16)


def message_rows(capacity):
    return PIECES * capacity + TAG_ROWS


def make_subgrids(first, outs, token, capacity, listed, plan, uv, res, vis):
    tiles = vis // LANES
    destinations = sum(outs)
    quads = destinations * capacity // QUAD
    vmem = pl.BlockSpec(memory_space=pltpu.VMEM)
    smem = pl.BlockSpec(memory_space=pltpu.SMEM)
    return pl.pallas_call(
        functools.partial(subgrid_kernel, first, destinations, capacity, listed),
        out_shape=[
            jax.ShapeDtypeStruct((n * message_rows(capacity), LANES), jnp.bfloat16) for n in outs
        ]
        + [jax.ShapeDtypeStruct(token.shape, token.dtype)],
        in_specs=[smem] + [vmem] * 3,
        out_specs=[vmem] * (len(outs) + 1),
        scratch_shapes=[
            pltpu.VMEM((4 * tiles * GROUP, LANES), jnp.float32),
            pltpu.VMEM((quads + 1, FEATURE // SUB, 4 * LANES), jnp.bfloat16),
            pltpu.VMEM((quads + 1, QUAD, LANES), jnp.float32),
            pltpu.VMEM((4 * LANES, LANES), jnp.bfloat16),
        ],
        compiler_params=pltpu.CompilerParams(vmem_limit_bytes=VMEM_LIMIT),
        cost_estimate=pl.CostEstimate(
            flops=quads * 32 * SUB * SUB * vis, bytes_accessed=16 * quads * FEATURE, transcendentals=0
        ),
        name="subgrids",
    )(plan, token, uv, res)


def pick_rows(hot, xs, part, out_ref, half):
    lane = lax.broadcasted_iota(jnp.int32, (GROUP, LANES), 1) >> 5
    for piece in range(PIECES):
        c, rows, parity = piece // 8, piece // 2 % 4 - 2 * half, piece % 2
        if not 0 <= rows < 2:
            continue
        part[...] = jnp.dot(hot[...], xs[piece], preferred_element_type=jnp.float32)
        for grp in range(4):
            given = [part[pl.ds(32 * jl + 8 * grp, 8), :] for jl in range(4)]
            for a in range(4):
                total = None
                for jl in range(4):
                    moved = given[jl]
                    if a != jl:
                        moved = pltpu.roll(moved, ((jl - a) % 4) * SUB, 1)
                    total = moved if total is None else jnp.where(lane == jl, moved, total)
                p = rows * 8 + a * 2 + parity
                out_ref[pl.ds(p * 64 + grp * 16 + c, 8, stride=2), :] = total


def first_half_kernel(capacity, *refs):
    x_refs, (out_ref, xs, hot, tags, part) = refs[:-5], refs[-5:]
    shares = capacity // TAG_ROWS
    at = 0
    for x_ref in x_refs:
        for base in range(0, x_ref.shape[0], message_rows(capacity)):
            for piece in range(PIECES):
                xs[piece, pl.ds(at, capacity), :] = x_ref[pl.ds(base + piece * capacity, capacity), :]
            tag = x_ref[pl.ds(base + PIECES * capacity, TAG_ROWS), :].astype(jnp.float32)
            for n in range(shares):
                column = n * (LANES // shares)
                tags[pl.ds(at + n * TAG_ROWS, TAG_ROWS), :] = jnp.broadcast_to(
                    tag[:, column : column + 1], (TAG_ROWS, LANES)
                )
            at += capacity
    wanted = lax.broadcasted_iota(jnp.int32, tags.shape, 1)
    wanted = ((wanted & 31) << 2) + (wanted >> 5) + 1
    hot[...] = jnp.where(tags[...] == wanted.astype(jnp.float32), 1.0, 0.0).T.astype(jnp.bfloat16)
    pick_rows(hot, xs, part, out_ref, 0)


def second_half_kernel(xs, hot, out_ref, part):
    pick_rows(hot, xs, part, out_ref, 1)


def sum_slots(arrived, capacity):
    rows = sum(x.shape[0] for x in arrived) // message_rows(capacity) * capacity
    vmem = pl.BlockSpec(memory_space=pltpu.VMEM)
    half = jax.ShapeDtypeStruct((SUB * 32, LANES), jnp.float32)
    params = pltpu.CompilerParams(vmem_limit_bytes=VMEM_LIMIT)
    part = pltpu.VMEM((SLOTS, LANES), jnp.float32)
    first, xs, hot = pl.pallas_call(
        functools.partial(first_half_kernel, capacity),
        out_shape=[
            half,
            jax.ShapeDtypeStruct((PIECES, rows, LANES), jnp.bfloat16),
            jax.ShapeDtypeStruct((SLOTS, rows), jnp.bfloat16),
        ],
        in_specs=[vmem] * len(arrived),
        out_specs=[vmem] * 3,
        scratch_shapes=[pltpu.VMEM((rows, LANES), jnp.float32), part],
        compiler_params=params,
        name="sum_first",
    )(*arrived)
    second = pl.pallas_call(
        second_half_kernel,
        out_shape=half,
        in_specs=[vmem] * 2,
        out_specs=vmem,
        scratch_shapes=[part],
        compiler_params=params,
        name="sum_second",
    )(xs, hot)
    return first, second


def add_kernel(at, mine_ref, theirs_ref, *refs):
    out_ref, total, sems = refs[-3:]
    step = total.shape[0] // sems.shape[0]
    copies = []
    for k in range(sems.shape[0]):
        here = pl.ds(k * step, step)
        total[here, :] = mine_ref[here, :] + theirs_ref[here, :]
        copy = pltpu.make_async_copy(
            total.at[here], out_ref.at[pl.ds(at + k * step, step)], sems.at[k]
        )
        copy.start()
        copies.append(copy)
    for copy in copies:
        copy.wait()


def add_half(at, mine, theirs, *whole):
    vmem, anywhere = pl.BlockSpec(memory_space=pltpu.VMEM), pl.BlockSpec(memory_space=pl.ANY)
    return pl.pallas_call(
        functools.partial(add_kernel, at),
        out_shape=jax.ShapeDtypeStruct((2 * mine.shape[0], LANES), jnp.float32),
        in_specs=[vmem, vmem] + [anywhere] * len(whole),
        out_specs=anywhere,
        scratch_shapes=[pltpu.VMEM(mine.shape, jnp.float32), pltpu.SemaphoreType.DMA((4,))],
        input_output_aliases={2: 0} if whole else {},
        compiler_params=pltpu.CompilerParams(vmem_limit_bytes=VMEM_LIMIT),
        name="add_half",
    )(mine, theirs, *whole)


def rows_of(array):
    blocks, parts, vis = array.shape
    tiles = vis // LANES
    split = array.reshape(blocks, parts, tiles, LANES)
    return split.transpose(0, 2, 1, 3).reshape(blocks * tiles * parts, LANES)


def sending_order(owners):
    across, near = list(range(max(owners // 2, 1), owners)), list(range(1, owners // 2))
    order = [across.pop() for _ in range(owners // 4)]
    while across or near:
        order += [group.pop() for group in (across, near) if group]
    return order + [0]


def in_rows(array):
    return with_layout_constraint(array, Layout(major_to_minor=(0, 1)))


def local(residual, uv_offsets, counts, tile_of_block, slot_of_block, owner_map):
    blocks, _, vis = uv_offsets.shape
    owners = owner_map.shape[0]
    capacity = -(-max(CAP_MIN, 2 * blocks // owners) // 32) * 16
    core = lax.axis_index("samp")
    me = lax.axis_index(("blk", "tile"))
    swap = [(0, 1), (1, 0)]
    own = in_rows(rows_of(residual[0]))
    other = in_rows(lax.ppermute(own, "samp", swap))

    lists = jnp.concatenate([tile_of_block[:, 0], slot_of_block, counts, owner_map])
    lists = lax.optimization_barrier(lists)
    tile_ids, slots, counts, owner_map = [
        lists[k * blocks : min((k + 1) * blocks, 3 * blocks + owners)] for k in range(4)
    ]
    owner_range = jnp.arange(owners, dtype=jnp.int32)
    owner_ids = jnp.sum(
        jnp.where(tile_ids[:, None] == owner_range[None, :], owner_map[None, :], 0), 1
    )
    paired = owners <= PAIRED_MAX and owners & (owners - 1) == 0
    distances = sending_order(owners)
    offset = owner_ids
    if paired:
        offset = jnp.bitwise_xor(owner_ids, me)
        offset = sum(jnp.where(offset == d, k, 0) for k, d in enumerate(distances) if k)
    index = jnp.arange(blocks, dtype=jnp.int32)
    same = (offset[None, :] == offset[:, None]) & (index[None, :] < index[:, None])
    rank = jnp.sum(same.astype(jnp.int32), 1)
    mine = (rank & 1) == core
    counted = jnp.sum((mine[None, :] & (offset[None, :] == owner_range[:, None])).astype(jnp.int32), 1)
    quads = (counted + QUAD - 1) >> 2
    edges = jnp.arange(owners + 1, dtype=jnp.int32)
    start = jnp.sum(jnp.where(owner_range[None, :] < edges[:, None], quads[None, :], 0), 1)
    before = jnp.sum(jnp.where(owner_range[None, :] < offset[:, None], quads[None, :], 0), 1)
    place = jnp.where(mine, before * QUAD + (rank >> 1), -1)
    longest = ((blocks + owners) // 2 + owners * (QUAD - 1)) // GROUP * GROUP + GROUP
    wanted = jnp.arange(longest, dtype=jnp.int32)
    chosen = place[None, :] == wanted[:, None]
    block_and_count = (index << COUNT_BITS) + counts
    row_and_tag = ((offset * capacity + (rank >> 1)) << TAG_BITS) + slots + 1
    block = jnp.sum(jnp.where(chosen, block_and_count[None, :], 0), 1)
    row = jnp.sum(jnp.where(chosen, row_and_tag[None, :], 0), 1)

    subgrids = functools.partial(
        make_subgrids, capacity=capacity, listed=longest, plan=jnp.concatenate([block, row, start]), uv=rows_of(uv_offsets),
        res=own.astype(jnp.float32) + other.astype(jnp.float32), vis=vis,
    )
    token = jnp.zeros((GROUP, LANES), jnp.int32)
    if paired:
        rows = []
        for first, last in zip(CALLS[:-1], CALLS[1:]):
            first, last = owners * first // CALLS[-1], owners * last // CALLS[-1]
            if first < last:
                *more, token = subgrids(first, (1,) * (last - first), token)
                rows += more
        arrived = []
        for distance, piece in zip(distances, rows):
            if distance:
                pairs = [(k, k ^ distance) for k in range(owners)]
                piece = lax.ppermute(piece, ("blk", "tile"), pairs)
            arrived.append(piece)
    else:
        each = max(d for d in range(1, 17) if owners % d == 0)
        rows = [subgrids(k, (each,), token)[0] for k in range(0, owners, each)]
        rows = jnp.concatenate(rows, 0).reshape(owners, message_rows(capacity), LANES)
        rows = lax.all_to_all(rows, ("blk", "tile"), split_axis=0, concat_axis=0, tiled=True)
        arrived = [rows.reshape(owners * message_rows(capacity), LANES)]
    first, second = sum_slots(arrived, capacity)
    whole = add_half(0, first, lax.ppermute(first, "samp", swap))
    whole = add_half(first.shape[0], second, lax.ppermute(second, "samp", swap), whole)
    whole = whole.reshape(SUB, SLOTS // 4, 2, LANES).transpose(0, 2, 1, 3)
    return whole.reshape(SUB, 2, SLOTS * SUB)


def solution(mesh):
    in_specs = (
        P("samp", ("cuts", "blk", "tile"), None, None),
        P(("cuts", "blk", "tile"), None, None),
        P(("cuts", "blk", "tile")),
        P(("cuts", "blk", "tile"), None),
        P(("cuts", "blk", "tile")),
        P(),
    )
    out_specs = P(("cuts", "blk", "tile"), None, None)
    return jax.shard_map(local, mesh=mesh, in_specs=in_specs, out_specs=out_specs, check_vma=False)
```

```python
import functools

import jax
import jax.numpy as jnp
import numpy as np
from jax import lax
from jax.experimental import pallas as pl
from jax.experimental.layout import Layout, with_layout_constraint
from jax.experimental.pallas import tpu as pltpu
from jax.sharding import PartitionSpec as P

SUB = 32
STEPS = SUB // 2
SLOTS = 128
LANES = 128
FEATURE = 2 * SUB * SUB
PIECES = FEATURE // LANES
CAP_MIN = 8
GROUP = 8
QUAD = 4
TAG_ROWS = 16
COUNT_BITS = 12
TAG_BITS = 8
CHUNK = 4 * LANES
PAIRED_MAX = 16
CALLS = (0, 2, 4, 6, 8)
VMEM_LIMIT = 48 * 1024 * 1024


def turn_coefficients():
    knots = np.cos(np.pi * (np.arange(400) + 0.5) / 400)
    cheb = np.polynomial.chebyshev
    even = cheb.cheb2poly(cheb.chebfit(knots, np.cos(np.pi * knots), 12))[0::2]
    odd = cheb.cheb2poly(cheb.chebfit(knots, np.sin(np.pi * knots), 13))[1::2]
    return [float(x) for x in even], [float(x) for x in odd]


COS_COEF, SIN_COEF = turn_coefficients()


def horner(coef, x):
    total = coef[-1] * x + coef[-2]
    for value in coef[-3::-1]:
        total = total * x + value
    return total


def first_angle(offset):
    y = offset * (1.0 / STEPS)
    x = y * y
    return horner(COS_COEF, x), horner(SIN_COEF, x) * y


def tile_of(value, t):
    return value[:, t * LANES : (t + 1) * LANES]


def by_quad(even, odd):
    top = lax.broadcasted_iota(jnp.int32, even.shape, 0) < QUAD
    return (
        jnp.where(top, even, pltpu.roll(odd, QUAD, 0)),
        jnp.where(top, pltpu.roll(even, QUAD, 0), odd),
    )


def sequence(before, middle, factor):
    def pair(*two):
        return jnp.concatenate(two, 0).astype(jnp.bfloat16)

    up, down = [], []
    last, value = before, middle
    for _ in range(STEPS // 4):
        after = factor * value - last
        up.append(pair(value, after))
        last, value = after, factor * after - value
    last, value = middle, before
    for _ in range(STEPS // 4):
        after = factor * value - last
        down.append(pair(after, value))
        last, value = after, factor * after - value
    return down[::-1] + up


def subgrid_kernel(
    first, destinations, capacity, listed, plan_ref, token_ref, uv_ref, res_ref, *refs
):
    out_refs, (next_ref, gathered, found, tags, mover) = refs[:-5], refs[-5:]
    next_ref[...] = jnp.zeros_like(next_ref)
    tiles = gathered.shape[0] // (4 * GROUP)
    spare = destinations * capacity // QUAD

    def start_of(destination):
        return plan_ref[2 * listed + destination]

    low, high = start_of(first), start_of(first + destinations)
    last = listed - 1
    vis_at = lax.broadcasted_iota(jnp.int32, (2 * tiles, LANES), 1) + LANES * (
        lax.broadcasted_iota(jnp.int32, (2 * tiles, LANES), 0) >> 1
    )
    same_block = (
        lax.broadcasted_iota(jnp.int32, (GROUP, LANES), 0) & (QUAD - 1)
        == lax.broadcasted_iota(jnp.int32, (GROUP, LANES), 1) & (QUAD - 1)
    )
    quad_row = lax.broadcasted_iota(jnp.int32, (QUAD, LANES), 0)
    top = lax.broadcasted_iota(jnp.int32, (GROUP, LANES), 0) < QUAD

    source = lax.broadcasted_iota(jnp.int32, mover.shape, 0)
    lane = lax.broadcasted_iota(jnp.int32, mover.shape, 1)
    moves = (source >> 7 == lane >> 5) & ((source & (LANES - 1)) >> 2 == lane & (SUB - 1))
    mover[...] = jnp.where(moves, 1.0, 0.0).astype(jnp.bfloat16)
    tags[...] = jnp.zeros_like(tags)

    def angles(quad_at):
        for i in range(GROUP):
            packed = plan_ref[jnp.minimum(quad_at * QUAD + i, last)]
            block, count = packed >> COUNT_BITS, packed & ((1 << COUNT_BITS) - 1)
            at = pl.ds(pl.multiple_of(block * 2 * tiles, 2 * tiles), 2 * tiles)
            both = jnp.where(vis_at < count, res_ref[at, :], 0.0)
            gathered[pl.ds(i, 2 * tiles, stride=GROUP), :] = uv_ref[at, :]
            gathered[pl.ds(2 * tiles * GROUP + i, 2 * tiles, stride=GROUP), :] = both
        u, v, re, im = [
            jnp.concatenate(
                [
                    gathered[pl.ds(((k // 2) * 2 * tiles + 2 * t + k % 2) * GROUP, GROUP), :]
                    for t in range(tiles)
                ],
                1,
            )
            for k in range(4)
        ]
        c, s = first_angle(u)
        a, b, e, f = re * c, im * s, im * c, re * s
        after = (a - b, e + f)
        before = (a + b, e - f)
        second = [2.0 * c * near - far for near, far in zip(before, (re, im))]
        factor = 2.0 - 4.0 * s * s
        left_factor = by_quad(factor, factor)
        left = [(by_quad(x, y), by_quad(z, w)) for x, y, z, w in zip(second, before, (re, im), after)]
        c, s = first_angle(v)
        c2, s2 = 1.0 - 2.0 * s * s, 2.0 * s * c
        factor = 2.0 * c2
        right_factor = by_quad(factor, factor)
        right = [
            (by_quad(c2, c), by_quad(jnp.ones_like(c), c)),
            (by_quad(-s2, -s), by_quad(jnp.zeros_like(s), s)),
        ]
        return [
            [
                (left[0][0][q], left[0][1][q], left[1][0][q], left[1][1][q], left_factor[q]),
                (right[0][0][q], right[0][1][q], right[1][0][q], right[1][1][q], right_factor[q]),
            ]
            for q in range(2)
        ]

    def finish(seeds, quad_at):
        product = None
        for lanes in range(0, tiles * LANES, CHUNK):
            operands = []
            for side in seeds[::-1]:
                before, middle, before_imag, middle_imag, factor = [
                    x[:, lanes : lanes + CHUNK] for x in side
                ]
                operands.append(
                    jnp.concatenate(
                        sequence(before, middle, factor)
                        + sequence(before_imag, middle_imag, factor),
                        0,
                    )
                )
            term = lax.dot_general(
                operands[1], operands[0], (((1,), (1,)), ((), ())),
                preferred_element_type=jnp.float32,
            )
            product = term if product is None else product + term
        half = product.shape[0] // 2
        wholes = (
            product[:half, :LANES] - product[half:, LANES:],
            product[half:, :LANES] + product[:half, LANES:],
        )
        rows = []
        for whole in wholes:
            for j in range(0, STEPS, 4):
                four = [whole[(j + k) * GROUP : (j + k + 1) * GROUP] for k in range(4)]
                rows.append(jnp.concatenate([jnp.where(same_block, x, 0.0) for x in four], 1))
        index = jnp.clip(quad_at * QUAD, 0, last + 1 - QUAD)
        place = (plan_ref[listed + index] >> (TAG_BITS + 2)) - first * (capacity // QUAD)
        place = jnp.where((quad_at >= low) & (quad_at < high), place, spare)
        found[place] = jnp.concatenate(rows, 0).astype(jnp.bfloat16)
        tag = jnp.zeros((QUAD, LANES), jnp.int32)
        for b in range(QUAD):
            tag = jnp.where(quad_row == b, plan_ref[listed + index + b] & ((1 << TAG_BITS) - 1), tag)
        tags[place] = tag.astype(jnp.float32)

    def turn(g, seeds):
        quad_at = low + 2 * g
        for q in range(2):
            finish(seeds[q], quad_at + q)
        return angles(quad_at + 2)

    lax.fori_loop(0, (high - low + 1) // 2, turn, angles(low))

    shares = capacity // TAG_ROWS
    share = lax.broadcasted_iota(jnp.int32, (TAG_ROWS, LANES), 1) // (LANES // shares)

    def write_share(out_ref, base, slot, sent, n):
        rows = jnp.concatenate([found[slot + k] for k in range(4)], 0)
        moved = jnp.dot(rows, mover[...], preferred_element_type=jnp.float32)
        for piece in range(PIECES // 2):
            part = []
            for k in range(4):
                value = moved[(k * 8 + piece) * GROUP : (k * 8 + piece + 1) * GROUP]
                part.append(jnp.where(n * 4 + k < sent, value, 0.0))
            first_two, last_two = [], []
            for even, odd in (part[:2], part[2:]):
                first_two.append(jnp.where(top, even, pltpu.roll(odd, QUAD, 0)))
                last_two.append(jnp.where(top, pltpu.roll(even, QUAD, 0), odd))
            for parity, two in enumerate((first_two, last_two)):
                put = base + (piece * 2 + parity) * capacity + n * TAG_ROWS
                out_ref[pl.ds(put, TAG_ROWS), :] = jnp.concatenate(two, 0).astype(jnp.bfloat16)

    for d, out_ref in enumerate(out_refs):
        for m in range(out_ref.shape[0] // message_rows(capacity)):
            base = m * message_rows(capacity)
            sent = start_of(first + d + m + 1) - start_of(first + d + m)
            slot = (d + m) * (capacity // QUAD)
            tag = jnp.zeros((TAG_ROWS, LANES), jnp.float32)
            for n in range(shares):
                at = slot + n * 4
                four = jnp.concatenate([tags[at + k] for k in range(4)], 0)
                tag = jnp.where(share == n, four, tag)

                @pl.when(n * 4 < sent)
                def _():
                    write_share(out_ref, base, at, sent, n)

                @pl.when(n * 4 >= sent)
                def _():
                    for piece in range(PIECES):
                        put = base + piece * capacity + n * TAG_ROWS
                        out_ref[pl.ds(put, TAG_ROWS), :] = jnp.zeros((TAG_ROWS, LANES), jnp.bfloat16)

            out_ref[pl.ds(base + PIECES * capacity, TAG_ROWS), :] = tag.astype(jnp.bfloat16)


def message_rows(capacity):
    return PIECES * capacity + TAG_ROWS


def make_subgrids(first, outs, token, capacity, listed, plan, uv, res, vis):
    tiles = vis // LANES
    destinations = sum(outs)
    quads = destinations * capacity // QUAD
    vmem = pl.BlockSpec(memory_space=pltpu.VMEM)
    smem = pl.BlockSpec(memory_space=pltpu.SMEM)
    return pl.pallas_call(
        functools.partial(subgrid_kernel, first, destinations, capacity, listed),
        out_shape=[
            jax.ShapeDtypeStruct((n * message_rows(capacity), LANES), jnp.bfloat16) for n in outs
        ]
        + [jax.ShapeDtypeStruct(token.shape, token.dtype)],
        in_specs=[smem] + [vmem] * 3,
        out_specs=[vmem] * (len(outs) + 1),
        scratch_shapes=[
            pltpu.VMEM((4 * tiles * GROUP, LANES), jnp.float32),
            pltpu.VMEM((quads + 1, FEATURE // SUB, 4 * LANES), jnp.bfloat16),
            pltpu.VMEM((quads + 1, QUAD, LANES), jnp.float32),
            pltpu.VMEM((4 * LANES, LANES), jnp.bfloat16),
        ],
        compiler_params=pltpu.CompilerParams(vmem_limit_bytes=VMEM_LIMIT),
        cost_estimate=pl.CostEstimate(
            flops=quads * 32 * SUB * SUB * vis, bytes_accessed=16 * quads * FEATURE, transcendentals=0
        ),
        name="subgrids",
    )(plan, token, uv, res)


def pick_rows(hot, xs, part, out_ref, half):
    lane = lax.broadcasted_iota(jnp.int32, (GROUP, LANES), 1) >> 5
    for piece in range(PIECES):
        c, rows, parity = piece // 8, piece // 2 % 4 - 2 * half, piece % 2
        if not 0 <= rows < 2:
            continue
        part[...] = jnp.dot(hot[...], xs[piece], preferred_element_type=jnp.float32)
        for grp in range(4):
            given = [part[pl.ds(32 * jl + 8 * grp, 8), :] for jl in range(4)]
            for a in range(4):
                total = None
                for jl in range(4):
                    moved = given[jl]
                    if a != jl:
                        moved = pltpu.roll(moved, ((jl - a) % 4) * SUB, 1)
                    total = moved if total is None else jnp.where(lane == jl, moved, total)
                p = rows * 8 + a * 2 + parity
                out_ref[pl.ds(p * 64 + grp * 16 + c, 8, stride=2), :] = total


def first_half_kernel(capacity, *refs):
    x_refs, (out_ref, xs, hot, tags, part) = refs[:-5], refs[-5:]
    shares = capacity // TAG_ROWS
    at = 0
    for x_ref in x_refs:
        for base in range(0, x_ref.shape[0], message_rows(capacity)):
            for piece in range(PIECES):
                xs[piece, pl.ds(at, capacity), :] = x_ref[pl.ds(base + piece * capacity, capacity), :]
            tag = x_ref[pl.ds(base + PIECES * capacity, TAG_ROWS), :].astype(jnp.float32)
            for n in range(shares):
                column = n * (LANES // shares)
                tags[pl.ds(at + n * TAG_ROWS, TAG_ROWS), :] = jnp.broadcast_to(
                    tag[:, column : column + 1], (TAG_ROWS, LANES)
                )
            at += capacity
    wanted = lax.broadcasted_iota(jnp.int32, tags.shape, 1)
    wanted = ((wanted & 31) << 2) + (wanted >> 5) + 1
    hot[...] = jnp.where(tags[...] == wanted.astype(jnp.float32), 1.0, 0.0).T.astype(jnp.bfloat16)
    pick_rows(hot, xs, part, out_ref, 0)


def second_half_kernel(xs, hot, out_ref, part):
    pick_rows(hot, xs, part, out_ref, 1)


def sum_slots(arrived, capacity):
    rows = sum(x.shape[0] for x in arrived) // message_rows(capacity) * capacity
    vmem = pl.BlockSpec(memory_space=pltpu.VMEM)
    half = jax.ShapeDtypeStruct((SUB * 32, LANES), jnp.float32)
    params = pltpu.CompilerParams(vmem_limit_bytes=VMEM_LIMIT)
    part = pltpu.VMEM((SLOTS, LANES), jnp.float32)
    first, xs, hot = pl.pallas_call(
        functools.partial(first_half_kernel, capacity),
        out_shape=[
            half,
            jax.ShapeDtypeStruct((PIECES, rows, LANES), jnp.bfloat16),
            jax.ShapeDtypeStruct((SLOTS, rows), jnp.bfloat16),
        ],
        in_specs=[vmem] * len(arrived),
        out_specs=[vmem] * 3,
        scratch_shapes=[pltpu.VMEM((rows, LANES), jnp.float32), part],
        compiler_params=params,
        name="sum_first",
    )(*arrived)
    second = pl.pallas_call(
        second_half_kernel,
        out_shape=half,
        in_specs=[vmem] * 2,
        out_specs=vmem,
        scratch_shapes=[part],
        compiler_params=params,
        name="sum_second",
    )(xs, hot)
    return first, second


def add_kernel(at, mine_ref, theirs_ref, *refs):
    out_ref, total, sems = refs[-3:]
    step = total.shape[0] // sems.shape[0]
    copies = []
    for k in range(sems.shape[0]):
        here = pl.ds(k * step, step)
        total[here, :] = mine_ref[here, :] + theirs_ref[here, :]
        copy = pltpu.make_async_copy(
            total.at[here], out_ref.at[pl.ds(at + k * step, step)], sems.at[k]
        )
        copy.start()
        copies.append(copy)
    for copy in copies:
        copy.wait()


def add_half(at, mine, theirs, *whole):
    vmem, anywhere = pl.BlockSpec(memory_space=pltpu.VMEM), pl.BlockSpec(memory_space=pl.ANY)
    return pl.pallas_call(
        functools.partial(add_kernel, at),
        out_shape=jax.ShapeDtypeStruct((2 * mine.shape[0], LANES), jnp.float32),
        in_specs=[vmem, vmem] + [anywhere] * len(whole),
        out_specs=anywhere,
        scratch_shapes=[pltpu.VMEM(mine.shape, jnp.float32), pltpu.SemaphoreType.DMA((4,))],
        input_output_aliases={2: 0} if whole else {},
        compiler_params=pltpu.CompilerParams(vmem_limit_bytes=VMEM_LIMIT),
        name="add_half",
    )(mine, theirs, *whole)


def rows_of(array):
    blocks, parts, vis = array.shape
    tiles = vis // LANES
    split = array.reshape(blocks, parts, tiles, LANES)
    return split.transpose(0, 2, 1, 3).reshape(blocks * tiles * parts, LANES)


def sending_order(owners):
    return list(range(owners - 1, -1, -1))


def in_rows(array):
    return with_layout_constraint(array, Layout(major_to_minor=(0, 1)))


def local(residual, uv_offsets, counts, tile_of_block, slot_of_block, owner_map):
    blocks, _, vis = uv_offsets.shape
    owners = owner_map.shape[0]
    capacity = -(-max(CAP_MIN, 2 * blocks // owners) // 32) * 16
    core = lax.axis_index("samp")
    me = lax.axis_index(("blk", "tile"))
    swap = [(0, 1), (1, 0)]
    own = in_rows(rows_of(residual[0]))
    other = in_rows(lax.ppermute(own, "samp", swap))

    lists = jnp.concatenate([tile_of_block[:, 0], slot_of_block, counts, owner_map])
    lists = lax.optimization_barrier(lists)
    tile_ids, slots, counts, owner_map = [
        lists[k * blocks : min((k + 1) * blocks, 3 * blocks + owners)] for k in range(4)
    ]
    owner_range = jnp.arange(owners, dtype=jnp.int32)
    owner_ids = jnp.sum(
        jnp.where(tile_ids[:, None] == owner_range[None, :], owner_map[None, :], 0), 1
    )
    paired = owners <= PAIRED_MAX and owners & (owners - 1) == 0
    distances = sending_order(owners)
    offset = owner_ids
    if paired:
        offset = jnp.bitwise_xor(owner_ids, me)
        offset = sum(jnp.where(offset == d, k, 0) for k, d in enumerate(distances) if k)
    index = jnp.arange(blocks, dtype=jnp.int32)
    same = (offset[None, :] == offset[:, None]) & (index[None, :] < index[:, None])
    rank = jnp.sum(same.astype(jnp.int32), 1)
    mine = (rank & 1) == core
    counted = jnp.sum((mine[None, :] & (offset[None, :] == owner_range[:, None])).astype(jnp.int32), 1)
    quads = (counted + QUAD - 1) >> 2
    edges = jnp.arange(owners + 1, dtype=jnp.int32)
    start = jnp.sum(jnp.where(owner_range[None, :] < edges[:, None], quads[None, :], 0), 1)
    before = jnp.sum(jnp.where(owner_range[None, :] < offset[:, None], quads[None, :], 0), 1)
    place = jnp.where(mine, before * QUAD + (rank >> 1), -1)
    longest = ((blocks + owners) // 2 + owners * (QUAD - 1)) // GROUP * GROUP + GROUP
    wanted = jnp.arange(longest, dtype=jnp.int32)
    chosen = place[None, :] == wanted[:, None]
    block_and_count = (index << COUNT_BITS) + counts
    row_and_tag = ((offset * capacity + (rank >> 1)) << TAG_BITS) + slots + 1
    block = jnp.sum(jnp.where(chosen, block_and_count[None, :], 0), 1)
    row = jnp.sum(jnp.where(chosen, row_and_tag[None, :], 0), 1)

    subgrids = functools.partial(
        make_subgrids, capacity=capacity, listed=longest, plan=jnp.concatenate([block, row, start]), uv=rows_of(uv_offsets),
        res=own.astype(jnp.float32) + other.astype(jnp.float32), vis=vis,
    )
    token = jnp.zeros((GROUP, LANES), jnp.int32)
    if paired:
        rows = []
        for first, last in zip(CALLS[:-1], CALLS[1:]):
            first, last = owners * first // CALLS[-1], owners * last // CALLS[-1]
            if first < last:
                *more, token = subgrids(first, (1,) * (last - first), token)
                rows += more
        arrived = []
        for distance, piece in zip(distances, rows):
            if distance:
                pairs = [(k, k ^ distance) for k in range(owners)]
                piece = lax.ppermute(piece, ("blk", "tile"), pairs)
            arrived.append(piece)
    else:
        each = max(d for d in range(1, 17) if owners % d == 0)
        rows = [subgrids(k, (each,), token)[0] for k in range(0, owners, each)]
        rows = jnp.concatenate(rows, 0).reshape(owners, message_rows(capacity), LANES)
        rows = lax.all_to_all(rows, ("blk", "tile"), split_axis=0, concat_axis=0, tiled=True)
        arrived = [rows.reshape(owners * message_rows(capacity), LANES)]
    first, second = sum_slots(arrived, capacity)
    whole = add_half(0, first, lax.ppermute(first, "samp", swap))
    whole = add_half(first.shape[0], second, lax.ppermute(second, "samp", swap), whole)
    whole = whole.reshape(SUB, SLOTS // 4, 2, LANES).transpose(0, 2, 1, 3)
    return whole.reshape(SUB, 2, SLOTS * SUB)


def solution(mesh):
    in_specs = (
        P("samp", ("cuts", "blk", "tile"), None, None),
        P(("cuts", "blk", "tile"), None, None),
        P(("cuts", "blk", "tile")),
        P(("cuts", "blk", "tile"), None),
        P(("cuts", "blk", "tile")),
        P(),
    )
    out_specs = P(("cuts", "blk", "tile"), None, None)
    return jax.shard_map(local, mesh=mesh, in_specs=in_specs, out_specs=out_specs, check_vma=False)
```

```python
import functools

import jax
import jax.numpy as jnp
import numpy as np
from jax import lax
from jax.experimental import pallas as pl
from jax.experimental.layout import Layout, with_layout_constraint
from jax.experimental.pallas import tpu as pltpu
from jax.sharding import PartitionSpec as P

SUB = 32
STEPS = SUB // 2
SLOTS = 128
LANES = 128
FEATURE = 2 * SUB * SUB
PIECES = FEATURE // LANES
CAP_MIN = 8
GROUP = 8
QUAD = 4
TAG_ROWS = 16
COUNT_BITS = 12
TAG_BITS = 8
CHUNK = 4 * LANES
PAIRED_MAX = 16
CALLS = (0, 2, 5, 7, 8)
VMEM_LIMIT = 48 * 1024 * 1024


def turn_coefficients():
    knots = np.cos(np.pi * (np.arange(400) + 0.5) / 400)
    cheb = np.polynomial.chebyshev
    even = cheb.cheb2poly(cheb.chebfit(knots, np.cos(np.pi * knots), 12))[0::2]
    odd = cheb.cheb2poly(cheb.chebfit(knots, np.sin(np.pi * knots), 13))[1::2]
    return [float(x) for x in even], [float(x) for x in odd]


COS_COEF, SIN_COEF = turn_coefficients()


def horner(coef, x):
    total = coef[-1] * x + coef[-2]
    for value in coef[-3::-1]:
        total = total * x + value
    return total


def first_angle(offset):
    y = offset * (1.0 / STEPS)
    x = y * y
    return horner(COS_COEF, x), horner(SIN_COEF, x) * y


def tile_of(value, t):
    return value[:, t * LANES : (t + 1) * LANES]


def by_quad(even, odd):
    top = lax.broadcasted_iota(jnp.int32, even.shape, 0) < QUAD
    return (
        jnp.where(top, even, pltpu.roll(odd, QUAD, 0)),
        jnp.where(top, pltpu.roll(even, QUAD, 0), odd),
    )


def sequence(before, middle, factor):
    def pair(*two):
        return jnp.concatenate(two, 0).astype(jnp.bfloat16)

    up, down = [], []
    last, value = before, middle
    for _ in range(STEPS // 4):
        after = factor * value - last
        up.append(pair(value, after))
        last, value = after, factor * after - value
    last, value = middle, before
    for _ in range(STEPS // 4):
        after = factor * value - last
        down.append(pair(after, value))
        last, value = after, factor * after - value
    return down[::-1] + up


def subgrid_kernel(
    first, destinations, capacity, listed, plan_ref, token_ref, uv_ref, res_ref, *refs
):
    out_refs, (next_ref, gathered, found, tags, mover) = refs[:-5], refs[-5:]
    next_ref[...] = jnp.zeros_like(next_ref)
    tiles = gathered.shape[0] // (4 * GROUP)
    spare = destinations * capacity // QUAD

    def start_of(destination):
        return plan_ref[2 * listed + destination]

    low, high = start_of(first), start_of(first + destinations)
    last = listed - 1
    vis_at = lax.broadcasted_iota(jnp.int32, (2 * tiles, LANES), 1) + LANES * (
        lax.broadcasted_iota(jnp.int32, (2 * tiles, LANES), 0) >> 1
    )
    same_block = (
        lax.broadcasted_iota(jnp.int32, (GROUP, LANES), 0) & (QUAD - 1)
        == lax.broadcasted_iota(jnp.int32, (GROUP, LANES), 1) & (QUAD - 1)
    )
    quad_row = lax.broadcasted_iota(jnp.int32, (QUAD, LANES), 0)
    top = lax.broadcasted_iota(jnp.int32, (GROUP, LANES), 0) < QUAD

    source = lax.broadcasted_iota(jnp.int32, mover.shape, 0)
    lane = lax.broadcasted_iota(jnp.int32, mover.shape, 1)
    moves = (source >> 7 == lane >> 5) & ((source & (LANES - 1)) >> 2 == lane & (SUB - 1))
    mover[...] = jnp.where(moves, 1.0, 0.0).astype(jnp.bfloat16)
    tags[...] = jnp.zeros_like(tags)

    def angles(quad_at):
        for i in range(GROUP):
            packed = plan_ref[jnp.minimum(quad_at * QUAD + i, last)]
            block, count = packed >> COUNT_BITS, packed & ((1 << COUNT_BITS) - 1)
            at = pl.ds(pl.multiple_of(block * 2 * tiles, 2 * tiles), 2 * tiles)
            both = jnp.where(vis_at < count, res_ref[at, :], 0.0)
            gathered[pl.ds(i, 2 * tiles, stride=GROUP), :] = uv_ref[at, :]
            gathered[pl.ds(2 * tiles * GROUP + i, 2 * tiles, stride=GROUP), :] = both
        u, v, re, im = [
            jnp.concatenate(
                [
                    gathered[pl.ds(((k // 2) * 2 * tiles + 2 * t + k % 2) * GROUP, GROUP), :]
                    for t in range(tiles)
                ],
                1,
            )
            for k in range(4)
        ]
        c, s = first_angle(u)
        a, b, e, f = re * c, im * s, im * c, re * s
        after = (a - b, e + f)
        before = (a + b, e - f)
        second = [2.0 * c * near - far for near, far in zip(before, (re, im))]
        factor = 2.0 - 4.0 * s * s
        left_factor = by_quad(factor, factor)
        left = [(by_quad(x, y), by_quad(z, w)) for x, y, z, w in zip(second, before, (re, im), after)]
        c, s = first_angle(v)
        c2, s2 = 1.0 - 2.0 * s * s, 2.0 * s * c
        factor = 2.0 * c2
        right_factor = by_quad(factor, factor)
        right = [
            (by_quad(c2, c), by_quad(jnp.ones_like(c), c)),
            (by_quad(-s2, -s), by_quad(jnp.zeros_like(s), s)),
        ]
        return [
            [
                (left[0][0][q], left[0][1][q], left[1][0][q], left[1][1][q], left_factor[q]),
                (right[0][0][q], right[0][1][q], right[1][0][q], right[1][1][q], right_factor[q]),
            ]
            for q in range(2)
        ]

    def finish(seeds, quad_at):
        product = None
        for lanes in range(0, tiles * LANES, CHUNK):
            operands = []
            for side in seeds[::-1]:
                before, middle, before_imag, middle_imag, factor = [
                    x[:, lanes : lanes + CHUNK] for x in side
                ]
                operands.append(
                    jnp.concatenate(
                        sequence(before, middle, factor)
                        + sequence(before_imag, middle_imag, factor),
                        0,
                    )
                )
            term = lax.dot_general(
                operands[1], operands[0], (((1,), (1,)), ((), ())),
                preferred_element_type=jnp.float32,
            )
            product = term if product is None else product + term
        half = product.shape[0] // 2
        wholes = (
            product[:half, :LANES] - product[half:, LANES:],
            product[half:, :LANES] + product[:half, LANES:],
        )
        rows = []
        for whole in wholes:
            for j in range(0, STEPS, 4):
                four = [whole[(j + k) * GROUP : (j + k + 1) * GROUP] for k in range(4)]
                rows.append(jnp.concatenate([jnp.where(same_block, x, 0.0) for x in four], 1))
        index = jnp.clip(quad_at * QUAD, 0, last + 1 - QUAD)
        place = (plan_ref[listed + index] >> (TAG_BITS + 2)) - first * (capacity // QUAD)
        place = jnp.where((quad_at >= low) & (quad_at < high), place, spare)
        found[place] = jnp.concatenate(rows, 0).astype(jnp.bfloat16)
        tag = jnp.zeros((QUAD, LANES), jnp.int32)
        for b in range(QUAD):
            tag = jnp.where(quad_row == b, plan_ref[listed + index + b] & ((1 << TAG_BITS) - 1), tag)
        tags[place] = tag.astype(jnp.float32)

    def turn(g, seeds):
        quad_at = low + 2 * g
        for q in range(2):
            finish(seeds[q], quad_at + q)
        return angles(quad_at + 2)

    lax.fori_loop(0, (high - low + 1) // 2, turn, angles(low))

    shares = capacity // TAG_ROWS
    share = lax.broadcasted_iota(jnp.int32, (TAG_ROWS, LANES), 1) // (LANES // shares)

    def write_share(out_ref, base, slot, sent, n):
        rows = jnp.concatenate([found[slot + k] for k in range(4)], 0)
        moved = jnp.dot(rows, mover[...], preferred_element_type=jnp.float32)
        for piece in range(PIECES // 2):
            part = []
            for k in range(4):
                value = moved[(k * 8 + piece) * GROUP : (k * 8 + piece + 1) * GROUP]
                part.append(jnp.where(n * 4 + k < sent, value, 0.0))
            first_two, last_two = [], []
            for even, odd in (part[:2], part[2:]):
                first_two.append(jnp.where(top, even, pltpu.roll(odd, QUAD, 0)))
                last_two.append(jnp.where(top, pltpu.roll(even, QUAD, 0), odd))
            for parity, two in enumerate((first_two, last_two)):
                put = base + (piece * 2 + parity) * capacity + n * TAG_ROWS
                out_ref[pl.ds(put, TAG_ROWS), :] = jnp.concatenate(two, 0).astype(jnp.bfloat16)

    for d, out_ref in enumerate(out_refs):
        for m in range(out_ref.shape[0] // message_rows(capacity)):
            base = m * message_rows(capacity)
            sent = start_of(first + d + m + 1) - start_of(first + d + m)
            slot = (d + m) * (capacity // QUAD)
            tag = jnp.zeros((TAG_ROWS, LANES), jnp.float32)
            for n in range(shares):
                at = slot + n * 4
                four = jnp.concatenate([tags[at + k] for k in range(4)], 0)
                tag = jnp.where(share == n, four, tag)

                @pl.when(n * 4 < sent)
                def _():
                    write_share(out_ref, base, at, sent, n)

                @pl.when(n * 4 >= sent)
                def _():
                    for piece in range(PIECES):
                        put = base + piece * capacity + n * TAG_ROWS
                        out_ref[pl.ds(put, TAG_ROWS), :] = jnp.zeros((TAG_ROWS, LANES), jnp.bfloat16)

            out_ref[pl.ds(base + PIECES * capacity, TAG_ROWS), :] = tag.astype(jnp.bfloat16)


def message_rows(capacity):
    return PIECES * capacity + TAG_ROWS


def make_subgrids(first, outs, token, capacity, listed, plan, uv, res, vis):
    tiles = vis // LANES
    destinations = sum(outs)
    quads = destinations * capacity // QUAD
    vmem = pl.BlockSpec(memory_space=pltpu.VMEM)
    smem = pl.BlockSpec(memory_space=pltpu.SMEM)
    return pl.pallas_call(
        functools.partial(subgrid_kernel, first, destinations, capacity, listed),
        out_shape=[
            jax.ShapeDtypeStruct((n * message_rows(capacity), LANES), jnp.bfloat16) for n in outs
        ]
        + [jax.ShapeDtypeStruct(token.shape, token.dtype)],
        in_specs=[smem] + [vmem] * 3,
        out_specs=[vmem] * (len(outs) + 1),
        scratch_shapes=[
            pltpu.VMEM((4 * tiles * GROUP, LANES), jnp.float32),
            pltpu.VMEM((quads + 1, FEATURE // SUB, 4 * LANES), jnp.bfloat16),
            pltpu.VMEM((quads + 1, QUAD, LANES), jnp.float32),
            pltpu.VMEM((4 * LANES, LANES), jnp.bfloat16),
        ],
        compiler_params=pltpu.CompilerParams(vmem_limit_bytes=VMEM_LIMIT),
        cost_estimate=pl.CostEstimate(
            flops=quads * 32 * SUB * SUB * vis, bytes_accessed=16 * quads * FEATURE, transcendentals=0
        ),
        name="subgrids",
    )(plan, token, uv, res)


def pick_rows(hot, xs, part, out_ref, half):
    lane = lax.broadcasted_iota(jnp.int32, (GROUP, LANES), 1) >> 5
    for piece in range(PIECES):
        c, rows, parity = piece // 8, piece // 2 % 4 - 2 * half, piece % 2
        if not 0 <= rows < 2:
            continue
        part[...] = jnp.dot(hot[...], xs[piece], preferred_element_type=jnp.float32)
        for grp in range(4):
            given = [part[pl.ds(32 * jl + 8 * grp, 8), :] for jl in range(4)]
            for a in range(4):
                total = None
                for jl in range(4):
                    moved = given[jl]
                    if a != jl:
                        moved = pltpu.roll(moved, ((jl - a) % 4) * SUB, 1)
                    total = moved if total is None else jnp.where(lane == jl, moved, total)
                p = rows * 8 + a * 2 + parity
                out_ref[pl.ds(p * 64 + grp * 16 + c, 8, stride=2), :] = total


def first_half_kernel(capacity, *refs):
    x_refs, (out_ref, xs, hot, tags, part) = refs[:-5], refs[-5:]
    shares = capacity // TAG_ROWS
    at = 0
    for x_ref in x_refs:
        for base in range(0, x_ref.shape[0], message_rows(capacity)):
            for piece in range(PIECES):
                xs[piece, pl.ds(at, capacity), :] = x_ref[pl.ds(base + piece * capacity, capacity), :]
            tag = x_ref[pl.ds(base + PIECES * capacity, TAG_ROWS), :].astype(jnp.float32)
            for n in range(shares):
                column = n * (LANES // shares)
                tags[pl.ds(at + n * TAG_ROWS, TAG_ROWS), :] = jnp.broadcast_to(
                    tag[:, column : column + 1], (TAG_ROWS, LANES)
                )
            at += capacity
    wanted = lax.broadcasted_iota(jnp.int32, tags.shape, 1)
    wanted = ((wanted & 31) << 2) + (wanted >> 5) + 1
    hot[...] = jnp.where(tags[...] == wanted.astype(jnp.float32), 1.0, 0.0).T.astype(jnp.bfloat16)
    pick_rows(hot, xs, part, out_ref, 0)


def second_half_kernel(xs, hot, out_ref, part):
    pick_rows(hot, xs, part, out_ref, 1)


def sum_slots(arrived, capacity):
    rows = sum(x.shape[0] for x in arrived) // message_rows(capacity) * capacity
    vmem = pl.BlockSpec(memory_space=pltpu.VMEM)
    half = jax.ShapeDtypeStruct((SUB * 32, LANES), jnp.float32)
    params = pltpu.CompilerParams(vmem_limit_bytes=VMEM_LIMIT)
    part = pltpu.VMEM((SLOTS, LANES), jnp.float32)
    first, xs, hot = pl.pallas_call(
        functools.partial(first_half_kernel, capacity),
        out_shape=[
            half,
            jax.ShapeDtypeStruct((PIECES, rows, LANES), jnp.bfloat16),
            jax.ShapeDtypeStruct((SLOTS, rows), jnp.bfloat16),
        ],
        in_specs=[vmem] * len(arrived),
        out_specs=[vmem] * 3,
        scratch_shapes=[pltpu.VMEM((rows, LANES), jnp.float32), part],
        compiler_params=params,
        name="sum_first",
    )(*arrived)
    second = pl.pallas_call(
        second_half_kernel,
        out_shape=half,
        in_specs=[vmem] * 2,
        out_specs=vmem,
        scratch_shapes=[part],
        compiler_params=params,
        name="sum_second",
    )(xs, hot)
    return first, second


def add_kernel(at, mine_ref, theirs_ref, *refs):
    out_ref, total, sems = refs[-3:]
    step = total.shape[0] // sems.shape[0]
    copies = []
    for k in range(sems.shape[0]):
        here = pl.ds(k * step, step)
        total[here, :] = mine_ref[here, :] + theirs_ref[here, :]
        copy = pltpu.make_async_copy(
            total.at[here], out_ref.at[pl.ds(at + k * step, step)], sems.at[k]
        )
        copy.start()
        copies.append(copy)
    for copy in copies:
        copy.wait()


def add_half(at, mine, theirs, *whole):
    vmem, anywhere = pl.BlockSpec(memory_space=pltpu.VMEM), pl.BlockSpec(memory_space=pl.ANY)
    return pl.pallas_call(
        functools.partial(add_kernel, at),
        out_shape=jax.ShapeDtypeStruct((2 * mine.shape[0], LANES), jnp.float32),
        in_specs=[vmem, vmem] + [anywhere] * len(whole),
        out_specs=anywhere,
        scratch_shapes=[pltpu.VMEM(mine.shape, jnp.float32), pltpu.SemaphoreType.DMA((4,))],
        input_output_aliases={2: 0} if whole else {},
        compiler_params=pltpu.CompilerParams(vmem_limit_bytes=VMEM_LIMIT),
        name="add_half",
    )(mine, theirs, *whole)


def rows_of(array):
    blocks, parts, vis = array.shape
    tiles = vis // LANES
    split = array.reshape(blocks, parts, tiles, LANES)
    return split.transpose(0, 2, 1, 3).reshape(blocks * tiles * parts, LANES)


def sending_order(owners):
    across, near = list(range(max(owners // 2, 1), owners)), list(range(1, owners // 2))
    order = [across.pop() for _ in range(owners // 4)]
    while across or near:
        order += [group.pop() for group in (across, near) if group]
    return order + [0]


def in_rows(array):
    return with_layout_constraint(array, Layout(major_to_minor=(0, 1)))


def local(residual, uv_offsets, counts, tile_of_block, slot_of_block, owner_map):
    blocks, _, vis = uv_offsets.shape
    owners = owner_map.shape[0]
    capacity = -(-max(CAP_MIN, 2 * blocks // owners) // 32) * 16
    core = lax.axis_index("samp")
    me = lax.axis_index(("blk", "tile"))
    swap = [(0, 1), (1, 0)]
    own = in_rows(rows_of(residual[0]))
    other = in_rows(lax.ppermute(own, "samp", swap))

    lists = jnp.concatenate([tile_of_block[:, 0], slot_of_block, counts, owner_map])
    lists = lax.optimization_barrier(lists)
    tile_ids, slots, counts, owner_map = [
        lists[k * blocks : min((k + 1) * blocks, 3 * blocks + owners)] for k in range(4)
    ]
    owner_range = jnp.arange(owners, dtype=jnp.int32)
    owner_ids = jnp.sum(
        jnp.where(tile_ids[:, None] == owner_range[None, :], owner_map[None, :], 0), 1
    )
    paired = owners <= PAIRED_MAX and owners & (owners - 1) == 0
    distances = sending_order(owners)
    offset = owner_ids
    if paired:
        offset = jnp.bitwise_xor(owner_ids, me)
        offset = sum(jnp.where(offset == d, k, 0) for k, d in enumerate(distances) if k)
    index = jnp.arange(blocks, dtype=jnp.int32)
    same = (offset[None, :] == offset[:, None]) & (index[None, :] < index[:, None])
    rank = jnp.sum(same.astype(jnp.int32), 1)
    mine = (rank & 1) == core
    counted = jnp.sum((mine[None, :] & (offset[None, :] == owner_range[:, None])).astype(jnp.int32), 1)
    quads = (counted + QUAD - 1) >> 2
    edges = jnp.arange(owners + 1, dtype=jnp.int32)
    start = jnp.sum(jnp.where(owner_range[None, :] < edges[:, None], quads[None, :], 0), 1)
    before = jnp.sum(jnp.where(owner_range[None, :] < offset[:, None], quads[None, :], 0), 1)
    place = jnp.where(mine, before * QUAD + (rank >> 1), -1)
    longest = ((blocks + owners) // 2 + owners * (QUAD - 1)) // GROUP * GROUP + GROUP
    wanted = jnp.arange(longest, dtype=jnp.int32)
    chosen = place[None, :] == wanted[:, None]
    block_and_count = (index << COUNT_BITS) + counts
    row_and_tag = ((offset * capacity + (rank >> 1)) << TAG_BITS) + slots + 1
    block = jnp.sum(jnp.where(chosen, block_and_count[None, :], 0), 1)
    row = jnp.sum(jnp.where(chosen, row_and_tag[None, :], 0), 1)

    subgrids = functools.partial(
        make_subgrids, capacity=capacity, listed=longest, plan=jnp.concatenate([block, row, start]), uv=rows_of(uv_offsets),
        res=own.astype(jnp.float32) + other.astype(jnp.float32), vis=vis,
    )
    token = jnp.zeros((GROUP, LANES), jnp.int32)
    if paired:
        rows = []
        for first, last in zip(CALLS[:-1], CALLS[1:]):
            first, last = owners * first // CALLS[-1], owners * last // CALLS[-1]
            if first < last:
                *more, token = subgrids(first, (1,) * (last - first), token)
                rows += more
        arrived = []
        for distance, piece in zip(distances, rows):
            if distance:
                pairs = [(k, k ^ distance) for k in range(owners)]
                piece = lax.ppermute(piece, ("blk", "tile"), pairs)
            arrived.append(piece)
    else:
        each = max(d for d in range(1, 17) if owners % d == 0)
        rows = [subgrids(k, (each,), token)[0] for k in range(0, owners, each)]
        rows = jnp.concatenate(rows, 0).reshape(owners, message_rows(capacity), LANES)
        rows = lax.all_to_all(rows, ("blk", "tile"), split_axis=0, concat_axis=0, tiled=True)
        arrived = [rows.reshape(owners * message_rows(capacity), LANES)]
    first, second = sum_slots(arrived, capacity)
    whole = add_half(0, first, lax.ppermute(first, "samp", swap))
    whole = add_half(first.shape[0], second, lax.ppermute(second, "samp", swap), whole)
    whole = whole.reshape(SUB, SLOTS // 4, 2, LANES).transpose(0, 2, 1, 3)
    return whole.reshape(SUB, 2, SLOTS * SUB)


def solution(mesh):
    in_specs = (
        P("samp", ("cuts", "blk", "tile"), None, None),
        P(("cuts", "blk", "tile"), None, None),
        P(("cuts", "blk", "tile")),
        P(("cuts", "blk", "tile"), None),
        P(("cuts", "blk", "tile")),
        P(),
    )
    out_specs = P(("cuts", "blk", "tile"), None, None)
    return jax.shard_map(local, mesh=mesh, in_specs=in_specs, out_specs=out_specs, check_vma=False)
```

```python
import functools

import jax
import jax.numpy as jnp
import numpy as np
from jax import lax
from jax.experimental import pallas as pl
from jax.experimental.layout import Layout, with_layout_constraint
from jax.experimental.pallas import tpu as pltpu
from jax.sharding import PartitionSpec as P

SUB = 32
STEPS = SUB // 2
SLOTS = 128
LANES = 128
FEATURE = 2 * SUB * SUB
PIECES = FEATURE // LANES
CAP_MIN = 8
GROUP = 8
QUAD = 4
TAG_ROWS = 16
COUNT_BITS = 12
TAG_BITS = 8
CHUNK = 4 * LANES
PAIRED_MAX = 16
CALLS = (0, 2, 4, 8)
VMEM_LIMIT = 48 * 1024 * 1024


def turn_coefficients():
    knots = np.cos(np.pi * (np.arange(400) + 0.5) / 400)
    cheb = np.polynomial.chebyshev
    even = cheb.cheb2poly(cheb.chebfit(knots, np.cos(np.pi * knots), 12))[0::2]
    odd = cheb.cheb2poly(cheb.chebfit(knots, np.sin(np.pi * knots), 13))[1::2]
    return [float(x) for x in even], [float(x) for x in odd]


COS_COEF, SIN_COEF = turn_coefficients()


def horner(coef, x):
    total = coef[-1] * x + coef[-2]
    for value in coef[-3::-1]:
        total = total * x + value
    return total


def first_angle(offset):
    y = offset * (1.0 / STEPS)
    x = y * y
    return horner(COS_COEF, x), horner(SIN_COEF, x) * y


def tile_of(value, t):
    return value[:, t * LANES : (t + 1) * LANES]


def by_quad(even, odd):
    top = lax.broadcasted_iota(jnp.int32, even.shape, 0) < QUAD
    return (
        jnp.where(top, even, pltpu.roll(odd, QUAD, 0)),
        jnp.where(top, pltpu.roll(even, QUAD, 0), odd),
    )


def sequence(before, middle, factor):
    def pair(*two):
        return jnp.concatenate(two, 0).astype(jnp.bfloat16)

    up, down = [], []
    last, value = before, middle
    for _ in range(STEPS // 4):
        after = factor * value - last
        up.append(pair(value, after))
        last, value = after, factor * after - value
    last, value = middle, before
    for _ in range(STEPS // 4):
        after = factor * value - last
        down.append(pair(after, value))
        last, value = after, factor * after - value
    return down[::-1] + up


def subgrid_kernel(
    first, destinations, capacity, listed, plan_ref, token_ref, uv_ref, res_ref, *refs
):
    out_refs, (next_ref, gathered, recent, found, tags, mover) = refs[:-6], refs[-6:]
    next_ref[...] = jnp.zeros_like(next_ref)
    tiles = gathered.shape[0] // (4 * GROUP)
    spare = destinations * capacity // QUAD

    def start_of(destination):
        return plan_ref[2 * listed + destination]

    low, high = start_of(first), start_of(first + destinations)
    last = listed - 1
    vis_at = lax.broadcasted_iota(jnp.int32, (2 * tiles, LANES), 1) + LANES * (
        lax.broadcasted_iota(jnp.int32, (2 * tiles, LANES), 0) >> 1
    )
    same_block = (
        lax.broadcasted_iota(jnp.int32, (GROUP, LANES), 0) & (QUAD - 1)
        == lax.broadcasted_iota(jnp.int32, (GROUP, LANES), 1) & (QUAD - 1)
    )
    quad_row = lax.broadcasted_iota(jnp.int32, (QUAD, LANES), 0)
    top = lax.broadcasted_iota(jnp.int32, (GROUP, LANES), 0) < QUAD

    source = lax.broadcasted_iota(jnp.int32, mover.shape, 0)
    lane = lax.broadcasted_iota(jnp.int32, mover.shape, 1)
    moves = (source >> 7 == lane >> 5) & ((source & (LANES - 1)) >> 2 == lane & (SUB - 1))
    mover[...] = jnp.where(moves, 1.0, 0.0).astype(jnp.bfloat16)
    tags[...] = jnp.zeros_like(tags)

    def angles(quad_at):
        for i in range(GROUP):
            packed = plan_ref[jnp.minimum(quad_at * QUAD + i, last)]
            block, count = packed >> COUNT_BITS, packed & ((1 << COUNT_BITS) - 1)
            at = pl.ds(pl.multiple_of(block * 2 * tiles, 2 * tiles), 2 * tiles)
            both = jnp.where(vis_at < count, res_ref[at, :], 0.0)
            gathered[pl.ds(i, 2 * tiles, stride=GROUP), :] = uv_ref[at, :]
            gathered[pl.ds(2 * tiles * GROUP + i, 2 * tiles, stride=GROUP), :] = both
        u, v, re, im = [
            jnp.concatenate(
                [
                    gathered[pl.ds(((k // 2) * 2 * tiles + 2 * t + k % 2) * GROUP, GROUP), :]
                    for t in range(tiles)
                ],
                1,
            )
            for k in range(4)
        ]
        c, s = first_angle(u)
        a, b, e, f = re * c, im * s, im * c, re * s
        after = (a - b, e + f)
        before = (a + b, e - f)
        second = [2.0 * c * near - far for near, far in zip(before, (re, im))]
        factor = 2.0 - 4.0 * s * s
        left_factor = by_quad(factor, factor)
        left = [(by_quad(x, y), by_quad(z, w)) for x, y, z, w in zip(second, before, (re, im), after)]
        c, s = first_angle(v)
        c2, s2 = 1.0 - 2.0 * s * s, 2.0 * s * c
        factor = 2.0 * c2
        right_factor = by_quad(factor, factor)
        right = [
            (by_quad(c2, c), by_quad(jnp.ones_like(c), c)),
            (by_quad(-s2, -s), by_quad(jnp.zeros_like(s), s)),
        ]
        return [
            [
                (left[0][0][q], left[0][1][q], left[1][0][q], left[1][1][q], left_factor[q]),
                (right[0][0][q], right[0][1][q], right[1][0][q], right[1][1][q], right_factor[q]),
            ]
            for q in range(2)
        ]

    def place_of(quad_at):
        index = jnp.clip(quad_at * QUAD, 0, last + 1 - QUAD)
        place = (plan_ref[listed + index] >> (TAG_BITS + 2)) - first * (capacity // QUAD)
        return index, jnp.where((quad_at >= low) & (quad_at < high), place, spare)

    def settle(quad_at):
        moved = jnp.dot(recent[...], mover[...], preferred_element_type=jnp.float32)
        for q in range(2):
            _, place = place_of(quad_at + q)
            found[place] = moved[q * found.shape[1] : (q + 1) * found.shape[1]]

    def finish(seeds, quad_at, q):
        product = None
        for lanes in range(0, tiles * LANES, CHUNK):
            operands = []
            for side in seeds[::-1]:
                before, middle, before_imag, middle_imag, factor = [
                    x[:, lanes : lanes + CHUNK] for x in side
                ]
                operands.append(
                    jnp.concatenate(
                        sequence(before, middle, factor)
                        + sequence(before_imag, middle_imag, factor),
                        0,
                    )
                )
            term = lax.dot_general(
                operands[1], operands[0], (((1,), (1,)), ((), ())),
                preferred_element_type=jnp.float32,
            )
            product = term if product is None else product + term
        half = product.shape[0] // 2
        wholes = (
            product[:half, :LANES] - product[half:, LANES:],
            product[half:, :LANES] + product[:half, LANES:],
        )
        rows = []
        for whole in wholes:
            for j in range(0, STEPS, 4):
                four = [whole[(j + k) * GROUP : (j + k + 1) * GROUP] for k in range(4)]
                rows.append(jnp.concatenate([jnp.where(same_block, x, 0.0) for x in four], 1))
        size = found.shape[1]
        recent[pl.ds(q * size, size), :] = jnp.concatenate(rows, 0).astype(jnp.bfloat16)
        index, place = place_of(quad_at)
        tag = jnp.zeros((QUAD, LANES), jnp.int32)
        for b in range(QUAD):
            tag = jnp.where(quad_row == b, plan_ref[listed + index + b] & ((1 << TAG_BITS) - 1), tag)
        tags[place] = tag.astype(jnp.float32)

    def turn(g, seeds):
        quad_at = low + 2 * g
        settle(quad_at - 2)
        for q in range(2):
            finish(seeds[q], quad_at + q, q)
        return angles(quad_at + 2)

    turns = (high - low + 1) >> 1
    lax.fori_loop(0, turns, turn, angles(low))
    settle(low + 2 * turns - 2)

    shares = capacity // TAG_ROWS
    share = lax.broadcasted_iota(jnp.int32, (TAG_ROWS, LANES), 1) // (LANES // shares)

    def write_share(out_ref, base, slot, sent, n):
        for piece in range(PIECES // 2):
            part = []
            for k in range(4):
                value = found[slot + k, pl.ds(piece * GROUP, GROUP), :]
                part.append(jnp.where(n * 4 + k < sent, value, 0.0))
            first_two, last_two = [], []
            for even, odd in (part[:2], part[2:]):
                first_two.append(jnp.where(top, even, pltpu.roll(odd, QUAD, 0)))
                last_two.append(jnp.where(top, pltpu.roll(even, QUAD, 0), odd))
            for parity, two in enumerate((first_two, last_two)):
                put = base + (piece * 2 + parity) * capacity + n * TAG_ROWS
                out_ref[pl.ds(put, TAG_ROWS), :] = jnp.concatenate(two, 0).astype(jnp.bfloat16)

    for d, out_ref in enumerate(out_refs):
        for m in range(out_ref.shape[0] // message_rows(capacity)):
            base = m * message_rows(capacity)
            sent = start_of(first + d + m + 1) - start_of(first + d + m)
            slot = (d + m) * (capacity // QUAD)
            tag = jnp.zeros((TAG_ROWS, LANES), jnp.float32)
            for n in range(shares):
                at = slot + n * 4
                four = jnp.concatenate([tags[at + k] for k in range(4)], 0)
                tag = jnp.where(share == n, four, tag)
                write_share(out_ref, base, at, sent, n)
            out_ref[pl.ds(base + PIECES * capacity, TAG_ROWS), :] = tag.astype(jnp.bfloat16)


def message_rows(capacity):
    return PIECES * capacity + TAG_ROWS


def make_subgrids(first, outs, token, capacity, listed, plan, uv, res, vis):
    tiles = vis // LANES
    destinations = sum(outs)
    quads = destinations * capacity // QUAD
    vmem = pl.BlockSpec(memory_space=pltpu.VMEM)
    smem = pl.BlockSpec(memory_space=pltpu.SMEM)
    return pl.pallas_call(
        functools.partial(subgrid_kernel, first, destinations, capacity, listed),
        out_shape=[
            jax.ShapeDtypeStruct((n * message_rows(capacity), LANES), jnp.bfloat16) for n in outs
        ]
        + [jax.ShapeDtypeStruct(token.shape, token.dtype)],
        in_specs=[smem] + [vmem] * 3,
        out_specs=[vmem] * (len(outs) + 1),
        scratch_shapes=[
            pltpu.VMEM((4 * tiles * GROUP, LANES), jnp.float32),
            pltpu.VMEM((2 * FEATURE // SUB, 4 * LANES), jnp.bfloat16),
            pltpu.VMEM((quads + 1, FEATURE // SUB, LANES), jnp.float32),
            pltpu.VMEM((quads + 1, QUAD, LANES), jnp.float32),
            pltpu.VMEM((4 * LANES, LANES), jnp.bfloat16),
        ],
        compiler_params=pltpu.CompilerParams(vmem_limit_bytes=VMEM_LIMIT),
        cost_estimate=pl.CostEstimate(
            flops=quads * 32 * SUB * SUB * vis, bytes_accessed=16 * quads * FEATURE, transcendentals=0
        ),
        name="subgrids",
    )(plan, token, uv, res)


def pick_rows(hot, xs, part, out_ref, half):
    lane = lax.broadcasted_iota(jnp.int32, (GROUP, LANES), 1) >> 5
    for piece in range(PIECES):
        c, rows, parity = piece // 8, piece // 2 % 4 - 2 * half, piece % 2
        if not 0 <= rows < 2:
            continue
        part[...] = jnp.dot(hot[...], xs[piece], preferred_element_type=jnp.float32)
        for grp in range(4):
            given = [part[pl.ds(32 * jl + 8 * grp, 8), :] for jl in range(4)]
            for a in range(4):
                total = None
                for jl in range(4):
                    moved = given[jl]
                    if a != jl:
                        moved = pltpu.roll(moved, ((jl - a) % 4) * SUB, 1)
                    total = moved if total is None else jnp.where(lane == jl, moved, total)
                p = rows * 8 + a * 2 + parity
                out_ref[pl.ds(p * 64 + grp * 16 + c, 8, stride=2), :] = total


def first_half_kernel(capacity, *refs):
    x_refs, (out_ref, xs, hot, tags, part) = refs[:-5], refs[-5:]
    shares = capacity // TAG_ROWS
    at = 0
    for x_ref in x_refs:
        for base in range(0, x_ref.shape[0], message_rows(capacity)):
            for piece in range(PIECES):
                xs[piece, pl.ds(at, capacity), :] = x_ref[pl.ds(base + piece * capacity, capacity), :]
            tag = x_ref[pl.ds(base + PIECES * capacity, TAG_ROWS), :].astype(jnp.float32)
            for n in range(shares):
                column = n * (LANES // shares)
                tags[pl.ds(at + n * TAG_ROWS, TAG_ROWS), :] = jnp.broadcast_to(
                    tag[:, column : column + 1], (TAG_ROWS, LANES)
                )
            at += capacity
    wanted = lax.broadcasted_iota(jnp.int32, tags.shape, 1)
    wanted = ((wanted & 31) << 2) + (wanted >> 5) + 1
    hot[...] = jnp.where(tags[...] == wanted.astype(jnp.float32), 1.0, 0.0).T.astype(jnp.bfloat16)
    pick_rows(hot, xs, part, out_ref, 0)


def second_half_kernel(xs, hot, out_ref, part):
    pick_rows(hot, xs, part, out_ref, 1)


def sum_slots(arrived, capacity):
    rows = sum(x.shape[0] for x in arrived) // message_rows(capacity) * capacity
    vmem = pl.BlockSpec(memory_space=pltpu.VMEM)
    half = jax.ShapeDtypeStruct((SUB * 32, LANES), jnp.float32)
    params = pltpu.CompilerParams(vmem_limit_bytes=VMEM_LIMIT)
    part = pltpu.VMEM((SLOTS, LANES), jnp.float32)
    first, xs, hot = pl.pallas_call(
        functools.partial(first_half_kernel, capacity),
        out_shape=[
            half,
            jax.ShapeDtypeStruct((PIECES, rows, LANES), jnp.bfloat16),
            jax.ShapeDtypeStruct((SLOTS, rows), jnp.bfloat16),
        ],
        in_specs=[vmem] * len(arrived),
        out_specs=[vmem] * 3,
        scratch_shapes=[pltpu.VMEM((rows, LANES), jnp.float32), part],
        compiler_params=params,
        name="sum_first",
    )(*arrived)
    second = pl.pallas_call(
        second_half_kernel,
        out_shape=half,
        in_specs=[vmem] * 2,
        out_specs=vmem,
        scratch_shapes=[part],
        compiler_params=params,
        name="sum_second",
    )(xs, hot)
    return first, second


def add_kernel(at, mine_ref, theirs_ref, *refs):
    out_ref, total, sems = refs[-3:]
    step = total.shape[0] // sems.shape[0]
    copies = []
    for k in range(sems.shape[0]):
        here = pl.ds(k * step, step)
        total[here, :] = mine_ref[here, :] + theirs_ref[here, :]
        copy = pltpu.make_async_copy(
            total.at[here], out_ref.at[pl.ds(at + k * step, step)], sems.at[k]
        )
        copy.start()
        copies.append(copy)
    for copy in copies:
        copy.wait()


def add_half(at, mine, theirs, *whole):
    vmem, anywhere = pl.BlockSpec(memory_space=pltpu.VMEM), pl.BlockSpec(memory_space=pl.ANY)
    return pl.pallas_call(
        functools.partial(add_kernel, at),
        out_shape=jax.ShapeDtypeStruct((2 * mine.shape[0], LANES), jnp.float32),
        in_specs=[vmem, vmem] + [anywhere] * len(whole),
        out_specs=anywhere,
        scratch_shapes=[pltpu.VMEM(mine.shape, jnp.float32), pltpu.SemaphoreType.DMA((4,))],
        input_output_aliases={2: 0} if whole else {},
        compiler_params=pltpu.CompilerParams(vmem_limit_bytes=VMEM_LIMIT),
        name="add_half",
    )(mine, theirs, *whole)


def rows_of(array):
    blocks, parts, vis = array.shape
    tiles = vis // LANES
    split = array.reshape(blocks, parts, tiles, LANES)
    return split.transpose(0, 2, 1, 3).reshape(blocks * tiles * parts, LANES)


def sending_order(owners):
    across, near = list(range(max(owners // 2, 1), owners)), list(range(1, owners // 2))
    order = [across.pop() for _ in range(owners // 4)]
    while across or near:
        order += [group.pop() for group in (across, near) if group]
    return order + [0]


def in_rows(array):
    return with_layout_constraint(array, Layout(major_to_minor=(0, 1)))


def local(residual, uv_offsets, counts, tile_of_block, slot_of_block, owner_map):
    blocks, _, vis = uv_offsets.shape
    owners = owner_map.shape[0]
    capacity = -(-max(CAP_MIN, 2 * blocks // owners) // 32) * 16
    core = lax.axis_index("samp")
    me = lax.axis_index(("blk", "tile"))
    swap = [(0, 1), (1, 0)]
    own = in_rows(rows_of(residual[0]))
    other = in_rows(lax.ppermute(own, "samp", swap))

    lists = jnp.concatenate([tile_of_block[:, 0], slot_of_block, counts, owner_map])
    lists = lax.optimization_barrier(lists)
    tile_ids, slots, counts, owner_map = [
        lists[k * blocks : min((k + 1) * blocks, 3 * blocks + owners)] for k in range(4)
    ]
    owner_range = jnp.arange(owners, dtype=jnp.int32)
    owner_ids = jnp.sum(
        jnp.where(tile_ids[:, None] == owner_range[None, :], owner_map[None, :], 0), 1
    )
    paired = owners <= PAIRED_MAX and owners & (owners - 1) == 0
    distances = sending_order(owners)
    offset = owner_ids
    if paired:
        offset = jnp.bitwise_xor(owner_ids, me)
        offset = sum(jnp.where(offset == d, k, 0) for k, d in enumerate(distances) if k)
    index = jnp.arange(blocks, dtype=jnp.int32)
    same = (offset[None, :] == offset[:, None]) & (index[None, :] < index[:, None])
    rank = jnp.sum(same.astype(jnp.int32), 1)
    mine = (rank & 1) == core
    counted = jnp.sum((mine[None, :] & (offset[None, :] == owner_range[:, None])).astype(jnp.int32), 1)
    quads = (counted + QUAD - 1) >> 2
    edges = jnp.arange(owners + 1, dtype=jnp.int32)
    start = jnp.sum(jnp.where(owner_range[None, :] < edges[:, None], quads[None, :], 0), 1)
    before = jnp.sum(jnp.where(owner_range[None, :] < offset[:, None], quads[None, :], 0), 1)
    place = jnp.where(mine, before * QUAD + (rank >> 1), -1)
    longest = ((blocks + owners) // 2 + owners * (QUAD - 1)) // GROUP * GROUP + GROUP
    wanted = jnp.arange(longest, dtype=jnp.int32)
    chosen = place[None, :] == wanted[:, None]
    block_and_count = (index << COUNT_BITS) + counts
    row_and_tag = ((offset * capacity + (rank >> 1)) << TAG_BITS) + slots + 1
    block = jnp.sum(jnp.where(chosen, block_and_count[None, :], 0), 1)
    row = jnp.sum(jnp.where(chosen, row_and_tag[None, :], 0), 1)

    subgrids = functools.partial(
        make_subgrids, capacity=capacity, listed=longest, plan=jnp.concatenate([block, row, start]),
        uv=rows_of(uv_offsets), res=own.astype(jnp.float32) + other.astype(jnp.float32), vis=vis,
    )
    token = jnp.zeros((GROUP, LANES), jnp.int32)
    if paired:
        rows = []
        for first, last in zip(CALLS[:-1], CALLS[1:]):
            first, last = owners * first // CALLS[-1], owners * last // CALLS[-1]
            if first < last:
                *more, token = subgrids(first, (1,) * (last - first), token)
                rows += more
        arrived = []
        for distance, piece in zip(distances, rows):
            if distance:
                pairs = [(k, k ^ distance) for k in range(owners)]
                piece = lax.ppermute(piece, ("blk", "tile"), pairs)
            arrived.append(piece)
    else:
        each = max(d for d in range(1, 17) if owners % d == 0)
        rows = [subgrids(k, (each,), token)[0] for k in range(0, owners, each)]
        rows = jnp.concatenate(rows, 0).reshape(owners, message_rows(capacity), LANES)
        rows = lax.all_to_all(rows, ("blk", "tile"), split_axis=0, concat_axis=0, tiled=True)
        arrived = [rows.reshape(owners * message_rows(capacity), LANES)]
    first, second = sum_slots(arrived, capacity)
    whole = add_half(0, first, lax.ppermute(first, "samp", swap))
    whole = add_half(first.shape[0], second, lax.ppermute(second, "samp", swap), whole)
    whole = whole.reshape(SUB, SLOTS // 4, 2, LANES).transpose(0, 2, 1, 3)
    return whole.reshape(SUB, 2, SLOTS * SUB)


def solution(mesh):
    in_specs = (
        P("samp", ("cuts", "blk", "tile"), None, None),
        P(("cuts", "blk", "tile"), None, None),
        P(("cuts", "blk", "tile")),
        P(("cuts", "blk", "tile"), None),
        P(("cuts", "blk", "tile")),
        P(),
    )
    out_specs = P(("cuts", "blk", "tile"), None, None)
    return jax.shard_map(local, mesh=mesh, in_specs=in_specs, out_specs=out_specs, check_vma=False)
```

```python
import functools

import jax
import jax.numpy as jnp
import numpy as np
from jax import lax
from jax.experimental import pallas as pl
from jax.experimental.layout import Layout, with_layout_constraint
from jax.experimental.pallas import tpu as pltpu
from jax.sharding import PartitionSpec as P

SUB = 32
STEPS = SUB // 2
SLOTS = 128
LANES = 128
FEATURE = 2 * SUB * SUB
PIECES = FEATURE // LANES
CAP_MIN = 8
GROUP = 8
QUAD = 4
TAG_ROWS = 16
COUNT_BITS = 12
TAG_BITS = 8
CHUNK = 4 * LANES
PAIRED_MAX = 16
CALLS = (0, 2, 5, 7, 8)
VMEM_LIMIT = 48 * 1024 * 1024


def turn_coefficients():
    knots = np.cos(np.pi * (np.arange(400) + 0.5) / 400)
    cheb = np.polynomial.chebyshev
    even = cheb.cheb2poly(cheb.chebfit(knots, np.cos(np.pi * knots), 12))[0::2]
    odd = cheb.cheb2poly(cheb.chebfit(knots, np.sin(np.pi * knots), 13))[1::2]
    return [float(x) for x in even], [float(x) for x in odd]


COS_COEF, SIN_COEF = turn_coefficients()


def horner(coef, x):
    total = coef[-1] * x + coef[-2]
    for value in coef[-3::-1]:
        total = total * x + value
    return total


def first_angle(offset):
    y = offset * (1.0 / STEPS)
    x = y * y
    return horner(COS_COEF, x), horner(SIN_COEF, x) * y


def tile_of(value, t):
    return value[:, t * LANES : (t + 1) * LANES]


def by_quad(even, odd):
    top = lax.broadcasted_iota(jnp.int32, even.shape, 0) < QUAD
    return (
        jnp.where(top, even, pltpu.roll(odd, QUAD, 0)),
        jnp.where(top, pltpu.roll(even, QUAD, 0), odd),
    )


def sequence(before, middle, factor):
    def pair(*two):
        return jnp.concatenate(two, 0).astype(jnp.bfloat16)

    up, down = [], []
    last, value = before, middle
    for _ in range(STEPS // 4):
        after = factor * value - last
        up.append(pair(value, after))
        last, value = after, factor * after - value
    last, value = middle, before
    for _ in range(STEPS // 4):
        after = factor * value - last
        down.append(pair(after, value))
        last, value = after, factor * after - value
    return down[::-1] + up


def subgrid_kernel(
    first, destinations, capacity, listed, plan_ref, token_ref, uv_ref, res_ref, *refs
):
    out_refs, (next_ref, gathered, recent, found, tags, mover) = refs[:-6], refs[-6:]
    next_ref[...] = jnp.zeros_like(next_ref)
    tiles = gathered.shape[0] // (4 * GROUP)
    spare = destinations * capacity // QUAD

    def start_of(destination):
        return plan_ref[2 * listed + destination]

    low, high = start_of(first), start_of(first + destinations)
    last = listed - 1
    vis_at = lax.broadcasted_iota(jnp.int32, (2 * tiles, LANES), 1) + LANES * (
        lax.broadcasted_iota(jnp.int32, (2 * tiles, LANES), 0) >> 1
    )
    same_block = (
        lax.broadcasted_iota(jnp.int32, (GROUP, LANES), 0) & (QUAD - 1)
        == lax.broadcasted_iota(jnp.int32, (GROUP, LANES), 1) & (QUAD - 1)
    )
    quad_row = lax.broadcasted_iota(jnp.int32, (QUAD, LANES), 0)
    top = lax.broadcasted_iota(jnp.int32, (GROUP, LANES), 0) < QUAD

    source = lax.broadcasted_iota(jnp.int32, mover.shape, 0)
    lane = lax.broadcasted_iota(jnp.int32, mover.shape, 1)
    moves = (source >> 7 == lane >> 5) & ((source & (LANES - 1)) >> 2 == lane & (SUB - 1))
    mover[...] = jnp.where(moves, 1.0, 0.0).astype(jnp.bfloat16)
    tags[...] = jnp.zeros_like(tags)

    def angles(quad_at):
        for i in range(GROUP):
            packed = plan_ref[jnp.minimum(quad_at * QUAD + i, last)]
            block, count = packed >> COUNT_BITS, packed & ((1 << COUNT_BITS) - 1)
            at = pl.ds(pl.multiple_of(block * 2 * tiles, 2 * tiles), 2 * tiles)
            both = jnp.where(vis_at < count, res_ref[at, :], 0.0)
            gathered[pl.ds(i, 2 * tiles, stride=GROUP), :] = uv_ref[at, :]
            gathered[pl.ds(2 * tiles * GROUP + i, 2 * tiles, stride=GROUP), :] = both
        u, v, re, im = [
            jnp.concatenate(
                [
                    gathered[pl.ds(((k // 2) * 2 * tiles + 2 * t + k % 2) * GROUP, GROUP), :]
                    for t in range(tiles)
                ],
                1,
            )
            for k in range(4)
        ]
        c, s = first_angle(u)
        a, b, e, f = re * c, im * s, im * c, re * s
        after = (a - b, e + f)
        before = (a + b, e - f)
        second = [2.0 * c * near - far for near, far in zip(before, (re, im))]
        factor = 2.0 - 4.0 * s * s
        left_factor = by_quad(factor, factor)
        left = [(by_quad(x, y), by_quad(z, w)) for x, y, z, w in zip(second, before, (re, im), after)]
        c, s = first_angle(v)
        c2, s2 = 1.0 - 2.0 * s * s, 2.0 * s * c
        factor = 2.0 * c2
        right_factor = by_quad(factor, factor)
        right = [
            (by_quad(c2, c), by_quad(jnp.ones_like(c), c)),
            (by_quad(-s2, -s), by_quad(jnp.zeros_like(s), s)),
        ]
        return [
            [
                (left[0][0][q], left[0][1][q], left[1][0][q], left[1][1][q], left_factor[q]),
                (right[0][0][q], right[0][1][q], right[1][0][q], right[1][1][q], right_factor[q]),
            ]
            for q in range(2)
        ]

    def place_of(quad_at):
        index = jnp.clip(quad_at * QUAD, 0, last + 1 - QUAD)
        place = (plan_ref[listed + index] >> (TAG_BITS + 2)) - first * (capacity // QUAD)
        return index, jnp.where((quad_at >= low) & (quad_at < high), place, spare)

    def settle(quad_at):
        moved = jnp.dot(recent[...], mover[...], preferred_element_type=jnp.float32)
        for q in range(2):
            _, place = place_of(quad_at + q)
            found[place] = moved[q * found.shape[1] : (q + 1) * found.shape[1]]

    def finish(seeds, quad_at, q):
        product = None
        for lanes in range(0, tiles * LANES, CHUNK):
            operands = []
            for side in seeds[::-1]:
                before, middle, before_imag, middle_imag, factor = [
                    x[:, lanes : lanes + CHUNK] for x in side
                ]
                operands.append(
                    jnp.concatenate(
                        sequence(before, middle, factor)
                        + sequence(before_imag, middle_imag, factor),
                        0,
                    )
                )
            term = lax.dot_general(
                operands[1], operands[0], (((1,), (1,)), ((), ())),
                preferred_element_type=jnp.float32,
            )
            product = term if product is None else product + term
        half = product.shape[0] // 2
        wholes = (
            product[:half, :LANES] - product[half:, LANES:],
            product[half:, :LANES] + product[:half, LANES:],
        )
        rows = []
        for whole in wholes:
            for j in range(0, STEPS, 4):
                four = [whole[(j + k) * GROUP : (j + k + 1) * GROUP] for k in range(4)]
                rows.append(jnp.concatenate([jnp.where(same_block, x, 0.0) for x in four], 1))
        size = found.shape[1]
        recent[pl.ds(q * size, size), :] = jnp.concatenate(rows, 0).astype(jnp.bfloat16)
        index, place = place_of(quad_at)
        tag = jnp.zeros((QUAD, LANES), jnp.int32)
        for b in range(QUAD):
            tag = jnp.where(quad_row == b, plan_ref[listed + index + b] & ((1 << TAG_BITS) - 1), tag)
        tags[place] = tag.astype(jnp.float32)

    def turn(g, seeds):
        quad_at = low + 2 * g
        settle(quad_at - 2)
        for q in range(2):
            finish(seeds[q], quad_at + q, q)
        return angles(quad_at + 2)

    turns = (high - low + 1) >> 1
    lax.fori_loop(0, turns, turn, angles(low))
    settle(low + 2 * turns - 2)

    shares = capacity // TAG_ROWS
    share = lax.broadcasted_iota(jnp.int32, (TAG_ROWS, LANES), 1) // (LANES // shares)

    def write_share(out_ref, base, slot, sent, n):
        for piece in range(PIECES // 2):
            part = []
            for k in range(4):
                value = found[slot + k, pl.ds(piece * GROUP, GROUP), :]
                part.append(jnp.where(n * 4 + k < sent, value, 0.0))
            first_two, last_two = [], []
            for even, odd in (part[:2], part[2:]):
                first_two.append(jnp.where(top, even, pltpu.roll(odd, QUAD, 0)))
                last_two.append(jnp.where(top, pltpu.roll(even, QUAD, 0), odd))
            for parity, two in enumerate((first_two, last_two)):
                put = base + (piece * 2 + parity) * capacity + n * TAG_ROWS
                out_ref[pl.ds(put, TAG_ROWS), :] = jnp.concatenate(two, 0).astype(jnp.bfloat16)

    for d, out_ref in enumerate(out_refs):
        for m in range(out_ref.shape[0] // message_rows(capacity)):
            base = m * message_rows(capacity)
            sent = start_of(first + d + m + 1) - start_of(first + d + m)
            slot = (d + m) * (capacity // QUAD)
            tag = jnp.zeros((TAG_ROWS, LANES), jnp.float32)
            for n in range(shares):
                at = slot + n * 4
                four = jnp.concatenate([tags[at + k] for k in range(4)], 0)
                tag = jnp.where(share == n, four, tag)
                write_share(out_ref, base, at, sent, n)
            out_ref[pl.ds(base + PIECES * capacity, TAG_ROWS), :] = tag.astype(jnp.bfloat16)


def message_rows(capacity):
    return PIECES * capacity + TAG_ROWS


def make_subgrids(first, outs, token, capacity, listed, plan, uv, res, vis):
    tiles = vis // LANES
    destinations = sum(outs)
    quads = destinations * capacity // QUAD
    vmem = pl.BlockSpec(memory_space=pltpu.VMEM)
    smem = pl.BlockSpec(memory_space=pltpu.SMEM)
    return pl.pallas_call(
        functools.partial(subgrid_kernel, first, destinations, capacity, listed),
        out_shape=[
            jax.ShapeDtypeStruct((n * message_rows(capacity), LANES), jnp.bfloat16) for n in outs
        ]
        + [jax.ShapeDtypeStruct(token.shape, token.dtype)],
        in_specs=[smem] + [vmem] * 3,
        out_specs=[vmem] * (len(outs) + 1),
        scratch_shapes=[
            pltpu.VMEM((4 * tiles * GROUP, LANES), jnp.float32),
            pltpu.VMEM((2 * FEATURE // SUB, 4 * LANES), jnp.bfloat16),
            pltpu.VMEM((quads + 1, FEATURE // SUB, LANES), jnp.float32),
            pltpu.VMEM((quads + 1, QUAD, LANES), jnp.float32),
            pltpu.VMEM((4 * LANES, LANES), jnp.bfloat16),
        ],
        compiler_params=pltpu.CompilerParams(vmem_limit_bytes=VMEM_LIMIT),
        cost_estimate=pl.CostEstimate(
            flops=quads * 32 * SUB * SUB * vis, bytes_accessed=16 * quads * FEATURE, transcendentals=0
        ),
        name="subgrids",
    )(plan, token, uv, res)


def pick_rows(hot, xs, part, out_ref, half):
    lane = lax.broadcasted_iota(jnp.int32, (GROUP, LANES), 1) >> 5
    for piece in range(PIECES):
        c, rows, parity = piece // 8, piece // 2 % 4 - 2 * half, piece % 2
        if not 0 <= rows < 2:
            continue
        part[...] = jnp.dot(hot[...], xs[piece], preferred_element_type=jnp.float32)
        for grp in range(4):
            given = [part[pl.ds(32 * jl + 8 * grp, 8), :] for jl in range(4)]
            for a in range(4):
                total = None
                for jl in range(4):
                    moved = given[jl]
                    if a != jl:
                        moved = pltpu.roll(moved, ((jl - a) % 4) * SUB, 1)
                    total = moved if total is None else jnp.where(lane == jl, moved, total)
                p = rows * 8 + a * 2 + parity
                out_ref[pl.ds(p * 64 + grp * 16 + c, 8, stride=2), :] = total


def first_half_kernel(capacity, *refs):
    x_refs, (out_ref, xs, hot, tags, part) = refs[:-5], refs[-5:]
    shares = capacity // TAG_ROWS
    at = 0
    for x_ref in x_refs:
        for base in range(0, x_ref.shape[0], message_rows(capacity)):
            for piece in range(PIECES):
                xs[piece, pl.ds(at, capacity), :] = x_ref[pl.ds(base + piece * capacity, capacity), :]
            tag = x_ref[pl.ds(base + PIECES * capacity, TAG_ROWS), :].astype(jnp.float32)
            for n in range(shares):
                column = n * (LANES // shares)
                tags[pl.ds(at + n * TAG_ROWS, TAG_ROWS), :] = jnp.broadcast_to(
                    tag[:, column : column + 1], (TAG_ROWS, LANES)
                )
            at += capacity
    wanted = lax.broadcasted_iota(jnp.int32, tags.shape, 1)
    wanted = ((wanted & 31) << 2) + (wanted >> 5) + 1
    hot[...] = jnp.where(tags[...] == wanted.astype(jnp.float32), 1.0, 0.0).T.astype(jnp.bfloat16)
    pick_rows(hot, xs, part, out_ref, 0)


def second_half_kernel(xs, hot, out_ref, part):
    pick_rows(hot, xs, part, out_ref, 1)


def sum_slots(arrived, capacity):
    rows = sum(x.shape[0] for x in arrived) // message_rows(capacity) * capacity
    vmem = pl.BlockSpec(memory_space=pltpu.VMEM)
    half = jax.ShapeDtypeStruct((SUB * 32, LANES), jnp.float32)
    params = pltpu.CompilerParams(vmem_limit_bytes=VMEM_LIMIT)
    part = pltpu.VMEM((SLOTS, LANES), jnp.float32)
    first, xs, hot = pl.pallas_call(
        functools.partial(first_half_kernel, capacity),
        out_shape=[
            half,
            jax.ShapeDtypeStruct((PIECES, rows, LANES), jnp.bfloat16),
            jax.ShapeDtypeStruct((SLOTS, rows), jnp.bfloat16),
        ],
        in_specs=[vmem] * len(arrived),
        out_specs=[vmem] * 3,
        scratch_shapes=[pltpu.VMEM((rows, LANES), jnp.float32), part],
        compiler_params=params,
        name="sum_first",
    )(*arrived)
    second = pl.pallas_call(
        second_half_kernel,
        out_shape=half,
        in_specs=[vmem] * 2,
        out_specs=vmem,
        scratch_shapes=[part],
        compiler_params=params,
        name="sum_second",
    )(xs, hot)
    return first, second


def add_kernel(at, mine_ref, theirs_ref, *refs):
    out_ref, total, sems = refs[-3:]
    step = total.shape[0] // sems.shape[0]
    copies = []
    for k in range(sems.shape[0]):
        here = pl.ds(k * step, step)
        total[here, :] = mine_ref[here, :] + theirs_ref[here, :]
        copy = pltpu.make_async_copy(
            total.at[here], out_ref.at[pl.ds(at + k * step, step)], sems.at[k]
        )
        copy.start()
        copies.append(copy)
    for copy in copies:
        copy.wait()


def add_half(at, mine, theirs, *whole):
    vmem, anywhere = pl.BlockSpec(memory_space=pltpu.VMEM), pl.BlockSpec(memory_space=pl.ANY)
    return pl.pallas_call(
        functools.partial(add_kernel, at),
        out_shape=jax.ShapeDtypeStruct((2 * mine.shape[0], LANES), jnp.float32),
        in_specs=[vmem, vmem] + [anywhere] * len(whole),
        out_specs=anywhere,
        scratch_shapes=[pltpu.VMEM(mine.shape, jnp.float32), pltpu.SemaphoreType.DMA((4,))],
        input_output_aliases={2: 0} if whole else {},
        compiler_params=pltpu.CompilerParams(vmem_limit_bytes=VMEM_LIMIT),
        name="add_half",
    )(mine, theirs, *whole)


def rows_of(array):
    blocks, parts, vis = array.shape
    tiles = vis // LANES
    split = array.reshape(blocks, parts, tiles, LANES)
    return split.transpose(0, 2, 1, 3).reshape(blocks * tiles * parts, LANES)


def sending_order(owners):
    across, near = list(range(max(owners // 2, 1), owners)), list(range(1, owners // 2))
    order = [across.pop() for _ in range(owners // 4)]
    while across or near:
        order += [group.pop() for group in (across, near) if group]
    return order + [0]


def in_rows(array):
    return with_layout_constraint(array, Layout(major_to_minor=(0, 1)))


def local(residual, uv_offsets, counts, tile_of_block, slot_of_block, owner_map):
    blocks, _, vis = uv_offsets.shape
    owners = owner_map.shape[0]
    capacity = -(-max(CAP_MIN, 2 * blocks // owners) // 32) * 16
    core = lax.axis_index("samp")
    me = lax.axis_index(("blk", "tile"))
    swap = [(0, 1), (1, 0)]
    own = in_rows(rows_of(residual[0]))
    other = in_rows(lax.ppermute(own, "samp", swap))

    lists = jnp.concatenate([tile_of_block[:, 0], slot_of_block, counts, owner_map])
    lists = lax.optimization_barrier(lists)
    tile_ids, slots, counts, owner_map = [
        lists[k * blocks : min((k + 1) * blocks, 3 * blocks + owners)] for k in range(4)
    ]
    owner_range = jnp.arange(owners, dtype=jnp.int32)
    owner_ids = jnp.sum(
        jnp.where(tile_ids[:, None] == owner_range[None, :], owner_map[None, :], 0), 1
    )
    paired = owners <= PAIRED_MAX and owners & (owners - 1) == 0
    distances = sending_order(owners)
    offset = owner_ids
    if paired:
        offset = jnp.bitwise_xor(owner_ids, me)
        offset = sum(jnp.where(offset == d, k, 0) for k, d in enumerate(distances) if k)
    index = jnp.arange(blocks, dtype=jnp.int32)
    same = (offset[None, :] == offset[:, None]) & (index[None, :] < index[:, None])
    rank = jnp.sum(same.astype(jnp.int32), 1)
    mine = (rank & 1) == core
    counted = jnp.sum((mine[None, :] & (offset[None, :] == owner_range[:, None])).astype(jnp.int32), 1)
    quads = (counted + QUAD - 1) >> 2
    edges = jnp.arange(owners + 1, dtype=jnp.int32)
    start = jnp.sum(jnp.where(owner_range[None, :] < edges[:, None], quads[None, :], 0), 1)
    before = jnp.sum(jnp.where(owner_range[None, :] < offset[:, None], quads[None, :], 0), 1)
    place = jnp.where(mine, before * QUAD + (rank >> 1), -1)
    longest = ((blocks + owners) // 2 + owners * (QUAD - 1)) // GROUP * GROUP + GROUP
    wanted = jnp.arange(longest, dtype=jnp.int32)
    chosen = place[None, :] == wanted[:, None]
    block_and_count = (index << COUNT_BITS) + counts
    row_and_tag = ((offset * capacity + (rank >> 1)) << TAG_BITS) + slots + 1
    block = jnp.sum(jnp.where(chosen, block_and_count[None, :], 0), 1)
    row = jnp.sum(jnp.where(chosen, row_and_tag[None, :], 0), 1)

    subgrids = functools.partial(
        make_subgrids, capacity=capacity, listed=longest, plan=jnp.concatenate([block, row, start]),
        uv=rows_of(uv_offsets), res=own.astype(jnp.float32) + other.astype(jnp.float32), vis=vis,
    )
    token = jnp.zeros((GROUP, LANES), jnp.int32)
    if paired:
        rows = []
        for first, last in zip(CALLS[:-1], CALLS[1:]):
            first, last = owners * first // CALLS[-1], owners * last // CALLS[-1]
            if first < last:
                *more, token = subgrids(first, (1,) * (last - first), token)
                rows += more
        arrived = []
        for distance, piece in zip(distances, rows):
            if distance:
                pairs = [(k, k ^ distance) for k in range(owners)]
                piece = lax.ppermute(piece, ("blk", "tile"), pairs)
            arrived.append(piece)
    else:
        each = max(d for d in range(1, 17) if owners % d == 0)
        rows = [subgrids(k, (each,), token)[0] for k in range(0, owners, each)]
        rows = jnp.concatenate(rows, 0).reshape(owners, message_rows(capacity), LANES)
        rows = lax.all_to_all(rows, ("blk", "tile"), split_axis=0, concat_axis=0, tiled=True)
        arrived = [rows.reshape(owners * message_rows(capacity), LANES)]
    first, second = sum_slots(arrived, capacity)
    whole = add_half(0, first, lax.ppermute(first, "samp", swap))
    whole = add_half(first.shape[0], second, lax.ppermute(second, "samp", swap), whole)
    whole = whole.reshape(SUB, SLOTS // 4, 2, LANES).transpose(0, 2, 1, 3)
    return whole.reshape(SUB, 2, SLOTS * SUB)


def solution(mesh):
    in_specs = (
        P("samp", ("cuts", "blk", "tile"), None, None),
        P(("cuts", "blk", "tile"), None, None),
        P(("cuts", "blk", "tile")),
        P(("cuts", "blk", "tile"), None),
        P(("cuts", "blk", "tile")),
        P(),
    )
    out_specs = P(("cuts", "blk", "tile"), None, None)
    return jax.shard_map(local, mesh=mesh, in_specs=in_specs, out_specs=out_specs, check_vma=False)
```

```python
import functools

import jax
import jax.numpy as jnp
import numpy as np
from jax import lax
from jax.experimental import pallas as pl
from jax.experimental.layout import Layout, with_layout_constraint
from jax.experimental.pallas import tpu as pltpu
from jax.sharding import PartitionSpec as P

SUB = 32
STEPS = SUB // 2
SLOTS = 128
LANES = 128
FEATURE = 2 * SUB * SUB
PIECES = FEATURE // LANES
CAP_MIN = 8
GROUP = 8
QUAD = 4
TAG_ROWS = 16
COUNT_BITS = 12
TAG_BITS = 8
CHUNK = 4 * LANES
PAIRED_MAX = 16
CALLS = (0, 2, 5, 7, 8)
VMEM_LIMIT = 48 * 1024 * 1024


def turn_coefficients():
    knots = np.cos(np.pi * (np.arange(400) + 0.5) / 400)
    cheb = np.polynomial.chebyshev
    even = cheb.cheb2poly(cheb.chebfit(knots, np.cos(np.pi * knots), 12))[0::2]
    odd = cheb.cheb2poly(cheb.chebfit(knots, np.sin(np.pi * knots), 13))[1::2]
    return [float(x) for x in even], [float(x) for x in odd]


COS_COEF, SIN_COEF = turn_coefficients()


def horner(coef, x):
    total = coef[-1] * x + coef[-2]
    for value in coef[-3::-1]:
        total = total * x + value
    return total


def first_angle(offset):
    y = offset * (1.0 / STEPS)
    x = y * y
    return horner(COS_COEF, x), horner(SIN_COEF, x) * y


def tile_of(value, t):
    return value[:, t * LANES : (t + 1) * LANES]


def by_quad(even, odd):
    top = lax.broadcasted_iota(jnp.int32, even.shape, 0) < QUAD
    return (
        jnp.where(top, even, pltpu.roll(odd, QUAD, 0)),
        jnp.where(top, pltpu.roll(even, QUAD, 0), odd),
    )


def sequence(before, middle, factor):
    def pair(*two):
        return jnp.concatenate(two, 0).astype(jnp.bfloat16)

    up, down = [], []
    last, value = before, middle
    for _ in range(STEPS // 4):
        after = factor * value - last
        up.append(pair(value, after))
        last, value = after, factor * after - value
    last, value = middle, before
    for _ in range(STEPS // 4):
        after = factor * value - last
        down.append(pair(after, value))
        last, value = after, factor * after - value
    return down[::-1] + up


def subgrid_kernel(
    first, destinations, capacity, listed, plan_ref, token_ref, uv_ref, res_ref, *refs
):
    out_refs, (next_ref, gathered, recent, found, tags, mover) = refs[:-6], refs[-6:]
    next_ref[...] = jnp.zeros_like(next_ref)
    tiles = gathered.shape[0] // (4 * GROUP)
    spare = destinations * capacity // QUAD

    def start_of(destination):
        return plan_ref[2 * listed + destination]

    low, high = start_of(first), start_of(first + destinations)
    last = listed - 1
    vis_at = lax.broadcasted_iota(jnp.int32, (2 * tiles, LANES), 1) + LANES * (
        lax.broadcasted_iota(jnp.int32, (2 * tiles, LANES), 0) >> 1
    )
    same_block = (
        lax.broadcasted_iota(jnp.int32, (GROUP, LANES), 0) & (QUAD - 1)
        == lax.broadcasted_iota(jnp.int32, (GROUP, LANES), 1) & (QUAD - 1)
    )
    quad_row = lax.broadcasted_iota(jnp.int32, (QUAD, LANES), 0)
    top = lax.broadcasted_iota(jnp.int32, (GROUP, LANES), 0) < QUAD

    source = lax.broadcasted_iota(jnp.int32, mover.shape, 0)
    lane = lax.broadcasted_iota(jnp.int32, mover.shape, 1)
    moves = (source >> 7 == lane >> 5) & ((source & (LANES - 1)) >> 2 == lane & (SUB - 1))
    mover[...] = jnp.where(moves, 1.0, 0.0).astype(jnp.bfloat16)
    tags[...] = jnp.zeros_like(tags)

    def angles(quad_at):
        for i in range(GROUP):
            packed = plan_ref[jnp.minimum(quad_at * QUAD + i, last)]
            block, count = packed >> COUNT_BITS, packed & ((1 << COUNT_BITS) - 1)
            at = pl.ds(pl.multiple_of(block * 2 * tiles, 2 * tiles), 2 * tiles)
            both = jnp.where(vis_at < count, res_ref[at, :], 0.0)
            gathered[pl.ds(i, 2 * tiles, stride=GROUP), :] = uv_ref[at, :]
            gathered[pl.ds(2 * tiles * GROUP + i, 2 * tiles, stride=GROUP), :] = both
        u, v, re, im = [
            jnp.concatenate(
                [
                    gathered[pl.ds(((k // 2) * 2 * tiles + 2 * t + k % 2) * GROUP, GROUP), :]
                    for t in range(tiles)
                ],
                1,
            )
            for k in range(4)
        ]
        c, s = first_angle(u)
        a, b, e, f = re * c, im * s, im * c, re * s
        after = (a - b, e + f)
        before = (a + b, e - f)
        second = [2.0 * c * near - far for near, far in zip(before, (re, im))]
        factor = 2.0 - 4.0 * s * s
        left_factor = by_quad(factor, factor)
        left = [(by_quad(x, y), by_quad(z, w)) for x, y, z, w in zip(second, before, (re, im), after)]
        c, s = first_angle(v)
        c2, s2 = 1.0 - 2.0 * s * s, 2.0 * s * c
        factor = 2.0 * c2
        right_factor = by_quad(factor, factor)
        right = [
            (by_quad(c2, c), by_quad(jnp.ones_like(c), c)),
            (by_quad(-s2, -s), by_quad(jnp.zeros_like(s), s)),
        ]
        return [
            [
                (left[0][0][q], left[0][1][q], left[1][0][q], left[1][1][q], left_factor[q]),
                (right[0][0][q], right[0][1][q], right[1][0][q], right[1][1][q], right_factor[q]),
            ]
            for q in range(2)
        ]

    def place_of(quad_at):
        index = jnp.clip(quad_at * QUAD, 0, last + 1 - QUAD)
        place = (plan_ref[listed + index] >> (TAG_BITS + 2)) - first * (capacity // QUAD)
        return index, jnp.where((quad_at >= low) & (quad_at < high), place, spare)

    def settle(quad_at):
        moved = jnp.dot(recent[...], mover[...], preferred_element_type=jnp.float32)
        for q in range(2):
            _, place = place_of(quad_at + q)
            found[place] = moved[q * found.shape[1] : (q + 1) * found.shape[1]]

    def finish(seeds, quad_at, q):
        product = None
        for lanes in range(0, tiles * LANES, CHUNK):
            operands = []
            for side in seeds[::-1]:
                before, middle, before_imag, middle_imag, factor = [
                    x[:, lanes : lanes + CHUNK] for x in side
                ]
                operands.append(
                    jnp.concatenate(
                        sequence(before, middle, factor)
                        + sequence(before_imag, middle_imag, factor),
                        0,
                    )
                )
            term = lax.dot_general(
                operands[1], operands[0], (((1,), (1,)), ((), ())),
                preferred_element_type=jnp.float32,
            )
            product = term if product is None else product + term
        half = product.shape[0] // 2
        wholes = (
            product[:half, :LANES] - product[half:, LANES:],
            product[half:, :LANES] + product[:half, LANES:],
        )
        rows = []
        for whole in wholes:
            for j in range(0, STEPS, 4):
                four = [whole[(j + k) * GROUP : (j + k + 1) * GROUP] for k in range(4)]
                rows.append(jnp.concatenate([jnp.where(same_block, x, 0.0) for x in four], 1))
        size = found.shape[1]
        recent[pl.ds(q * size, size), :] = jnp.concatenate(rows, 0).astype(jnp.bfloat16)
        index, place = place_of(quad_at)
        tag = jnp.zeros((QUAD, LANES), jnp.int32)
        for b in range(QUAD):
            tag = jnp.where(quad_row == b, plan_ref[listed + index + b] & ((1 << TAG_BITS) - 1), tag)
        tags[place] = tag.astype(jnp.float32)

    def turn(g, seeds):
        quad_at = low + 2 * g
        settle(quad_at - 2)
        for q in range(2):
            finish(seeds[q], quad_at + q, q)
        return angles(quad_at + 2)

    turns = (high - low + 1) >> 1
    lax.fori_loop(0, turns, turn, angles(low))
    settle(low + 2 * turns - 2)

    shares = capacity // TAG_ROWS
    share = lax.broadcasted_iota(jnp.int32, (TAG_ROWS, LANES), 1) // (LANES // shares)

    def write_share(out_ref, base, slot, sent, n):
        for piece in range(PIECES // 2):
            part = []
            for k in range(4):
                value = found[slot + k, pl.ds(piece * GROUP, GROUP), :]
                part.append(jnp.where(n * 4 + k < sent, value, 0.0))
            first_two, last_two = [], []
            for even, odd in (part[:2], part[2:]):
                first_two.append(jnp.where(top, even, pltpu.roll(odd, QUAD, 0)))
                last_two.append(jnp.where(top, pltpu.roll(even, QUAD, 0), odd))
            for parity, two in enumerate((first_two, last_two)):
                put = base + (piece * 2 + parity) * capacity + n * TAG_ROWS
                out_ref[pl.ds(put, TAG_ROWS), :] = jnp.concatenate(two, 0).astype(jnp.bfloat16)

    for d, out_ref in enumerate(out_refs):
        for m in range(out_ref.shape[0] // message_rows(capacity)):
            base = m * message_rows(capacity)
            sent = start_of(first + d + m + 1) - start_of(first + d + m)
            slot = (d + m) * (capacity // QUAD)
            tag = jnp.zeros((TAG_ROWS, LANES), jnp.float32)
            for n in range(shares):
                at = slot + n * 4
                four = jnp.concatenate([tags[at + k] for k in range(4)], 0)
                tag = jnp.where(share == n, four, tag)
                write_share(out_ref, base, at, sent, n)
            out_ref[pl.ds(base + PIECES * capacity, TAG_ROWS), :] = tag.astype(jnp.bfloat16)


def message_rows(capacity):
    return PIECES * capacity + TAG_ROWS


def make_subgrids(first, outs, token, capacity, listed, plan, uv, res, vis):
    tiles = vis // LANES
    destinations = sum(outs)
    quads = destinations * capacity // QUAD
    vmem = pl.BlockSpec(memory_space=pltpu.VMEM)
    smem = pl.BlockSpec(memory_space=pltpu.SMEM)
    return pl.pallas_call(
        functools.partial(subgrid_kernel, first, destinations, capacity, listed),
        out_shape=[
            jax.ShapeDtypeStruct((n * message_rows(capacity), LANES), jnp.bfloat16) for n in outs
        ]
        + [jax.ShapeDtypeStruct(token.shape, token.dtype)],
        in_specs=[smem] + [vmem] * 3,
        out_specs=[vmem] * (len(outs) + 1),
        scratch_shapes=[
            pltpu.VMEM((4 * tiles * GROUP, LANES), jnp.float32),
            pltpu.VMEM((2 * FEATURE // SUB, 4 * LANES), jnp.bfloat16),
            pltpu.VMEM((quads + 1, FEATURE // SUB, LANES), jnp.float32),
            pltpu.VMEM((quads + 1, QUAD, LANES), jnp.float32),
            pltpu.VMEM((4 * LANES, LANES), jnp.bfloat16),
        ],
        compiler_params=pltpu.CompilerParams(vmem_limit_bytes=VMEM_LIMIT),
        cost_estimate=pl.CostEstimate(
            flops=quads * 32 * SUB * SUB * vis, bytes_accessed=16 * quads * FEATURE, transcendentals=0
        ),
        name="subgrids",
    )(plan, token, uv, res)


def pick_rows(hot, xs, part, whole, out_ref, half):
    lane = lax.broadcasted_iota(jnp.int32, (GROUP, LANES), 1) >> 5
    for piece in range(PIECES):
        c, rows, parity = piece // 8, piece // 2 % 4 - 2 * half, piece % 2
        if not 0 <= rows < 2:
            continue
        part[...] = jnp.dot(hot[...], xs[piece], preferred_element_type=jnp.float32)
        for grp in range(4):
            given = [part[pl.ds(32 * jl + 8 * grp, 8), :] for jl in range(4)]
            for a in range(4):
                total = None
                for jl in range(4):
                    moved = given[jl]
                    if a != jl:
                        moved = pltpu.roll(moved, ((jl - a) % 4) * SUB, 1)
                    total = moved if total is None else jnp.where(lane == jl, moved, total)
                p = rows * 8 + a * 2 + parity
                whole[pl.ds(p * 64 + grp * 16 + c, 8, stride=2), :] = total
    out_ref[...] = whole[...].astype(out_ref.dtype)


def first_half_kernel(capacity, *refs):
    x_refs, (out_ref, xs, hot, tags, part, whole) = refs[:-6], refs[-6:]
    shares = capacity // TAG_ROWS
    at = 0
    for x_ref in x_refs:
        for base in range(0, x_ref.shape[0], message_rows(capacity)):
            for piece in range(PIECES):
                xs[piece, pl.ds(at, capacity), :] = x_ref[pl.ds(base + piece * capacity, capacity), :]
            tag = x_ref[pl.ds(base + PIECES * capacity, TAG_ROWS), :].astype(jnp.float32)
            for n in range(shares):
                column = n * (LANES // shares)
                tags[pl.ds(at + n * TAG_ROWS, TAG_ROWS), :] = jnp.broadcast_to(
                    tag[:, column : column + 1], (TAG_ROWS, LANES)
                )
            at += capacity
    wanted = lax.broadcasted_iota(jnp.int32, tags.shape, 1)
    wanted = ((wanted & 31) << 2) + (wanted >> 5) + 1
    hot[...] = jnp.where(tags[...] == wanted.astype(jnp.float32), 1.0, 0.0).T.astype(jnp.bfloat16)
    pick_rows(hot, xs, part, whole, out_ref, 0)


def second_half_kernel(xs, hot, out_ref, part, whole):
    pick_rows(hot, xs, part, whole, out_ref, 1)


def sum_slots(arrived, capacity):
    rows = sum(x.shape[0] for x in arrived) // message_rows(capacity) * capacity
    vmem = pl.BlockSpec(memory_space=pltpu.VMEM)
    half = jax.ShapeDtypeStruct((SUB * 32, LANES), jnp.bfloat16)
    params = pltpu.CompilerParams(vmem_limit_bytes=VMEM_LIMIT)
    parts = [pltpu.VMEM((SLOTS, LANES), jnp.float32), pltpu.VMEM(half.shape, jnp.float32)]
    first, xs, hot = pl.pallas_call(
        functools.partial(first_half_kernel, capacity),
        out_shape=[
            half,
            jax.ShapeDtypeStruct((PIECES, rows, LANES), jnp.bfloat16),
            jax.ShapeDtypeStruct((SLOTS, rows), jnp.bfloat16),
        ],
        in_specs=[vmem] * len(arrived),
        out_specs=[vmem] * 3,
        scratch_shapes=[pltpu.VMEM((rows, LANES), jnp.float32)] + parts,
        compiler_params=params,
        name="sum_first",
    )(*arrived)
    second = pl.pallas_call(
        second_half_kernel,
        out_shape=half,
        in_specs=[vmem] * 2,
        out_specs=vmem,
        scratch_shapes=parts,
        compiler_params=params,
        name="sum_second",
    )(xs, hot)
    return first, second


def add_kernel(at, mine_ref, theirs_ref, *refs):
    out_ref, total, sems = refs[-3:]
    step = total.shape[0] // sems.shape[0]
    copies = []
    for k in range(sems.shape[0]):
        here = pl.ds(k * step, step)
        total[here, :] = mine_ref[here, :].astype(jnp.float32) + theirs_ref[here, :].astype(
            jnp.float32
        )
        copy = pltpu.make_async_copy(
            total.at[here], out_ref.at[pl.ds(at + k * step, step)], sems.at[k]
        )
        copy.start()
        copies.append(copy)
    for copy in copies:
        copy.wait()


def add_half(at, mine, theirs, *whole):
    vmem, anywhere = pl.BlockSpec(memory_space=pltpu.VMEM), pl.BlockSpec(memory_space=pl.ANY)
    return pl.pallas_call(
        functools.partial(add_kernel, at),
        out_shape=jax.ShapeDtypeStruct((2 * mine.shape[0], LANES), jnp.float32),
        in_specs=[vmem, vmem] + [anywhere] * len(whole),
        out_specs=anywhere,
        scratch_shapes=[pltpu.VMEM(mine.shape, jnp.float32), pltpu.SemaphoreType.DMA((4,))],
        input_output_aliases={2: 0} if whole else {},
        compiler_params=pltpu.CompilerParams(vmem_limit_bytes=VMEM_LIMIT),
        name="add_half",
    )(mine, theirs, *whole)


def rows_of(array):
    blocks, parts, vis = array.shape
    tiles = vis // LANES
    split = array.reshape(blocks, parts, tiles, LANES)
    return split.transpose(0, 2, 1, 3).reshape(blocks * tiles * parts, LANES)


def sending_order(owners):
    across, near = list(range(max(owners // 2, 1), owners)), list(range(1, owners // 2))
    order = [across.pop() for _ in range(owners // 4)]
    while across or near:
        order += [group.pop() for group in (across, near) if group]
    return order + [0]


def in_rows(array):
    return with_layout_constraint(array, Layout(major_to_minor=(0, 1)))


def local(residual, uv_offsets, counts, tile_of_block, slot_of_block, owner_map):
    blocks, _, vis = uv_offsets.shape
    owners = owner_map.shape[0]
    capacity = -(-max(CAP_MIN, 2 * blocks // owners) // 32) * 16
    core = lax.axis_index("samp")
    me = lax.axis_index(("blk", "tile"))
    swap = [(0, 1), (1, 0)]
    own = in_rows(rows_of(residual[0]))
    other = in_rows(lax.ppermute(own, "samp", swap))

    lists = jnp.concatenate([tile_of_block[:, 0], slot_of_block, counts, owner_map])
    lists = lax.optimization_barrier(lists)
    tile_ids, slots, counts, owner_map = [
        lists[k * blocks : min((k + 1) * blocks, 3 * blocks + owners)] for k in range(4)
    ]
    owner_range = jnp.arange(owners, dtype=jnp.int32)
    owner_ids = jnp.sum(
        jnp.where(tile_ids[:, None] == owner_range[None, :], owner_map[None, :], 0), 1
    )
    paired = owners <= PAIRED_MAX and owners & (owners - 1) == 0
    distances = sending_order(owners)
    offset = owner_ids
    if paired:
        offset = jnp.bitwise_xor(owner_ids, me)
        offset = sum(jnp.where(offset == d, k, 0) for k, d in enumerate(distances) if k)
    index = jnp.arange(blocks, dtype=jnp.int32)
    same = (offset[None, :] == offset[:, None]) & (index[None, :] < index[:, None])
    rank = jnp.sum(same.astype(jnp.int32), 1)
    mine = (rank & 1) == core
    counted = jnp.sum((mine[None, :] & (offset[None, :] == owner_range[:, None])).astype(jnp.int32), 1)
    quads = (counted + QUAD - 1) >> 2
    edges = jnp.arange(owners + 1, dtype=jnp.int32)
    start = jnp.sum(jnp.where(owner_range[None, :] < edges[:, None], quads[None, :], 0), 1)
    before = jnp.sum(jnp.where(owner_range[None, :] < offset[:, None], quads[None, :], 0), 1)
    place = jnp.where(mine, before * QUAD + (rank >> 1), -1)
    longest = ((blocks + owners) // 2 + owners * (QUAD - 1)) // GROUP * GROUP + GROUP
    wanted = jnp.arange(longest, dtype=jnp.int32)
    chosen = place[None, :] == wanted[:, None]
    block_and_count = (index << COUNT_BITS) + counts
    row_and_tag = ((offset * capacity + (rank >> 1)) << TAG_BITS) + slots + 1
    block = jnp.sum(jnp.where(chosen, block_and_count[None, :], 0), 1)
    row = jnp.sum(jnp.where(chosen, row_and_tag[None, :], 0), 1)

    subgrids = functools.partial(
        make_subgrids, capacity=capacity, listed=longest, plan=jnp.concatenate([block, row, start]),
        uv=rows_of(uv_offsets), res=own.astype(jnp.float32) + other.astype(jnp.float32), vis=vis,
    )
    token = jnp.zeros((GROUP, LANES), jnp.int32)
    if paired:
        rows = []
        for first, last in zip(CALLS[:-1], CALLS[1:]):
            first, last = owners * first // CALLS[-1], owners * last // CALLS[-1]
            if first < last:
                *more, token = subgrids(first, (1,) * (last - first), token)
                rows += more
        arrived = []
        for distance, piece in zip(distances, rows):
            if distance:
                pairs = [(k, k ^ distance) for k in range(owners)]
                piece = lax.ppermute(piece, ("blk", "tile"), pairs)
            arrived.append(piece)
    else:
        each = max(d for d in range(1, 17) if owners % d == 0)
        rows = [subgrids(k, (each,), token)[0] for k in range(0, owners, each)]
        rows = jnp.concatenate(rows, 0).reshape(owners, message_rows(capacity), LANES)
        rows = lax.all_to_all(rows, ("blk", "tile"), split_axis=0, concat_axis=0, tiled=True)
        arrived = [rows.reshape(owners * message_rows(capacity), LANES)]
    first, second = sum_slots(arrived, capacity)
    whole = add_half(0, first, lax.ppermute(first, "samp", swap))
    whole = add_half(first.shape[0], second, lax.ppermute(second, "samp", swap), whole)
    whole = whole.reshape(SUB, SLOTS // 4, 2, LANES).transpose(0, 2, 1, 3)
    return whole.reshape(SUB, 2, SLOTS * SUB)


def solution(mesh):
    in_specs = (
        P("samp", ("cuts", "blk", "tile"), None, None),
        P(("cuts", "blk", "tile"), None, None),
        P(("cuts", "blk", "tile")),
        P(("cuts", "blk", "tile"), None),
        P(("cuts", "blk", "tile")),
        P(),
    )
    out_specs = P(("cuts", "blk", "tile"), None, None)
    return jax.shard_map(local, mesh=mesh, in_specs=in_specs, out_specs=out_specs, check_vma=False)
```

```python
import functools

import jax
import jax.numpy as jnp
import numpy as np
from jax import lax
from jax.experimental import pallas as pl
from jax.experimental.layout import Layout, with_layout_constraint
from jax.experimental.pallas import tpu as pltpu
from jax.sharding import PartitionSpec as P

SUB = 32
STEPS = SUB // 2
SLOTS = 128
LANES = 128
FEATURE = 2 * SUB * SUB
PIECES = FEATURE // LANES
CAP_MIN = 8
GROUP = 8
QUAD = 4
TAG_ROWS = 16
COUNT_BITS = 12
TAG_BITS = 8
CHUNK = 4 * LANES
PAIRED_MAX = 16
CALLS = (0, 2, 4, 7, 8)
VMEM_LIMIT = 48 * 1024 * 1024


def turn_coefficients():
    knots = np.cos(np.pi * (np.arange(400) + 0.5) / 400)
    cheb = np.polynomial.chebyshev
    even = cheb.cheb2poly(cheb.chebfit(knots, np.cos(np.pi * knots), 12))[0::2]
    odd = cheb.cheb2poly(cheb.chebfit(knots, np.sin(np.pi * knots), 13))[1::2]
    return [float(x) for x in even], [float(x) for x in odd]


COS_COEF, SIN_COEF = turn_coefficients()


def horner(coef, x):
    total = coef[-1] * x + coef[-2]
    for value in coef[-3::-1]:
        total = total * x + value
    return total


def first_angle(offset):
    y = offset * (1.0 / STEPS)
    x = y * y
    return horner(COS_COEF, x), horner(SIN_COEF, x) * y


def tile_of(value, t):
    return value[:, t * LANES : (t + 1) * LANES]


def by_quad(even, odd):
    top = lax.broadcasted_iota(jnp.int32, even.shape, 0) < QUAD
    return (
        jnp.where(top, even, pltpu.roll(odd, QUAD, 0)),
        jnp.where(top, pltpu.roll(even, QUAD, 0), odd),
    )


def sequence(before, middle, factor):
    def pair(*two):
        return jnp.concatenate(two, 0).astype(jnp.bfloat16)

    up, down = [], []
    last, value = before, middle
    for _ in range(STEPS // 4):
        after = factor * value - last
        up.append(pair(value, after))
        last, value = after, factor * after - value
    last, value = middle, before
    for _ in range(STEPS // 4):
        after = factor * value - last
        down.append(pair(after, value))
        last, value = after, factor * after - value
    return down[::-1] + up


def subgrid_kernel(
    first, destinations, capacity, listed, plan_ref, token_ref, uv_ref, res_ref, *refs
):
    out_refs, (next_ref, gathered, recent, found, tags, mover) = refs[:-6], refs[-6:]
    next_ref[...] = jnp.zeros_like(next_ref)
    tiles = gathered.shape[0] // (4 * GROUP)
    spare = destinations * capacity // QUAD

    def start_of(destination):
        return plan_ref[2 * listed + destination]

    low, high = start_of(first), start_of(first + destinations)
    last = listed - 1
    vis_at = lax.broadcasted_iota(jnp.int32, (2 * tiles, LANES), 1) + LANES * (
        lax.broadcasted_iota(jnp.int32, (2 * tiles, LANES), 0) >> 1
    )
    same_block = (
        lax.broadcasted_iota(jnp.int32, (GROUP, LANES), 0) & (QUAD - 1)
        == lax.broadcasted_iota(jnp.int32, (GROUP, LANES), 1) & (QUAD - 1)
    )
    quad_row = lax.broadcasted_iota(jnp.int32, (QUAD, LANES), 0)
    top = lax.broadcasted_iota(jnp.int32, (GROUP, LANES), 0) < QUAD

    source = lax.broadcasted_iota(jnp.int32, mover.shape, 0)
    lane = lax.broadcasted_iota(jnp.int32, mover.shape, 1)
    moves = (source >> 7 == lane >> 5) & ((source & (LANES - 1)) >> 2 == lane & (SUB - 1))
    mover[...] = jnp.where(moves, 1.0, 0.0).astype(jnp.bfloat16)
    tags[...] = jnp.zeros_like(tags)

    def angles(quad_at):
        for i in range(GROUP):
            packed = plan_ref[jnp.minimum(quad_at * QUAD + i, last)]
            block, count = packed >> COUNT_BITS, packed & ((1 << COUNT_BITS) - 1)
            at = pl.ds(pl.multiple_of(block * 2 * tiles, 2 * tiles), 2 * tiles)
            both = jnp.where(vis_at < count, res_ref[at, :], 0.0)
            gathered[pl.ds(i, 2 * tiles, stride=GROUP), :] = uv_ref[at, :]
            gathered[pl.ds(2 * tiles * GROUP + i, 2 * tiles, stride=GROUP), :] = both
        u, v, re, im = [
            jnp.concatenate(
                [
                    gathered[pl.ds(((k // 2) * 2 * tiles + 2 * t + k % 2) * GROUP, GROUP), :]
                    for t in range(tiles)
                ],
                1,
            )
            for k in range(4)
        ]
        c, s = first_angle(u)
        a, b, e, f = re * c, im * s, im * c, re * s
        after = (a - b, e + f)
        before = (a + b, e - f)
        second = [2.0 * c * near - far for near, far in zip(before, (re, im))]
        factor = 2.0 - 4.0 * s * s
        left_factor = by_quad(factor, factor)
        left = [(by_quad(x, y), by_quad(z, w)) for x, y, z, w in zip(second, before, (re, im), after)]
        c, s = first_angle(v)
        c2, s2 = 1.0 - 2.0 * s * s, 2.0 * s * c
        factor = 2.0 * c2
        right_factor = by_quad(factor, factor)
        right = [
            (by_quad(c2, c), by_quad(jnp.ones_like(c), c)),
            (by_quad(-s2, -s), by_quad(jnp.zeros_like(s), s)),
        ]
        return [
            [
                (left[0][0][q], left[0][1][q], left[1][0][q], left[1][1][q], left_factor[q]),
                (right[0][0][q], right[0][1][q], right[1][0][q], right[1][1][q], right_factor[q]),
            ]
            for q in range(2)
        ]

    def place_of(quad_at):
        index = jnp.clip(quad_at * QUAD, 0, last + 1 - QUAD)
        place = (plan_ref[listed + index] >> (TAG_BITS + 2)) - first * (capacity // QUAD)
        return index, jnp.where((quad_at >= low) & (quad_at < high), place, spare)

    def settle(quad_at):
        moved = jnp.dot(recent[...], mover[...], preferred_element_type=jnp.float32)
        for q in range(2):
            _, place = place_of(quad_at + q)
            found[place] = moved[q * found.shape[1] : (q + 1) * found.shape[1]]

    def finish(seeds, quad_at, q):
        product = None
        for lanes in range(0, tiles * LANES, CHUNK):
            operands = []
            for side in seeds[::-1]:
                before, middle, before_imag, middle_imag, factor = [
                    x[:, lanes : lanes + CHUNK] for x in side
                ]
                operands.append(
                    jnp.concatenate(
                        sequence(before, middle, factor)
                        + sequence(before_imag, middle_imag, factor),
                        0,
                    )
                )
            term = lax.dot_general(
                operands[1], operands[0], (((1,), (1,)), ((), ())),
                preferred_element_type=jnp.float32,
            )
            product = term if product is None else product + term
        half = product.shape[0] // 2
        wholes = (
            product[:half, :LANES] - product[half:, LANES:],
            product[half:, :LANES] + product[:half, LANES:],
        )
        rows = []
        for whole in wholes:
            for j in range(0, STEPS, 4):
                four = [whole[(j + k) * GROUP : (j + k + 1) * GROUP] for k in range(4)]
                rows.append(jnp.concatenate([jnp.where(same_block, x, 0.0) for x in four], 1))
        size = found.shape[1]
        recent[pl.ds(q * size, size), :] = jnp.concatenate(rows, 0).astype(jnp.bfloat16)
        index, place = place_of(quad_at)
        tag = jnp.zeros((QUAD, LANES), jnp.int32)
        for b in range(QUAD):
            tag = jnp.where(quad_row == b, plan_ref[listed + index + b] & ((1 << TAG_BITS) - 1), tag)
        tags[place] = tag.astype(jnp.float32)

    def turn(g, seeds):
        quad_at = low + 2 * g
        settle(quad_at - 2)
        for q in range(2):
            finish(seeds[q], quad_at + q, q)
        return angles(quad_at + 2)

    turns = (high - low + 1) >> 1
    lax.fori_loop(0, turns, turn, angles(low))
    settle(low + 2 * turns - 2)

    shares = capacity // TAG_ROWS
    share = lax.broadcasted_iota(jnp.int32, (TAG_ROWS, LANES), 1) // (LANES // shares)

    def write_share(out_ref, base, slot, sent, n):
        for piece in range(PIECES // 2):
            part = []
            for k in range(4):
                value = found[slot + k, pl.ds(piece * GROUP, GROUP), :]
                part.append(jnp.where(n * 4 + k < sent, value, 0.0))
            first_two, last_two = [], []
            for even, odd in (part[:2], part[2:]):
                first_two.append(jnp.where(top, even, pltpu.roll(odd, QUAD, 0)))
                last_two.append(jnp.where(top, pltpu.roll(even, QUAD, 0), odd))
            for parity, two in enumerate((first_two, last_two)):
                put = base + (piece * 2 + parity) * capacity + n * TAG_ROWS
                out_ref[pl.ds(put, TAG_ROWS), :] = jnp.concatenate(two, 0).astype(jnp.bfloat16)

    for d, out_ref in enumerate(out_refs):
        for m in range(out_ref.shape[0] // message_rows(capacity)):
            base = m * message_rows(capacity)
            sent = start_of(first + d + m + 1) - start_of(first + d + m)
            slot = (d + m) * (capacity // QUAD)
            tag = jnp.zeros((TAG_ROWS, LANES), jnp.float32)
            for n in range(shares):
                at = slot + n * 4
                four = jnp.concatenate([tags[at + k] for k in range(4)], 0)
                tag = jnp.where(share == n, four, tag)
                write_share(out_ref, base, at, sent, n)
            out_ref[pl.ds(base + PIECES * capacity, TAG_ROWS), :] = tag.astype(jnp.bfloat16)


def message_rows(capacity):
    return PIECES * capacity + TAG_ROWS


def make_subgrids(first, outs, token, capacity, listed, plan, uv, res, vis):
    tiles = vis // LANES
    destinations = sum(outs)
    quads = destinations * capacity // QUAD
    vmem = pl.BlockSpec(memory_space=pltpu.VMEM)
    smem = pl.BlockSpec(memory_space=pltpu.SMEM)
    return pl.pallas_call(
        functools.partial(subgrid_kernel, first, destinations, capacity, listed),
        out_shape=[
            jax.ShapeDtypeStruct((n * message_rows(capacity), LANES), jnp.bfloat16) for n in outs
        ]
        + [jax.ShapeDtypeStruct(token.shape, token.dtype)],
        in_specs=[smem] + [vmem] * 3,
        out_specs=[vmem] * (len(outs) + 1),
        scratch_shapes=[
            pltpu.VMEM((4 * tiles * GROUP, LANES), jnp.float32),
            pltpu.VMEM((2 * FEATURE // SUB, 4 * LANES), jnp.bfloat16),
            pltpu.VMEM((quads + 1, FEATURE // SUB, LANES), jnp.float32),
            pltpu.VMEM((quads + 1, QUAD, LANES), jnp.float32),
            pltpu.VMEM((4 * LANES, LANES), jnp.bfloat16),
        ],
        compiler_params=pltpu.CompilerParams(vmem_limit_bytes=VMEM_LIMIT),
        cost_estimate=pl.CostEstimate(
            flops=quads * 32 * SUB * SUB * vis, bytes_accessed=16 * quads * FEATURE, transcendentals=0
        ),
        name="subgrids",
    )(plan, token, uv, res)


def pick_rows(hot, xs, part, out_ref, half):
    lane = lax.broadcasted_iota(jnp.int32, (GROUP, LANES), 1) >> 5
    for piece in range(PIECES):
        c, rows, parity = piece // 8, piece // 2 % 4 - 2 * half, piece % 2
        if not 0 <= rows < 2:
            continue
        part[...] = jnp.dot(hot[...], xs[piece], preferred_element_type=jnp.float32)
        for grp in range(4):
            given = [part[pl.ds(32 * jl + 8 * grp, 8), :] for jl in range(4)]
            for a in range(4):
                total = None
                for jl in range(4):
                    moved = given[jl]
                    if a != jl:
                        moved = pltpu.roll(moved, ((jl - a) % 4) * SUB, 1)
                    total = moved if total is None else jnp.where(lane == jl, moved, total)
                p = rows * 8 + a * 2 + parity
                out_ref[pl.ds(p * 64 + grp * 16 + c, 8, stride=2), :] = total


def first_half_kernel(capacity, *refs):
    x_refs, (out_ref, xs, hot, tags, part) = refs[:-5], refs[-5:]
    shares = capacity // TAG_ROWS
    at = 0
    for x_ref in x_refs:
        for base in range(0, x_ref.shape[0], message_rows(capacity)):
            for piece in range(PIECES):
                xs[piece, pl.ds(at, capacity), :] = x_ref[pl.ds(base + piece * capacity, capacity), :]
            tag = x_ref[pl.ds(base + PIECES * capacity, TAG_ROWS), :].astype(jnp.float32)
            for n in range(shares):
                column = n * (LANES // shares)
                tags[pl.ds(at + n * TAG_ROWS, TAG_ROWS), :] = jnp.broadcast_to(
                    tag[:, column : column + 1], (TAG_ROWS, LANES)
                )
            at += capacity
    wanted = lax.broadcasted_iota(jnp.int32, tags.shape, 1)
    wanted = ((wanted & 31) << 2) + (wanted >> 5) + 1
    hot[...] = jnp.where(tags[...] == wanted.astype(jnp.float32), 1.0, 0.0).T.astype(jnp.bfloat16)
    pick_rows(hot, xs, part, out_ref, 0)


def second_half_kernel(xs, hot, out_ref, part):
    pick_rows(hot, xs, part, out_ref, 1)


def sum_slots(arrived, capacity):
    rows = sum(x.shape[0] for x in arrived) // message_rows(capacity) * capacity
    vmem = pl.BlockSpec(memory_space=pltpu.VMEM)
    half = jax.ShapeDtypeStruct((SUB * 32, LANES), jnp.float32)
    params = pltpu.CompilerParams(vmem_limit_bytes=VMEM_LIMIT)
    part = pltpu.VMEM((SLOTS, LANES), jnp.float32)
    first, xs, hot = pl.pallas_call(
        functools.partial(first_half_kernel, capacity),
        out_shape=[
            half,
            jax.ShapeDtypeStruct((PIECES, rows, LANES), jnp.bfloat16),
            jax.ShapeDtypeStruct((SLOTS, rows), jnp.bfloat16),
        ],
        in_specs=[vmem] * len(arrived),
        out_specs=[vmem] * 3,
        scratch_shapes=[pltpu.VMEM((rows, LANES), jnp.float32), part],
        compiler_params=params,
        name="sum_first",
    )(*arrived)
    second = pl.pallas_call(
        second_half_kernel,
        out_shape=half,
        in_specs=[vmem] * 2,
        out_specs=vmem,
        scratch_shapes=[part],
        compiler_params=params,
        name="sum_second",
    )(xs, hot)
    return first, second


def add_kernel(at, mine_ref, theirs_ref, *refs):
    out_ref, total, sems = refs[-3:]
    step = total.shape[0] // sems.shape[0]
    copies = []
    for k in range(sems.shape[0]):
        here = pl.ds(k * step, step)
        total[here, :] = mine_ref[here, :] + theirs_ref[here, :]
        copy = pltpu.make_async_copy(
            total.at[here], out_ref.at[pl.ds(at + k * step, step)], sems.at[k]
        )
        copy.start()
        copies.append(copy)
    for copy in copies:
        copy.wait()


def add_half(at, mine, theirs, *whole):
    vmem, anywhere = pl.BlockSpec(memory_space=pltpu.VMEM), pl.BlockSpec(memory_space=pl.ANY)
    return pl.pallas_call(
        functools.partial(add_kernel, at),
        out_shape=jax.ShapeDtypeStruct((2 * mine.shape[0], LANES), jnp.float32),
        in_specs=[vmem, vmem] + [anywhere] * len(whole),
        out_specs=anywhere,
        scratch_shapes=[pltpu.VMEM(mine.shape, jnp.float32), pltpu.SemaphoreType.DMA((4,))],
        input_output_aliases={2: 0} if whole else {},
        compiler_params=pltpu.CompilerParams(vmem_limit_bytes=VMEM_LIMIT),
        name="add_half",
    )(mine, theirs, *whole)


def rows_of(array):
    blocks, parts, vis = array.shape
    tiles = vis // LANES
    split = array.reshape(blocks, parts, tiles, LANES)
    return split.transpose(0, 2, 1, 3).reshape(blocks * tiles * parts, LANES)


def sending_order(owners):
    return list(range(owners - 1, -1, -1))


def in_rows(array):
    return with_layout_constraint(array, Layout(major_to_minor=(0, 1)))


def local(residual, uv_offsets, counts, tile_of_block, slot_of_block, owner_map):
    blocks, _, vis = uv_offsets.shape
    owners = owner_map.shape[0]
    capacity = -(-max(CAP_MIN, 2 * blocks // owners) // 32) * 16
    core = lax.axis_index("samp")
    me = lax.axis_index(("blk", "tile"))
    swap = [(0, 1), (1, 0)]
    own = in_rows(rows_of(residual[0]))
    other = in_rows(lax.ppermute(own, "samp", swap))

    lists = jnp.concatenate([tile_of_block[:, 0], slot_of_block, counts, owner_map])
    lists = lax.optimization_barrier(lists)
    tile_ids, slots, counts, owner_map = [
        lists[k * blocks : min((k + 1) * blocks, 3 * blocks + owners)] for k in range(4)
    ]
    owner_range = jnp.arange(owners, dtype=jnp.int32)
    owner_ids = jnp.sum(
        jnp.where(tile_ids[:, None] == owner_range[None, :], owner_map[None, :], 0), 1
    )
    paired = owners <= PAIRED_MAX and owners & (owners - 1) == 0
    distances = sending_order(owners)
    offset = owner_ids
    if paired:
        offset = jnp.bitwise_xor(owner_ids, me)
        offset = sum(jnp.where(offset == d, k, 0) for k, d in enumerate(distances) if k)
    index = jnp.arange(blocks, dtype=jnp.int32)
    same = (offset[None, :] == offset[:, None]) & (index[None, :] < index[:, None])
    rank = jnp.sum(same.astype(jnp.int32), 1)
    mine = (rank & 1) == core
    counted = jnp.sum((mine[None, :] & (offset[None, :] == owner_range[:, None])).astype(jnp.int32), 1)
    quads = (counted + QUAD - 1) >> 2
    edges = jnp.arange(owners + 1, dtype=jnp.int32)
    start = jnp.sum(jnp.where(owner_range[None, :] < edges[:, None], quads[None, :], 0), 1)
    before = jnp.sum(jnp.where(owner_range[None, :] < offset[:, None], quads[None, :], 0), 1)
    place = jnp.where(mine, before * QUAD + (rank >> 1), -1)
    longest = ((blocks + owners) // 2 + owners * (QUAD - 1)) // GROUP * GROUP + GROUP
    wanted = jnp.arange(longest, dtype=jnp.int32)
    chosen = place[None, :] == wanted[:, None]
    block_and_count = (index << COUNT_BITS) + counts
    row_and_tag = ((offset * capacity + (rank >> 1)) << TAG_BITS) + slots + 1
    block = jnp.sum(jnp.where(chosen, block_and_count[None, :], 0), 1)
    row = jnp.sum(jnp.where(chosen, row_and_tag[None, :], 0), 1)

    subgrids = functools.partial(
        make_subgrids, capacity=capacity, listed=longest, plan=jnp.concatenate([block, row, start]),
        uv=rows_of(uv_offsets), res=own.astype(jnp.float32) + other.astype(jnp.float32), vis=vis,
    )
    token = jnp.zeros((GROUP, LANES), jnp.int32)
    if paired:
        rows = []
        for first, last in zip(CALLS[:-1], CALLS[1:]):
            first, last = owners * first // CALLS[-1], owners * last // CALLS[-1]
            if first < last:
                *more, token = subgrids(first, (1,) * (last - first), token)
                rows += more
        arrived = []
        for distance, piece in zip(distances, rows):
            if distance:
                pairs = [(k, k ^ distance) for k in range(owners)]
                piece = lax.ppermute(piece, ("blk", "tile"), pairs)
            arrived.append(piece)
    else:
        each = max(d for d in range(1, 17) if owners % d == 0)
        rows = [subgrids(k, (each,), token)[0] for k in range(0, owners, each)]
        rows = jnp.concatenate(rows, 0).reshape(owners, message_rows(capacity), LANES)
        rows = lax.all_to_all(rows, ("blk", "tile"), split_axis=0, concat_axis=0, tiled=True)
        arrived = [rows.reshape(owners * message_rows(capacity), LANES)]
    first, second = sum_slots(arrived, capacity)
    whole = add_half(0, first, lax.ppermute(first, "samp", swap))
    whole = add_half(first.shape[0], second, lax.ppermute(second, "samp", swap), whole)
    whole = whole.reshape(SUB, SLOTS // 4, 2, LANES).transpose(0, 2, 1, 3)
    return whole.reshape(SUB, 2, SLOTS * SUB)


def solution(mesh):
    in_specs = (
        P("samp", ("cuts", "blk", "tile"), None, None),
        P(("cuts", "blk", "tile"), None, None),
        P(("cuts", "blk", "tile")),
        P(("cuts", "blk", "tile"), None),
        P(("cuts", "blk", "tile")),
        P(),
    )
    out_specs = P(("cuts", "blk", "tile"), None, None)
    return jax.shard_map(local, mesh=mesh, in_specs=in_specs, out_specs=out_specs, check_vma=False)
```

```python
import functools

import jax
import jax.numpy as jnp
import numpy as np
from jax import lax
from jax.experimental import pallas as pl
from jax.experimental.layout import Layout, with_layout_constraint
from jax.experimental.pallas import tpu as pltpu
from jax.sharding import PartitionSpec as P

SUB = 32
STEPS = SUB // 2
SLOTS = 128
LANES = 128
FEATURE = 2 * SUB * SUB
PIECES = FEATURE // LANES
CAP_MIN = 8
GROUP = 8
QUAD = 4
TAG_ROWS = 16
COUNT_BITS = 12
TAG_BITS = 8
CHUNK = 4 * LANES
PAIRED_MAX = 16
CALLS = (0, 2, 5, 7, 8)
VMEM_LIMIT = 48 * 1024 * 1024


def turn_coefficients():
    knots = np.cos(np.pi * (np.arange(400) + 0.5) / 400)
    cheb = np.polynomial.chebyshev
    even = cheb.cheb2poly(cheb.chebfit(knots, np.cos(np.pi * knots), 12))[0::2]
    odd = cheb.cheb2poly(cheb.chebfit(knots, np.sin(np.pi * knots), 13))[1::2]
    return [float(x) for x in even], [float(x) for x in odd]


COS_COEF, SIN_COEF = turn_coefficients()


def horner(coef, x):
    total = coef[-1] * x + coef[-2]
    for value in coef[-3::-1]:
        total = total * x + value
    return total


def first_angle(offset):
    y = offset * (1.0 / STEPS)
    x = y * y
    return horner(COS_COEF, x), horner(SIN_COEF, x) * y


def tile_of(value, t):
    return value[:, t * LANES : (t + 1) * LANES]


def by_quad(even, odd):
    top = lax.broadcasted_iota(jnp.int32, even.shape, 0) < QUAD
    return (
        jnp.where(top, even, pltpu.roll(odd, QUAD, 0)),
        jnp.where(top, pltpu.roll(even, QUAD, 0), odd),
    )


def sequence(before, middle, factor):
    def pair(*two):
        return jnp.concatenate(two, 0).astype(jnp.bfloat16)

    up, down = [], []
    last, value = before, middle
    for _ in range(STEPS // 4):
        after = factor * value - last
        up.append(pair(value, after))
        last, value = after, factor * after - value
    last, value = middle, before
    for _ in range(STEPS // 4):
        after = factor * value - last
        down.append(pair(after, value))
        last, value = after, factor * after - value
    return down[::-1] + up


def subgrid_kernel(
    first, destinations, capacity, listed, plan_ref, token_ref, uv_ref, res_ref, *refs
):
    out_refs, (next_ref, gathered, recent, found, tags, mover) = refs[:-6], refs[-6:]
    next_ref[...] = jnp.zeros_like(next_ref)
    tiles = gathered.shape[0] // (4 * GROUP)
    spare = destinations * capacity // QUAD

    def start_of(destination):
        return plan_ref[2 * listed + destination]

    low, high = start_of(first), start_of(first + destinations)
    last = listed - 1
    vis_at = lax.broadcasted_iota(jnp.int32, (2 * tiles, LANES), 1) + LANES * (
        lax.broadcasted_iota(jnp.int32, (2 * tiles, LANES), 0) >> 1
    )
    same_block = (
        lax.broadcasted_iota(jnp.int32, (GROUP, LANES), 0) & (QUAD - 1)
        == lax.broadcasted_iota(jnp.int32, (GROUP, LANES), 1) & (QUAD - 1)
    )
    quad_row = lax.broadcasted_iota(jnp.int32, (QUAD, LANES), 0)
    top = lax.broadcasted_iota(jnp.int32, (GROUP, LANES), 0) < QUAD

    source = lax.broadcasted_iota(jnp.int32, mover.shape, 0)
    lane = lax.broadcasted_iota(jnp.int32, mover.shape, 1)
    moves = (source >> 7 == lane >> 5) & ((source & (LANES - 1)) >> 2 == lane & (SUB - 1))
    mover[...] = jnp.where(moves, 1.0, 0.0).astype(jnp.bfloat16)
    tags[...] = jnp.zeros_like(tags)

    def angles(quad_at):
        for i in range(GROUP):
            packed = plan_ref[jnp.minimum(quad_at * QUAD + i, last)]
            block, count = packed >> COUNT_BITS, packed & ((1 << COUNT_BITS) - 1)
            at = pl.ds(pl.multiple_of(block * 2 * tiles, 2 * tiles), 2 * tiles)
            both = jnp.where(vis_at < count, res_ref[at, :], 0.0)
            gathered[pl.ds(i, 2 * tiles, stride=GROUP), :] = uv_ref[at, :]
            gathered[pl.ds(2 * tiles * GROUP + i, 2 * tiles, stride=GROUP), :] = both
        u, v, re, im = [
            jnp.concatenate(
                [
                    gathered[pl.ds(((k // 2) * 2 * tiles + 2 * t + k % 2) * GROUP, GROUP), :]
                    for t in range(tiles)
                ],
                1,
            )
            for k in range(4)
        ]
        c, s = first_angle(u)
        a, b, e, f = re * c, im * s, im * c, re * s
        after = (a - b, e + f)
        before = (a + b, e - f)
        second = [2.0 * c * near - far for near, far in zip(before, (re, im))]
        factor = 2.0 - 4.0 * s * s
        left_factor = by_quad(factor, factor)
        left = [(by_quad(x, y), by_quad(z, w)) for x, y, z, w in zip(second, before, (re, im), after)]
        c, s = first_angle(v)
        c2, s2 = 1.0 - 2.0 * s * s, 2.0 * s * c
        factor = 2.0 * c2
        right_factor = by_quad(factor, factor)
        right = [
            (by_quad(c2, c), by_quad(jnp.ones_like(c), c)),
            (by_quad(-s2, -s), by_quad(jnp.zeros_like(s), s)),
        ]
        return [
            [
                (left[0][0][q], left[0][1][q], left[1][0][q], left[1][1][q], left_factor[q]),
                (right[0][0][q], right[0][1][q], right[1][0][q], right[1][1][q], right_factor[q]),
            ]
            for q in range(2)
        ]

    def place_of(quad_at):
        index = jnp.clip(quad_at * QUAD, 0, last + 1 - QUAD)
        place = (plan_ref[listed + index] >> (TAG_BITS + 2)) - first * (capacity // QUAD)
        return index, jnp.where((quad_at >= low) & (quad_at < high), place, spare)

    def settle(quad_at):
        moved = jnp.dot(recent[...], mover[...], preferred_element_type=jnp.float32)
        for q in range(2):
            _, place = place_of(quad_at + q)
            found[place] = moved[q * found.shape[1] : (q + 1) * found.shape[1]]

    def finish(seeds, quad_at, q):
        product = None
        for lanes in range(0, tiles * LANES, CHUNK):
            operands = []
            for side in seeds[::-1]:
                before, middle, before_imag, middle_imag, factor = [
                    x[:, lanes : lanes + CHUNK] for x in side
                ]
                operands.append(
                    jnp.concatenate(
                        sequence(before, middle, factor)
                        + sequence(before_imag, middle_imag, factor),
                        0,
                    )
                )
            term = lax.dot_general(
                operands[1], operands[0], (((1,), (1,)), ((), ())),
                preferred_element_type=jnp.float32,
            )
            product = term if product is None else product + term
        half = product.shape[0] // 2
        wholes = (
            product[:half, :LANES] - product[half:, LANES:],
            product[half:, :LANES] + product[:half, LANES:],
        )
        rows = []
        for whole in wholes:
            for j in range(0, STEPS, 4):
                four = [whole[(j + k) * GROUP : (j + k + 1) * GROUP] for k in range(4)]
                rows.append(jnp.concatenate([jnp.where(same_block, x, 0.0) for x in four], 1))
        size = found.shape[1]
        recent[pl.ds(q * size, size), :] = jnp.concatenate(rows, 0).astype(jnp.bfloat16)
        index, place = place_of(quad_at)
        tag = jnp.zeros((QUAD, LANES), jnp.int32)
        for b in range(QUAD):
            tag = jnp.where(quad_row == b, plan_ref[listed + index + b] & ((1 << TAG_BITS) - 1), tag)
        tags[place] = tag.astype(jnp.float32)

    def turn(g, seeds):
        quad_at = low + 2 * g
        settle(quad_at - 2)
        for q in range(2):
            finish(seeds[q], quad_at + q, q)
        return angles(quad_at + 2)

    turns = (high - low + 1) >> 1
    lax.fori_loop(0, turns, turn, angles(low))
    settle(low + 2 * turns - 2)

    shares = capacity // TAG_ROWS
    share = lax.broadcasted_iota(jnp.int32, (TAG_ROWS, LANES), 1) // (LANES // shares)

    def write_share(out_ref, base, slot, sent, n):
        for piece in range(PIECES // 2):
            part = []
            for k in range(4):
                value = found[slot + k, pl.ds(piece * GROUP, GROUP), :]
                part.append(jnp.where(n * 4 + k < sent, value, 0.0))
            first_two, last_two = [], []
            for even, odd in (part[:2], part[2:]):
                first_two.append(jnp.where(top, even, pltpu.roll(odd, QUAD, 0)))
                last_two.append(jnp.where(top, pltpu.roll(even, QUAD, 0), odd))
            for parity, two in enumerate((first_two, last_two)):
                put = base + (piece * 2 + parity) * capacity + n * TAG_ROWS
                out_ref[pl.ds(put, TAG_ROWS), :] = jnp.concatenate(two, 0).astype(jnp.bfloat16)

    for d, out_ref in enumerate(out_refs):
        for m in range(out_ref.shape[0] // message_rows(capacity)):
            base = m * message_rows(capacity)
            sent = start_of(first + d + m + 1) - start_of(first + d + m)
            slot = (d + m) * (capacity // QUAD)
            tag = jnp.zeros((TAG_ROWS, LANES), jnp.float32)
            for n in range(shares):
                at = slot + n * 4
                four = jnp.concatenate([tags[at + k] for k in range(4)], 0)
                tag = jnp.where(share == n, four, tag)
                write_share(out_ref, base, at, sent, n)
            out_ref[pl.ds(base + PIECES * capacity, TAG_ROWS), :] = tag.astype(jnp.bfloat16)


def message_rows(capacity):
    return PIECES * capacity + TAG_ROWS


def make_subgrids(first, outs, token, capacity, listed, plan, uv, res, vis):
    tiles = vis // LANES
    destinations = sum(outs)
    quads = destinations * capacity // QUAD
    vmem = pl.BlockSpec(memory_space=pltpu.VMEM)
    smem = pl.BlockSpec(memory_space=pltpu.SMEM)
    return pl.pallas_call(
        functools.partial(subgrid_kernel, first, destinations, capacity, listed),
        out_shape=[
            jax.ShapeDtypeStruct((n * message_rows(capacity), LANES), jnp.bfloat16) for n in outs
        ]
        + [jax.ShapeDtypeStruct(token.shape, token.dtype)],
        in_specs=[smem] + [vmem] * 3,
        out_specs=[vmem] * (len(outs) + 1),
        scratch_shapes=[
            pltpu.VMEM((4 * tiles * GROUP, LANES), jnp.float32),
            pltpu.VMEM((2 * FEATURE // SUB, 4 * LANES), jnp.bfloat16),
            pltpu.VMEM((quads + 1, FEATURE // SUB, LANES), jnp.float32),
            pltpu.VMEM((quads + 1, QUAD, LANES), jnp.float32),
            pltpu.VMEM((4 * LANES, LANES), jnp.bfloat16),
        ],
        compiler_params=pltpu.CompilerParams(vmem_limit_bytes=VMEM_LIMIT),
        cost_estimate=pl.CostEstimate(
            flops=quads * 32 * SUB * SUB * vis, bytes_accessed=16 * quads * FEATURE, transcendentals=0
        ),
        name="subgrids",
    )(plan, token, uv, res)


def pick_rows(hot, xs, part, out_ref, half):
    lane = lax.broadcasted_iota(jnp.int32, (GROUP, LANES), 1) >> 5
    for piece in range(PIECES):
        c, rows, parity = piece // 8, piece // 2 % 4 - 2 * half, piece % 2
        if not 0 <= rows < 2:
            continue
        part[...] = jnp.dot(hot[...], xs[piece], preferred_element_type=jnp.float32)
        for grp in range(4):
            given = [part[pl.ds(32 * jl + 8 * grp, 8), :] for jl in range(4)]
            for a in range(4):
                total = None
                for jl in range(4):
                    moved = given[jl]
                    if a != jl:
                        moved = pltpu.roll(moved, ((jl - a) % 4) * SUB, 1)
                    total = moved if total is None else jnp.where(lane == jl, moved, total)
                p = rows * 8 + a * 2 + parity
                out_ref[pl.ds(p * 64 + grp * 16 + c, 8, stride=2), :] = total


def first_half_kernel(capacity, *refs):
    x_refs, (out_ref, xs, hot, tags, part) = refs[:-5], refs[-5:]
    shares = capacity // TAG_ROWS
    at = 0
    for x_ref in x_refs:
        for base in range(0, x_ref.shape[0], message_rows(capacity)):
            for piece in range(PIECES):
                xs[piece, pl.ds(at, capacity), :] = x_ref[pl.ds(base + piece * capacity, capacity), :]
            tag = x_ref[pl.ds(base + PIECES * capacity, TAG_ROWS), :].astype(jnp.float32)
            for n in range(shares):
                column = n * (LANES // shares)
                tags[pl.ds(at + n * TAG_ROWS, TAG_ROWS), :] = jnp.broadcast_to(
                    tag[:, column : column + 1], (TAG_ROWS, LANES)
                )
            at += capacity
    wanted = lax.broadcasted_iota(jnp.int32, tags.shape, 1)
    wanted = ((wanted & 31) << 2) + (wanted >> 5) + 1
    hot[...] = jnp.where(tags[...] == wanted.astype(jnp.float32), 1.0, 0.0).T.astype(jnp.bfloat16)
    pick_rows(hot, xs, part, out_ref, 0)


def second_half_kernel(xs, hot, out_ref, part):
    pick_rows(hot, xs, part, out_ref, 1)


def sum_slots(arrived, capacity):
    rows = sum(x.shape[0] for x in arrived) // message_rows(capacity) * capacity
    vmem = pl.BlockSpec(memory_space=pltpu.VMEM)
    half = jax.ShapeDtypeStruct((SUB * 32, LANES), jnp.float32)
    params = pltpu.CompilerParams(vmem_limit_bytes=VMEM_LIMIT)
    part = pltpu.VMEM((SLOTS, LANES), jnp.float32)
    first, xs, hot = pl.pallas_call(
        functools.partial(first_half_kernel, capacity),
        out_shape=[
            half,
            jax.ShapeDtypeStruct((PIECES, rows, LANES), jnp.bfloat16),
            jax.ShapeDtypeStruct((SLOTS, rows), jnp.bfloat16),
        ],
        in_specs=[vmem] * len(arrived),
        out_specs=[vmem] * 3,
        scratch_shapes=[pltpu.VMEM((rows, LANES), jnp.float32), part],
        compiler_params=params,
        name="sum_first",
    )(*arrived)
    second = pl.pallas_call(
        second_half_kernel,
        out_shape=half,
        in_specs=[vmem] * 2,
        out_specs=vmem,
        scratch_shapes=[part],
        compiler_params=params,
        name="sum_second",
    )(xs, hot)
    return first, second


def add_kernel(at, mine_ref, theirs_ref, *refs):
    out_ref, total, sems = refs[-3:]
    step = total.shape[0] // sems.shape[0]
    copies = []
    for k in range(sems.shape[0]):
        here = pl.ds(k * step, step)
        total[here, :] = mine_ref[here, :] + theirs_ref[here, :]
        copy = pltpu.make_async_copy(
            total.at[here], out_ref.at[pl.ds(at + k * step, step)], sems.at[k]
        )
        copy.start()
        copies.append(copy)
    for copy in copies:
        copy.wait()


def add_half(at, mine, theirs, *whole):
    vmem, anywhere = pl.BlockSpec(memory_space=pltpu.VMEM), pl.BlockSpec(memory_space=pl.ANY)
    return pl.pallas_call(
        functools.partial(add_kernel, at),
        out_shape=jax.ShapeDtypeStruct((2 * mine.shape[0], LANES), jnp.float32),
        in_specs=[vmem, vmem] + [anywhere] * len(whole),
        out_specs=anywhere,
        scratch_shapes=[pltpu.VMEM(mine.shape, jnp.float32), pltpu.SemaphoreType.DMA((4,))],
        input_output_aliases={2: 0} if whole else {},
        compiler_params=pltpu.CompilerParams(vmem_limit_bytes=VMEM_LIMIT),
        name="add_half",
    )(mine, theirs, *whole)


def rows_of(array):
    blocks, parts, vis = array.shape
    tiles = vis // LANES
    split = array.reshape(blocks, parts, tiles, LANES)
    return split.transpose(0, 2, 1, 3).reshape(blocks * tiles * parts, LANES)


def sending_order(owners):
    return list(range(owners - 1, -1, -1))


def in_rows(array):
    return with_layout_constraint(array, Layout(major_to_minor=(0, 1)))


def local(residual, uv_offsets, counts, tile_of_block, slot_of_block, owner_map):
    blocks, _, vis = uv_offsets.shape
    owners = owner_map.shape[0]
    capacity = -(-max(CAP_MIN, 2 * blocks // owners) // 32) * 16
    core = lax.axis_index("samp")
    me = lax.axis_index(("blk", "tile"))
    swap = [(0, 1), (1, 0)]
    own = in_rows(rows_of(residual[0]))
    other = in_rows(lax.ppermute(own, "samp", swap))

    lists = jnp.concatenate([tile_of_block[:, 0], slot_of_block, counts, owner_map])
    lists = lax.optimization_barrier(lists)
    tile_ids, slots, counts, owner_map = [
        lists[k * blocks : min((k + 1) * blocks, 3 * blocks + owners)] for k in range(4)
    ]
    owner_range = jnp.arange(owners, dtype=jnp.int32)
    owner_ids = jnp.sum(
        jnp.where(tile_ids[:, None] == owner_range[None, :], owner_map[None, :], 0), 1
    )
    paired = owners <= PAIRED_MAX and owners & (owners - 1) == 0
    distances = sending_order(owners)
    offset = owner_ids
    if paired:
        offset = jnp.bitwise_xor(owner_ids, me)
        offset = sum(jnp.where(offset == d, k, 0) for k, d in enumerate(distances) if k)
    index = jnp.arange(blocks, dtype=jnp.int32)
    same = (offset[None, :] == offset[:, None]) & (index[None, :] < index[:, None])
    rank = jnp.sum(same.astype(jnp.int32), 1)
    mine = (rank & 1) == core
    counted = jnp.sum((mine[None, :] & (offset[None, :] == owner_range[:, None])).astype(jnp.int32), 1)
    quads = (counted + QUAD - 1) >> 2
    edges = jnp.arange(owners + 1, dtype=jnp.int32)
    start = jnp.sum(jnp.where(owner_range[None, :] < edges[:, None], quads[None, :], 0), 1)
    before = jnp.sum(jnp.where(owner_range[None, :] < offset[:, None], quads[None, :], 0), 1)
    place = jnp.where(mine, before * QUAD + (rank >> 1), -1)
    longest = ((blocks + owners) // 2 + owners * (QUAD - 1)) // GROUP * GROUP + GROUP
    wanted = jnp.arange(longest, dtype=jnp.int32)
    chosen = place[None, :] == wanted[:, None]
    block_and_count = (index << COUNT_BITS) + counts
    row_and_tag = ((offset * capacity + (rank >> 1)) << TAG_BITS) + slots + 1
    block = jnp.sum(jnp.where(chosen, block_and_count[None, :], 0), 1)
    row = jnp.sum(jnp.where(chosen, row_and_tag[None, :], 0), 1)

    subgrids = functools.partial(
        make_subgrids, capacity=capacity, listed=longest, plan=jnp.concatenate([block, row, start]),
        uv=rows_of(uv_offsets), res=own.astype(jnp.float32) + other.astype(jnp.float32), vis=vis,
    )
    token = jnp.zeros((GROUP, LANES), jnp.int32)
    if paired:
        rows = []
        for first, last in zip(CALLS[:-1], CALLS[1:]):
            first, last = owners * first // CALLS[-1], owners * last // CALLS[-1]
            if first < last:
                *more, token = subgrids(first, (1,) * (last - first), token)
                rows += more
        arrived = []
        for distance, piece in zip(distances, rows):
            if distance:
                pairs = [(k, k ^ distance) for k in range(owners)]
                piece = lax.ppermute(piece, ("blk", "tile"), pairs)
            arrived.append(piece)
    else:
        each = max(d for d in range(1, 17) if owners % d == 0)
        rows = [subgrids(k, (each,), token)[0] for k in range(0, owners, each)]
        rows = jnp.concatenate(rows, 0).reshape(owners, message_rows(capacity), LANES)
        rows = lax.all_to_all(rows, ("blk", "tile"), split_axis=0, concat_axis=0, tiled=True)
        arrived = [rows.reshape(owners * message_rows(capacity), LANES)]
    first, second = sum_slots(arrived, capacity)
    whole = add_half(0, first, lax.ppermute(first, "samp", swap))
    whole = add_half(first.shape[0], second, lax.ppermute(second, "samp", swap), whole)
    whole = whole.reshape(SUB, SLOTS // 4, 2, LANES).transpose(0, 2, 1, 3)
    return whole.reshape(SUB, 2, SLOTS * SUB)


def solution(mesh):
    in_specs = (
        P("samp", ("cuts", "blk", "tile"), None, None),
        P(("cuts", "blk", "tile"), None, None),
        P(("cuts", "blk", "tile")),
        P(("cuts", "blk", "tile"), None),
        P(("cuts", "blk", "tile")),
        P(),
    )
    out_specs = P(("cuts", "blk", "tile"), None, None)
    return jax.shard_map(local, mesh=mesh, in_specs=in_specs, out_specs=out_specs, check_vma=False)
```
